32 devices in a mesh: dp: 8 (over z, y), bank: 4 (over x, core).
Axes of the slice: x: 2, y: 2, z: 4, core: 2. Of those that a mesh axis runs over, the one named last changes fastest.
Arguments:
- char_ids: int32 [1024, 4, 50], P('dp'), may hold values from 0 to 261
- resets: int32 [1024, 4], P(('dp', 'bank')), may hold values 0 or 1
- out_grad: bfloat16 [1024, 4, 1024], P(('dp', 'bank')), may hold values from -6 to 6
- char_table: bfloat16 [262, 16], replicated, may hold values from -6 to 6
- conv_weight: bfloat16 [4, 7, 16, 1024], P('bank'), may hold values from -0.75 to 0.75
- conv_bias: bfloat16 [4, 1024], P('bank'), may hold values from -3 to 3
- highway_weight: bfloat16 [2, 2048, 4096], P(None, ('dp', 'bank')), may hold values from -0.125 to 0.125
- highway_bias: bfloat16 [2, 4096], P(None, ('dp', 'bank')), may hold values from -3 to 3
- proj_weight: bfloat16 [2048, 512], P(('dp', 'bank')), may hold values from -0.125 to 0.125
- proj_bias: bfloat16 [512], P(('dp', 'bank')), may hold values from -3 to 3
- lstm_weight: bfloat16 [2, 1024, 16384], P(None, ('dp', 'bank')), may hold values from -0.1875 to 0.1875
- lstm_bias: bfloat16 [2, 16384], P(None, ('dp', 'bank')), may hold values from -3 to 3
- lstm_proj: bfloat16 [2, 4096, 512], P(None, None, ('dp', 'bank')), may hold values from -0.25 to 0.25
Outputs:
- table_grad: float32 [262, 16], replicated
- conv_weight_grad: float32 [4, 7, 16, 1024], P('bank')
- conv_bias_grad: float32 [4, 1024], P('bank')
- highway_weight_grad: float32 [2, 2048, 4096], P(None, ('dp', 'bank'))
- highway_bias_grad: float32 [2, 4096], P(None, ('dp', 'bank'))
- proj_weight_grad: float32 [2048, 512], P(('dp', 'bank'))
- proj_bias_grad: float32 [512], P(('dp', 'bank'))
- lstm_weight_grad: float32 [2, 1024, 16384], P(None, ('dp', 'bank'))
- lstm_bias_grad: float32 [2, 16384], P(None, ('dp', 'bank'))
- lstm_proj_grad: float32 [2, 4096, 512], P(None, None, ('dp', 'bank'))
The draws below stay inside these ranges and needn't reach their ends.
All inputs are finite; a program needn't handle non-finite values. No bound on the sum of `resets` on one device may be relied on, other than what follows from the above.
Results may differ from the reference program's by a relative error of at most 0.015.
Values may be sent and summed in bfloat16 or wider, within the bound.
A program may use at most 576 MiB of HBM per device.

```python
import math
import jax
import jax.numpy as jnp
from jax import lax

CHAR_IDS = 262
CHAR_DIM = 16
BANK_COLS = 1024
PROJ = 512
CELL = 4096
CHARS = 50
STEPS = 4
FILTERS = 2048
STREAMS = 1024


def touch_ends(values, key, least, top_value):
    shape = values.shape
    place = [jax.random.randint(jax.random.fold_in(key, axis), (), 0, shape[axis]) for axis in range(len(shape))]
    values = values.at[tuple(place)].set(least)
    longest = shape.index(max(shape))
    place[longest] = (place[longest] + 1) % shape[longest]
    return values.at[tuple(place)].set(top_value)


def block_scale(rng, shape, cuts, least, largest):
    def one(axis_at, blocks):
        draws = jax.random.uniform(jax.random.fold_in(jax.random.fold_in(rng, 6), axis_at), (blocks,), jnp.float32, least / len(cuts), largest / len(cuts))
        return jnp.repeat(jnp.exp(draws), shape[axis_at] // blocks).reshape((-1,) + (1,) * (len(shape) - axis_at - 1))

    factor_of = one(*cuts[0])
    for cut in cuts[1:]:
        factor_of = factor_of * one(*cut)
    return factor_of


def normal_values(own_key, dims, deviation, limit, cuts=(), kind=jnp.bfloat16):
    factor_of = block_scale(own_key, dims, cuts, -0.22, 0.18) if cuts else 1.0
    array = jax.random.normal(own_key, dims, jnp.float32) * deviation * factor_of
    return jnp.minimum(jnp.maximum(array, -limit), limit).astype(kind)


def setup_inputs(seed: int = 0) -> dict:
    key_of = jax.random.split(jax.random.key(seed), 14)
    return {
        "char_ids": touch_ends(jax.random.randint(key_of[0], (STREAMS, STEPS, CHARS), 0, CHAR_IDS), jax.random.fold_in(key_of[0], 1), 0, CHAR_IDS - 1).astype(jnp.int32),
        "resets": touch_ends((jax.random.randint(key_of[1], (STREAMS, STEPS), 0, 8) < 1).astype(jnp.int32), jax.random.fold_in(key_of[1], 1), 0, 1),
        "out_grad": normal_values(key_of[2], (STREAMS, STEPS, 2 * PROJ), 1.0, 6.0, ((0, 32),)),
        "char_table": normal_values(key_of[3], (CHAR_IDS, CHAR_DIM), 1.0, 6.0),
        "conv_weight": normal_values(key_of[4], (4, 7, CHAR_DIM, BANK_COLS), (4 * CHAR_DIM) ** -0.5, 0.75, ((0, 4),)),
        "conv_bias": normal_values(key_of[5], (4, BANK_COLS), 0.5, 3.0, ((0, 4),)),
        "highway_weight": normal_values(key_of[6], (2, FILTERS, 2 * FILTERS), FILTERS ** -0.5, 0.125, ((1, 32),)),
        "highway_bias": normal_values(key_of[7], (2, 2 * FILTERS), 0.5, 3.0, ((1, 32),)),
        "proj_weight": normal_values(key_of[8], (FILTERS, PROJ), FILTERS ** -0.5, 0.125, ((0, 32),)),
        "proj_bias": normal_values(key_of[9], (PROJ,), 0.5, 3.0, ((0, 32),)),
        "lstm_weight": normal_values(key_of[10], (2, 2 * PROJ, 4 * CELL), (2 * PROJ) ** -0.5, 0.1875, ((1, 32),)),
        "lstm_bias": normal_values(key_of[11], (2, 4 * CELL), 0.5, 3.0, ((1, 32),)),
        "lstm_proj": normal_values(key_of[12], (2, CELL, PROJ), (CELL // 8) ** -0.5, 0.25, ((2, 32),)),
    }


@jax.custom_vjp
def low(v):
    return lax.optimization_barrier(v.astype(jnp.bfloat16)).astype(jnp.float32)

@jax.custom_vjp
def low_back(v):
    return v

def low_keep(v):
    return (low(v), None)

def low_pass(kept, grad):
    return (grad,)

def back_keep(v):
    return (v, None)

def back_low(kept, grad):
    return (low(grad),)
low.defvjp(low_keep, low_pass)
low_back.defvjp(back_keep, back_low)

def matmul(former, latter):
    return jnp.dot(former, latter, precision=lax.Precision.HIGHEST, preferred_element_type=jnp.float32)

def filter_layout():
    return [(1, 0, 0, BANK_COLS // 32), (2, 0, BANK_COLS // 32, BANK_COLS // 32), (3, 0, BANK_COLS // 16, BANK_COLS // 16), (4, 0, BANK_COLS // 8, BANK_COLS // 8), (5, 1, 0, BANK_COLS // 4), (6, 2, 0, BANK_COLS // 2), (7, 3, 0, BANK_COLS)]

def log_sum_exp(values):
    highest = lax.optimization_barrier(jnp.max(values, axis=1, keepdims=True))
    return highest[:, 0, :] + jnp.log(lax.optimization_barrier(jnp.sum(jnp.exp(values - highest), axis=1)))

def char_block(block_ids, char_table, conv_weight, conv_bias):
    row_count = block_ids.shape[0]
    embedded = jnp.take(char_table, block_ids, axis=0)
    pieces = []
    for filter_width, bank_index, first_col, columns in filter_layout():
        positions = CHARS - filter_width + 1
        windows = jnp.concatenate([embedded[:, offset:offset + positions, :] for offset in range(filter_width)], axis=2)
        kernel = conv_weight[bank_index, :filter_width, :, first_col:first_col + columns].reshape(filter_width * CHAR_DIM, columns)
        conv_out = matmul(windows.reshape(row_count * positions, filter_width * CHAR_DIM), kernel) + conv_bias[bank_index, first_col:first_col + columns]
        conv_out = low_back(conv_out).reshape(row_count, positions, columns)
        pieces.append(jax.nn.silu(log_sum_exp(conv_out) - math.log(positions)))
    return low_back(low(jnp.concatenate(pieces, axis=1)))

def layer_forward(char_ids, resets, char_table, conv_weight, conv_bias, highway_weight, highway_bias, proj_weight, proj_bias, lstm_weight, lstm_bias, lstm_proj):
    block_count = math.gcd(STREAMS, 64)
    id_blocks = char_ids.reshape(block_count, STREAMS * STEPS // block_count, CHARS)
    features = lax.map(jax.checkpoint(lambda block_ids: char_block(block_ids, char_table, conv_weight, conv_bias)), id_blocks)
    hidden = features.reshape(STREAMS * STEPS, FILTERS)
    for highway_level in range(2):
        operand = hidden if highway_level == 0 else low(hidden)
        mixed = low_back(matmul(operand, highway_weight[highway_level]) + highway_bias[highway_level])
        carry_gate = jax.nn.sigmoid(mixed[:, FILTERS:])
        hidden = carry_gate * hidden + (1.0 - carry_gate) * jax.nn.silu(mixed[:, :FILTERS])
    lstm_in = low(low_back(matmul(low(hidden), proj_weight) + proj_bias)).reshape(STREAMS, STEPS, PROJ)
    cleared = resets.astype(jnp.float32)
    keep_forward = 1.0 - cleared
    keep_backward = 1.0 - jnp.concatenate([cleared[:, 1:], jnp.zeros((STREAMS, 1), jnp.float32)], axis=1)
    results = []
    for direction in range(2):
        keep_mask = keep_forward if direction == 0 else keep_backward
        weight_in = lstm_weight[direction, :PROJ]
        weight_rec = lstm_weight[direction, PROJ:]
        bias_row = lstm_bias[direction]
        proj_mat = lstm_proj[direction]

        def lstm_step(carry, sliced):
            cell_state, hidden_state = carry
            token_in, keep_now = sliced
            keep_col = keep_now[:, None]
            cell_start = cell_state * keep_col
            state_start = hidden_state * keep_col
            gates_pre = low_back(matmul(token_in, weight_in) + bias_row + matmul(state_start, weight_rec))
            in_gate = jax.nn.sigmoid(gates_pre[:, :CELL])
            forget_gate = jax.nn.sigmoid(gates_pre[:, CELL:2 * CELL])
            candidate = jnp.tanh(gates_pre[:, 2 * CELL:3 * CELL])
            out_gate = jax.nn.sigmoid(gates_pre[:, 3 * CELL:])
            cell_new = 3.0 * jnp.tanh((forget_gate * cell_start + in_gate * candidate) / 3.0)
            full_state = low(out_gate * jnp.tanh(cell_new))
            projected = low_back(matmul(full_state, proj_mat))
            state_new = low(3.0 * jnp.tanh(projected / 3.0))
            return ((cell_new, state_new), state_new)
        initial = (jnp.zeros((STREAMS, CELL), jnp.float32), jnp.zeros((STREAMS, PROJ), jnp.float32))
        sequence = (jnp.swapaxes(lstm_in, 0, 1), jnp.swapaxes(keep_mask, 0, 1))
        states = lax.scan(jax.checkpoint(lstm_step), initial, sequence, reverse=direction == 1)[1]
        results.append(jnp.swapaxes(states, 0, 1))
    return jnp.concatenate(results, axis=2)

def reference(char_ids, resets, out_grad, char_table, conv_weight, conv_bias, highway_weight, highway_bias, proj_weight, proj_bias, lstm_weight, lstm_bias, lstm_proj):
    weights = tuple((value.astype(jnp.float32) for value in (char_table, conv_weight, conv_bias, highway_weight, highway_bias, proj_weight, proj_bias, lstm_weight, lstm_bias, lstm_proj)))

    def evaluate(*params):
        return layer_forward(char_ids, resets, *params)
    outputs, pullback = jax.vjp(evaluate, *weights)
    grad_table, grad_conv_w, grad_conv_b, grad_high_w, grad_high_b, grad_proj_w, grad_proj_b, grad_lstm_w, grad_lstm_b, grad_lstm_p = pullback(out_grad.astype(jnp.float32))
    return (grad_table, grad_conv_w, grad_conv_b, grad_high_w, grad_high_b, grad_proj_w, grad_proj_b, grad_lstm_w, grad_lstm_b, grad_lstm_p)
```

```python
from functools import partial
import math

import jax
import jax.numpy as jnp
from jax import lax
from jax.experimental import pallas as pl
from jax.experimental.pallas import tpu as pltpu
from jax.sharding import PartitionSpec as P

CHAR_COUNT = 50
EMBED = 16
WIDEST = 7
TAPS = WIDEST * EMBED
LANES = 128
PLACES = 64
TIGHT = 48
CHUNK = 256
TOKEN_BLOCK = 16


def bank_plan(bank_cols):
    return [
        [
            (1, 0, bank_cols // 32),
            (2, bank_cols // 32, bank_cols // 32),
            (3, bank_cols // 16, bank_cols // 16),
            (4, bank_cols // 8, bank_cols // 8),
        ],
        [(5, 0, bank_cols // 4)],
        [(6, 0, bank_cols // 2)],
        [(7, 0, bank_cols)],
    ]


def transposed(former, latter):
    return lax.dot_general(
        former, latter, (((1,), (1,)), ((), ())), preferred_element_type=jnp.float32
    )


def outer_sum(former, latter):
    return lax.dot_general(
        former, latter, (((0,), (0,)), ((), ())), preferred_element_type=jnp.float32
    )


def column_sum(values):
    ones_row = jnp.ones((1, values.shape[0]), values.dtype)
    return jnp.dot(ones_row, values, preferred_element_type=jnp.float32)[0]


def filter_columns(bank_cols):
    columns = []
    for bank_index, bank_specs in enumerate(bank_plan(bank_cols)):
        for filter_width, first_col, count in bank_specs:
            columns.append((filter_width, bank_index, first_col, count))
    return columns


def shift_rows(values, amount):
    count = values.shape[0]
    return values if amount % count == 0 else pltpu.roll(values, amount % count, 0)


def block_windows(tiled_ref, windows_wide, windows_tight):
    tokens, places, lanes = tiled_ref.shape
    rows = tokens * places
    tiled = tiled_ref[...].astype(jnp.float32).reshape(rows, lanes)
    lane = lax.broadcasted_iota(jnp.int32, (rows, lanes), 1)
    place = lax.broadcasted_iota(jnp.int32, (rows, lanes), 0) % places
    windows = tiled
    for offset in range(1, WIDEST):
        windows = jnp.where(lane // EMBED == offset, shift_rows(tiled, rows - offset), windows)
    late = place >= CHAR_COUNT - WIDEST + 1 + (lane - TAPS - 1)
    extra = jnp.where((lane == TAPS) | ((lane <= TAPS + WIDEST) & late), 1.0, 0.0)
    windows = jnp.where(lane < TAPS, windows, extra)
    windows_wide[...] = windows.astype(jnp.bfloat16)
    windows_tight[...] = (
        windows.reshape(tokens, places, lanes)[:, :TIGHT]
        .reshape(tokens * TIGHT, lanes)
        .astype(jnp.bfloat16)
    )


def column_chunks(total, tight_from):
    return [
        (start, start < tight_from) for start in range(0, total, CHUNK)
    ]


def pool_kernel(tight_from, tiled_ref, weight_ref, count_ref, features_ref, lse_ref, wide, tight):
    tokens, places, lanes = tiled_ref.shape
    block_windows(tiled_ref, wide, tight)
    for start, is_wide in column_chunks(weight_ref.shape[1], tight_from):
        cols = pl.ds(start, CHUNK)
        windows = wide if is_wide else tight
        conv_out = jnp.dot(
            windows[...], weight_ref[:, cols], preferred_element_type=jnp.float32
        ).reshape(tokens, -1, CHUNK)
        highest = jnp.max(conv_out, axis=1)
        total = jnp.sum(jnp.exp(conv_out - highest[:, None, :]), axis=1)
        pooled_lse = highest + jnp.log(total)
        lse_ref[:, cols] = pooled_lse
        pooled_pre = pooled_lse - count_ref[0:1, cols]
        features_ref[:, cols] = (pooled_pre * jax.nn.sigmoid(pooled_pre)).astype(jnp.bfloat16)


def pool_grad_kernel(
    tight_from,
    tiled_ref,
    weight_ref,
    count_ref,
    lse_ref,
    upstream_ref,
    grad_weight_ref,
    aligned_ref,
    wide,
    tight,
    spread,
):
    tokens, places, lanes = tiled_ref.shape
    block_windows(tiled_ref, wide, tight)

    @pl.when(pl.program_id(0) == 0)
    def _():
        grad_weight_ref[...] = jnp.zeros_like(grad_weight_ref)

    spread[...] = jnp.zeros_like(spread)
    wide_turned = wide[...].T
    tight_turned = tight[...].T
    for start, is_wide in column_chunks(weight_ref.shape[1], tight_from):
        cols = pl.ds(start, CHUNK)
        windows, turned = (wide, wide_turned) if is_wide else (tight, tight_turned)
        weights = weight_ref[:, cols]
        conv_out = jnp.dot(
            windows[...], weights, preferred_element_type=jnp.float32
        ).reshape(tokens, -1, CHUNK)
        pooled_lse = lse_ref[:, cols]
        pooled_pre = pooled_lse - count_ref[0:1, cols]
        squashed = jax.nn.sigmoid(pooled_pre)
        upstream = (
            upstream_ref[:, cols].astype(jnp.float32)
            * squashed
            * (1.0 + pooled_pre * (1.0 - squashed))
        )
        softened = jnp.exp(conv_out - pooled_lse[:, None, :])
        grad_conv = (softened * upstream[:, None, :]).astype(jnp.bfloat16)
        places_here = grad_conv.shape[1]
        grad_conv = grad_conv.reshape(tokens * places_here, CHUNK)
        grad_weight_ref[:, cols] += jnp.dot(turned, grad_conv, preferred_element_type=jnp.float32)
        part = lax.dot_general(
            grad_conv, weights, (((1,), (1,)), ((), ())), preferred_element_type=jnp.float32
        ).reshape(tokens, places_here, lanes)
        spread[:, :places_here, :] += part
    rows = tokens * places
    flat = spread[...].reshape(rows, lanes)
    lane = lax.broadcasted_iota(jnp.int32, (rows, lanes), 1)
    aligned = jnp.where(lane < EMBED, flat, 0.0)
    for offset in range(1, WIDEST):
        aligned = jnp.where(lane // EMBED == offset, shift_rows(flat, offset), aligned)
    aligned_ref[...] = aligned.reshape(tokens, places, lanes)


def filter_matrix(conv_weight, conv_bias):
    bank_cols = conv_bias.shape[1]
    taps, biases, masks, counts = [], [], [], []
    for filter_width, bank_index, first_col, count in filter_columns(bank_cols):
        piece = conv_weight[bank_index, :filter_width, :, first_col : first_col + count]
        piece = piece.reshape(filter_width * EMBED, count)
        taps.append(jnp.pad(piece, ((0, TAPS - filter_width * EMBED), (0, 0))))
        biases.append(conv_bias[bank_index, first_col : first_col + count])
        rows = lax.broadcasted_iota(jnp.int32, (LANES - TAPS - 1, count), 0)
        masks.append(jnp.where(rows == WIDEST - filter_width, -1e30, 0.0).astype(jnp.bfloat16))
        counts.append(jnp.full((8, count), math.log(CHAR_COUNT - filter_width + 1), jnp.float32))
    weights = jnp.concatenate(
        [
            jnp.concatenate(taps, axis=1),
            jnp.concatenate(biases)[None],
            jnp.concatenate(masks, axis=1),
        ],
        axis=0,
    )
    return (weights, jnp.concatenate(counts, axis=1))


def wide_columns(bank_cols):
    total = sum(count for width, bank, first, count in filter_columns(bank_cols) if CHAR_COUNT - width + 1 > TIGHT - 2)
    return -(-total // CHUNK) * CHUNK


def char_selector(token_ids, vocab_size):
    return token_ids.reshape(-1)[:, None] == lax.broadcasted_iota(jnp.int32, (1, vocab_size), 1)


def pool_tokens(token_ids, char_table, weights, counts, tight_from):
    tokens = token_ids.shape[0]
    padded = jnp.pad(token_ids, ((0, 0), (0, PLACES - token_ids.shape[1])), constant_values=-1)
    table_tiled = jnp.pad(jnp.tile(char_table, (1, WIDEST)), ((0, 0), (0, LANES - TAPS)))
    selector = char_selector(padded, char_table.shape[0]).astype(jnp.bfloat16)
    tiled = jnp.dot(selector, table_tiled, preferred_element_type=jnp.float32)
    tiled = tiled.astype(jnp.bfloat16).reshape(tokens, PLACES, LANES)
    block = math.gcd(tokens, TOKEN_BLOCK)
    total = weights.shape[1]
    features, pooled_lse = pl.pallas_call(
        partial(pool_kernel, tight_from),
        grid=(tokens // block,),
        in_specs=[
            pl.BlockSpec((block, PLACES, LANES), lambda i: (i, 0, 0)),
            pl.BlockSpec((LANES, total), lambda i: (0, 0)),
            pl.BlockSpec((8, total), lambda i: (0, 0)),
        ],
        out_specs=[
            pl.BlockSpec((block, total), lambda i: (i, 0)),
            pl.BlockSpec((block, total), lambda i: (i, 0)),
        ],
        out_shape=[
            jax.ShapeDtypeStruct((tokens, total), jnp.bfloat16),
            jax.ShapeDtypeStruct((tokens, total), jnp.float32),
        ],
        scratch_shapes=[
            pltpu.VMEM((block * PLACES, LANES), jnp.bfloat16),
            pltpu.VMEM((block * TIGHT, LANES), jnp.bfloat16),
        ],
        compiler_params=pltpu.CompilerParams(vmem_limit_bytes=40 * 1024 * 1024),
        name="pool_tokens",
    )(tiled, weights, counts)
    return (padded, tiled, features, pooled_lse)


def pool_grads(padded, tiled, weights, counts, pooled_lse, upstream, vocab_size, tight_from):
    tokens = tiled.shape[0]
    block = math.gcd(tokens, TOKEN_BLOCK)
    total = weights.shape[1]
    grad_weight, aligned = pl.pallas_call(
        partial(pool_grad_kernel, tight_from),
        grid=(tokens // block,),
        in_specs=[
            pl.BlockSpec((block, PLACES, LANES), lambda i: (i, 0, 0)),
            pl.BlockSpec((LANES, total), lambda i: (0, 0)),
            pl.BlockSpec((8, total), lambda i: (0, 0)),
            pl.BlockSpec((block, total), lambda i: (i, 0)),
            pl.BlockSpec((block, total), lambda i: (i, 0)),
        ],
        out_specs=[
            pl.BlockSpec((LANES, total), lambda i: (0, 0)),
            pl.BlockSpec((block, PLACES, LANES), lambda i: (i, 0, 0)),
        ],
        out_shape=[
            jax.ShapeDtypeStruct((LANES, total), jnp.float32),
            jax.ShapeDtypeStruct((tokens, PLACES, LANES), jnp.float32),
        ],
        scratch_shapes=[
            pltpu.VMEM((block * PLACES, LANES), jnp.bfloat16),
            pltpu.VMEM((block * TIGHT, LANES), jnp.bfloat16),
            pltpu.VMEM((block, PLACES, LANES), jnp.float32),
        ],
        compiler_params=pltpu.CompilerParams(vmem_limit_bytes=40 * 1024 * 1024),
        name="pool_grads",
    )(tiled, weights, counts, pooled_lse, upstream)
    aligned = aligned.reshape(tokens * PLACES, LANES)
    selector = char_selector(padded, vocab_size).astype(jnp.bfloat16)
    high = aligned.astype(jnp.bfloat16)
    low = (aligned - high.astype(jnp.float32)).astype(jnp.bfloat16)
    by_tap = outer_sum(selector, high) + outer_sum(selector, low)
    grad_table = by_tap[:, :TAPS].reshape(vocab_size, WIDEST, EMBED).sum(axis=1)
    return (grad_weight, grad_table)


def split_banks(grad_weight, bank_cols):
    taps = grad_weight[:TAPS].reshape(WIDEST, EMBED, -1)
    bias_row = grad_weight[TAPS]
    kernels, biases, at = [], [], 0
    for bank_specs in bank_plan(bank_cols):
        pieces, bias_pieces, used = [], [], 0
        for filter_width, first_col, count in bank_specs:
            piece = taps[:filter_width, :, at : at + count]
            pieces.append(jnp.pad(piece, ((0, WIDEST - filter_width), (0, 0), (0, 0))))
            bias_pieces.append(bias_row[at : at + count])
            at += count
            used += count
        kernels.append(
            jnp.pad(jnp.concatenate(pieces, axis=2), ((0, 0), (0, 0), (0, bank_cols - used)))
        )
        biases.append(jnp.pad(jnp.concatenate(bias_pieces), (0, bank_cols - used)))
    return (jnp.stack(kernels), jnp.stack(biases))


def gate_parts(gates_pre, cell_width):
    in_gate = jax.nn.sigmoid(gates_pre[:, :cell_width])
    forget_gate = jax.nn.sigmoid(gates_pre[:, cell_width : 2 * cell_width])
    candidate = jnp.tanh(gates_pre[:, 2 * cell_width : 3 * cell_width])
    out_gate = jax.nn.sigmoid(gates_pre[:, 3 * cell_width :])
    return (in_gate, forget_gate, candidate, out_gate)


def forward_step(weight_rec, proj_mat, carry, sliced):
    cell_state, hidden_state = carry
    gate_inputs, keep_now = sliced
    keep_col = keep_now[:, None]
    cell_start = cell_state * keep_col
    state_start = hidden_state * keep_col.astype(jnp.bfloat16)
    gates_pre = gate_inputs + jnp.dot(state_start, weight_rec, preferred_element_type=jnp.float32)
    in_gate, forget_gate, candidate, out_gate = gate_parts(gates_pre, cell_state.shape[1])
    cell_new = 3.0 * jnp.tanh((forget_gate * cell_start + in_gate * candidate) / 3.0)
    full_state = (out_gate * jnp.tanh(cell_new)).astype(jnp.bfloat16)
    projected = jnp.dot(full_state, proj_mat, preferred_element_type=jnp.float32)
    state_new = (3.0 * jnp.tanh(projected / 3.0)).astype(jnp.bfloat16)
    return ((cell_new, state_new), (gates_pre, cell_start, state_start, full_state, projected))


def backward_step(weight_rec, proj_mat, carry, sliced):
    grad_cell, grad_state = carry
    gates_pre, cell_start, projected, keep_now, grad_out_now = sliced
    grad_state = grad_state + grad_out_now.astype(jnp.float32)
    squashed = jnp.tanh(projected / 3.0)
    grad_projected = (grad_state * (1.0 - squashed * squashed)).astype(jnp.bfloat16)
    grad_full = transposed(grad_projected, proj_mat)
    in_gate, forget_gate, candidate, out_gate = gate_parts(gates_pre, cell_start.shape[1])
    clipped = jnp.tanh((forget_gate * cell_start + in_gate * candidate) / 3.0)
    tanh_cell = jnp.tanh(3.0 * clipped)
    grad_cell_total = grad_cell + grad_full * out_gate * (1.0 - tanh_cell * tanh_cell)
    grad_raw = grad_cell_total * (1.0 - clipped * clipped)
    grad_gates = jnp.concatenate(
        [
            grad_raw * candidate * in_gate * (1.0 - in_gate),
            grad_raw * cell_start * forget_gate * (1.0 - forget_gate),
            grad_raw * in_gate * (1.0 - candidate * candidate),
            grad_full * tanh_cell * out_gate * (1.0 - out_gate),
        ],
        axis=1,
    ).astype(jnp.bfloat16)
    keep_col = keep_now[:, None]
    grad_state_prev = transposed(grad_gates, weight_rec) * keep_col
    grad_cell_prev = grad_raw * forget_gate * keep_col
    return ((grad_cell_prev, grad_state_prev), (grad_gates, grad_projected))


def run_direction(
    time_input, keep_time, grad_out_time, weight_full, bias_full, proj_mat, backwards
):
    step_count, own_streams = keep_time.shape
    proj_width = time_input.shape[1]
    gate_width = weight_full.shape[1]
    cell_width = proj_mat.shape[0]
    weight_in = weight_full[:proj_width]
    weight_rec = weight_full[proj_width:]
    input_gates = (
        jnp.dot(time_input, weight_in, preferred_element_type=jnp.float32)
        + bias_full.astype(jnp.float32)
    ).reshape(step_count, own_streams, gate_width)
    initial = (
        jnp.zeros((own_streams, cell_width), jnp.float32),
        jnp.zeros((own_streams, proj_width), jnp.bfloat16),
    )
    history = lax.scan(
        partial(forward_step, weight_rec, proj_mat),
        initial,
        (input_gates, keep_time),
        reverse=backwards,
    )[1]
    gates_all, cell_starts, state_starts, full_states, projected_all = history
    initial_grad = (
        jnp.zeros((own_streams, cell_width), jnp.float32),
        jnp.zeros((own_streams, proj_width), jnp.float32),
    )
    grad_history = lax.scan(
        partial(backward_step, weight_rec, proj_mat),
        initial_grad,
        (gates_all, cell_starts, projected_all, keep_time, grad_out_time),
        reverse=not backwards,
    )[1]
    grad_gates, grad_projected = grad_history
    flat_gates = grad_gates.reshape(step_count * own_streams, gate_width)
    grad_weight = jnp.concatenate(
        [
            outer_sum(time_input, flat_gates),
            outer_sum(state_starts.reshape(step_count * own_streams, proj_width), flat_gates),
        ],
        axis=0,
    )
    grad_bias = column_sum(flat_gates)
    grad_proj = outer_sum(
        full_states.reshape(step_count * own_streams, cell_width),
        grad_projected.reshape(step_count * own_streams, proj_width),
    )
    grad_input = transposed(flat_gates, weight_in)
    return (grad_input, grad_weight, grad_bias, grad_proj)


def scatter_sum(values, axes, scatter_dimension, tiled):
    return lax.psum_scatter(
        values.astype(jnp.bfloat16), axes, scatter_dimension=scatter_dimension, tiled=tiled
    ).astype(jnp.float32)


def shards(
    char_ids,
    resets,
    out_grad,
    char_table,
    conv_weight,
    conv_bias,
    highway_weight,
    highway_bias,
    proj_weight,
    proj_bias,
    lstm_weight,
    lstm_bias,
    lstm_proj,
):
    own_streams, step_count = resets.shape
    bank_cols = conv_weight.shape[3]
    (
        highway_full,
        highway_bias_full,
        project_full,
        project_bias,
        lstm_first,
        bias_first,
        proj_first,
    ) = (
        lax.all_gather(highway_weight, ("dp", "bank"), axis=1, tiled=True),
        lax.all_gather(highway_bias, ("dp", "bank"), axis=1, tiled=True),
        lax.all_gather(proj_weight, ("dp", "bank"), axis=0, tiled=True),
        lax.all_gather(proj_bias, ("dp", "bank"), axis=0, tiled=True),
        lax.all_gather(lstm_weight[0], ("dp", "bank"), axis=0, tiled=True),
        lax.all_gather(lstm_bias[0], ("dp", "bank"), axis=0, tiled=True),
        lax.all_gather(lstm_proj[0], ("dp", "bank"), axis=1, tiled=True),
    )
    conv_weight_all = lax.all_gather(conv_weight, "bank", axis=0, tiled=True)
    conv_bias_all = lax.all_gather(conv_bias, "bank", axis=0, tiled=True)
    own_ids = lax.dynamic_slice_in_dim(
        char_ids, lax.axis_index("bank") * own_streams, own_streams, axis=0
    ).reshape(own_streams * step_count, char_ids.shape[2])
    filters, counts = filter_matrix(conv_weight_all, conv_bias_all)
    tight_from = wide_columns(bank_cols)
    padded_ids, tiled, features, pooled_lse = pool_tokens(
        own_ids, char_table, filters, counts, tight_from
    )
    feature_count = features.shape[1]
    hidden_f32 = features.astype(jnp.float32)
    saved = []
    for highway_level in range(2):
        operand = features if highway_level == 0 else hidden_f32.astype(jnp.bfloat16)
        mixed = jnp.dot(
            operand, highway_full[highway_level], preferred_element_type=jnp.float32
        ) + highway_bias_full[highway_level].astype(jnp.float32)
        saved.append((operand, hidden_f32, mixed))
        carry_gate = jax.nn.sigmoid(mixed[:, feature_count:])
        hidden_f32 = carry_gate * hidden_f32 + (1.0 - carry_gate) * jax.nn.silu(
            mixed[:, :feature_count]
        )
    top_rows = hidden_f32.astype(jnp.bfloat16)
    lstm_input = (
        jnp.dot(top_rows, project_full, preferred_element_type=jnp.float32)
        + project_bias.astype(jnp.float32)
    ).astype(jnp.bfloat16)
    proj_width = lstm_input.shape[1]
    time_input = jnp.swapaxes(
        lstm_input.reshape(own_streams, step_count, proj_width), 0, 1
    ).reshape(step_count * own_streams, proj_width)
    cleared = resets.astype(jnp.float32)
    keep_forward = jnp.swapaxes(1.0 - cleared, 0, 1)
    keep_backward = jnp.swapaxes(
        1.0 - jnp.concatenate([cleared[:, 1:], jnp.zeros((own_streams, 1), jnp.float32)], axis=1),
        0,
        1,
    )
    grad_time = jnp.swapaxes(out_grad, 0, 1)
    results_first = run_direction(
        time_input,
        keep_forward,
        grad_time[:, :, :proj_width],
        lstm_first,
        bias_first,
        proj_first,
        False,
    )
    shard_first = (
        scatter_sum(results_first[1], ("dp", "bank"), scatter_dimension=0, tiled=True),
        lax.psum_scatter(results_first[2], ("dp", "bank"), scatter_dimension=0, tiled=True),
        scatter_sum(results_first[3], ("dp", "bank"), scatter_dimension=1, tiled=True),
    )
    lstm_second, bias_second, proj_second = (
        lax.all_gather(lstm_weight[1], ("dp", "bank"), axis=0, tiled=True),
        lax.all_gather(lstm_bias[1], ("dp", "bank"), axis=0, tiled=True),
        lax.all_gather(lstm_proj[1], ("dp", "bank"), axis=1, tiled=True),
    )
    results_second = run_direction(
        time_input,
        keep_backward,
        grad_time[:, :, proj_width:],
        lstm_second,
        bias_second,
        proj_second,
        True,
    )
    grad_time_input = results_first[0] + results_second[0]
    grad_input = (
        jnp.swapaxes(grad_time_input.reshape(step_count, own_streams, proj_width), 0, 1)
        .reshape(own_streams * step_count, proj_width)
        .astype(jnp.bfloat16)
    )
    grad_project_w = outer_sum(top_rows, grad_input)
    grad_project_b = column_sum(grad_input)
    grad_hidden = transposed(grad_input, project_full)
    weight_levels = [None, None]
    bias_levels = [None, None]
    for highway_level in (1, 0):
        operand, hidden_in, mixed = saved[highway_level]
        carry_gate = jax.nn.sigmoid(mixed[:, feature_count:])
        pre_act = mixed[:, :feature_count]
        act_sig = jax.nn.sigmoid(pre_act)
        grad_act = grad_hidden * (1.0 - carry_gate) * act_sig * (1.0 + pre_act * (1.0 - act_sig))
        grad_carry = grad_hidden * (hidden_in - pre_act * act_sig) * carry_gate * (1.0 - carry_gate)
        grad_mixed = jnp.concatenate([grad_act, grad_carry], axis=1).astype(jnp.bfloat16)
        weight_levels[highway_level] = outer_sum(operand, grad_mixed)
        bias_levels[highway_level] = column_sum(grad_mixed)
        grad_hidden = grad_hidden * carry_gate + transposed(grad_mixed, highway_full[highway_level])
    grad_features = grad_hidden.astype(jnp.bfloat16)
    shard_last = (
        scatter_sum(results_second[1], ("dp", "bank"), scatter_dimension=0, tiled=True),
        lax.psum_scatter(results_second[2], ("dp", "bank"), scatter_dimension=0, tiled=True),
        scatter_sum(results_second[3], ("dp", "bank"), scatter_dimension=1, tiled=True),
        scatter_sum(jnp.stack(weight_levels), ("dp", "bank"), scatter_dimension=1, tiled=True),
        lax.psum_scatter(jnp.stack(bias_levels), ("dp", "bank"), scatter_dimension=1, tiled=True),
        scatter_sum(grad_project_w, ("dp", "bank"), scatter_dimension=0, tiled=True),
        lax.psum_scatter(grad_project_b, ("dp", "bank"), scatter_dimension=0, tiled=True),
    )
    grad_filters, grad_table = pool_grads(
        padded_ids,
        tiled,
        filters,
        counts,
        pooled_lse,
        grad_features,
        char_table.shape[0],
        tight_from,
    )
    grad_kernel, grad_bias = split_banks(grad_filters, bank_cols)
    grad_kernel = lax.psum(
        lax.psum_scatter(grad_kernel, "bank", scatter_dimension=0, tiled=True), "dp"
    )
    grad_bias = lax.psum(lax.psum_scatter(grad_bias, "bank", scatter_dimension=0, tiled=True), "dp")
    grad_table = lax.psum(grad_table, ("dp", "bank"))
    lstm_weight_grad = jnp.stack([shard_first[0], shard_last[0]])
    lstm_bias_grad = jnp.stack([shard_first[1], shard_last[1]])
    lstm_proj_grad = jnp.stack([shard_first[2], shard_last[2]])
    return (
        grad_table,
        grad_kernel,
        grad_bias,
        shard_last[3],
        shard_last[4],
        shard_last[5],
        shard_last[6],
        lstm_weight_grad,
        lstm_bias_grad,
        lstm_proj_grad,
    )


def solution(mesh):
    placed = (
        P("dp", None, None),
        P(("dp", "bank"), None),
        P(("dp", "bank"), None, None),
        P(),
        P("bank", None, None, None),
        P("bank", None),
        P(None, ("dp", "bank"), None),
        P(None, ("dp", "bank")),
        P(("dp", "bank"), None),
        P(("dp", "bank")),
        P(None, ("dp", "bank"), None),
        P(None, ("dp", "bank")),
        P(None, None, ("dp", "bank")),
    )
    return jax.shard_map(
        shards,
        mesh=mesh,
        in_specs=placed,
        out_specs=(
            P(),
            P("bank", None, None, None),
            P("bank", None),
            P(None, ("dp", "bank"), None),
            P(None, ("dp", "bank")),
            P(("dp", "bank"), None),
            P(("dp", "bank")),
            P(None, ("dp", "bank"), None),
            P(None, ("dp", "bank")),
            P(None, None, ("dp", "bank")),
        ),
        check_vma=False,
    )
```

```python
from functools import partial
import math

import jax
import jax.numpy as jnp
from jax import lax
from jax.experimental import pallas as pl
from jax.experimental.pallas import tpu as pltpu
from jax.sharding import Mesh, PartitionSpec as P

CHAR_COUNT = 50
EMBED = 16
WIDEST = 7
TAPS = WIDEST * EMBED
LANES = 128
PLACES = 64
TIGHT = 48
CHUNK = 256
TOKEN_BLOCK = 16


def bank_plan(bank_cols):
    return [
        [
            (1, 0, bank_cols // 32),
            (2, bank_cols // 32, bank_cols // 32),
            (3, bank_cols // 16, bank_cols // 16),
            (4, bank_cols // 8, bank_cols // 8),
        ],
        [(5, 0, bank_cols // 4)],
        [(6, 0, bank_cols // 2)],
        [(7, 0, bank_cols)],
    ]


def transposed(former, latter):
    return lax.dot_general(
        former, latter, (((1,), (1,)), ((), ())), preferred_element_type=jnp.float32
    )


def outer_sum(former, latter):
    return lax.dot_general(
        former, latter, (((0,), (0,)), ((), ())), preferred_element_type=jnp.float32
    )


def column_sum(values):
    ones_row = jnp.ones((1, values.shape[0]), values.dtype)
    return jnp.dot(ones_row, values, preferred_element_type=jnp.float32)[0]


def filter_columns(bank_cols):
    columns = []
    for bank_index, bank_specs in enumerate(bank_plan(bank_cols)):
        for filter_width, first_col, count in bank_specs:
            columns.append((filter_width, bank_index, first_col, count))
    return columns


def shift_rows(values, amount):
    count = values.shape[0]
    return values if amount % count == 0 else pltpu.roll(values, amount % count, 0)


def block_windows(tiled_ref, windows_wide, windows_tight):
    tokens, places, lanes = tiled_ref.shape
    rows = tokens * places
    tiled = tiled_ref[...].astype(jnp.float32).reshape(rows, lanes)
    lane = lax.broadcasted_iota(jnp.int32, (rows, lanes), 1)
    place = lax.broadcasted_iota(jnp.int32, (rows, lanes), 0) % places
    windows = tiled
    for offset in range(1, WIDEST):
        windows = jnp.where(lane // EMBED == offset, shift_rows(tiled, rows - offset), windows)
    late = place >= CHAR_COUNT - WIDEST + 1 + (lane - TAPS - 1)
    extra = jnp.where((lane == TAPS) | ((lane <= TAPS + WIDEST) & late), 1.0, 0.0)
    windows = jnp.where(lane < TAPS, windows, extra)
    windows_wide[...] = windows.astype(jnp.bfloat16)
    windows_tight[...] = (
        windows.reshape(tokens, places, lanes)[:, :TIGHT]
        .reshape(tokens * TIGHT, lanes)
        .astype(jnp.bfloat16)
    )


def column_chunks(total, tight_from):
    return [
        (start, start < tight_from) for start in range(0, total, CHUNK)
    ]


def pool_kernel(tight_from, tiled_ref, weight_ref, count_ref, features_ref, lse_ref, wide, tight):
    tokens, places, lanes = tiled_ref.shape
    block_windows(tiled_ref, wide, tight)
    for start, is_wide in column_chunks(weight_ref.shape[1], tight_from):
        cols = pl.ds(start, CHUNK)
        windows = wide if is_wide else tight
        conv_out = jnp.dot(
            windows[...], weight_ref[:, cols], preferred_element_type=jnp.float32
        ).reshape(tokens, -1, CHUNK)
        highest = jnp.max(conv_out, axis=1)
        total = jnp.sum(jnp.exp(conv_out - highest[:, None, :]), axis=1)
        pooled_lse = highest + jnp.log(total)
        lse_ref[:, cols] = pooled_lse
        pooled_pre = pooled_lse - count_ref[0:1, cols]
        features_ref[:, cols] = (pooled_pre * jax.nn.sigmoid(pooled_pre)).astype(jnp.bfloat16)


def pool_grad_kernel(
    tight_from,
    tiled_ref,
    weight_ref,
    count_ref,
    lse_ref,
    upstream_ref,
    grad_weight_ref,
    aligned_ref,
    wide,
    tight,
    spread,
):
    tokens, places, lanes = tiled_ref.shape
    block_windows(tiled_ref, wide, tight)

    @pl.when(pl.program_id(0) == 0)
    def _():
        grad_weight_ref[...] = jnp.zeros_like(grad_weight_ref)

    spread[...] = jnp.zeros_like(spread)
    wide_turned = wide[...].T
    tight_turned = tight[...].T
    for start, is_wide in column_chunks(weight_ref.shape[1], tight_from):
        cols = pl.ds(start, CHUNK)
        windows, turned = (wide, wide_turned) if is_wide else (tight, tight_turned)
        weights = weight_ref[:, cols]
        conv_out = jnp.dot(
            windows[...], weights, preferred_element_type=jnp.float32
        ).reshape(tokens, -1, CHUNK)
        pooled_lse = lse_ref[:, cols]
        pooled_pre = pooled_lse - count_ref[0:1, cols]
        squashed = jax.nn.sigmoid(pooled_pre)
        upstream = (
            upstream_ref[:, cols].astype(jnp.float32)
            * squashed
            * (1.0 + pooled_pre * (1.0 - squashed))
        )
        softened = jnp.exp(conv_out - pooled_lse[:, None, :])
        grad_conv = (softened * upstream[:, None, :]).astype(jnp.bfloat16)
        places_here = grad_conv.shape[1]
        grad_conv = grad_conv.reshape(tokens * places_here, CHUNK)
        grad_weight_ref[:, cols] += jnp.dot(turned, grad_conv, preferred_element_type=jnp.float32)
        part = lax.dot_general(
            grad_conv, weights, (((1,), (1,)), ((), ())), preferred_element_type=jnp.float32
        ).reshape(tokens, places_here, lanes)
        spread[:, :places_here, :] += part
    rows = tokens * places
    flat = spread[...].reshape(rows, lanes)
    lane = lax.broadcasted_iota(jnp.int32, (rows, lanes), 1)
    aligned = jnp.where(lane < EMBED, flat, 0.0)
    for offset in range(1, WIDEST):
        aligned = jnp.where(lane // EMBED == offset, shift_rows(flat, offset), aligned)
    aligned_ref[...] = aligned.reshape(tokens, places, lanes)


def filter_matrix(conv_weight, conv_bias):
    bank_cols = conv_bias.shape[1]
    taps, biases, masks, counts = [], [], [], []
    for filter_width, bank_index, first_col, count in filter_columns(bank_cols):
        piece = conv_weight[bank_index, :filter_width, :, first_col : first_col + count]
        piece = piece.reshape(filter_width * EMBED, count)
        taps.append(jnp.pad(piece, ((0, TAPS - filter_width * EMBED), (0, 0))))
        biases.append(conv_bias[bank_index, first_col : first_col + count])
        rows = lax.broadcasted_iota(jnp.int32, (LANES - TAPS - 1, count), 0)
        masks.append(jnp.where(rows == WIDEST - filter_width, -1e30, 0.0).astype(jnp.bfloat16))
        counts.append(jnp.full((8, count), math.log(CHAR_COUNT - filter_width + 1), jnp.float32))
    weights = jnp.concatenate(
        [
            jnp.concatenate(taps, axis=1),
            jnp.concatenate(biases)[None],
            jnp.concatenate(masks, axis=1),
        ],
        axis=0,
    )
    return (weights, jnp.concatenate(counts, axis=1))


def wide_columns(bank_cols):
    total = sum(count for width, bank, first, count in filter_columns(bank_cols) if CHAR_COUNT - width + 1 > TIGHT - 2)
    return -(-total // CHUNK) * CHUNK


def char_selector(token_ids, vocab_size):
    return token_ids.reshape(-1)[:, None] == lax.broadcasted_iota(jnp.int32, (1, vocab_size), 1)


def pool_tokens(token_ids, char_table, weights, counts, tight_from):
    tokens = token_ids.shape[0]
    padded = jnp.pad(token_ids, ((0, 0), (0, PLACES - token_ids.shape[1])), constant_values=-1)
    table_tiled = jnp.pad(jnp.tile(char_table, (1, WIDEST)), ((0, 0), (0, LANES - TAPS)))
    selector = char_selector(padded, char_table.shape[0]).astype(jnp.bfloat16)
    tiled = jnp.dot(selector, table_tiled, preferred_element_type=jnp.float32)
    tiled = tiled.astype(jnp.bfloat16).reshape(tokens, PLACES, LANES)
    block = math.gcd(tokens, TOKEN_BLOCK)
    total = weights.shape[1]
    features, pooled_lse = pl.pallas_call(
        partial(pool_kernel, tight_from),
        grid=(tokens // block,),
        in_specs=[
            pl.BlockSpec((block, PLACES, LANES), lambda i: (i, 0, 0)),
            pl.BlockSpec((LANES, total), lambda i: (0, 0)),
            pl.BlockSpec((8, total), lambda i: (0, 0)),
        ],
        out_specs=[
            pl.BlockSpec((block, total), lambda i: (i, 0)),
            pl.BlockSpec((block, total), lambda i: (i, 0)),
        ],
        out_shape=[
            jax.ShapeDtypeStruct((tokens, total), jnp.bfloat16),
            jax.ShapeDtypeStruct((tokens, total), jnp.float32),
        ],
        scratch_shapes=[
            pltpu.VMEM((block * PLACES, LANES), jnp.bfloat16),
            pltpu.VMEM((block * TIGHT, LANES), jnp.bfloat16),
        ],
        compiler_params=pltpu.CompilerParams(vmem_limit_bytes=40 * 1024 * 1024),
        name="pool_tokens",
    )(tiled, weights, counts)
    return (padded, tiled, features, pooled_lse)


def pool_grads(padded, tiled, weights, counts, pooled_lse, upstream, vocab_size, tight_from):
    tokens = tiled.shape[0]
    block = math.gcd(tokens, TOKEN_BLOCK)
    total = weights.shape[1]
    grad_weight, aligned = pl.pallas_call(
        partial(pool_grad_kernel, tight_from),
        grid=(tokens // block,),
        in_specs=[
            pl.BlockSpec((block, PLACES, LANES), lambda i: (i, 0, 0)),
            pl.BlockSpec((LANES, total), lambda i: (0, 0)),
            pl.BlockSpec((8, total), lambda i: (0, 0)),
            pl.BlockSpec((block, total), lambda i: (i, 0)),
            pl.BlockSpec((block, total), lambda i: (i, 0)),
        ],
        out_specs=[
            pl.BlockSpec((LANES, total), lambda i: (0, 0)),
            pl.BlockSpec((block, PLACES, LANES), lambda i: (i, 0, 0)),
        ],
        out_shape=[
            jax.ShapeDtypeStruct((LANES, total), jnp.float32),
            jax.ShapeDtypeStruct((tokens, PLACES, LANES), jnp.float32),
        ],
        scratch_shapes=[
            pltpu.VMEM((block * PLACES, LANES), jnp.bfloat16),
            pltpu.VMEM((block * TIGHT, LANES), jnp.bfloat16),
            pltpu.VMEM((block, PLACES, LANES), jnp.float32),
        ],
        compiler_params=pltpu.CompilerParams(vmem_limit_bytes=40 * 1024 * 1024),
        name="pool_grads",
    )(tiled, weights, counts, pooled_lse, upstream)
    aligned = aligned.reshape(tokens * PLACES, LANES)
    selector = char_selector(padded, vocab_size).astype(jnp.bfloat16)
    high = aligned.astype(jnp.bfloat16)
    low = (aligned - high.astype(jnp.float32)).astype(jnp.bfloat16)
    by_tap = outer_sum(selector, high) + outer_sum(selector, low)
    grad_table = by_tap[:, :TAPS].reshape(vocab_size, WIDEST, EMBED).sum(axis=1)
    return (grad_weight, grad_table)


def split_banks(grad_weight, bank_cols):
    taps = grad_weight[:TAPS].reshape(WIDEST, EMBED, -1)
    bias_row = grad_weight[TAPS]
    kernels, biases, at = [], [], 0
    for bank_specs in bank_plan(bank_cols):
        pieces, bias_pieces, used = [], [], 0
        for filter_width, first_col, count in bank_specs:
            piece = taps[:filter_width, :, at : at + count]
            pieces.append(jnp.pad(piece, ((0, WIDEST - filter_width), (0, 0), (0, 0))))
            bias_pieces.append(bias_row[at : at + count])
            at += count
            used += count
        kernels.append(
            jnp.pad(jnp.concatenate(pieces, axis=2), ((0, 0), (0, 0), (0, bank_cols - used)))
        )
        biases.append(jnp.pad(jnp.concatenate(bias_pieces), (0, bank_cols - used)))
    return (jnp.stack(kernels), jnp.stack(biases))


TEAM = ("t", "x", "c")
GRID = ("g", "y")
EVERY = ("g", "t", "y", "x", "c")


def team_place():
    x_size, c_size = lax.axis_size("x"), lax.axis_size("c")
    return (lax.axis_index("t") * x_size + lax.axis_index("x")) * c_size + lax.axis_index("c")


def team_size():
    return lax.axis_size("t") * lax.axis_size("x") * lax.axis_size("c")


def team_coords(place):
    x_size, c_size = lax.axis_size("x"), lax.axis_size("c")
    return {
        "t": place // (x_size * c_size),
        "x": lax.rem(place // c_size, x_size),
        "c": lax.rem(place, c_size),
    }


def swap_team(values):
    return lax.all_to_all(values, TEAM, split_axis=0, concat_axis=0, tiled=True)


def share_team(values):
    team = team_size()
    return swap_team(jnp.broadcast_to(values[None], (team,) + values.shape))


def sigmoid(values):
    return 0.5 * jnp.tanh(0.5 * values) + 0.5


def wait_bytes(ref, sem):
    pltpu.make_async_copy(ref, ref, sem).wait()


def lstm_kernel(
    team,
    lin_ref,
    out_grad_ref,
    weight_ref,
    proj_ref,
    bias_ref,
    keep_ref,
    grad_lin_ref,
    grad_gates_ref,
    lin_all_ref,
    state_ref,
    full_ref,
    grad_proj_ref,
    gates,
    cell_start,
    projected,
    stage,
    received,
    received_back,
    grad_cell,
    grad_lin_sum,
    stage_lin,
    received_lin,
    lin_sems,
    send_sems,
    sum_sems,
    share_send_sems,
    share_sems,
):
    steps, own, width = lin_ref.shape
    group = team * own
    cells = proj_ref.shape[2]
    row_block = 32
    place = team_place()
    own_rows = pl.ds(pl.multiple_of(place * own, own), own)
    peers = [lax.rem(place + k, team) for k in range(1, team)]
    last = steps - 1

    barrier = pltpu.get_barrier_semaphore()
    for peer in peers:
        pl.semaphore_signal(
            barrier, inc=1, device_id=team_coords(peer), device_id_type=pl.DeviceIdType.MESH
        )
    pl.semaphore_wait(barrier, team - 1)

    def send(source, target, send_sem, recv_sem, peer):
        pltpu.make_async_remote_copy(
            src_ref=source,
            dst_ref=target,
            send_sem=send_sem,
            recv_sem=recv_sem,
            device_id=team_coords(peer),
            device_id_type=pl.DeviceIdType.MESH,
        ).start()

    for peer in peers:
        send(lin_ref, lin_all_ref.at[:, own_rows], lin_sems.at[0], lin_sems.at[1], peer)
    lin_all_ref[:, own_rows] = lin_ref[...]
    for d in range(2):
        first = 0 if d == 0 else last
        state_ref[d, first] = jnp.zeros((group, width), jnp.bfloat16)
        cell_start[d, first] = jnp.zeros((group, cells), jnp.float32)
        grad_cell[d] = jnp.zeros((group, cells), jnp.float32)
    grad_lin_sum[...] = jnp.zeros_like(grad_lin_sum)
    others = pl.ds(0, team - 1)
    wait_bytes(lin_all_ref.at[:, pl.ds(0, (team - 1) * own)], lin_sems.at[1])

    @pl.loop(0, steps)
    def _(t):
        for d in range(2):
            for q in range(4):
                cols = pl.ds(q * cells, cells)
                gates[d, t, :, cols] = (
                    jnp.dot(
                        lin_all_ref[t],
                        weight_ref[d, :width, cols],
                        preferred_element_type=jnp.float32,
                    )
                    + bias_ref[d, :, cols]
                )

    def time_of(d, s):
        return s if d == 0 else last - s

    @pl.loop(0, steps)
    def _(s):
        for d in range(2):
            t = time_of(d, s)
            later = time_of(d, jnp.minimum(s + 1, last))

            @pl.when(s > 0)
            def _():
                wait_bytes(
                    state_ref.at[d, t, pl.ds(0, (team - 1) * own)], share_sems.at[0, d, s]
                )
                for q in range(4):
                    cols = pl.ds(q * cells, cells)
                    gates[d, t, :, cols] += jnp.dot(
                        state_ref[d, t],
                        weight_ref[d, width:, cols],
                        preferred_element_type=jnp.float32,
                    )

            @pl.loop(0, group // row_block)
            def _(block):
                rows = pl.ds(pl.multiple_of(block * row_block, row_block), row_block)
                in_gate = sigmoid(gates[d, t, rows, pl.ds(0, cells)])
                forget_gate = sigmoid(gates[d, t, rows, pl.ds(cells, cells)])
                candidate = jnp.tanh(gates[d, t, rows, pl.ds(2 * cells, cells)])
                out_gate = sigmoid(gates[d, t, rows, pl.ds(3 * cells, cells)])
                gates[d, t, rows, pl.ds(0, cells)] = in_gate
                gates[d, t, rows, pl.ds(cells, cells)] = forget_gate
                gates[d, t, rows, pl.ds(2 * cells, cells)] = candidate
                gates[d, t, rows, pl.ds(3 * cells, cells)] = out_gate
                mixed = forget_gate * cell_start[d, t, rows] + in_gate * candidate
                cell_new = 3.0 * jnp.tanh(mixed * (1.0 / 3.0))
                full_ref[d, t, rows] = (out_gate * jnp.tanh(cell_new)).astype(jnp.bfloat16)

                @pl.when(s < last)
                def _():
                    cell_start[d, later, rows] = cell_new * keep_ref[d, later, rows]

            @pl.when(s > 0)
            def _():
                wait_bytes(stage.at[d, others], send_sems.at[d])

            part = lax.dot_general(
                full_ref[d, t],
                proj_ref[d],
                (((1,), (1,)), ((), ())),
                preferred_element_type=jnp.float32,
            )
            part = part.astype(jnp.bfloat16).reshape(team, own, width)
            stage[d] = part
            received[d, s, place] = stage[d, place]
            for peer in peers:
                send(
                    stage.at[d, peer],
                    received.at[d, s, place],
                    send_sems.at[d],
                    sum_sems.at[0, d, s],
                    peer,
                )
        for d in range(2):
            t = time_of(d, s)
            later = time_of(d, jnp.minimum(s + 1, last))
            wait_bytes(received.at[d, s, others], sum_sems.at[0, d, s])
            total = jnp.sum(received[d, s].astype(jnp.float32), axis=0)
            projected[d, t] = total

            @pl.when(s > 0)
            def _():
                wait_bytes(
                    state_ref.at[d, t, pl.ds(0, (team - 1) * own)], share_send_sems.at[0, d]
                )

            @pl.when(s < last)
            def _():
                state_new = (3.0 * jnp.tanh(total * (1.0 / 3.0))).astype(jnp.bfloat16)
                kept = state_new.astype(jnp.float32) * keep_ref[d, later, own_rows]
                state_ref[d, later, own_rows] = kept.astype(jnp.bfloat16)
                for peer in peers:
                    send(
                        state_ref.at[d, later, own_rows],
                        state_ref.at[d, later, own_rows],
                        share_send_sems.at[0, d],
                        share_sems.at[0, d, s + 1],
                        peer,
                    )

    @pl.loop(0, steps)
    def _(s):
        for d in range(2):
            t = time_of(1 - d, s)

            @pl.when(s > 0)
            def _():
                wait_bytes(
                    received_back.at[d, jnp.maximum(s - 1, 0), others],
                    sum_sems.at[1, d, jnp.maximum(s - 1, 0)],
                )
                grad_lin_ref[0] = jnp.sum(
                    received_back[d, jnp.maximum(s - 1, 0)].astype(jnp.float32), axis=0
                )

            @pl.when(s == 0)
            def _():
                grad_lin_ref[0] = jnp.zeros((own, width), jnp.float32)

            grad_state = grad_lin_ref[0] + out_grad_ref[d, t].astype(jnp.float32)
            squashed = jnp.tanh(projected[d, t] * (1.0 / 3.0))
            grad_proj_ref[d, t, own_rows] = (grad_state * (1.0 - squashed * squashed)).astype(
                jnp.bfloat16
            )
            for peer in peers:
                send(
                    grad_proj_ref.at[d, t, own_rows],
                    grad_proj_ref.at[d, t, own_rows],
                    share_send_sems.at[1, d],
                    share_sems.at[1, d, s],
                    peer,
                )
        for d in range(2):
            t = time_of(1 - d, s)
            wait_bytes(grad_proj_ref.at[d, t, pl.ds(0, (team - 1) * own)], share_sems.at[1, d, s])
            wait_bytes(
                grad_proj_ref.at[d, t, pl.ds(0, (team - 1) * own)], share_send_sems.at[1, d]
            )

            @pl.loop(0, group // row_block)
            def _(block):
                rows = pl.ds(pl.multiple_of(block * row_block, row_block), row_block)
                grad_full = jnp.dot(
                    grad_proj_ref[d, t, rows], proj_ref[d], preferred_element_type=jnp.float32
                )
                in_gate = gates[d, t, rows, pl.ds(0, cells)]
                forget_gate = gates[d, t, rows, pl.ds(cells, cells)]
                candidate = gates[d, t, rows, pl.ds(2 * cells, cells)]
                out_gate = gates[d, t, rows, pl.ds(3 * cells, cells)]
                start = cell_start[d, t, rows]
                clipped = jnp.tanh((forget_gate * start + in_gate * candidate) * (1.0 / 3.0))
                tanh_cell = jnp.tanh(3.0 * clipped)
                total = grad_cell[d, rows] + grad_full * out_gate * (1.0 - tanh_cell * tanh_cell)
                grad_raw = total * (1.0 - clipped * clipped)
                grad_gates_ref[d, t, rows, pl.ds(0, cells)] = (
                    grad_raw * candidate * in_gate * (1.0 - in_gate)
                ).astype(jnp.bfloat16)
                grad_gates_ref[d, t, rows, pl.ds(cells, cells)] = (
                    grad_raw * start * forget_gate * (1.0 - forget_gate)
                ).astype(jnp.bfloat16)
                grad_gates_ref[d, t, rows, pl.ds(2 * cells, cells)] = (
                    grad_raw * in_gate * (1.0 - candidate * candidate)
                ).astype(jnp.bfloat16)
                grad_gates_ref[d, t, rows, pl.ds(3 * cells, cells)] = (
                    grad_full * tanh_cell * out_gate * (1.0 - out_gate)
                ).astype(jnp.bfloat16)
                grad_cell[d, rows] = grad_raw * forget_gate * keep_ref[d, t, rows]

            wait_bytes(stage.at[d, others], send_sems.at[d])

            @pl.when(s < last)
            def _():
                part = (
                    lax.dot_general(
                        grad_gates_ref[d, t],
                        weight_ref[d, width:],
                        (((1,), (1,)), ((), ())),
                        preferred_element_type=jnp.float32,
                    )
                    * keep_ref[d, t]
                )
                stage[d] = part.astype(jnp.bfloat16).reshape(team, own, width)
                received_back[d, s, place] = stage[d, place]
                for peer in peers:
                    send(
                        stage.at[d, peer],
                        received_back.at[d, s, place],
                        send_sems.at[d],
                        sum_sems.at[1, d, s],
                        peer,
                    )

            grad_lin_sum[t] += lax.dot_general(
                grad_gates_ref[d, t],
                weight_ref[d, :width],
                (((1,), (1,)), ((), ())),
                preferred_element_type=jnp.float32,
            )

    for t in range(steps):
        stage_lin[:, t] = grad_lin_sum[t].astype(jnp.bfloat16).reshape(team, own, width)
    received_lin[place] = stage_lin[place]
    for peer in peers:
        send(
            stage_lin.at[peer], received_lin.at[place], lin_sems.at[2], lin_sems.at[3], peer
        )
    wait_bytes(received_lin.at[others], lin_sems.at[3])
    grad_lin_ref[...] = jnp.sum(received_lin[...].astype(jnp.float32), axis=0)
    wait_bytes(stage_lin.at[others], lin_sems.at[2])
    wait_bytes(lin_all_ref.at[:, pl.ds(0, (team - 1) * own)], lin_sems.at[0])


def run_lstm(lin_own, out_grad, weights, proj_turned, bias, keep):
    team = team_size()
    steps, own, width = lin_own.shape
    group = team * own
    cells = proj_turned.shape[2]
    bf16, f32 = jnp.bfloat16, jnp.float32
    vmem = pl.BlockSpec(memory_space=pltpu.VMEM)
    return pl.pallas_call(
        partial(lstm_kernel, team),
        in_specs=[vmem] * 6,
        out_specs=[vmem] * 6,
        out_shape=[
            jax.ShapeDtypeStruct((steps, own, width), f32),
            jax.ShapeDtypeStruct((2, steps, group, 4 * cells), bf16),
            jax.ShapeDtypeStruct((steps, group, width), bf16),
            jax.ShapeDtypeStruct((2, steps, group, width), bf16),
            jax.ShapeDtypeStruct((2, steps, group, cells), bf16),
            jax.ShapeDtypeStruct((2, steps, group, width), bf16),
        ],
        scratch_shapes=[
            pltpu.VMEM((2, steps, group, 4 * cells), f32),
            pltpu.VMEM((2, steps, group, cells), f32),
            pltpu.VMEM((2, steps, own, width), f32),
            pltpu.VMEM((2, team, own, width), bf16),
            pltpu.VMEM((2, steps, team, own, width), bf16),
            pltpu.VMEM((2, steps, team, own, width), bf16),
            pltpu.VMEM((2, group, cells), f32),
            pltpu.VMEM((steps, group, width), f32),
            pltpu.VMEM((team, steps, own, width), bf16),
            pltpu.VMEM((team, steps, own, width), bf16),
            pltpu.SemaphoreType.DMA((4,)),
            pltpu.SemaphoreType.DMA((2,)),
            pltpu.SemaphoreType.DMA((2, 2, steps)),
            pltpu.SemaphoreType.DMA((2, 2)),
            pltpu.SemaphoreType.DMA((2, 2, steps)),
        ],
        compiler_params=pltpu.CompilerParams(
            collective_id=1, has_side_effects=True, vmem_limit_bytes=62 * 1024 * 1024
        ),
        name="lstm_team",
    )(lin_own, out_grad, weights, proj_turned, bias, keep)


def natural_rows(gathered, rows):
    g, y = lax.axis_size("g"), lax.axis_size("y")
    t, x, c = lax.axis_size("t"), lax.axis_size("x"), lax.axis_size("c")
    lanes = gathered.shape[-1]
    split = gathered.reshape(g, y, t, x, c, 2, rows, lanes)
    return split.transpose(5, 0, 2, 1, 3, 4, 6, 7).reshape(2, g * y * t * x * c * rows, lanes)


def owner_rows(values):
    g, y = lax.axis_size("g"), lax.axis_size("y")
    t, x, c = lax.axis_size("t"), lax.axis_size("x"), lax.axis_size("c")
    rows = values.shape[1] // (g * y * t * x * c)
    lanes = values.shape[2]
    split = values.reshape(2, g, t, y, x, c, rows, lanes).transpose(1, 3, 2, 4, 5, 0, 6, 7)
    return split.reshape(g * y, t * x * c, 2 * rows, lanes)


def team_slices(values, parts):
    team = team_size()
    two, rows, columns = values.shape
    lanes = columns // (parts * team)
    split = values.reshape(two, rows, parts, team, lanes).transpose(3, 0, 1, 2, 4)
    return split.reshape(team, two * rows, parts * lanes)


def whole_columns(received, parts):
    team, two_rows, lanes = received.shape
    split = received.reshape(team, 2, two_rows // 2, parts, lanes // parts)
    return split.transpose(1, 2, 3, 0, 4).reshape(2, two_rows // 2, team * lanes)


def shards(
    char_ids,
    resets,
    out_grad,
    char_table,
    conv_weight,
    conv_bias,
    highway_weight,
    highway_bias,
    proj_weight,
    proj_bias,
    lstm_weight,
    lstm_bias,
    lstm_proj,
):
    f32, bf16 = jnp.float32, jnp.bfloat16
    own, steps = resets.shape
    team = team_size()
    place = team_place()
    devices = team * lax.axis_size("g") * lax.axis_size("y")
    bank_cols = conv_weight.shape[3]
    highway_rows = highway_weight.shape[1]
    features_all = highway_rows * devices
    part = features_all // team
    lstm_rows = lstm_weight.shape[1]
    width = proj_weight.shape[1]
    cells_all = lstm_proj.shape[1]
    cells = cells_all // team

    sizes = [highway_bias.size, proj_bias.size, lstm_bias.size, resets.size]
    small = jnp.concatenate(
        [
            highway_bias.reshape(-1),
            proj_bias.reshape(-1),
            lstm_bias.reshape(-1),
            resets.astype(bf16).reshape(-1),
        ]
    )
    small_all = lax.all_gather(small[None], EVERY, axis=0, tiled=True)
    cut = [sum(sizes[:k]) for k in range(5)]
    highway_bias_all = small_all[:, cut[0] : cut[1]].reshape(devices, 2, -1)
    highway_bias_all = highway_bias_all.transpose(1, 0, 2).reshape(2, 2, team, part)
    proj_bias_all = small_all[:, cut[1] : cut[2]].reshape(-1).astype(f32)
    lstm_bias_all = small_all[:, cut[2] : cut[3]].reshape(devices, 2, -1)
    lstm_bias_all = lstm_bias_all.transpose(1, 0, 2).reshape(2, 4, team, cells)
    resets_all = small_all[:, cut[3] : cut[4]].reshape(
        lax.axis_size("g"), lax.axis_size("t"), lax.axis_size("y"), -1, own, steps
    )
    resets_team = lax.dynamic_index_in_dim(resets_all, lax.axis_index("g"), 0, False)
    resets_team = lax.dynamic_index_in_dim(resets_team, lax.axis_index("y"), 1, False)
    resets_team = resets_team.reshape(team * own, steps).astype(f32)
    highway_bias_own = lax.dynamic_index_in_dim(highway_bias_all, place, 2, False)
    highway_bias_own = highway_bias_own.reshape(2, 2 * part).astype(f32)
    lstm_bias_own = lax.dynamic_index_in_dim(lstm_bias_all, place, 2, False)
    lstm_bias_own = lstm_bias_own.reshape(2, 1, 4 * cells).astype(f32)

    highway_swapped = swap_team(team_slices(highway_weight, 2))
    highway_own = natural_rows(
        lax.all_gather(highway_swapped, GRID, axis=0, tiled=False), highway_rows
    )
    lstm_swapped = swap_team(team_slices(lstm_weight, 4))
    lstm_own = natural_rows(lax.all_gather(lstm_swapped, GRID, axis=0, tiled=False), lstm_rows)
    turned_swapped = swap_team(team_slices(jnp.swapaxes(lstm_proj, 1, 2), 1))
    turned_own = natural_rows(
        lax.all_gather(turned_swapped, GRID, axis=0, tiled=False), lstm_proj.shape[2]
    )
    project_full = lax.all_gather(proj_weight, EVERY, axis=0, tiled=True)

    conv_weight_all = lax.all_gather(conv_weight, ("x", "c"), axis=0, tiled=True)
    conv_bias_all = lax.all_gather(conv_bias, ("x", "c"), axis=0, tiled=True)
    bank = lax.axis_index("x") * lax.axis_size("c") + lax.axis_index("c")
    own_ids = lax.dynamic_slice_in_dim(char_ids, bank * own, own, axis=0).reshape(
        own * steps, char_ids.shape[2]
    )
    filters, counts = filter_matrix(conv_weight_all, conv_bias_all)
    tight_from = wide_columns(bank_cols)
    padded_ids, tiled, features, pooled_lse = pool_tokens(
        own_ids, char_table, filters, counts, tight_from
    )

    tokens = own * steps
    operands, hiddens, mixes = [], [], []
    operand = share_team(features).reshape(team * tokens, features_all)
    hidden = lax.dynamic_slice_in_dim(operand, place * part, part, axis=1).astype(f32)
    for level in range(2):
        mixed = (
            jnp.dot(operand, highway_own[level], preferred_element_type=f32)
            + highway_bias_own[level]
        )
        operands.append(operand)
        hiddens.append(hidden)
        mixes.append(mixed)
        carry_gate = jax.nn.sigmoid(mixed[:, part:])
        hidden = carry_gate * hidden + (1.0 - carry_gate) * jax.nn.silu(mixed[:, :part])
        if level == 0:
            operand = share_team(hidden.astype(bf16)).transpose(1, 0, 2)
            operand = operand.reshape(team * tokens, features_all)
    top = swap_team(hidden.astype(bf16).reshape(team, tokens, part))
    top_rows = top.transpose(1, 0, 2).reshape(tokens, features_all)
    lin = (jnp.dot(top_rows, project_full, preferred_element_type=f32) + proj_bias_all).astype(bf16)

    keep_forward = 1.0 - resets_team
    keep_backward = 1.0 - jnp.concatenate(
        [resets_team[:, 1:], jnp.zeros((team * own, 1), f32)], axis=1
    )
    keep = jnp.stack([keep_forward.T, keep_backward.T])[..., None]
    lin_own = jnp.swapaxes(lin.reshape(own, steps, width), 0, 1)
    grad_time = out_grad.reshape(own, steps, 2, width).transpose(2, 1, 0, 3)
    grad_lin, grad_gates, lin_all, states, fulls, grad_projected = run_lstm(
        lin_own, grad_time, lstm_own, turned_own, lstm_bias_own, keep
    )

    count = steps * team * own
    flat_lin = lin_all.reshape(count, width)
    weight_parts, turned_parts, bias_parts = [], [], []
    for d in range(2):
        flat_gates = grad_gates[d].reshape(count, 4 * cells)
        weight_parts.append(
            jnp.concatenate(
                [
                    outer_sum(flat_lin, flat_gates).astype(bf16),
                    outer_sum(states[d].reshape(count, width), flat_gates).astype(bf16),
                ],
                axis=0,
            )
        )
        turned_parts.append(
            outer_sum(
                grad_projected[d].reshape(count, width), fulls[d].reshape(count, cells)
            ).astype(bf16)
        )
        bias_parts.append(column_sum(flat_gates))
    lstm_summed = lax.psum_scatter(
        owner_rows(jnp.stack(weight_parts)), GRID, scatter_dimension=0, tiled=False
    )
    turned_summed = lax.psum_scatter(
        owner_rows(jnp.stack(turned_parts)), GRID, scatter_dimension=0, tiled=False
    )

    grad_input = jnp.swapaxes(grad_lin, 0, 1).reshape(tokens, width).astype(bf16)
    grad_project_w = outer_sum(top_rows, grad_input)
    grad_project_b = column_sum(grad_input)
    grad_top = transposed(grad_input, project_full).astype(bf16)
    grad_top = swap_team(grad_top.reshape(tokens, team, part).transpose(1, 0, 2))
    grad_hidden = grad_top.reshape(team * tokens, part).astype(f32)
    highway_parts, highway_bias_parts = [None, None], [None, None]
    for level in (1, 0):
        operand, hidden_in, mixed = operands[level], hiddens[level], mixes[level]
        carry_gate = jax.nn.sigmoid(mixed[:, part:])
        pre_act = mixed[:, :part]
        act_sig = jax.nn.sigmoid(pre_act)
        grad_act = grad_hidden * (1.0 - carry_gate) * act_sig * (1.0 + pre_act * (1.0 - act_sig))
        grad_carry = grad_hidden * (hidden_in - pre_act * act_sig) * carry_gate * (1.0 - carry_gate)
        grad_mixed = jnp.concatenate([grad_act, grad_carry], axis=1).astype(bf16)
        highway_parts[level] = outer_sum(operand, grad_mixed).astype(bf16)
        highway_bias_parts[level] = column_sum(grad_mixed)
        direct = grad_hidden * carry_gate
        spread = transposed(grad_mixed, highway_own[level])
        if level == 1:
            spread = spread.astype(bf16).reshape(team * tokens, team, part).transpose(1, 0, 2)
            grad_hidden = direct + swap_team(spread).astype(f32).sum(axis=0)
        else:
            held = lax.dynamic_slice_in_dim(spread, place * part, part, axis=1)
            spread = lax.dynamic_update_slice_in_dim(spread, held + direct, place * part, axis=1)
            spread = spread.astype(bf16).reshape(team, tokens, features_all)
            grad_features = swap_team(spread).astype(f32).sum(axis=0).astype(bf16)

    highway_summed = lax.psum_scatter(
        owner_rows(jnp.stack(highway_parts)), GRID, scatter_dimension=0, tiled=False
    )
    project_grad = lax.psum_scatter(
        grad_project_w.astype(bf16), EVERY, scatter_dimension=0, tiled=True
    ).astype(f32)

    grad_filters, grad_table = pool_grads(
        padded_ids,
        tiled,
        filters,
        counts,
        pooled_lse,
        grad_features,
        char_table.shape[0],
        tight_from,
    )
    lstm_weight_grad = whole_columns(swap_team(lstm_summed), 4).astype(f32)
    turned_grad = whole_columns(swap_team(turned_summed), 1).astype(f32)
    lstm_proj_grad = jnp.swapaxes(turned_grad, 1, 2)
    highway_weight_grad = whole_columns(swap_team(highway_summed), 2).astype(f32)

    def own_place(values, parts):
        lanes = values.shape[-1] // parts
        split = values.reshape(2, parts, 1, lanes)
        full = jnp.zeros((2, parts, team, lanes), f32)
        return lax.dynamic_update_slice(full, split, (0, 0, place, 0)).reshape(2, -1)

    lstm_bias_parts = own_place(jnp.stack(bias_parts), 4)
    highway_bias_parts = own_place(jnp.stack(highway_bias_parts), 2)
    pieces = [
        lstm_bias_parts.reshape(2, devices, -1).transpose(1, 0, 2).reshape(devices, -1),
        highway_bias_parts.reshape(2, devices, -1).transpose(1, 0, 2).reshape(devices, -1),
        grad_project_b.reshape(devices, -1),
    ]
    lengths = [piece.shape[1] for piece in pieces]
    mine = lax.all_to_all(
        jnp.concatenate(pieces, axis=1), EVERY, split_axis=0, concat_axis=0, tiled=True
    ).sum(axis=0)
    lstm_bias_grad = mine[: lengths[0]].reshape(2, -1)
    highway_bias_grad = mine[lengths[0] : lengths[0] + lengths[1]].reshape(2, -1)
    proj_bias_grad = mine[lengths[0] + lengths[1] :]

    grad_kernel, grad_bias = split_banks(grad_filters, bank_cols)
    grad_kernel = lax.psum(
        lax.psum_scatter(grad_kernel, ("x", "c"), scatter_dimension=0, tiled=True), ("g", "t", "y")
    )
    grad_bias = lax.psum(
        lax.psum_scatter(grad_bias, ("x", "c"), scatter_dimension=0, tiled=True), ("g", "t", "y")
    )
    grad_table = lax.psum(grad_table, EVERY)
    return (
        grad_table,
        grad_kernel,
        grad_bias,
        highway_weight_grad,
        highway_bias_grad,
        project_grad,
        proj_bias_grad,
        lstm_weight_grad,
        lstm_bias_grad,
        lstm_proj_grad,
    )


def solution(mesh):
    dp, bank = mesh.shape["dp"], mesh.shape["bank"]
    fine = Mesh(mesh.devices.reshape(dp // 4, 2, 2, bank // 2, 2), EVERY)
    rows, banks = ("g", "t", "y"), ("x", "c")
    whole = rows + banks
    placed = (
        P(rows, None, None),
        P(whole, None),
        P(whole, None, None),
        P(),
        P(banks, None, None, None),
        P(banks, None),
        P(None, whole, None),
        P(None, whole),
        P(whole, None),
        P(whole),
        P(None, whole, None),
        P(None, whole),
        P(None, None, whole),
    )
    return jax.shard_map(
        shards,
        mesh=fine,
        in_specs=placed,
        out_specs=(
            P(),
            P(banks, None, None, None),
            P(banks, None),
            P(None, whole, None),
            P(None, whole),
            P(whole, None),
            P(whole),
            P(None, whole, None),
            P(None, whole),
            P(None, None, whole),
        ),
        check_vma=False,
    )
```

```python
from functools import partial
import math

import jax
import jax.numpy as jnp
from jax import lax
from jax.experimental import pallas as pl
from jax.experimental.pallas import tpu as pltpu
from jax.sharding import Mesh, PartitionSpec as P

CHAR_COUNT = 50
EMBED = 16
WIDEST = 7
TAPS = WIDEST * EMBED
LANES = 128
PLACES = 64
TIGHT = 48
CHUNK = 256
TOKEN_BLOCK = 16


def bank_plan(bank_cols):
    return [
        [
            (1, 0, bank_cols // 32),
            (2, bank_cols // 32, bank_cols // 32),
            (3, bank_cols // 16, bank_cols // 16),
            (4, bank_cols // 8, bank_cols // 8),
        ],
        [(5, 0, bank_cols // 4)],
        [(6, 0, bank_cols // 2)],
        [(7, 0, bank_cols)],
    ]


def transposed(former, latter):
    return lax.dot_general(
        former, latter, (((1,), (1,)), ((), ())), preferred_element_type=jnp.float32
    )


def outer_sum(former, latter):
    return lax.dot_general(
        former, latter, (((0,), (0,)), ((), ())), preferred_element_type=jnp.float32
    )


def column_sum(values):
    ones_row = jnp.ones((1, values.shape[0]), values.dtype)
    return jnp.dot(ones_row, values, preferred_element_type=jnp.float32)[0]


def filter_columns(bank_cols):
    columns = []
    for bank_index, bank_specs in enumerate(bank_plan(bank_cols)):
        for filter_width, first_col, count in bank_specs:
            columns.append((filter_width, bank_index, first_col, count))
    return columns


def shift_rows(values, amount):
    count = values.shape[0]
    return values if amount % count == 0 else pltpu.roll(values, amount % count, 0)


def block_windows(tiled_ref, windows_wide, windows_tight):
    tokens, places, lanes = tiled_ref.shape
    rows = tokens * places
    tiled = tiled_ref[...].astype(jnp.float32).reshape(rows, lanes)
    lane = lax.broadcasted_iota(jnp.int32, (rows, lanes), 1)
    place = lax.broadcasted_iota(jnp.int32, (rows, lanes), 0) % places
    windows = tiled
    for offset in range(1, WIDEST):
        windows = jnp.where(lane // EMBED == offset, shift_rows(tiled, rows - offset), windows)
    late = place >= CHAR_COUNT - WIDEST + 1 + (lane - TAPS - 1)
    extra = jnp.where((lane == TAPS) | ((lane <= TAPS + WIDEST) & late), 1.0, 0.0)
    windows = jnp.where(lane < TAPS, windows, extra)
    windows_wide[...] = windows.astype(jnp.bfloat16)
    windows_tight[...] = (
        windows.reshape(tokens, places, lanes)[:, :TIGHT]
        .reshape(tokens * TIGHT, lanes)
        .astype(jnp.bfloat16)
    )


def column_chunks(total, tight_from):
    return [
        (start, start < tight_from) for start in range(0, total, CHUNK)
    ]


def pool_kernel(tight_from, tiled_ref, weight_ref, count_ref, features_ref, lse_ref, wide, tight):
    tokens, places, lanes = tiled_ref.shape
    block_windows(tiled_ref, wide, tight)
    for start, is_wide in column_chunks(weight_ref.shape[1], tight_from):
        cols = pl.ds(start, CHUNK)
        windows = wide if is_wide else tight
        conv_out = jnp.dot(
            windows[...], weight_ref[:, cols], preferred_element_type=jnp.float32
        ).reshape(tokens, -1, CHUNK)
        highest = jnp.max(conv_out, axis=1)
        total = jnp.sum(jnp.exp(conv_out - highest[:, None, :]), axis=1)
        pooled_lse = highest + jnp.log(total)
        lse_ref[:, cols] = pooled_lse
        pooled_pre = pooled_lse - count_ref[0:1, cols]
        features_ref[:, cols] = (pooled_pre * jax.nn.sigmoid(pooled_pre)).astype(jnp.bfloat16)


def pool_grad_kernel(
    tight_from,
    tiled_ref,
    weight_ref,
    count_ref,
    lse_ref,
    upstream_ref,
    grad_weight_ref,
    aligned_ref,
    wide,
    tight,
    spread,
):
    tokens, places, lanes = tiled_ref.shape
    block_windows(tiled_ref, wide, tight)

    @pl.when(pl.program_id(0) == 0)
    def _():
        grad_weight_ref[...] = jnp.zeros_like(grad_weight_ref)

    spread[...] = jnp.zeros_like(spread)
    wide_turned = wide[...].T
    tight_turned = tight[...].T
    for start, is_wide in column_chunks(weight_ref.shape[1], tight_from):
        cols = pl.ds(start, CHUNK)
        windows, turned = (wide, wide_turned) if is_wide else (tight, tight_turned)
        weights = weight_ref[:, cols]
        conv_out = jnp.dot(
            windows[...], weights, preferred_element_type=jnp.float32
        ).reshape(tokens, -1, CHUNK)
        pooled_lse = lse_ref[:, cols]
        pooled_pre = pooled_lse - count_ref[0:1, cols]
        squashed = jax.nn.sigmoid(pooled_pre)
        upstream = (
            upstream_ref[:, cols].astype(jnp.float32)
            * squashed
            * (1.0 + pooled_pre * (1.0 - squashed))
        )
        softened = jnp.exp(conv_out - pooled_lse[:, None, :])
        grad_conv = (softened * upstream[:, None, :]).astype(jnp.bfloat16)
        places_here = grad_conv.shape[1]
        grad_conv = grad_conv.reshape(tokens * places_here, CHUNK)
        grad_weight_ref[:, cols] += jnp.dot(turned, grad_conv, preferred_element_type=jnp.float32)
        part = lax.dot_general(
            grad_conv, weights, (((1,), (1,)), ((), ())), preferred_element_type=jnp.float32
        ).reshape(tokens, places_here, lanes)
        spread[:, :places_here, :] += part
    rows = tokens * places
    flat = spread[...].reshape(rows, lanes)
    lane = lax.broadcasted_iota(jnp.int32, (rows, lanes), 1)
    aligned = jnp.where(lane < EMBED, flat, 0.0)
    for offset in range(1, WIDEST):
        aligned = jnp.where(lane // EMBED == offset, shift_rows(flat, offset), aligned)
    aligned_ref[...] = aligned.reshape(tokens, places, lanes)


def filter_matrix(conv_weight, conv_bias):
    bank_cols = conv_bias.shape[1]
    taps, biases, masks, counts = [], [], [], []
    for filter_width, bank_index, first_col, count in filter_columns(bank_cols):
        piece = conv_weight[bank_index, :filter_width, :, first_col : first_col + count]
        piece = piece.reshape(filter_width * EMBED, count)
        taps.append(jnp.pad(piece, ((0, TAPS - filter_width * EMBED), (0, 0))))
        biases.append(conv_bias[bank_index, first_col : first_col + count])
        rows = lax.broadcasted_iota(jnp.int32, (LANES - TAPS - 1, count), 0)
        masks.append(jnp.where(rows == WIDEST - filter_width, -1e30, 0.0).astype(jnp.bfloat16))
        counts.append(jnp.full((8, count), math.log(CHAR_COUNT - filter_width + 1), jnp.float32))
    weights = jnp.concatenate(
        [
            jnp.concatenate(taps, axis=1),
            jnp.concatenate(biases)[None],
            jnp.concatenate(masks, axis=1),
        ],
        axis=0,
    )
    return (weights, jnp.concatenate(counts, axis=1))


def wide_columns(bank_cols):
    total = sum(count for width, bank, first, count in filter_columns(bank_cols) if CHAR_COUNT - width + 1 > TIGHT - 2)
    return -(-total // CHUNK) * CHUNK


def char_selector(token_ids, vocab_size):
    return token_ids.reshape(-1)[:, None] == lax.broadcasted_iota(jnp.int32, (1, vocab_size), 1)


def pool_tokens(token_ids, char_table, weights, counts, tight_from):
    tokens = token_ids.shape[0]
    padded = jnp.pad(token_ids, ((0, 0), (0, PLACES - token_ids.shape[1])), constant_values=-1)
    table_tiled = jnp.pad(jnp.tile(char_table, (1, WIDEST)), ((0, 0), (0, LANES - TAPS)))
    selector = char_selector(padded, char_table.shape[0]).astype(jnp.bfloat16)
    tiled = jnp.dot(selector, table_tiled, preferred_element_type=jnp.float32)
    tiled = tiled.astype(jnp.bfloat16).reshape(tokens, PLACES, LANES)
    block = math.gcd(tokens, TOKEN_BLOCK)
    total = weights.shape[1]
    features, pooled_lse = pl.pallas_call(
        partial(pool_kernel, tight_from),
        grid=(tokens // block,),
        in_specs=[
            pl.BlockSpec((block, PLACES, LANES), lambda i: (i, 0, 0)),
            pl.BlockSpec((LANES, total), lambda i: (0, 0)),
            pl.BlockSpec((8, total), lambda i: (0, 0)),
        ],
        out_specs=[
            pl.BlockSpec((block, total), lambda i: (i, 0)),
            pl.BlockSpec((block, total), lambda i: (i, 0)),
        ],
        out_shape=[
            jax.ShapeDtypeStruct((tokens, total), jnp.bfloat16),
            jax.ShapeDtypeStruct((tokens, total), jnp.float32),
        ],
        scratch_shapes=[
            pltpu.VMEM((block * PLACES, LANES), jnp.bfloat16),
            pltpu.VMEM((block * TIGHT, LANES), jnp.bfloat16),
        ],
        compiler_params=pltpu.CompilerParams(vmem_limit_bytes=40 * 1024 * 1024),
        name="pool_tokens",
    )(tiled, weights, counts)
    return (padded, tiled, features, pooled_lse)


def pool_grads(padded, tiled, weights, counts, pooled_lse, upstream, vocab_size, tight_from):
    tokens = tiled.shape[0]
    block = math.gcd(tokens, TOKEN_BLOCK)
    total = weights.shape[1]
    grad_weight, aligned = pl.pallas_call(
        partial(pool_grad_kernel, tight_from),
        grid=(tokens // block,),
        in_specs=[
            pl.BlockSpec((block, PLACES, LANES), lambda i: (i, 0, 0)),
            pl.BlockSpec((LANES, total), lambda i: (0, 0)),
            pl.BlockSpec((8, total), lambda i: (0, 0)),
            pl.BlockSpec((block, total), lambda i: (i, 0)),
            pl.BlockSpec((block, total), lambda i: (i, 0)),
        ],
        out_specs=[
            pl.BlockSpec((LANES, total), lambda i: (0, 0)),
            pl.BlockSpec((block, PLACES, LANES), lambda i: (i, 0, 0)),
        ],
        out_shape=[
            jax.ShapeDtypeStruct((LANES, total), jnp.float32),
            jax.ShapeDtypeStruct((tokens, PLACES, LANES), jnp.float32),
        ],
        scratch_shapes=[
            pltpu.VMEM((block * PLACES, LANES), jnp.bfloat16),
            pltpu.VMEM((block * TIGHT, LANES), jnp.bfloat16),
            pltpu.VMEM((block, PLACES, LANES), jnp.float32),
        ],
        compiler_params=pltpu.CompilerParams(vmem_limit_bytes=40 * 1024 * 1024),
        name="pool_grads",
    )(tiled, weights, counts, pooled_lse, upstream)
    aligned = aligned.reshape(tokens * PLACES, LANES)
    selector = char_selector(padded, vocab_size).astype(jnp.bfloat16)
    high = aligned.astype(jnp.bfloat16)
    low = (aligned - high.astype(jnp.float32)).astype(jnp.bfloat16)
    by_tap = outer_sum(selector, high) + outer_sum(selector, low)
    grad_table = by_tap[:, :TAPS].reshape(vocab_size, WIDEST, EMBED).sum(axis=1)
    return (grad_weight, grad_table)


TEAM = ("t", "x", "c")
GRID = ("g", "y")
EVERY = ("g", "t", "y", "x", "c")


def team_place():
    x_size, c_size = lax.axis_size("x"), lax.axis_size("c")
    return (lax.axis_index("t") * x_size + lax.axis_index("x")) * c_size + lax.axis_index("c")


def team_size():
    return lax.axis_size("t") * lax.axis_size("x") * lax.axis_size("c")


def team_coords(place):
    x_size, c_size = lax.axis_size("x"), lax.axis_size("c")
    return {
        "t": place // (x_size * c_size),
        "x": lax.rem(place // c_size, x_size),
        "c": lax.rem(place, c_size),
    }


def swap_team(values):
    return lax.all_to_all(values, TEAM, split_axis=0, concat_axis=0, tiled=True)


def share_team(values):
    team = team_size()
    return swap_team(jnp.broadcast_to(values[None], (team,) + values.shape))


def sigmoid(values):
    return 0.5 * jnp.tanh(0.5 * values) + 0.5


def wait_bytes(ref, sem):
    pltpu.make_async_copy(ref, ref, sem).wait()


def lstm_kernel(
    team,
    parts_ref,
    lin_bias_ref,
    out_grad_ref,
    weight_hbm,
    turned_hbm,
    bias_ref,
    keep_ref,
    grad_lin_all_ref,
    grad_weight_hbm,
    grad_turned_hbm,
    grad_bias_ref,
    weight_ref,
    proj_ref,
    grad_gates_ref,
    lin_all_ref,
    state_ref,
    full_ref,
    grad_proj_ref,
    gates,
    cell_start,
    projected,
    stage,
    received,
    received_back,
    grad_cell,
    grad_lin_sum,
    stage_lin,
    received_lin,
    grad_state_own,
    grad_stage,
    turned_stage,
    load_sems,
    lin_sems,
    send_sems,
    sum_sems,
    share_send_sems,
    share_sems,
    out_sems,
):
    _, steps, own, width = parts_ref.shape
    group = team * own
    cells = proj_ref.shape[2]
    row_block = 32
    place = team_place()
    own_rows = pl.ds(pl.multiple_of(place * own, own), own)
    peers = [lax.rem(place + k, team) for k in range(1, team)]
    last = steps - 1
    others = pl.ds(0, team - 1)
    other_rows = pl.ds(0, (team - 1) * own)
    g_size, y_size = lax.axis_size("g"), lax.axis_size("y")
    t_size = lax.axis_size("t")
    blocks = [
        (g * y_size + y, t, (g * t_size + t) * y_size + y)
        for g in range(g_size)
        for t in range(t_size)
        for y in range(y_size)
    ]
    run = weight_hbm.shape[3]
    turned_run = turned_hbm.shape[3]

    for d in range(2):
        for source, t, at in blocks:
            pltpu.make_async_copy(
                weight_hbm.at[source, t, d],
                weight_ref.at[d, pl.ds(at * run, run)],
                load_sems.at[0],
            ).start()
            pltpu.make_async_copy(
                turned_hbm.at[source, t, d],
                proj_ref.at[d, pl.ds(at * turned_run, turned_run)],
                load_sems.at[1],
            ).start()

    barrier = pltpu.get_barrier_semaphore()
    for peer in peers:
        pl.semaphore_signal(
            barrier, inc=1, device_id=team_coords(peer), device_id_type=pl.DeviceIdType.MESH
        )
    pl.semaphore_wait(barrier, team - 1)

    def send(source, target, send_sem, recv_sem, peer):
        pltpu.make_async_remote_copy(
            src_ref=source,
            dst_ref=target,
            send_sem=send_sem,
            recv_sem=recv_sem,
            device_id=team_coords(peer),
            device_id_type=pl.DeviceIdType.MESH,
        ).start()

    for peer in peers:
        send(parts_ref.at[peer], stage_lin.at[place], lin_sems.at[0], lin_sems.at[1], peer)
    stage_lin[place] = parts_ref[place]
    for d in range(2):
        first = 0 if d == 0 else last
        state_ref[d, first] = jnp.zeros((group, width), jnp.bfloat16)
        cell_start[d, first] = jnp.zeros((group, cells), jnp.float32)
        grad_cell[d] = jnp.zeros((group, cells), jnp.float32)
    grad_lin_sum[...] = jnp.zeros_like(grad_lin_sum)
    wait_bytes(stage_lin.at[others], lin_sems.at[1])
    lin_own = jnp.sum(stage_lin[...].astype(jnp.float32), axis=0) + lin_bias_ref[...]
    lin_all_ref[:, own_rows] = lin_own.astype(jnp.bfloat16)
    for peer in peers:
        send(
            lin_all_ref.at[:, own_rows],
            lin_all_ref.at[:, own_rows],
            lin_sems.at[2],
            lin_sems.at[3],
            peer,
        )
    wait_bytes(weight_ref, load_sems.at[0])
    wait_bytes(proj_ref, load_sems.at[1])
    wait_bytes(lin_all_ref.at[:, other_rows], lin_sems.at[3])

    @pl.loop(0, steps)
    def _(t):
        for d in range(2):
            for q in range(4):
                cols = pl.ds(q * cells, cells)
                gates[d, t, :, cols] = (
                    jnp.dot(
                        lin_all_ref[t],
                        weight_ref[d, :width, cols],
                        preferred_element_type=jnp.float32,
                    )
                    + bias_ref[d, :, cols]
                )

    def time_of(d, s):
        return s if d == 0 else last - s

    @pl.loop(0, steps)
    def _(s):
        for d in range(2):
            t = time_of(d, s)
            later = time_of(d, jnp.minimum(s + 1, last))

            @pl.when(s > 0)
            def _():
                wait_bytes(
                    state_ref.at[d, t, other_rows], share_sems.at[0, d, s]
                )
                for q in range(4):
                    cols = pl.ds(q * cells, cells)
                    gates[d, t, :, cols] += jnp.dot(
                        state_ref[d, t],
                        weight_ref[d, width:, cols],
                        preferred_element_type=jnp.float32,
                    )

            @pl.loop(0, group // row_block)
            def _(block):
                rows = pl.ds(pl.multiple_of(block * row_block, row_block), row_block)
                in_gate = sigmoid(gates[d, t, rows, pl.ds(0, cells)])
                forget_gate = sigmoid(gates[d, t, rows, pl.ds(cells, cells)])
                candidate = jnp.tanh(gates[d, t, rows, pl.ds(2 * cells, cells)])
                out_gate = sigmoid(gates[d, t, rows, pl.ds(3 * cells, cells)])
                gates[d, t, rows, pl.ds(0, cells)] = in_gate
                gates[d, t, rows, pl.ds(cells, cells)] = forget_gate
                gates[d, t, rows, pl.ds(2 * cells, cells)] = candidate
                gates[d, t, rows, pl.ds(3 * cells, cells)] = out_gate
                mixed = forget_gate * cell_start[d, t, rows] + in_gate * candidate
                cell_new = 3.0 * jnp.tanh(mixed * (1.0 / 3.0))
                full_ref[d, t, rows] = (out_gate * jnp.tanh(cell_new)).astype(jnp.bfloat16)

                @pl.when(s < last)
                def _():
                    cell_start[d, later, rows] = cell_new * keep_ref[d, later, rows]

            @pl.when(s > 0)
            def _():
                wait_bytes(stage.at[d, others], send_sems.at[d])

            part = lax.dot_general(
                full_ref[d, t],
                proj_ref[d],
                (((1,), (1,)), ((), ())),
                preferred_element_type=jnp.float32,
            )
            part = part.astype(jnp.bfloat16).reshape(team, own, width)
            stage[d] = part
            received[d, s, place] = stage[d, place]
            for peer in peers:
                send(
                    stage.at[d, peer],
                    received.at[d, s, place],
                    send_sems.at[d],
                    sum_sems.at[0, d, s],
                    peer,
                )
        for d in range(2):
            t = time_of(d, s)
            later = time_of(d, jnp.minimum(s + 1, last))
            wait_bytes(received.at[d, s, others], sum_sems.at[0, d, s])
            total = jnp.sum(received[d, s].astype(jnp.float32), axis=0)
            projected[d, t] = total

            @pl.when(s > 0)
            def _():
                wait_bytes(
                    state_ref.at[d, t, other_rows], share_send_sems.at[0, d]
                )

            @pl.when(s < last)
            def _():
                state_new = (3.0 * jnp.tanh(total * (1.0 / 3.0))).astype(jnp.bfloat16)
                kept = state_new.astype(jnp.float32) * keep_ref[d, later, own_rows]
                state_ref[d, later, own_rows] = kept.astype(jnp.bfloat16)
                for peer in peers:
                    send(
                        state_ref.at[d, later, own_rows],
                        state_ref.at[d, later, own_rows],
                        share_send_sems.at[0, d],
                        share_sems.at[0, d, s + 1],
                        peer,
                    )

    @pl.loop(0, steps)
    def _(s):
        for d in range(2):
            t = time_of(1 - d, s)

            @pl.when(s > 0)
            def _():
                wait_bytes(
                    received_back.at[d, jnp.maximum(s - 1, 0), others],
                    sum_sems.at[1, d, jnp.maximum(s - 1, 0)],
                )
                grad_state_own[...] = jnp.sum(
                    received_back[d, jnp.maximum(s - 1, 0)].astype(jnp.float32), axis=0
                )

            @pl.when(s == 0)
            def _():
                grad_state_own[...] = jnp.zeros((own, width), jnp.float32)

            grad_state = grad_state_own[...] + out_grad_ref[d, t].astype(jnp.float32)
            squashed = jnp.tanh(projected[d, t] * (1.0 / 3.0))
            grad_proj_ref[d, t, own_rows] = (grad_state * (1.0 - squashed * squashed)).astype(
                jnp.bfloat16
            )
            for peer in peers:
                send(
                    grad_proj_ref.at[d, t, own_rows],
                    grad_proj_ref.at[d, t, own_rows],
                    share_send_sems.at[1, d],
                    share_sems.at[1, d, s],
                    peer,
                )
        for d in range(2):
            t = time_of(1 - d, s)
            wait_bytes(grad_proj_ref.at[d, t, other_rows], share_sems.at[1, d, s])
            wait_bytes(
                grad_proj_ref.at[d, t, other_rows], share_send_sems.at[1, d]
            )

            @pl.loop(0, group // row_block)
            def _(block):
                rows = pl.ds(pl.multiple_of(block * row_block, row_block), row_block)
                grad_full = jnp.dot(
                    grad_proj_ref[d, t, rows], proj_ref[d], preferred_element_type=jnp.float32
                )
                in_gate = gates[d, t, rows, pl.ds(0, cells)]
                forget_gate = gates[d, t, rows, pl.ds(cells, cells)]
                candidate = gates[d, t, rows, pl.ds(2 * cells, cells)]
                out_gate = gates[d, t, rows, pl.ds(3 * cells, cells)]
                start = cell_start[d, t, rows]
                clipped = jnp.tanh((forget_gate * start + in_gate * candidate) * (1.0 / 3.0))
                tanh_cell = jnp.tanh(3.0 * clipped)
                total = grad_cell[d, rows] + grad_full * out_gate * (1.0 - tanh_cell * tanh_cell)
                grad_raw = total * (1.0 - clipped * clipped)
                grad_gates_ref[d, t, rows, pl.ds(0, cells)] = (
                    grad_raw * candidate * in_gate * (1.0 - in_gate)
                ).astype(jnp.bfloat16)
                grad_gates_ref[d, t, rows, pl.ds(cells, cells)] = (
                    grad_raw * start * forget_gate * (1.0 - forget_gate)
                ).astype(jnp.bfloat16)
                grad_gates_ref[d, t, rows, pl.ds(2 * cells, cells)] = (
                    grad_raw * in_gate * (1.0 - candidate * candidate)
                ).astype(jnp.bfloat16)
                grad_gates_ref[d, t, rows, pl.ds(3 * cells, cells)] = (
                    grad_full * tanh_cell * out_gate * (1.0 - out_gate)
                ).astype(jnp.bfloat16)
                grad_cell[d, rows] = grad_raw * forget_gate * keep_ref[d, t, rows]

            wait_bytes(stage.at[d, others], send_sems.at[d])

            @pl.when(s < last)
            def _():
                part = (
                    lax.dot_general(
                        grad_gates_ref[d, t],
                        weight_ref[d, width:],
                        (((1,), (1,)), ((), ())),
                        preferred_element_type=jnp.float32,
                    )
                    * keep_ref[d, t]
                )
                stage[d] = part.astype(jnp.bfloat16).reshape(team, own, width)
                received_back[d, s, place] = stage[d, place]
                for peer in peers:
                    send(
                        stage.at[d, peer],
                        received_back.at[d, s, place],
                        send_sems.at[d],
                        sum_sems.at[1, d, s],
                        peer,
                    )

            grad_lin_sum[t] += lax.dot_general(
                grad_gates_ref[d, t],
                weight_ref[d, :width],
                (((1,), (1,)), ((), ())),
                preferred_element_type=jnp.float32,
            )

    wait_bytes(parts_ref.at[others], lin_sems.at[0])
    wait_bytes(lin_all_ref.at[:, other_rows], lin_sems.at[2])
    for t in range(steps):
        stage_lin[:, t] = grad_lin_sum[t].astype(jnp.bfloat16).reshape(team, own, width)
    received_lin[place] = stage_lin[place]
    for peer in peers:
        send(stage_lin.at[peer], received_lin.at[place], lin_sems.at[4], lin_sems.at[5], peer)

    count = steps * group
    half_blocks = len(blocks) // 2

    def weight_grads(d):
        for half in range(2):

            @pl.loop(0, 4)
            def _(q):
                cols = pl.ds(pl.multiple_of(q * cells, cells), cells)
                slot = lax.rem(q, 2)
                rows_in = (lin_all_ref[...] if half == 0 else state_ref[d]).reshape(count, width)
                gate_part = grad_gates_ref[d, :, :, cols].reshape(count, cells)
                part = lax.dot_general(
                    rows_in,
                    gate_part,
                    (((0,), (0,)), ((), ())),
                    preferred_element_type=jnp.float32,
                )

                @pl.when(q >= 2)
                def _():
                    wait_bytes(grad_stage.at[slot], out_sems.at[slot])

                grad_stage[slot] = part.astype(jnp.bfloat16)
                for source, t, at in blocks[half * half_blocks : (half + 1) * half_blocks]:
                    pltpu.make_async_copy(
                        grad_stage.at[slot, pl.ds((at - half * half_blocks) * run, run)],
                        grad_weight_hbm.at[source, t, d, :, cols],
                        out_sems.at[slot],
                    ).start()

            for slot in range(2):
                wait_bytes(grad_stage.at[slot], out_sems.at[slot])
        turned = lax.dot_general(
            grad_proj_ref[d].reshape(count, width),
            full_ref[d].reshape(count, cells),
            (((0,), (0,)), ((), ())),
            preferred_element_type=jnp.float32,
        )
        turned_stage[d] = turned.astype(jnp.bfloat16)
        for source, t, at in blocks:
            pltpu.make_async_copy(
                turned_stage.at[d, pl.ds(at * turned_run, turned_run)],
                grad_turned_hbm.at[source, t, d],
                out_sems.at[2 + d],
            ).start()
        ones = jnp.ones((8, count), jnp.bfloat16)
        for q in range(4):
            cols = pl.ds(q * cells, cells)
            grad_bias_ref[d, :, cols] = jnp.dot(
                ones,
                grad_gates_ref[d, :, :, cols].reshape(count, cells),
                preferred_element_type=jnp.float32,
            )

    weight_grads(0)
    wait_bytes(received_lin.at[others], lin_sems.at[5])
    grad_lin_all_ref[place] = jnp.sum(received_lin[...].astype(jnp.float32), axis=0).astype(
        jnp.bfloat16
    )
    for peer in peers:
        send(
            grad_lin_all_ref.at[place],
            grad_lin_all_ref.at[place],
            lin_sems.at[6],
            lin_sems.at[7],
            peer,
        )
    weight_grads(1)
    wait_bytes(grad_lin_all_ref.at[others], lin_sems.at[7])
    wait_bytes(stage_lin.at[others], lin_sems.at[4])
    wait_bytes(grad_lin_all_ref.at[others], lin_sems.at[6])
    for d in range(2):
        wait_bytes(turned_stage.at[d], out_sems.at[2 + d])


def run_lstm(parts, lin_bias, out_grad, weights, turned, bias, keep):
    team, steps, own, width = parts.shape
    group = team * own
    cells = turned.shape[4]
    bf16, f32 = jnp.bfloat16, jnp.float32
    vmem = pl.BlockSpec(memory_space=pltpu.VMEM)
    hbm = pl.BlockSpec(memory_space=pl.ANY)
    return pl.pallas_call(
        partial(lstm_kernel, team),
        in_specs=[vmem, vmem, vmem, hbm, hbm, vmem, vmem],
        out_specs=[vmem, hbm, hbm, vmem],
        out_shape=[
            jax.ShapeDtypeStruct(parts.shape, bf16),
            jax.ShapeDtypeStruct(weights.shape, bf16),
            jax.ShapeDtypeStruct(turned.shape, bf16),
            jax.ShapeDtypeStruct((2, 8, 4 * cells), f32),
        ],
        scratch_shapes=[
            pltpu.VMEM((2, 2 * width, 4 * cells), bf16),
            pltpu.VMEM((2, width, cells), bf16),
            pltpu.VMEM((2, steps, group, 4 * cells), bf16),
            pltpu.VMEM((steps, group, width), bf16),
            pltpu.VMEM((2, steps, group, width), bf16),
            pltpu.VMEM((2, steps, group, cells), bf16),
            pltpu.VMEM((2, steps, group, width), bf16),
            pltpu.VMEM((2, steps, group, 4 * cells), f32),
            pltpu.VMEM((2, steps, group, cells), f32),
            pltpu.VMEM((2, steps, own, width), f32),
            pltpu.VMEM((2, team, own, width), bf16),
            pltpu.VMEM((2, steps, team, own, width), bf16),
            pltpu.VMEM((2, steps, team, own, width), bf16),
            pltpu.VMEM((2, group, cells), f32),
            pltpu.VMEM((steps, group, width), f32),
            pltpu.VMEM((team, steps, own, width), bf16),
            pltpu.VMEM((team, steps, own, width), bf16),
            pltpu.VMEM((own, width), f32),
            pltpu.VMEM((2, width, cells), bf16),
            pltpu.VMEM((2, width, cells), bf16),
            pltpu.SemaphoreType.DMA((2,)),
            pltpu.SemaphoreType.DMA((8,)),
            pltpu.SemaphoreType.DMA((2,)),
            pltpu.SemaphoreType.DMA((2, 2, steps)),
            pltpu.SemaphoreType.DMA((2, 2)),
            pltpu.SemaphoreType.DMA((2, 2, steps)),
            pltpu.SemaphoreType.DMA((4,)),
        ],
        compiler_params=pltpu.CompilerParams(
            collective_id=1, has_side_effects=True, vmem_limit_bytes=63 * 1024 * 1024
        ),
        name="lstm_team",
    )(parts, lin_bias, out_grad, weights, turned, bias, keep)


def axis_sizes():
    return tuple(lax.axis_size(name) for name in EVERY)


def run_rows(received):
    g, t, y, x, c = axis_sizes()
    lanes = received.shape[-1]
    split = received.reshape(t, x * c, 2, -1, lanes).transpose(0, 2, 1, 3, 4)
    return split.reshape(t, 2, -1, lanes)


def member_rows(runs):
    g, t, y, x, c = axis_sizes()
    lanes = runs.shape[-1]
    split = runs.reshape(t, 2, x * c, -1, lanes).transpose(0, 2, 1, 3, 4)
    return split.reshape(t * x * c, -1, lanes)


def team_rows(gathered):
    grid, team, two_rows, lanes = gathered.shape
    split = gathered.reshape(grid, team, 2, two_rows // 2, lanes)
    return split.transpose(2, 1, 0, 3, 4).reshape(2, -1, lanes)


def owner_team_rows(values):
    g, t, y, x, c = axis_sizes()
    lanes = values.shape[2]
    split = values.reshape(2, t * x * c, g * y, -1, lanes).transpose(2, 1, 0, 3, 4)
    return split.reshape(g * y, t * x * c, -1, lanes)


def team_slices(values, parts):
    team = team_size()
    two, rows, columns = values.shape
    lanes = columns // (parts * team)
    split = values.reshape(two, rows, parts, team, lanes).transpose(3, 0, 1, 2, 4)
    return split.reshape(team, two * rows, parts * lanes)


def whole_columns(received, parts):
    team, two_rows, lanes = received.shape
    split = received.reshape(team, 2, two_rows // 2, parts, lanes // parts)
    return split.transpose(1, 2, 3, 0, 4).reshape(2, two_rows // 2, team * lanes)


def team_first(values):
    g, t, y, x, c = axis_sizes()
    rows = values.shape[0]
    split = values.reshape(rows, -1, g, t, y, x, c, values.shape[1] // (2 * g * t * y * x * c))
    return split.transpose(3, 5, 6, 0, 1, 2, 4, 7)


def permuted_columns(values):
    g, t, y, x, c = axis_sizes()
    split = values.reshape(values.shape[0], g, t, y, x, c, -1)
    return split.transpose(0, 2, 4, 5, 1, 3, 6).reshape(values.shape)


def restored_columns(values):
    g, t, y, x, c = axis_sizes()
    split = values.reshape(values.shape[0], t, x, c, g, y, -1)
    return split.transpose(0, 4, 1, 5, 2, 3, 6).reshape(values.shape)


def padded_rows(values, rows):
    blocks = values.shape[0]
    flat = values.reshape(blocks, -1)
    return jnp.pad(flat, ((0, 0), (0, rows * LANES - flat.shape[1]))).reshape(blocks, rows, LANES)


def row_count(items):
    return -(-items // LANES)


def bank_blocks(grad_filters, bank_cols, groups):
    turned = grad_filters.T
    blocks, at = [], 0
    for bank_specs in bank_plan(bank_cols):
        used = sum(count for width, first, count in bank_specs)
        piece = turned[at : at + used].reshape(groups, used // groups, LANES)
        blocks.append(jnp.pad(piece, ((0, 0), (0, (bank_cols - used) // groups), (0, 0))))
        at += used
    return jnp.stack(blocks, axis=1).reshape(groups * len(blocks), bank_cols // groups, LANES)


def bank_filters(blocks, bank, bank_cols, groups):
    taps = [
        [width * EMBED for width, first, count in bank_specs for _ in range(count)]
        for bank_specs in bank_plan(bank_cols)
    ]
    taps = [row + [0] * (bank_cols - len(row)) for row in taps]
    limit = lax.dynamic_index_in_dim(jnp.asarray(taps, jnp.int32), bank, 0, False)
    used = [sum(count for width, first, count in specs) for specs in bank_plan(bank_cols)]
    choices = [
        lambda value, each=count // groups: jnp.pad(
            value[:, :each].reshape(groups * each, LANES), ((0, bank_cols - groups * each), (0, 0))
        )
        for count in used
    ]
    turned = lax.switch(bank, choices, blocks).T
    row = lax.broadcasted_iota(jnp.int32, (TAPS, 1), 0)
    kernel = jnp.where(row < limit[None, :], turned[:TAPS], 0.0)
    bias = jnp.where(limit > 0, turned[TAPS], 0.0)
    return (kernel.reshape(1, WIDEST, EMBED, bank_cols), bias[None])


def shards(
    char_ids,
    resets,
    out_grad,
    char_table,
    conv_weight,
    conv_bias,
    highway_weight,
    highway_bias,
    proj_weight,
    proj_bias,
    lstm_weight,
    lstm_bias,
    lstm_proj,
):
    f32, bf16 = jnp.float32, jnp.bfloat16
    own, steps = resets.shape
    team = team_size()
    place = team_place()
    devices = team * lax.axis_size("g") * lax.axis_size("y")
    bank_cols = conv_weight.shape[3]
    highway_rows = highway_weight.shape[1]
    features_all = highway_rows * devices
    part = features_all // team
    lstm_rows = lstm_weight.shape[1]
    width = proj_weight.shape[1]
    cells_all = lstm_proj.shape[1]
    cells = cells_all // team

    highway_slices = team_first(highway_weight.reshape(2 * highway_rows, -1))
    highway_swapped = swap_team(highway_slices.reshape(team, 2 * highway_rows, 2 * part))
    first_all = lax.all_gather(
        jnp.concatenate([highway_swapped.reshape(-1, 2 * part), proj_weight], axis=0),
        GRID,
        axis=0,
        tiled=False,
    )
    highway_bias, proj_bias, lstm_bias, highway_swapped = lax.optimization_barrier(
        (highway_bias, proj_bias, lstm_bias, highway_swapped)
    )
    sizes = [highway_bias.size, proj_bias.size, lstm_bias.size, resets.size]
    small = jnp.concatenate(
        [
            highway_bias.reshape(-1),
            proj_bias.reshape(-1),
            lstm_bias.reshape(-1),
            resets.astype(bf16).reshape(-1),
        ]
    )
    small_all = lax.all_to_all(
        jnp.broadcast_to(small[None], (devices, small.size)),
        EVERY,
        split_axis=0,
        concat_axis=0,
        tiled=True,
    )
    cut = [sum(sizes[:k]) for k in range(5)]
    highway_bias_all = small_all[:, cut[0] : cut[1]].reshape(devices, 2, -1)
    highway_bias_all = highway_bias_all.transpose(1, 0, 2).reshape(2, 2 * features_all)
    highway_bias_all = team_first(highway_bias_all).reshape(team, 2, 2 * part)
    proj_bias_all = small_all[:, cut[1] : cut[2]].reshape(-1).astype(f32)
    lstm_bias_all = small_all[:, cut[2] : cut[3]].reshape(devices, 2, -1)
    lstm_bias_all = lstm_bias_all.transpose(1, 0, 2).reshape(2, 4, team, cells)
    resets_all = small_all[:, cut[3] : cut[4]].reshape(
        lax.axis_size("g"), lax.axis_size("t"), lax.axis_size("y"), -1, own, steps
    )
    resets_team = lax.dynamic_index_in_dim(resets_all, lax.axis_index("g"), 0, False)
    resets_team = lax.dynamic_index_in_dim(resets_team, lax.axis_index("y"), 1, False)
    resets_team = resets_team.reshape(team * own, steps).astype(f32)
    highway_bias_own = lax.dynamic_index_in_dim(highway_bias_all, place, 0, False).astype(f32)
    lstm_bias_own = lax.dynamic_index_in_dim(lstm_bias_all, place, 2, False)
    lstm_bias_own = lstm_bias_own.reshape(2, 1, 4 * cells).astype(f32)

    cut_rows = team * 2 * highway_rows
    grid = first_all.shape[0]
    highway_own = team_rows(first_all[:, :cut_rows].reshape(-1, team, 2 * highway_rows, 2 * part))
    project_own = first_all[:, cut_rows:].reshape(part, width)
    lstm_weight, lstm_proj, highway_swapped = lax.optimization_barrier(
        (lstm_weight, lstm_proj, highway_swapped)
    )
    turned_rows = lstm_proj.shape[2]
    turned_slices = team_slices(jnp.swapaxes(lstm_proj, 1, 2), 1)
    lstm_swapped = swap_team(team_slices(lstm_weight, 4))
    turned_swapped = swap_team(turned_slices)
    lstm_own = lax.all_gather(run_rows(lstm_swapped), GRID, axis=0, tiled=False)
    turned_own = lax.all_gather(run_rows(turned_swapped), GRID, axis=0, tiled=False)

    conv_own = jnp.concatenate([conv_weight.reshape(-1, bank_cols), conv_bias], axis=0)
    banks = lax.axis_size("x") * lax.axis_size("c")
    conv_all = lax.all_to_all(
        jnp.broadcast_to(conv_own[None], (banks,) + conv_own.shape),
        ("x", "c"),
        split_axis=0,
        concat_axis=0,
        tiled=True,
    )
    conv_weight_all = conv_all[:, :-1].reshape((banks,) + conv_weight.shape[1:])
    conv_bias_all = conv_all[:, -1]
    bank = lax.axis_index("x") * lax.axis_size("c") + lax.axis_index("c")
    own_ids = lax.dynamic_slice_in_dim(char_ids, bank * own, own, axis=0)
    own_ids = jnp.swapaxes(own_ids, 0, 1).reshape(own * steps, char_ids.shape[2])
    filters, counts = filter_matrix(conv_weight_all, conv_bias_all)
    tight_from = wide_columns(bank_cols)
    padded_ids, tiled, features, pooled_lse = pool_tokens(
        own_ids, char_table, filters, counts, tight_from
    )

    tokens = own * steps
    operands, hiddens, mixes = [], [], []
    operand = share_team(permuted_columns(features)).reshape(team * tokens, features_all)
    hidden = lax.dynamic_slice_in_dim(operand, place * part, part, axis=1).astype(f32)
    for level in range(2):
        mixed = (
            jnp.dot(operand, highway_own[level], preferred_element_type=f32)
            + highway_bias_own[level]
        )
        operands.append(operand)
        hiddens.append(hidden)
        mixes.append(mixed)
        carry_gate = jax.nn.sigmoid(mixed[:, part:])
        hidden = carry_gate * hidden + (1.0 - carry_gate) * jax.nn.silu(mixed[:, :part])
        if level == 0:
            operand = share_team(hidden.astype(bf16)).transpose(1, 0, 2)
            operand = operand.reshape(team * tokens, features_all)
    top_own = hidden.astype(bf16)
    lin_parts = jnp.dot(top_own, project_own, preferred_element_type=f32).astype(bf16)
    keep_forward = 1.0 - resets_team
    keep_backward = 1.0 - jnp.concatenate(
        [resets_team[:, 1:], jnp.zeros((team * own, 1), f32)], axis=1
    )
    keep = jnp.stack([keep_forward.T, keep_backward.T])[..., None]
    grad_time = out_grad.reshape(own, steps, 2, width).transpose(2, 1, 0, 3)
    grad_lin_all, lstm_grads, turned_grads, bias_sums = run_lstm(
        lin_parts.reshape(team, steps, own, width),
        proj_bias_all[None],
        grad_time,
        lstm_own,
        turned_own,
        lstm_bias_own,
        keep,
    )
    lstm_summed = lax.psum_scatter(lstm_grads, GRID, scatter_dimension=0, tiled=False)
    turned_summed = lax.all_to_all(turned_grads, GRID, split_axis=0, concat_axis=0, tiled=True)
    turned_summed = turned_summed.astype(f32).sum(axis=0).astype(bf16)
    grad_input_team = grad_lin_all.reshape(team * tokens, width)
    grad_input = lax.dynamic_index_in_dim(grad_lin_all, place, 0, False).reshape(tokens, width)
    grad_project_b = column_sum(grad_input)
    grad_project_w = outer_sum(top_own, grad_input_team).astype(bf16)
    grad_hidden = transposed(grad_input_team, project_own)
    highway_parts, highway_bias_parts = [None, None], [None, None]
    for level in (1, 0):
        operand, hidden_in, mixed = operands[level], hiddens[level], mixes[level]
        carry_gate = jax.nn.sigmoid(mixed[:, part:])
        pre_act = mixed[:, :part]
        act_sig = jax.nn.sigmoid(pre_act)
        grad_act = grad_hidden * (1.0 - carry_gate) * act_sig * (1.0 + pre_act * (1.0 - act_sig))
        grad_carry = grad_hidden * (hidden_in - pre_act * act_sig) * carry_gate * (1.0 - carry_gate)
        grad_mixed = jnp.concatenate([grad_act, grad_carry], axis=1).astype(bf16)
        highway_parts[level] = outer_sum(operand, grad_mixed).astype(bf16)
        highway_bias_parts[level] = column_sum(grad_mixed)
        direct = grad_hidden * carry_gate
        spread = transposed(grad_mixed, highway_own[level])
        if level == 1:
            spread = spread.astype(bf16).reshape(team * tokens, team, part).transpose(1, 0, 2)
            grad_hidden = direct + swap_team(spread).astype(f32).sum(axis=0)
        else:
            held = lax.dynamic_slice_in_dim(spread, place * part, part, axis=1)
            spread = lax.dynamic_update_slice_in_dim(spread, held + direct, place * part, axis=1)
            spread = spread.astype(bf16).reshape(team, tokens, features_all)
            grad_features = restored_columns(
                swap_team(spread).astype(f32).sum(axis=0).astype(bf16)
            )

    first_parts = jnp.concatenate(
        [
            owner_team_rows(jnp.stack(highway_parts)).reshape(grid, cut_rows, 2 * part),
            grad_project_w.reshape(grid, -1, width),
        ],
        axis=1,
    )
    first_parts, lstm_summed = lax.optimization_barrier((first_parts, lstm_summed))
    first_summed = lax.psum_scatter(
        first_parts,
        GRID,
        scatter_dimension=0,
        tiled=False,
    )
    project_grad = first_summed[cut_rows:].astype(f32)

    grad_filters, grad_table = pool_grads(
        padded_ids,
        tiled,
        filters,
        counts,
        pooled_lse,
        grad_features,
        char_table.shape[0],
        tight_from,
    )
    lstm_returned = swap_team(member_rows(lstm_summed))
    lstm_weight_grad = whole_columns(lstm_returned, 4).astype(f32)
    turned_grad = whole_columns(swap_team(member_rows(turned_summed)), 1).astype(f32)
    lstm_proj_grad = jnp.swapaxes(turned_grad, 1, 2)
    highway_returned = swap_team(first_summed[:cut_rows].reshape(team, 2 * highway_rows, 2 * part))
    g, t, y, x, c = axis_sizes()
    highway_weight_grad = (
        highway_returned.reshape(t, x, c, 2 * highway_rows, 2, g, y, -1)
        .transpose(3, 4, 5, 0, 6, 1, 2, 7)
        .reshape(2, highway_rows, 2 * features_all)
        .astype(f32)
    )

    def own_place(values, parts):
        lanes = values.shape[-1] // parts
        split = values.reshape(2, parts, 1, lanes)
        full = jnp.zeros((2, parts, team, lanes), f32)
        return lax.dynamic_update_slice(full, split, (0, 0, place, 0)).reshape(2, -1)

    lstm_bias_parts = own_place(bias_sums[:, 0], 4)
    highway_bias_parts = own_place(jnp.stack(highway_bias_parts), 2)
    highway_bias_parts = (
        highway_bias_parts.reshape(2, 2, t, x, c, g, y, -1)
        .transpose(0, 1, 5, 2, 6, 3, 4, 7)
        .reshape(2, 2 * features_all)
    )
    biases = jnp.concatenate(
        [
            lstm_bias_parts.reshape(2, devices, -1).transpose(1, 0, 2).reshape(devices, -1),
            highway_bias_parts.reshape(2, devices, -1).transpose(1, 0, 2).reshape(devices, -1),
            grad_project_b.reshape(devices, -1),
        ],
        axis=1,
    )
    groups = g * t * y
    table_items = -(-grad_table.size // groups)
    table_flat = jnp.pad(grad_table.reshape(-1), (0, groups * table_items - grad_table.size))
    table_blocks = jnp.broadcast_to(
        padded_rows(table_flat.reshape(groups, table_items), row_count(table_items))[:, None],
        (groups, x * c, row_count(table_items), LANES),
    ).reshape(devices, -1, LANES)
    filter_blocks = bank_blocks(grad_filters, bank_cols, groups)
    mine = lax.all_to_all(
        jnp.concatenate(
            [filter_blocks, table_blocks, padded_rows(biases, row_count(biases.shape[1]))], axis=1
        ).astype(bf16),
        EVERY,
        split_axis=0,
        concat_axis=0,
        tiled=True,
    )
    mine = mine.astype(f32).sum(axis=0)
    shared = filter_blocks.shape[1] + table_blocks.shape[1]
    mine_biases = mine[shared:].reshape(-1)
    ends = [2 * lstm_bias.shape[1], 2 * lstm_bias.shape[1] + 2 * highway_bias.shape[1]]
    lstm_bias_grad = mine_biases[: ends[0]].reshape(2, -1)
    highway_bias_grad = mine_biases[ends[0] : ends[1]].reshape(2, -1)
    proj_bias_grad = mine_biases[ends[1] : ends[1] + proj_bias.size]
    both = lax.all_to_all(
        jnp.broadcast_to(mine[None, :shared], (groups, shared, LANES)),
        ("g", "t", "y"),
        split_axis=0,
        concat_axis=0,
        tiled=True,
    )
    grad_kernel, grad_bias = bank_filters(
        both[:, : filter_blocks.shape[1]], bank, bank_cols, groups
    )
    grad_table = both[:, filter_blocks.shape[1] :].reshape(groups, -1)[:, :table_items]
    grad_table = grad_table.reshape(-1)[: char_table.size].reshape(char_table.shape)
    return (
        grad_table,
        grad_kernel,
        grad_bias,
        highway_weight_grad,
        highway_bias_grad,
        project_grad,
        proj_bias_grad,
        lstm_weight_grad,
        lstm_bias_grad,
        lstm_proj_grad,
    )


def solution(mesh):
    dp, bank = mesh.shape["dp"], mesh.shape["bank"]
    fine = Mesh(mesh.devices.reshape(dp // 4, 2, 2, bank // 2, 2), EVERY)
    rows, banks = ("g", "t", "y"), ("x", "c")
    whole = rows + banks
    placed = (
        P(rows, None, None),
        P(whole, None),
        P(whole, None, None),
        P(),
        P(banks, None, None, None),
        P(banks, None),
        P(None, whole, None),
        P(None, whole),
        P(whole, None),
        P(whole),
        P(None, whole, None),
        P(None, whole),
        P(None, None, whole),
    )
    return jax.shard_map(
        shards,
        mesh=fine,
        in_specs=placed,
        out_specs=(
            P(),
            P(banks, None, None, None),
            P(banks, None),
            P(None, whole, None),
            P(None, whole),
            P(whole, None),
            P(whole),
            P(None, whole, None),
            P(None, whole),
            P(None, None, whole),
        ),
        check_vma=False,
    )
```

```python
from functools import partial
import math

import jax
import jax.numpy as jnp
from jax import lax
from jax.experimental import pallas as pl
from jax.experimental.pallas import tpu as pltpu
from jax.sharding import Mesh, PartitionSpec as P

CHAR_COUNT = 50
EMBED = 16
WIDEST = 7
TAPS = WIDEST * EMBED
LANES = 128
PLACES = 64
TIGHT = 48
CHUNK = 256
TOKEN_BLOCK = 16


def bank_plan(bank_cols):
    return [
        [
            (1, 0, bank_cols // 32),
            (2, bank_cols // 32, bank_cols // 32),
            (3, bank_cols // 16, bank_cols // 16),
            (4, bank_cols // 8, bank_cols // 8),
        ],
        [(5, 0, bank_cols // 4)],
        [(6, 0, bank_cols // 2)],
        [(7, 0, bank_cols)],
    ]


def transposed(former, latter):
    return lax.dot_general(
        former, latter, (((1,), (1,)), ((), ())), preferred_element_type=jnp.float32
    )


def outer_sum(former, latter):
    return lax.dot_general(
        former, latter, (((0,), (0,)), ((), ())), preferred_element_type=jnp.float32
    )


def column_sum(values):
    ones_row = jnp.ones((1, values.shape[0]), values.dtype)
    return jnp.dot(ones_row, values, preferred_element_type=jnp.float32)[0]


def filter_columns(bank_cols):
    columns = []
    for bank_index, bank_specs in enumerate(bank_plan(bank_cols)):
        for filter_width, first_col, count in bank_specs:
            columns.append((filter_width, bank_index, first_col, count))
    return columns


def shift_rows(values, amount):
    count = values.shape[0]
    return values if amount % count == 0 else pltpu.roll(values, amount % count, 0)


def block_windows(tiled_ref, windows_wide, windows_tight):
    tokens, places, lanes = tiled_ref.shape
    rows = tokens * places
    tiled = tiled_ref[...].astype(jnp.float32).reshape(rows, lanes)
    lane = lax.broadcasted_iota(jnp.int32, (rows, lanes), 1)
    place = lax.broadcasted_iota(jnp.int32, (rows, lanes), 0) % places
    windows = tiled
    for offset in range(1, WIDEST):
        windows = jnp.where(lane // EMBED == offset, shift_rows(tiled, rows - offset), windows)
    late = place >= CHAR_COUNT - WIDEST + 1 + (lane - TAPS - 1)
    extra = jnp.where((lane == TAPS) | ((lane <= TAPS + WIDEST) & late), 1.0, 0.0)
    windows = jnp.where(lane < TAPS, windows, extra)
    windows_wide[...] = windows.astype(jnp.bfloat16)
    windows_tight[...] = (
        windows.reshape(tokens, places, lanes)[:, :TIGHT]
        .reshape(tokens * TIGHT, lanes)
        .astype(jnp.bfloat16)
    )


def column_chunks(total, tight_from):
    return [
        (start, start < tight_from) for start in range(0, total, CHUNK)
    ]


def pool_kernel(tight_from, tiled_ref, weight_ref, count_ref, features_ref, lse_ref, wide, tight):
    tokens, places, lanes = tiled_ref.shape
    block_windows(tiled_ref, wide, tight)
    for start, is_wide in column_chunks(weight_ref.shape[1], tight_from):
        cols = pl.ds(start, CHUNK)
        windows = wide if is_wide else tight
        conv_out = jnp.dot(
            windows[...], weight_ref[:, cols], preferred_element_type=jnp.float32
        ).reshape(tokens, -1, CHUNK)
        highest = jnp.max(conv_out, axis=1)
        total = jnp.sum(jnp.exp(conv_out - highest[:, None, :]), axis=1)
        pooled_lse = highest + jnp.log(total)
        lse_ref[:, cols] = pooled_lse
        pooled_pre = pooled_lse - count_ref[0:1, cols]
        features_ref[:, cols] = (pooled_pre * jax.nn.sigmoid(pooled_pre)).astype(jnp.bfloat16)


def pool_grad_kernel(
    tight_from,
    tiled_ref,
    weight_ref,
    count_ref,
    lse_ref,
    upstream_ref,
    grad_weight_ref,
    aligned_ref,
    wide,
    tight,
    spread,
):
    tokens, places, lanes = tiled_ref.shape
    block_windows(tiled_ref, wide, tight)

    @pl.when(pl.program_id(0) == 0)
    def _():
        grad_weight_ref[...] = jnp.zeros_like(grad_weight_ref)

    spread[...] = jnp.zeros_like(spread)
    wide_turned = wide[...].T
    tight_turned = tight[...].T
    for start, is_wide in column_chunks(weight_ref.shape[1], tight_from):
        cols = pl.ds(start, CHUNK)
        windows, turned = (wide, wide_turned) if is_wide else (tight, tight_turned)
        weights = weight_ref[:, cols]
        conv_out = jnp.dot(
            windows[...], weights, preferred_element_type=jnp.float32
        ).reshape(tokens, -1, CHUNK)
        pooled_lse = lse_ref[:, cols]
        pooled_pre = pooled_lse - count_ref[0:1, cols]
        squashed = jax.nn.sigmoid(pooled_pre)
        upstream = (
            upstream_ref[:, cols].astype(jnp.float32)
            * squashed
            * (1.0 + pooled_pre * (1.0 - squashed))
        )
        softened = jnp.exp(conv_out - pooled_lse[:, None, :])
        grad_conv = (softened * upstream[:, None, :]).astype(jnp.bfloat16)
        places_here = grad_conv.shape[1]
        grad_conv = grad_conv.reshape(tokens * places_here, CHUNK)
        grad_weight_ref[:, cols] += jnp.dot(turned, grad_conv, preferred_element_type=jnp.float32)
        part = lax.dot_general(
            grad_conv, weights, (((1,), (1,)), ((), ())), preferred_element_type=jnp.float32
        ).reshape(tokens, places_here, lanes)
        spread[:, :places_here, :] += part
    rows = tokens * places
    flat = spread[...].reshape(rows, lanes)
    lane = lax.broadcasted_iota(jnp.int32, (rows, lanes), 1)
    aligned = jnp.where(lane < EMBED, flat, 0.0)
    for offset in range(1, WIDEST):
        aligned = jnp.where(lane // EMBED == offset, shift_rows(flat, offset), aligned)
    aligned_ref[...] = aligned.reshape(tokens, places, lanes)


def filter_matrix(conv_weight, conv_bias):
    bank_cols = conv_bias.shape[1]
    taps, biases, masks, counts = [], [], [], []
    for filter_width, bank_index, first_col, count in filter_columns(bank_cols):
        piece = conv_weight[bank_index, :filter_width, :, first_col : first_col + count]
        piece = piece.reshape(filter_width * EMBED, count)
        taps.append(jnp.pad(piece, ((0, TAPS - filter_width * EMBED), (0, 0))))
        biases.append(conv_bias[bank_index, first_col : first_col + count])
        rows = lax.broadcasted_iota(jnp.int32, (LANES - TAPS - 1, count), 0)
        masks.append(jnp.where(rows == WIDEST - filter_width, -1e30, 0.0).astype(jnp.bfloat16))
        counts.append(jnp.full((8, count), math.log(CHAR_COUNT - filter_width + 1), jnp.float32))
    weights = jnp.concatenate(
        [
            jnp.concatenate(taps, axis=1),
            jnp.concatenate(biases)[None],
            jnp.concatenate(masks, axis=1),
        ],
        axis=0,
    )
    return (weights, jnp.concatenate(counts, axis=1))


def wide_columns(bank_cols):
    total = sum(count for width, bank, first, count in filter_columns(bank_cols) if CHAR_COUNT - width + 1 > TIGHT - 2)
    return -(-total // CHUNK) * CHUNK


def char_selector(token_ids, vocab_size):
    return token_ids.reshape(-1)[:, None] == lax.broadcasted_iota(jnp.int32, (1, vocab_size), 1)


def embed_tokens(token_ids, char_table):
    tokens = token_ids.shape[0]
    padded = jnp.pad(token_ids, ((0, 0), (0, PLACES - token_ids.shape[1])), constant_values=-1)
    table_tiled = jnp.pad(jnp.tile(char_table, (1, WIDEST)), ((0, 0), (0, LANES - TAPS)))
    selector = char_selector(padded, char_table.shape[0]).astype(jnp.bfloat16)
    tiled = jnp.dot(selector, table_tiled, preferred_element_type=jnp.float32)
    tiled = tiled.astype(jnp.bfloat16).reshape(tokens, PLACES, LANES)
    return (padded, tiled)


def pool_grads(padded, tiled, weights, counts, pooled_lse, upstream, vocab_size, tight_from):
    tokens = tiled.shape[0]
    block = math.gcd(tokens, TOKEN_BLOCK)
    total = weights.shape[1]
    grad_weight, aligned = pl.pallas_call(
        partial(pool_grad_kernel, tight_from),
        grid=(tokens // block,),
        in_specs=[
            pl.BlockSpec((block, PLACES, LANES), lambda i: (i, 0, 0)),
            pl.BlockSpec((LANES, total), lambda i: (0, 0)),
            pl.BlockSpec((8, total), lambda i: (0, 0)),
            pl.BlockSpec((block, total), lambda i: (i, 0)),
            pl.BlockSpec((block, total), lambda i: (i, 0)),
        ],
        out_specs=[
            pl.BlockSpec((LANES, total), lambda i: (0, 0)),
            pl.BlockSpec((block, PLACES, LANES), lambda i: (i, 0, 0)),
        ],
        out_shape=[
            jax.ShapeDtypeStruct((LANES, total), jnp.float32),
            jax.ShapeDtypeStruct((tokens, PLACES, LANES), jnp.float32),
        ],
        scratch_shapes=[
            pltpu.VMEM((block * PLACES, LANES), jnp.bfloat16),
            pltpu.VMEM((block * TIGHT, LANES), jnp.bfloat16),
            pltpu.VMEM((block, PLACES, LANES), jnp.float32),
        ],
        compiler_params=pltpu.CompilerParams(vmem_limit_bytes=40 * 1024 * 1024),
        name="pool_grads",
    )(tiled, weights, counts, pooled_lse, upstream)
    aligned = aligned.reshape(tokens * PLACES, LANES)
    selector = char_selector(padded, vocab_size).astype(jnp.bfloat16)
    high = aligned.astype(jnp.bfloat16)
    low = (aligned - high.astype(jnp.float32)).astype(jnp.bfloat16)
    by_tap = outer_sum(selector, high) + outer_sum(selector, low)
    grad_table = by_tap[:, :TAPS].reshape(vocab_size, WIDEST, EMBED).sum(axis=1)
    return (grad_weight, grad_table)


TEAM = ("t", "x", "c")
GRID = ("g", "y")
EVERY = ("g", "t", "y", "x", "c")


def team_place():
    x_size, c_size = lax.axis_size("x"), lax.axis_size("c")
    return (lax.axis_index("t") * x_size + lax.axis_index("x")) * c_size + lax.axis_index("c")


def team_size():
    return lax.axis_size("t") * lax.axis_size("x") * lax.axis_size("c")


def team_coords(place):
    x_size, c_size = lax.axis_size("x"), lax.axis_size("c")
    return {
        "t": place // (x_size * c_size),
        "x": lax.rem(place // c_size, x_size),
        "c": lax.rem(place, c_size),
    }


def swap_team(values):
    return lax.all_to_all(values, TEAM, split_axis=0, concat_axis=0, tiled=True)


def share_team(values):
    team = team_size()
    return swap_team(jnp.broadcast_to(values[None], (team,) + values.shape))


def sigmoid(values):
    return 0.5 * jnp.tanh(0.5 * values) + 0.5


def wait_bytes(ref, sem):
    pltpu.make_async_copy(ref, ref, sem).wait()


def lstm_kernel(
    team,
    parts_ref,
    lin_bias_ref,
    out_grad_ref,
    weight_hbm,
    turned_hbm,
    bias_ref,
    keep_ref,
    grad_lin_all_ref,
    grad_weight_hbm,
    grad_turned_hbm,
    grad_bias_ref,
    weight_ref,
    proj_ref,
    grad_gates_ref,
    lin_all_ref,
    state_ref,
    full_ref,
    grad_proj_ref,
    gates,
    cell_start,
    projected,
    stage,
    received,
    received_back,
    grad_cell,
    grad_lin_sum,
    stage_lin,
    received_lin,
    grad_state_own,
    grad_stage,
    turned_stage,
    load_sems,
    lin_sems,
    send_sems,
    sum_sems,
    share_send_sems,
    share_sems,
    out_sems,
):
    _, steps, own, width = parts_ref.shape
    group = team * own
    cells = proj_ref.shape[2]
    row_block = 32
    place = team_place()
    own_rows = pl.ds(pl.multiple_of(place * own, own), own)
    peers = [lax.rem(place + k, team) for k in range(1, team)]
    last = steps - 1
    others = pl.ds(0, team - 1)
    other_rows = pl.ds(0, (team - 1) * own)
    g_size, y_size = lax.axis_size("g"), lax.axis_size("y")
    t_size = lax.axis_size("t")
    blocks = [
        (g * y_size + y, t, (g * t_size + t) * y_size + y)
        for g in range(g_size)
        for t in range(t_size)
        for y in range(y_size)
    ]
    run = weight_hbm.shape[4]
    turned_run = turned_hbm.shape[3]

    for d in range(2):
        for source, t, at in blocks:
            for q in range(4):
                pltpu.make_async_copy(
                    weight_hbm.at[source, t, d, q],
                    weight_ref.at[d, pl.ds(at * run, run), pl.ds(q * cells, cells)],
                    load_sems.at[0],
                ).start()
            pltpu.make_async_copy(
                turned_hbm.at[source, t, d],
                proj_ref.at[d, pl.ds(at * turned_run, turned_run)],
                load_sems.at[1],
            ).start()

    barrier = pltpu.get_barrier_semaphore()
    for peer in peers:
        pl.semaphore_signal(
            barrier, inc=1, device_id=team_coords(peer), device_id_type=pl.DeviceIdType.MESH
        )
    pl.semaphore_wait(barrier, team - 1)

    def send(source, target, send_sem, recv_sem, peer):
        pltpu.make_async_remote_copy(
            src_ref=source,
            dst_ref=target,
            send_sem=send_sem,
            recv_sem=recv_sem,
            device_id=team_coords(peer),
            device_id_type=pl.DeviceIdType.MESH,
        ).start()

    for peer in peers:
        send(parts_ref.at[peer], stage_lin.at[place], lin_sems.at[0], lin_sems.at[1], peer)
    stage_lin[place] = parts_ref[place]
    for d in range(2):
        first = 0 if d == 0 else last
        state_ref[d, first] = jnp.zeros((group, width), jnp.bfloat16)
        cell_start[d, first] = jnp.zeros((group, cells), jnp.float32)
        grad_cell[d] = jnp.zeros((group, cells), jnp.float32)
    grad_lin_sum[...] = jnp.zeros_like(grad_lin_sum)
    wait_bytes(stage_lin.at[others], lin_sems.at[1])
    lin_own = jnp.sum(stage_lin[...].astype(jnp.float32), axis=0) + lin_bias_ref[...]
    lin_all_ref[:, own_rows] = lin_own.astype(jnp.bfloat16)
    for peer in peers:
        send(
            lin_all_ref.at[:, own_rows],
            lin_all_ref.at[:, own_rows],
            lin_sems.at[2],
            lin_sems.at[3],
            peer,
        )
    wait_bytes(weight_ref, load_sems.at[0])
    wait_bytes(proj_ref, load_sems.at[1])
    wait_bytes(lin_all_ref.at[:, other_rows], lin_sems.at[3])

    @pl.loop(0, steps)
    def _(t):
        for d in range(2):
            for q in range(4):
                cols = pl.ds(q * cells, cells)
                gates[d, t, :, cols] = (
                    jnp.dot(
                        lin_all_ref[t],
                        weight_ref[d, :width, cols],
                        preferred_element_type=jnp.float32,
                    )
                    + bias_ref[d, :, cols]
                )

    def time_of(d, s):
        return s if d == 0 else last - s

    @pl.loop(0, steps)
    def _(s):
        for d in range(2):
            t = time_of(d, s)
            later = time_of(d, jnp.minimum(s + 1, last))

            @pl.when(s > 0)
            def _():
                wait_bytes(
                    state_ref.at[d, t, other_rows], share_sems.at[0, d, s]
                )
                for q in range(4):
                    cols = pl.ds(q * cells, cells)
                    gates[d, t, :, cols] += jnp.dot(
                        state_ref[d, t],
                        weight_ref[d, width:, cols],
                        preferred_element_type=jnp.float32,
                    )

            @pl.loop(0, group // row_block)
            def _(block):
                rows = pl.ds(pl.multiple_of(block * row_block, row_block), row_block)
                in_gate = sigmoid(gates[d, t, rows, pl.ds(0, cells)])
                forget_gate = sigmoid(gates[d, t, rows, pl.ds(cells, cells)])
                candidate = jnp.tanh(gates[d, t, rows, pl.ds(2 * cells, cells)])
                out_gate = sigmoid(gates[d, t, rows, pl.ds(3 * cells, cells)])
                gates[d, t, rows, pl.ds(0, cells)] = in_gate
                gates[d, t, rows, pl.ds(cells, cells)] = forget_gate
                gates[d, t, rows, pl.ds(2 * cells, cells)] = candidate
                gates[d, t, rows, pl.ds(3 * cells, cells)] = out_gate
                mixed = forget_gate * cell_start[d, t, rows] + in_gate * candidate
                cell_new = 3.0 * jnp.tanh(mixed * (1.0 / 3.0))
                full_ref[d, t, rows] = (out_gate * jnp.tanh(cell_new)).astype(jnp.bfloat16)

                @pl.when(s < last)
                def _():
                    cell_start[d, later, rows] = cell_new * keep_ref[d, later, rows]

            @pl.when(s > 0)
            def _():
                wait_bytes(stage.at[d, others], send_sems.at[d])

            part = lax.dot_general(
                full_ref[d, t],
                proj_ref[d],
                (((1,), (1,)), ((), ())),
                preferred_element_type=jnp.float32,
            )
            part = part.astype(jnp.bfloat16).reshape(team, own, width)
            stage[d] = part
            received[d, s, place] = stage[d, place]
            for peer in peers:
                send(
                    stage.at[d, peer],
                    received.at[d, s, place],
                    send_sems.at[d],
                    sum_sems.at[0, d, s],
                    peer,
                )
        for d in range(2):
            t = time_of(d, s)
            later = time_of(d, jnp.minimum(s + 1, last))
            wait_bytes(received.at[d, s, others], sum_sems.at[0, d, s])
            total = jnp.sum(received[d, s].astype(jnp.float32), axis=0)
            projected[d, t] = total

            @pl.when(s > 0)
            def _():
                wait_bytes(
                    state_ref.at[d, t, other_rows], share_send_sems.at[0, d]
                )

            @pl.when(s < last)
            def _():
                state_new = (3.0 * jnp.tanh(total * (1.0 / 3.0))).astype(jnp.bfloat16)
                kept = state_new.astype(jnp.float32) * keep_ref[d, later, own_rows]
                state_ref[d, later, own_rows] = kept.astype(jnp.bfloat16)
                for peer in peers:
                    send(
                        state_ref.at[d, later, own_rows],
                        state_ref.at[d, later, own_rows],
                        share_send_sems.at[0, d],
                        share_sems.at[0, d, s + 1],
                        peer,
                    )

    @pl.loop(0, steps)
    def _(s):
        for d in range(2):
            t = time_of(1 - d, s)

            @pl.when(s > 0)
            def _():
                wait_bytes(
                    received_back.at[d, jnp.maximum(s - 1, 0), others],
                    sum_sems.at[1, d, jnp.maximum(s - 1, 0)],
                )
                grad_state_own[...] = jnp.sum(
                    received_back[d, jnp.maximum(s - 1, 0)].astype(jnp.float32), axis=0
                )

            @pl.when(s == 0)
            def _():
                grad_state_own[...] = jnp.zeros((own, width), jnp.float32)

            grad_state = grad_state_own[...] + out_grad_ref[d, t].astype(jnp.float32)
            squashed = jnp.tanh(projected[d, t] * (1.0 / 3.0))
            grad_proj_ref[d, t, own_rows] = (grad_state * (1.0 - squashed * squashed)).astype(
                jnp.bfloat16
            )
            for peer in peers:
                send(
                    grad_proj_ref.at[d, t, own_rows],
                    grad_proj_ref.at[d, t, own_rows],
                    share_send_sems.at[1, d],
                    share_sems.at[1, d, s],
                    peer,
                )
        for d in range(2):
            t = time_of(1 - d, s)
            wait_bytes(grad_proj_ref.at[d, t, other_rows], share_sems.at[1, d, s])
            wait_bytes(
                grad_proj_ref.at[d, t, other_rows], share_send_sems.at[1, d]
            )

            @pl.loop(0, group // row_block)
            def _(block):
                rows = pl.ds(pl.multiple_of(block * row_block, row_block), row_block)
                grad_full = jnp.dot(
                    grad_proj_ref[d, t, rows], proj_ref[d], preferred_element_type=jnp.float32
                )
                in_gate = gates[d, t, rows, pl.ds(0, cells)]
                forget_gate = gates[d, t, rows, pl.ds(cells, cells)]
                candidate = gates[d, t, rows, pl.ds(2 * cells, cells)]
                out_gate = gates[d, t, rows, pl.ds(3 * cells, cells)]
                start = cell_start[d, t, rows]
                clipped = jnp.tanh((forget_gate * start + in_gate * candidate) * (1.0 / 3.0))
                tanh_cell = jnp.tanh(3.0 * clipped)
                total = grad_cell[d, rows] + grad_full * out_gate * (1.0 - tanh_cell * tanh_cell)
                grad_raw = total * (1.0 - clipped * clipped)
                grad_gates_ref[d, t, rows, pl.ds(0, cells)] = (
                    grad_raw * candidate * in_gate * (1.0 - in_gate)
                ).astype(jnp.bfloat16)
                grad_gates_ref[d, t, rows, pl.ds(cells, cells)] = (
                    grad_raw * start * forget_gate * (1.0 - forget_gate)
                ).astype(jnp.bfloat16)
                grad_gates_ref[d, t, rows, pl.ds(2 * cells, cells)] = (
                    grad_raw * in_gate * (1.0 - candidate * candidate)
                ).astype(jnp.bfloat16)
                grad_gates_ref[d, t, rows, pl.ds(3 * cells, cells)] = (
                    grad_full * tanh_cell * out_gate * (1.0 - out_gate)
                ).astype(jnp.bfloat16)
                grad_cell[d, rows] = grad_raw * forget_gate * keep_ref[d, t, rows]

            wait_bytes(stage.at[d, others], send_sems.at[d])

            @pl.when(s < last)
            def _():
                part = (
                    lax.dot_general(
                        grad_gates_ref[d, t],
                        weight_ref[d, width:],
                        (((1,), (1,)), ((), ())),
                        preferred_element_type=jnp.float32,
                    )
                    * keep_ref[d, t]
                )
                stage[d] = part.astype(jnp.bfloat16).reshape(team, own, width)
                received_back[d, s, place] = stage[d, place]
                for peer in peers:
                    send(
                        stage.at[d, peer],
                        received_back.at[d, s, place],
                        send_sems.at[d],
                        sum_sems.at[1, d, s],
                        peer,
                    )

            grad_lin_sum[t] += lax.dot_general(
                grad_gates_ref[d, t],
                weight_ref[d, :width],
                (((1,), (1,)), ((), ())),
                preferred_element_type=jnp.float32,
            )

    wait_bytes(parts_ref.at[others], lin_sems.at[0])
    wait_bytes(lin_all_ref.at[:, other_rows], lin_sems.at[2])
    for t in range(steps):
        stage_lin[:, t] = grad_lin_sum[t].astype(jnp.bfloat16).reshape(team, own, width)
    received_lin[place] = stage_lin[place]
    for peer in peers:
        send(stage_lin.at[peer], received_lin.at[place], lin_sems.at[4], lin_sems.at[5], peer)

    count = steps * group
    half_blocks = len(blocks) // 2

    def weight_grads(d):
        for half in range(2):

            @pl.loop(0, 4)
            def _(q):
                cols = pl.ds(pl.multiple_of(q * cells, cells), cells)
                slot = lax.rem(q, 2)
                rows_in = (lin_all_ref[...] if half == 0 else state_ref[d]).reshape(count, width)
                gate_part = grad_gates_ref[d, :, :, cols].reshape(count, cells)
                part = lax.dot_general(
                    rows_in,
                    gate_part,
                    (((0,), (0,)), ((), ())),
                    preferred_element_type=jnp.float32,
                )

                @pl.when(q >= 2)
                def _():
                    wait_bytes(grad_stage.at[slot], out_sems.at[slot])

                grad_stage[slot] = part.astype(jnp.bfloat16)
                for source, t, at in blocks[half * half_blocks : (half + 1) * half_blocks]:
                    pltpu.make_async_copy(
                        grad_stage.at[slot, pl.ds((at - half * half_blocks) * run, run)],
                        grad_weight_hbm.at[source, t, d, :, cols],
                        out_sems.at[slot],
                    ).start()

            for slot in range(2):
                wait_bytes(grad_stage.at[slot], out_sems.at[slot])
        turned = lax.dot_general(
            grad_proj_ref[d].reshape(count, width),
            full_ref[d].reshape(count, cells),
            (((0,), (0,)), ((), ())),
            preferred_element_type=jnp.float32,
        )
        turned_stage[d] = turned.astype(jnp.bfloat16)
        for source, t, at in blocks:
            pltpu.make_async_copy(
                turned_stage.at[d, pl.ds(at * turned_run, turned_run)],
                grad_turned_hbm.at[source, t, d],
                out_sems.at[2 + d],
            ).start()
        ones = jnp.ones((8, count), jnp.bfloat16)
        for q in range(4):
            cols = pl.ds(q * cells, cells)
            grad_bias_ref[d, :, cols] = jnp.dot(
                ones,
                grad_gates_ref[d, :, :, cols].reshape(count, cells),
                preferred_element_type=jnp.float32,
            )

    weight_grads(0)
    wait_bytes(received_lin.at[others], lin_sems.at[5])
    grad_lin_all_ref[place] = jnp.sum(received_lin[...].astype(jnp.float32), axis=0).astype(
        jnp.bfloat16
    )
    for peer in peers:
        send(
            grad_lin_all_ref.at[place],
            grad_lin_all_ref.at[place],
            lin_sems.at[6],
            lin_sems.at[7],
            peer,
        )
    weight_grads(1)
    wait_bytes(grad_lin_all_ref.at[others], lin_sems.at[7])
    wait_bytes(stage_lin.at[others], lin_sems.at[4])
    wait_bytes(grad_lin_all_ref.at[others], lin_sems.at[6])
    for d in range(2):
        wait_bytes(turned_stage.at[d], out_sems.at[2 + d])


def run_lstm(parts, lin_bias, out_grad, weights, turned, bias, keep):
    team, steps, own, width = parts.shape
    group = team * own
    cells = turned.shape[4]
    bf16, f32 = jnp.bfloat16, jnp.float32
    vmem = pl.BlockSpec(memory_space=pltpu.VMEM)
    hbm = pl.BlockSpec(memory_space=pl.ANY)
    return pl.pallas_call(
        partial(lstm_kernel, team),
        in_specs=[vmem, vmem, vmem, hbm, hbm, vmem, vmem],
        out_specs=[vmem, hbm, hbm, vmem],
        out_shape=[
            jax.ShapeDtypeStruct(parts.shape, bf16),
            jax.ShapeDtypeStruct(weights.shape[:3] + (weights.shape[4], 4 * cells), bf16),
            jax.ShapeDtypeStruct(turned.shape, bf16),
            jax.ShapeDtypeStruct((2, 8, 4 * cells), f32),
        ],
        scratch_shapes=[
            pltpu.VMEM((2, 2 * width, 4 * cells), bf16),
            pltpu.VMEM((2, width, cells), bf16),
            pltpu.VMEM((2, steps, group, 4 * cells), bf16),
            pltpu.VMEM((steps, group, width), bf16),
            pltpu.VMEM((2, steps, group, width), bf16),
            pltpu.VMEM((2, steps, group, cells), bf16),
            pltpu.VMEM((2, steps, group, width), bf16),
            pltpu.VMEM((2, steps, group, 4 * cells), f32),
            pltpu.VMEM((2, steps, group, cells), f32),
            pltpu.VMEM((2, steps, own, width), f32),
            pltpu.VMEM((2, team, own, width), bf16),
            pltpu.VMEM((2, steps, team, own, width), bf16),
            pltpu.VMEM((2, steps, team, own, width), bf16),
            pltpu.VMEM((2, group, cells), f32),
            pltpu.VMEM((steps, group, width), f32),
            pltpu.VMEM((team, steps, own, width), bf16),
            pltpu.VMEM((team, steps, own, width), bf16),
            pltpu.VMEM((own, width), f32),
            pltpu.VMEM((2, width, cells), bf16),
            pltpu.VMEM((2, width, cells), bf16),
            pltpu.SemaphoreType.DMA((2,)),
            pltpu.SemaphoreType.DMA((8,)),
            pltpu.SemaphoreType.DMA((2,)),
            pltpu.SemaphoreType.DMA((2, 2, steps)),
            pltpu.SemaphoreType.DMA((2, 2)),
            pltpu.SemaphoreType.DMA((2, 2, steps)),
            pltpu.SemaphoreType.DMA((4,)),
        ],
        compiler_params=pltpu.CompilerParams(
            collective_id=1, has_side_effects=True, vmem_limit_bytes=63 * 1024 * 1024
        ),
        name="lstm_team",
    )(parts, lin_bias, out_grad, weights, turned, bias, keep)


def member_at(offset):
    t_size, x_size, c_size = lax.axis_size("t"), lax.axis_size("x"), lax.axis_size("c")
    dt, dx, dc = offset // (x_size * c_size), lax.rem(offset // c_size, x_size), lax.rem(offset, c_size)
    t = lax.rem(lax.axis_index("t") + dt, t_size)
    x = lax.rem(lax.axis_index("x") + dx, x_size)
    c = lax.rem(lax.axis_index("c") + dc, c_size)
    return (t * x_size + x) * c_size + c


def opposite(offset):
    t_size, x_size, c_size = lax.axis_size("t"), lax.axis_size("x"), lax.axis_size("c")
    dt, dx, dc = offset // (x_size * c_size), offset // c_size % x_size, offset % c_size
    return (-dt % t_size * x_size + -dx % x_size) * c_size + -dc % c_size


def send_block(source, target, send_sem, recv_sem, peer):
    pltpu.make_async_remote_copy(
        src_ref=source,
        dst_ref=target,
        send_sem=send_sem,
        recv_sem=recv_sem,
        device_id=team_coords(peer),
        device_id_type=pl.DeviceIdType.MESH,
    ).start()


def greet(offsets, with_grid=False):
    barrier = pltpu.get_barrier_semaphore()
    for offset in offsets:
        pl.semaphore_signal(
            barrier,
            inc=1,
            device_id=team_coords(member_at(offset)),
            device_id_type=pl.DeviceIdType.MESH,
        )
    extra = greet_grid(barrier) if with_grid else 0
    pl.semaphore_wait(barrier, len(offsets) + extra)


def load_highway(first_hbm, weights, project, sems):
    grid = first_hbm.shape[0]
    team = team_size()
    run = project.shape[0] // grid

    @pl.loop(0, team)
    def _(member):
        for block in range(grid):
            for level in range(2):
                pltpu.make_async_copy(
                    first_hbm.at[
                        block, pl.ds(pl.multiple_of((member * 2 + level) * run, run), run)
                    ],
                    weights.at[
                        level, pl.ds(pl.multiple_of((member * grid + block) * run, run), run)
                    ],
                    sems.at[0],
                ).start()

    for block in range(grid):
        pltpu.make_async_copy(
            first_hbm.at[block, pl.ds(team * 2 * run, run)],
            project.at[pl.ds(block * run, run)],
            sems.at[1],
        ).start()


def grid_coords(dg, dy):
    g_size, y_size = lax.axis_size("g"), lax.axis_size("y")
    return {
        "g": lax.rem(lax.axis_index("g") + dg, g_size),
        "y": lax.rem(lax.axis_index("y") + dy, y_size),
    }


def grid_block(dg, dy):
    coords = grid_coords(dg, dy)
    return coords["g"] * lax.axis_size("y") + coords["y"]


def send_grid(source, target, send_sem, recv_sem, dg, dy):
    pltpu.make_async_remote_copy(
        src_ref=source,
        dst_ref=target,
        send_sem=send_sem,
        recv_sem=recv_sem,
        device_id=grid_coords(dg, dy),
        device_id_type=pl.DeviceIdType.MESH,
    ).start()


def greet_grid(barrier):
    for dg in range(1, lax.axis_size("g")):
        pl.semaphore_signal(
            barrier, inc=1, device_id=grid_coords(dg, 0), device_id_type=pl.DeviceIdType.MESH
        )
    pl.semaphore_signal(
        barrier, inc=1, device_id=grid_coords(0, 1), device_id_type=pl.DeviceIdType.MESH
    )
    return lax.axis_size("g")


class Gather:
    def __init__(self, blocks, targets, send_sem, recv_sems):
        self.blocks = blocks
        self.targets = targets
        self.send_sem = send_sem
        self.recv_sems = recv_sems

    def start(self, pieces):
        home = grid_block(0, 0)
        g_size = lax.axis_size("g")
        for piece in pieces:
            source = self.blocks[piece]
            target = self.targets[piece](home)
            for dg in range(1, g_size):
                send_grid(
                    source, target, self.send_sem, self.recv_sems.at[piece, g_size - dg, 0], dg, 0
                )
            send_grid(source, target, self.send_sem, self.recv_sems.at[piece, 0, 1], 0, 1)

    def forward(self, pieces):
        for piece in pieces:
            for dg in range(1, lax.axis_size("g")):
                target = self.targets[piece](grid_block(dg, 0))
                wait_bytes(target, self.recv_sems.at[piece, dg, 0])
                send_grid(target, target, self.send_sem, self.recv_sems.at[piece, dg, 1], 0, 1)

    def finish(self, pieces):
        for piece in pieces:
            for dg in range(lax.axis_size("g")):
                wait_bytes(self.targets[piece](grid_block(dg, 1)), self.recv_sems.at[piece, dg, 1])

    def sent(self, pieces):
        for piece in pieces:
            for _ in range(2 * lax.axis_size("g") - 1):
                wait_bytes(self.blocks[piece], self.send_sem)


def row_pieces(total, parts):
    step = -(-total // (parts * 16)) * 16
    return [(start, min(step, total - start)) for start in range(0, total, step)]


def highway_kernel(
    tight_from,
    tiled_ref,
    filter_ref,
    count_ref,
    block_hbm,
    lstm_block_hbm,
    turned_block_hbm,
    bias_ref,
    lse_ref,
    first_hbm,
    lstm_hbm,
    turned_hbm,
    first_ref,
    second_ref,
    mixed_ref,
    hidden_ref,
    top_ref,
    parts_ref,
    features_own,
    wide,
    tight,
    weights,
    project,
    load_sems,
    send_sems,
    first_sems,
    second_sems,
    gather_send_sems,
    block_sems,
    turned_sems,
    lstm_sems,
):
    team, tokens, features = first_ref.shape
    part = features // team
    cores = lax.axis_size("c")
    g_size, y_size = lax.axis_size("g"), lax.axis_size("y")
    place = team_place()
    sibling = member_at(1)
    near = list(range(cores, team, cores))
    chunks = lstm_block_hbm.shape[0]
    greet([1] + near, True)
    home = grid_block(0, 0)
    places = [pl.ds(start, size) for start, size in row_pieces(block_hbm.shape[0], 8)]
    block_gather = Gather(
        [block_hbm.at[rows] for rows in places],
        [lambda at, rows=rows: first_hbm.at[at, rows] for rows in places],
        gather_send_sems.at[0],
        block_sems,
    )
    turned_gather = Gather(
        [turned_block_hbm],
        [lambda at: turned_hbm.at[at]],
        gather_send_sems.at[1],
        turned_sems,
    )
    all_places = list(range(len(places)))
    block_gather.start(all_places)
    pltpu.make_async_copy(block_hbm, first_hbm.at[home], load_sems.at[2]).start()
    pltpu.make_async_copy(turned_block_hbm, turned_hbm.at[home], load_sems.at[3]).start()
    pltpu.make_async_copy(lstm_block_hbm, lstm_hbm.at[home], load_sems.at[4]).start()

    def columns(member):
        return pl.ds(pl.multiple_of(member * part, part), part)

    token_block = wide.shape[0] // tiled_ref.shape[1]

    @pl.loop(0, tokens // token_block)
    def _(step):
        rows = pl.ds(pl.multiple_of(step * token_block, token_block), token_block)
        pool_kernel(
            tight_from,
            tiled_ref.at[rows],
            filter_ref,
            count_ref,
            features_own.at[rows],
            lse_ref.at[rows],
            wide,
            tight,
        )

    g, t, y, x, c = axis_sizes()
    run = part // (g * y)
    natural = features_own[...]
    starts = [
        ((((gi * t + ti) * y + yi) * x + xi) * c + ci) * run
        for ti in range(t)
        for xi in range(x)
        for ci in range(c)
        for gi in range(g)
        for yi in range(y)
    ]
    features_own[...] = jnp.concatenate([natural[:, at : at + run] for at in starts], axis=1)

    for offset in near + [1]:
        send_block(
            features_own,
            first_ref.at[place],
            send_sems.at[0],
            first_sems.at[opposite(offset)],
            member_at(offset),
        )
    first_ref[place] = features_own[...]
    block_gather.forward(all_places)

    def lstm_start(chunk):
        for dg in range(1, g_size):
            send_grid(
                lstm_block_hbm.at[chunk],
                lstm_hbm.at[home, chunk],
                gather_send_sems.at[2],
                lstm_sems.at[chunk, g_size - dg, 0],
                dg,
                0,
            )

    def lstm_forward(chunk):
        for dg in range(1, g_size):
            target = lstm_hbm.at[grid_block(dg, 0), chunk]
            wait_bytes(target, lstm_sems.at[chunk, dg, 0])
            send_grid(
                target, target, gather_send_sems.at[3], lstm_sems.at[chunk, dg, 1], 0, 1
            )

    def pump(chunk):
        @pl.when(chunk < chunks)
        def _():
            lstm_forward(jnp.minimum(chunk, chunks - 1))

            @pl.when(chunk + 2 < chunks)
            def _():
                lstm_start(jnp.minimum(chunk + 2, chunks - 1))

    turned_gather.start([0])
    lstm_start(0)
    lstm_start(1)
    for offset in near:
        member = member_at(offset)
        wait_bytes(first_ref.at[member], first_sems.at[offset])
        send_block(
            first_ref.at[member],
            first_ref.at[member],
            send_sems.at[0],
            first_sems.at[offset + 1],
            sibling,
        )
    block_gather.finish(all_places)
    wait_bytes(block_hbm, load_sems.at[2])
    load_highway(first_hbm, weights, project, load_sems)

    @pl.loop(0, chunks)
    def _(chunk):
        send_grid(
            lstm_block_hbm.at[chunk],
            lstm_hbm.at[home, chunk],
            gather_send_sems.at[4],
            lstm_sems.at[chunk, 0, 1],
            0,
            1,
        )

    wait_bytes(weights, load_sems.at[0])
    wait_bytes(project, load_sems.at[1])

    def mix(level, member, operand):
        mixed = (
            jnp.dot(operand, weights[level], preferred_element_type=jnp.float32)
            + bias_ref[level : level + 1]
        )
        mixed_ref[level, member] = mixed
        gate = sigmoid(mixed[:, part:])
        pre_act = mixed[:, :part]
        return (gate, pre_act * sigmoid(pre_act))

    @pl.loop(0, team)
    def _(offset):
        member = member_at(offset)

        @pl.when(lax.rem(offset, cores) == 1)
        def _():
            wait_bytes(first_ref.at[member], first_sems.at[offset])

        gate, act = mix(0, member, first_ref[member])
        carried = first_ref[member, :, columns(place)].astype(jnp.float32)
        hidden = gate * carried + (1.0 - gate) * act
        hidden_ref[member] = hidden
        mine = second_ref.at[member, :, columns(place)]
        mine[...] = hidden.astype(jnp.bfloat16)
        for to in near + [1]:
            send_block(
                mine,
                mine,
                send_sems.at[1],
                second_sems.at[member, opposite(to)],
                member_at(to),
            )
        pump(offset)

    @pl.loop(0, team + 1)
    def _(step):
        @pl.when(step < team)
        def _():
            member = member_at(jnp.minimum(step, team - 1))
            for origin in near:
                piece = second_ref.at[member, :, columns(member_at(origin))]
                wait_bytes(piece, second_sems.at[member, origin])
                send_block(
                    piece,
                    piece,
                    send_sems.at[1],
                    second_sems.at[member, origin + 1],
                    sibling,
                )

        @pl.when(step > 0)
        def _():
            member = member_at(jnp.maximum(step - 1, 0))
            for origin in [0] + near:
                piece = second_ref.at[member, :, columns(member_at(origin + 1))]
                wait_bytes(piece, second_sems.at[member, origin + 1])
            gate, act = mix(1, member, second_ref[member])
            top = (gate * hidden_ref[member] + (1.0 - gate) * act).astype(jnp.bfloat16)
            top_ref[member] = top
            parts_ref[member] = jnp.dot(
                top, project[...], preferred_element_type=jnp.float32
            ).astype(jnp.bfloat16)

        pump(team + step)

    @pl.loop(2 * team + 1, max(chunks, 2 * team + 1))
    def _(chunk):
        pump(chunk)

    turned_gather.forward([0])
    turned_gather.finish([0])

    @pl.loop(0, chunks)
    def _(chunk):
        for dg in range(g_size):
            wait_bytes(lstm_hbm.at[grid_block(dg, 1), chunk], lstm_sems.at[chunk, dg, 1])

    wait_bytes(first_ref.at[pl.ds(0, team - 1)], send_sems.at[0])
    wait_bytes(second_ref.at[pl.ds(0, team - 1)], send_sems.at[1])
    block_gather.sent(all_places)
    turned_gather.sent([0])
    for _ in range(g_size - 1):
        wait_bytes(lstm_block_hbm, gather_send_sems.at[2])
        wait_bytes(lstm_block_hbm, gather_send_sems.at[3])
    wait_bytes(lstm_block_hbm, gather_send_sems.at[4])
    wait_bytes(turned_block_hbm, load_sems.at[3])
    wait_bytes(lstm_block_hbm, load_sems.at[4])


def run_highway(tight_from, tiled, filters, counts, block, lstm_block, turned_block, bias):
    team = team_size()
    tokens, features = tiled.shape[0], filters.shape[1]
    part = features // team
    g_size, y_size = lax.axis_size("g"), lax.axis_size("y")
    grid = g_size * y_size
    width = block.shape[1]
    bf16, f32 = jnp.bfloat16, jnp.float32
    vmem = pl.BlockSpec(memory_space=pltpu.VMEM)
    hbm = pl.BlockSpec(memory_space=pl.ANY)
    pieces = len(row_pieces(block.shape[0], 8))
    token_block = math.gcd(tokens, TOKEN_BLOCK)
    return pl.pallas_call(
        partial(highway_kernel, tight_from),
        in_specs=[vmem] * 3 + [hbm] * 3 + [vmem],
        out_specs=[vmem] + [hbm] * 3 + [vmem] * 6,
        out_shape=[
            jax.ShapeDtypeStruct((tokens, features), f32),
            jax.ShapeDtypeStruct((grid,) + block.shape, bf16),
            jax.ShapeDtypeStruct((grid,) + lstm_block.shape, bf16),
            jax.ShapeDtypeStruct((grid,) + turned_block.shape, bf16),
            jax.ShapeDtypeStruct((team, tokens, features), bf16),
            jax.ShapeDtypeStruct((team, tokens, features), bf16),
            jax.ShapeDtypeStruct((2, team, tokens, 2 * part), f32),
            jax.ShapeDtypeStruct((team, tokens, part), f32),
            jax.ShapeDtypeStruct((team, tokens, part), bf16),
            jax.ShapeDtypeStruct((team, tokens, width), bf16),
        ],
        scratch_shapes=[
            pltpu.VMEM((tokens, features), bf16),
            pltpu.VMEM((token_block * PLACES, LANES), bf16),
            pltpu.VMEM((token_block * TIGHT, LANES), bf16),
            pltpu.VMEM((2, features, 2 * part), bf16),
            pltpu.VMEM((part, width), bf16),
            pltpu.SemaphoreType.DMA((5,)),
            pltpu.SemaphoreType.DMA((2,)),
            pltpu.SemaphoreType.DMA((team,)),
            pltpu.SemaphoreType.DMA((team, team)),
            pltpu.SemaphoreType.DMA((5,)),
            pltpu.SemaphoreType.DMA((pieces, g_size, y_size)),
            pltpu.SemaphoreType.DMA((1, g_size, y_size)),
            pltpu.SemaphoreType.DMA((lstm_block.shape[0], g_size, y_size)),
        ],
        compiler_params=pltpu.CompilerParams(
            collective_id=2, has_side_effects=True, vmem_limit_bytes=60 * 1024 * 1024
        ),
        name="highway_team",
    )(tiled, filters, counts, block, lstm_block, turned_block, bias)


def highway_back_kernel(
    grad_lin_ref,
    first_hbm,
    first_ref,
    second_ref,
    mixed_ref,
    hidden_ref,
    top_ref,
    features_ref,
    grads_hbm,
    bias_ref,
    weights,
    project,
    grad_mixed,
    direct,
    column_parts,
    column_sibling,
    column_send,
    column_recv,
    column_sum_own,
    row_part,
    row_keep,
    row_give,
    row_sibling,
    row_send,
    row_recv,
    row_sum_own,
    grad_stage,
    load_sems,
    send_sems,
    column_sib_sems,
    column_sems,
    row_sib_sems,
    row_sems,
    out_sems,
):
    team, tokens, features = first_ref.shape
    part = features // team
    grid = first_hbm.shape[0]
    run = part // grid
    cores = lax.axis_size("c")
    chips = team // cores
    place = team_place()
    sibling = member_at(1)
    near = list(range(1, chips))
    load_highway(first_hbm, weights, project, load_sems)
    greet([1] + [chip * cores for chip in near])
    f32, bf16 = jnp.float32, jnp.bfloat16

    def columns(member):
        return pl.ds(pl.multiple_of(member * part, part), part)

    def opposite_chip(chip):
        return opposite(chip * cores) // cores

    wait_bytes(weights, load_sems.at[0])
    wait_bytes(project, load_sems.at[1])

    def mix_grads(level, member, grad, carried):
        pre_act = mixed_ref[level, member, :, pl.ds(0, part)]
        gate = sigmoid(mixed_ref[level, member, :, pl.ds(part, part)])
        act_sig = sigmoid(pre_act)
        grad_mixed[level, member, :, pl.ds(0, part)] = (
            grad * (1.0 - gate) * act_sig * (1.0 + pre_act * (1.0 - act_sig))
        ).astype(bf16)
        grad_mixed[level, member, :, pl.ds(part, part)] = (
            grad * (carried - pre_act * act_sig) * gate * (1.0 - gate)
        ).astype(bf16)
        return grad * gate

    def spread(level, member):
        return lax.dot_general(
            grad_mixed[level, member],
            weights[level],
            (((1,), (1,)), ((), ())),
            preferred_element_type=f32,
        )

    @pl.loop(0, team)
    def _(member):
        grad = lax.dot_general(
            grad_lin_ref[member], project[...], (((1,), (1,)), ((), ())), preferred_element_type=f32
        )
        direct[member] = mix_grads(1, member, grad, hidden_ref[member])
        column_parts[member] = spread(1, member).astype(bf16)
        for chip in range(chips):
            send_block(
                column_parts.at[member, :, columns(member_at(chip * cores + 1))],
                column_sibling.at[member, chip],
                send_sems.at[0],
                column_sib_sems.at[member],
                sibling,
            )

    @pl.loop(0, team)
    def _(member):
        wait_bytes(column_sibling.at[member], column_sib_sems.at[member])
        for chip in near + [0]:
            target = member_at(chip * cores)
            both = column_parts[member, :, columns(target)].astype(f32) + column_sibling[
                member, chip
            ].astype(f32)
            if chip == 0:
                column_sum_own[member] = both
            else:
                column_send[chip - 1, member] = both.astype(bf16)
                send_block(
                    column_send.at[chip - 1, member],
                    column_recv.at[opposite_chip(chip) - 1, member],
                    send_sems.at[1],
                    column_sems.at[member, opposite_chip(chip) - 1],
                    target,
                )

    def weight_grads(level, source_ref):
        @pl.loop(0, team)
        def _(member):
            slot = lax.rem(member, 2)

            @pl.when(member >= 2)
            def _():
                wait_bytes(grad_stage.at[slot], out_sems.at[slot])

            grad_stage[slot] = lax.dot_general(
                source_ref[:, :, columns(member)].reshape(team * tokens, part),
                grad_mixed[level].reshape(team * tokens, 2 * part),
                (((0,), (0,)), ((), ())),
                preferred_element_type=f32,
            ).astype(bf16)
            for block in range(grid):
                pltpu.make_async_copy(
                    grad_stage.at[slot, pl.ds(block * run, run)],
                    grads_hbm.at[
                        block, pl.ds(pl.multiple_of((member * 2 + level) * run, run), run)
                    ],
                    out_sems.at[slot],
                ).start()

        for slot in range(2):
            wait_bytes(grad_stage.at[slot], out_sems.at[slot])
        bias_ref[level] = jnp.dot(
            jnp.ones((8, team * tokens), bf16),
            grad_mixed[level].reshape(team * tokens, 2 * part),
            preferred_element_type=f32,
        )

    weight_grads(1, second_ref)

    @pl.loop(0, team)
    def _(step):
        offset = team - 1 - step
        member = member_at(offset)
        chip = offset // cores
        grad = column_sum_own[member] + direct[member]
        for other in near:
            wait_bytes(column_recv.at[other - 1, member], column_sems.at[member, other - 1])
            grad = grad + column_recv[other - 1, member].astype(f32)
        carried = first_ref[member, :, columns(place)].astype(f32)
        straight = mix_grads(0, member, grad, carried)
        row_part[...] = spread(0, member)
        row_part[:, columns(place)] += straight

        @pl.when(lax.rem(offset, cores) == 1)
        def _():
            row_give[chip] = row_part[...].astype(bf16)
            send_block(
                row_give.at[chip],
                row_sibling.at[chip],
                send_sems.at[2],
                row_sib_sems.at[chip],
                sibling,
            )

        @pl.when(lax.rem(offset, cores) == 0)
        def _():
            row_keep[chip] = row_part[...].astype(bf16)

    for chip in near[::-1] + [0]:
        wait_bytes(row_sibling.at[chip], row_sib_sems.at[chip])
        both = row_keep[chip].astype(f32) + row_sibling[chip].astype(f32)
        if chip == 0:
            row_sum_own[...] = both
        else:
            row_send[chip - 1] = both.astype(bf16)
            send_block(
                row_send.at[chip - 1],
                row_recv.at[opposite_chip(chip) - 1],
                send_sems.at[3],
                row_sems.at[opposite_chip(chip) - 1],
                member_at(chip * cores),
            )

    weight_grads(0, first_ref)
    grad_stage[0] = lax.dot_general(
        top_ref[...].reshape(team * tokens, part),
        grad_lin_ref[...].reshape(team * tokens, 2 * part),
        (((0,), (0,)), ((), ())),
        preferred_element_type=f32,
    ).astype(bf16)
    for block in range(grid):
        pltpu.make_async_copy(
            grad_stage.at[0, pl.ds(block * run, run)],
            grads_hbm.at[block, pl.ds(team * 2 * run, run)],
            out_sems.at[0],
        ).start()
    total = row_sum_own[...]
    for other in near:
        wait_bytes(row_recv.at[other - 1], row_sems.at[other - 1])
        total = total + row_recv[other - 1].astype(f32)
    features_ref[...] = total.astype(bf16)
    wait_bytes(grad_stage.at[0], out_sems.at[0])
    wait_bytes(column_sibling, send_sems.at[0])
    wait_bytes(column_send, send_sems.at[1])
    wait_bytes(row_give, send_sems.at[2])
    wait_bytes(row_send, send_sems.at[3])


def run_highway_back(grad_lin, first_all, first, second, mixed, hidden, top):
    team, tokens, features = first.shape
    part = features // team
    chips = team // lax.axis_size("c")
    width = first_all.shape[2]
    bf16, f32 = jnp.bfloat16, jnp.float32
    vmem = pl.BlockSpec(memory_space=pltpu.VMEM)
    hbm = pl.BlockSpec(memory_space=pl.ANY)
    return pl.pallas_call(
        highway_back_kernel,
        in_specs=[vmem, hbm] + [vmem] * 5,
        out_specs=[vmem, hbm, vmem],
        out_shape=[
            jax.ShapeDtypeStruct((tokens, features), bf16),
            jax.ShapeDtypeStruct(first_all.shape, bf16),
            jax.ShapeDtypeStruct((2, 8, 2 * part), f32),
        ],
        scratch_shapes=[
            pltpu.VMEM((2, features, 2 * part), bf16),
            pltpu.VMEM((part, width), bf16),
            pltpu.VMEM((2, team, tokens, 2 * part), bf16),
            pltpu.VMEM((team, tokens, part), f32),
            pltpu.VMEM((team, tokens, features), bf16),
            pltpu.VMEM((team, chips, tokens, part), bf16),
            pltpu.VMEM((chips - 1, team, tokens, part), bf16),
            pltpu.VMEM((chips - 1, team, tokens, part), bf16),
            pltpu.VMEM((team, tokens, part), f32),
            pltpu.VMEM((tokens, features), f32),
            pltpu.VMEM((chips, tokens, features), bf16),
            pltpu.VMEM((chips, tokens, features), bf16),
            pltpu.VMEM((chips, tokens, features), bf16),
            pltpu.VMEM((chips - 1, tokens, features), bf16),
            pltpu.VMEM((chips - 1, tokens, features), bf16),
            pltpu.VMEM((tokens, features), f32),
            pltpu.VMEM((2, part, width), bf16),
            pltpu.SemaphoreType.DMA((2,)),
            pltpu.SemaphoreType.DMA((4,)),
            pltpu.SemaphoreType.DMA((team,)),
            pltpu.SemaphoreType.DMA((team, chips - 1)),
            pltpu.SemaphoreType.DMA((chips,)),
            pltpu.SemaphoreType.DMA((chips - 1,)),
            pltpu.SemaphoreType.DMA((2,)),
        ],
        compiler_params=pltpu.CompilerParams(
            collective_id=3, has_side_effects=True, vmem_limit_bytes=60 * 1024 * 1024
        ),
        name="highway_team_back",
    )(grad_lin, first_all, first, second, mixed, hidden, top)


def every_coords(shift):
    g, t, y, x, c = axis_sizes()
    sizes = (g, t, y, x, c)
    coords, rest = {}, shift
    for name, size in list(zip(EVERY, sizes))[::-1]:
        coords[name] = lax.rem(lax.axis_index(name) + lax.rem(rest, size), size)
        rest = rest // size
    return coords


def every_place(coords):
    place = 0
    for name in EVERY:
        place = place * lax.axis_size(name) + coords[name]
    return place


def return_kernel(
    shared,
    grads_ref,
    small_ref,
    team_ref,
    project_ref,
    sums_ref,
    shared_ref,
    y_recv,
    g_send,
    g_recv,
    kept,
    team_send,
    small_recv,
    y_sems,
    g_sems,
    team_sems,
    small_sems,
    send_sems,
):
    grid, rows, lanes = grads_ref.shape
    team = team_size()
    g_size, y_size = lax.axis_size("g"), lax.axis_size("y")
    devices = small_ref.shape[0]
    groups = shared_ref.shape[0]
    cut = team_ref.shape[1] * team
    step = team_ref.shape[1]
    f32, bf16 = jnp.float32, jnp.bfloat16
    here = every_place({name: lax.axis_index(name) for name in EVERY})
    place = team_place()
    barrier = pltpu.get_barrier_semaphore()

    @pl.loop(1, devices)
    def _(shift):
        pl.semaphore_signal(
            barrier, inc=1, device_id=every_coords(shift), device_id_type=pl.DeviceIdType.MESH
        )

    pl.semaphore_wait(barrier, devices - 1)
    pieces = [pl.ds(k * step, step) for k in range(team)] + [pl.ds(cut, rows - cut)]
    g_index, y_index = lax.axis_index("g"), lax.axis_index("y")
    other_y = lax.rem(y_index + 1, y_size)
    for k, piece in enumerate(pieces):
        for dg in list(range(1, g_size)) + [0]:
            g = lax.rem(g_index + dg, g_size)
            send_grid(
                grads_ref.at[g * y_size + other_y, piece],
                y_recv.at[dg, piece],
                send_sems.at[0],
                y_sems.at[k, dg],
                0,
                1,
            )

    @pl.loop(1, devices)
    def _(shift):
        coords = every_coords(shift)
        pltpu.make_async_remote_copy(
            src_ref=small_ref.at[every_place(coords)],
            dst_ref=small_recv.at[here],
            send_sem=send_sems.at[3],
            recv_sem=small_sems.at[0],
            device_id=coords,
            device_id_type=pl.DeviceIdType.MESH,
        ).start()

    small_recv[here] = small_ref[here]
    for k, piece in enumerate(pieces):
        for dg in list(range(1, g_size)) + [0]:
            g = lax.rem(g_index + dg, g_size)
            wait_bytes(y_recv.at[dg, piece], y_sems.at[k, dg])
            both = grads_ref[g * y_size + y_index, piece].astype(f32) + y_recv[dg, piece].astype(f32)
            if dg == 0:
                kept[piece] = both
            else:
                g_send[dg - 1, piece] = both.astype(bf16)
                send_grid(
                    g_send.at[dg - 1, piece],
                    g_recv.at[g_size - dg - 1, piece],
                    send_sems.at[1],
                    g_sems.at[k, g_size - dg - 1],
                    dg,
                    0,
                )

    wait_bytes(small_recv.at[pl.ds(0, devices - 1)], small_sems.at[0])
    sums_ref[...] = jnp.sum(small_recv[...].astype(f32), axis=0)
    group = (g_index * lax.axis_size("t") + lax.axis_index("t")) * y_size + y_index
    banks = devices // groups

    @pl.loop(1, groups)
    def _(shift):
        coords = every_coords(shift * banks)
        pltpu.make_async_remote_copy(
            src_ref=sums_ref.at[pl.ds(0, shared)],
            dst_ref=shared_ref.at[group],
            send_sem=send_sems.at[4],
            recv_sem=small_sems.at[1],
            device_id=coords,
            device_id_type=pl.DeviceIdType.MESH,
        ).start()

    shared_ref[group] = sums_ref[pl.ds(0, shared)]
    for k, piece in enumerate(pieces):
        total = kept[piece]
        for dg in range(1, g_size):
            wait_bytes(g_recv.at[dg - 1, piece], g_sems.at[k, dg - 1])
            total = total + g_recv[dg - 1, piece].astype(f32)
        if k == team:
            project_ref[...] = total
        else:
            team_send[piece] = total.astype(bf16)

            @pl.when(place == k)
            def _():
                team_ref[k] = team_send[piece]

            @pl.when(place != k)
            def _():
                send_block(
                    team_send.at[piece], team_ref.at[place], send_sems.at[2], team_sems.at[0], k
                )

    wait_bytes(team_ref.at[pl.ds(0, team - 1)], team_sems.at[0])
    wait_bytes(shared_ref.at[pl.ds(0, groups - 1)], small_sems.at[1])
    wait_bytes(y_recv, send_sems.at[0])
    wait_bytes(g_recv, send_sems.at[1])
    wait_bytes(team_ref.at[pl.ds(0, team - 1)], send_sems.at[2])
    wait_bytes(small_recv.at[pl.ds(0, devices - 1)], send_sems.at[3])
    wait_bytes(shared_ref.at[pl.ds(0, groups - 1)], send_sems.at[4])


def run_return(grads, small, step, shared, groups):
    grid, rows, lanes = grads.shape
    team = team_size()
    g_size = lax.axis_size("g")
    bf16, f32 = jnp.bfloat16, jnp.float32
    vmem = pl.BlockSpec(memory_space=pltpu.VMEM)
    small_rows = small.shape[1]
    return pl.pallas_call(
        partial(return_kernel, shared),
        in_specs=[vmem, vmem],
        out_specs=[vmem] * 4,
        out_shape=[
            jax.ShapeDtypeStruct((team, step, lanes), bf16),
            jax.ShapeDtypeStruct((rows - team * step, lanes), f32),
            jax.ShapeDtypeStruct((small_rows, LANES), f32),
            jax.ShapeDtypeStruct((groups, shared, LANES), f32),
        ],
        scratch_shapes=[
            pltpu.VMEM((g_size, rows, lanes), bf16),
            pltpu.VMEM((g_size - 1, rows, lanes), bf16),
            pltpu.VMEM((g_size - 1, rows, lanes), bf16),
            pltpu.VMEM((rows, lanes), f32),
            pltpu.VMEM((rows, lanes), bf16),
            pltpu.VMEM(small.shape, bf16),
            pltpu.SemaphoreType.DMA((team + 1, g_size)),
            pltpu.SemaphoreType.DMA((team + 1, g_size - 1)),
            pltpu.SemaphoreType.DMA((1,)),
            pltpu.SemaphoreType.DMA((2,)),
            pltpu.SemaphoreType.DMA((5,)),
        ],
        compiler_params=pltpu.CompilerParams(
            collective_id=4, has_side_effects=True, vmem_limit_bytes=56 * 1024 * 1024
        ),
        name="return_sums",
    )(grads, small)


def axis_sizes():
    return tuple(lax.axis_size(name) for name in EVERY)


def run_rows(received):
    g, t, y, x, c = axis_sizes()
    lanes = received.shape[-1]
    split = received.reshape(t, x * c, 2, -1, lanes).transpose(0, 2, 1, 3, 4)
    return split.reshape(t, 2, -1, lanes)


def member_rows(runs):
    g, t, y, x, c = axis_sizes()
    lanes = runs.shape[-1]
    split = runs.reshape(t, 2, x * c, -1, lanes).transpose(0, 2, 1, 3, 4)
    return split.reshape(t * x * c, -1, lanes)


def team_slices(values, parts):
    team = team_size()
    two, rows, columns = values.shape
    lanes = columns // (parts * team)
    split = values.reshape(two, rows, parts, team, lanes).transpose(3, 0, 1, 2, 4)
    return split.reshape(team, two * rows, parts * lanes)


def whole_columns(received, parts):
    team, two_rows, lanes = received.shape
    split = received.reshape(team, 2, two_rows // 2, parts, lanes // parts)
    return split.transpose(1, 2, 3, 0, 4).reshape(2, two_rows // 2, team * lanes)


def team_first(values):
    g, t, y, x, c = axis_sizes()
    rows = values.shape[0]
    split = values.reshape(rows, -1, g, t, y, x, c, values.shape[1] // (2 * g * t * y * x * c))
    return split.transpose(3, 5, 6, 0, 1, 2, 4, 7)


def permuted_columns(values):
    g, t, y, x, c = axis_sizes()
    split = values.reshape(values.shape[0], g, t, y, x, c, -1)
    return split.transpose(0, 2, 4, 5, 1, 3, 6).reshape(values.shape)


def restored_columns(values):
    g, t, y, x, c = axis_sizes()
    split = values.reshape(values.shape[0], t, x, c, g, y, -1)
    return split.transpose(0, 4, 1, 5, 2, 3, 6).reshape(values.shape)


def padded_rows(values, rows):
    blocks = values.shape[0]
    flat = values.reshape(blocks, -1)
    return jnp.pad(flat, ((0, 0), (0, rows * LANES - flat.shape[1]))).reshape(blocks, rows, LANES)


def row_count(items):
    return -(-items // LANES)


def bank_blocks(grad_filters, bank_cols, groups):
    turned = grad_filters.T
    blocks, at = [], 0
    for bank_specs in bank_plan(bank_cols):
        used = sum(count for width, first, count in bank_specs)
        piece = turned[at : at + used].reshape(groups, used // groups, LANES)
        blocks.append(jnp.pad(piece, ((0, 0), (0, (bank_cols - used) // groups), (0, 0))))
        at += used
    return jnp.stack(blocks, axis=1).reshape(groups * len(blocks), bank_cols // groups, LANES)


def bank_filters(blocks, bank, bank_cols, groups):
    taps = [
        [width * EMBED for width, first, count in bank_specs for _ in range(count)]
        for bank_specs in bank_plan(bank_cols)
    ]
    taps = [row + [0] * (bank_cols - len(row)) for row in taps]
    limit = lax.dynamic_index_in_dim(jnp.asarray(taps, jnp.int32), bank, 0, False)
    used = [sum(count for width, first, count in specs) for specs in bank_plan(bank_cols)]
    choices = [
        lambda value, each=count // groups: jnp.pad(
            value[:, :each].reshape(groups * each, LANES), ((0, bank_cols - groups * each), (0, 0))
        )
        for count in used
    ]
    turned = lax.switch(bank, choices, blocks).T
    row = lax.broadcasted_iota(jnp.int32, (TAPS, 1), 0)
    kernel = jnp.where(row < limit[None, :], turned[:TAPS], 0.0)
    bias = jnp.where(limit > 0, turned[TAPS], 0.0)
    return (kernel.reshape(1, WIDEST, EMBED, bank_cols), bias[None])


def shards(
    char_ids,
    resets,
    out_grad,
    char_table,
    conv_weight,
    conv_bias,
    highway_weight,
    highway_bias,
    proj_weight,
    proj_bias,
    lstm_weight,
    lstm_bias,
    lstm_proj,
):
    f32, bf16 = jnp.float32, jnp.bfloat16
    own, steps = resets.shape
    team = team_size()
    place = team_place()
    devices = team * lax.axis_size("g") * lax.axis_size("y")
    bank_cols = conv_weight.shape[3]
    highway_rows = highway_weight.shape[1]
    features_all = highway_rows * devices
    part = features_all // team
    lstm_rows = lstm_weight.shape[1]
    width = proj_weight.shape[1]
    cells_all = lstm_proj.shape[1]
    cells = cells_all // team

    conv_own = jnp.concatenate([conv_weight.reshape(-1, bank_cols), conv_bias], axis=0)
    banks = lax.axis_size("x") * lax.axis_size("c")
    conv_all = lax.all_to_all(
        jnp.broadcast_to(conv_own[None], (banks,) + conv_own.shape),
        ("x", "c"),
        split_axis=0,
        concat_axis=0,
        tiled=True,
    )
    conv_weight_all = conv_all[:, :-1].reshape((banks,) + conv_weight.shape[1:])
    conv_bias_all = conv_all[:, -1]
    sizes = [highway_bias.size, proj_bias.size, lstm_bias.size, resets.size]
    small = jnp.concatenate(
        [
            highway_bias.reshape(-1),
            proj_bias.reshape(-1),
            lstm_bias.reshape(-1),
            resets.astype(bf16).reshape(-1),
        ]
    )
    small_all = lax.all_to_all(
        jnp.broadcast_to(small[None], (devices, small.size)),
        EVERY,
        split_axis=0,
        concat_axis=0,
        tiled=True,
    )
    cut = [sum(sizes[:k]) for k in range(5)]
    highway_bias_all = small_all[:, cut[0] : cut[1]].reshape(devices, 2, -1)
    highway_bias_all = highway_bias_all.transpose(1, 0, 2).reshape(2, 2 * features_all)
    highway_bias_all = team_first(highway_bias_all).reshape(team, 2, 2 * part)
    proj_bias_all = small_all[:, cut[1] : cut[2]].reshape(-1).astype(f32)
    lstm_bias_all = small_all[:, cut[2] : cut[3]].reshape(devices, 2, -1)
    lstm_bias_all = lstm_bias_all.transpose(1, 0, 2).reshape(2, 4, team, cells)
    resets_all = small_all[:, cut[3] : cut[4]].reshape(
        lax.axis_size("g"), lax.axis_size("t"), lax.axis_size("y"), -1, own, steps
    )
    resets_team = lax.dynamic_index_in_dim(resets_all, lax.axis_index("g"), 0, False)
    resets_team = lax.dynamic_index_in_dim(resets_team, lax.axis_index("y"), 1, False)
    resets_team = resets_team.reshape(team * own, steps).astype(f32)
    highway_bias_own = lax.dynamic_index_in_dim(highway_bias_all, place, 0, False).astype(f32)
    lstm_bias_own = lax.dynamic_index_in_dim(lstm_bias_all, place, 2, False)
    lstm_bias_own = lstm_bias_own.reshape(2, 1, 4 * cells).astype(f32)

    highway_slices = team_first(highway_weight.reshape(2 * highway_rows, -1))
    turned_rows = lstm_proj.shape[2]
    gate_slices = lstm_weight.reshape(2, lstm_rows, 4, team, cells).transpose(3, 0, 2, 1, 4)
    swapped = swap_team(
        jnp.concatenate(
            [
                highway_slices.reshape(team, 2 * highway_rows, 2 * part),
                gate_slices.reshape(team, 8 * lstm_rows, cells),
                team_slices(jnp.swapaxes(lstm_proj, 1, 2), 1),
            ],
            axis=1,
        )
    )
    ends = [2 * highway_rows, 2 * highway_rows + 8 * lstm_rows]
    block = jnp.concatenate([swapped[:, : ends[0]].reshape(-1, 2 * part), proj_weight], axis=0)
    t, x, c = lax.axis_size("t"), lax.axis_size("x"), lax.axis_size("c")
    lstm_block = (
        swapped[:, ends[0] : ends[1]]
        .reshape(t, x * c, 8, lstm_rows, cells)
        .transpose(0, 2, 1, 3, 4)
        .reshape(t * 8, x * c * lstm_rows, cells)
    )
    turned_block = run_rows(swapped[:, ends[1] :])
    cut_rows = team * 2 * highway_rows
    grid = lax.axis_size("g") * lax.axis_size("y")
    bank = lax.axis_index("x") * lax.axis_size("c") + lax.axis_index("c")
    own_ids = lax.dynamic_slice_in_dim(char_ids, bank * own, own, axis=0)
    own_ids = jnp.swapaxes(own_ids, 0, 1).reshape(own * steps, char_ids.shape[2])
    filters, counts = filter_matrix(conv_weight_all, conv_bias_all)
    tight_from = wide_columns(bank_cols)
    padded_ids, tiled = embed_tokens(own_ids, char_table)

    tokens = own * steps
    (
        pooled_lse,
        first_all,
        lstm_own,
        turned_own,
        first,
        second,
        mixed,
        hidden,
        top_own,
        lin_parts,
    ) = run_highway(
        tight_from, tiled, filters, counts, block, lstm_block, turned_block, highway_bias_own
    )
    lstm_own = lstm_own.reshape(grid, t, 2, 4, x * c * lstm_rows, cells)

    keep_forward = 1.0 - resets_team
    keep_backward = 1.0 - jnp.concatenate(
        [resets_team[:, 1:], jnp.zeros((team * own, 1), f32)], axis=1
    )
    keep = jnp.stack([keep_forward.T, keep_backward.T])[..., None]
    grad_time = out_grad.reshape(own, steps, 2, width).transpose(2, 1, 0, 3)
    grad_lin_all, lstm_grads, turned_grads, bias_sums = run_lstm(
        lin_parts.reshape(team, steps, own, width),
        proj_bias_all[None],
        grad_time,
        lstm_own,
        turned_own,
        lstm_bias_own,
        keep,
    )
    lstm_summed = lax.psum_scatter(lstm_grads, GRID, scatter_dimension=0, tiled=False)
    turned_summed = lax.all_to_all(turned_grads, GRID, split_axis=0, concat_axis=0, tiled=True)
    turned_summed = turned_summed.astype(f32).sum(axis=0).astype(bf16)
    grad_input = lax.dynamic_index_in_dim(grad_lin_all, place, 0, False).reshape(tokens, width)
    grad_project_b = column_sum(grad_input)
    grad_features, first_parts, highway_bias_sums = run_highway_back(
        grad_lin_all.reshape(team, tokens, width),
        first_all,
        first,
        second,
        mixed,
        hidden,
        top_own,
    )
    grad_features = restored_columns(grad_features)
    grad_filters, grad_table = pool_grads(
        padded_ids,
        tiled,
        filters,
        counts,
        pooled_lse,
        grad_features,
        char_table.shape[0],
        tight_from,
    )
    lstm_returned = swap_team(member_rows(lstm_summed))
    lstm_weight_grad = whole_columns(lstm_returned, 4).astype(f32)
    turned_grad = whole_columns(swap_team(member_rows(turned_summed)), 1).astype(f32)
    lstm_proj_grad = jnp.swapaxes(turned_grad, 1, 2)
    g, t, y, x, c = axis_sizes()

    def own_place(values, parts):
        lanes = values.shape[-1] // parts
        split = values.reshape(2, parts, 1, lanes)
        full = jnp.zeros((2, parts, team, lanes), f32)
        return lax.dynamic_update_slice(full, split, (0, 0, place, 0)).reshape(2, -1)

    lstm_bias_parts = own_place(bias_sums[:, 0], 4)
    highway_bias_parts = own_place(highway_bias_sums[:, 0], 2)
    highway_bias_parts = (
        highway_bias_parts.reshape(2, 2, t, x, c, g, y, -1)
        .transpose(0, 1, 5, 2, 6, 3, 4, 7)
        .reshape(2, 2 * features_all)
    )
    biases = jnp.concatenate(
        [
            lstm_bias_parts.reshape(2, devices, -1).transpose(1, 0, 2).reshape(devices, -1),
            highway_bias_parts.reshape(2, devices, -1).transpose(1, 0, 2).reshape(devices, -1),
            grad_project_b.reshape(devices, -1),
        ],
        axis=1,
    )
    groups = g * t * y
    table_items = -(-grad_table.size // groups)
    table_flat = jnp.pad(grad_table.reshape(-1), (0, groups * table_items - grad_table.size))
    table_blocks = jnp.broadcast_to(
        padded_rows(table_flat.reshape(groups, table_items), row_count(table_items))[:, None],
        (groups, x * c, row_count(table_items), LANES),
    ).reshape(devices, -1, LANES)
    filter_blocks = bank_blocks(grad_filters, bank_cols, groups)
    shared = -(-(filter_blocks.shape[1] + table_blocks.shape[1]) // 8) * 8
    fill = shared - filter_blocks.shape[1] - table_blocks.shape[1]
    bias_rows = -(-(shared + row_count(biases.shape[1])) // 16) * 16 - shared
    small = jnp.concatenate(
        [
            filter_blocks,
            jnp.pad(table_blocks, ((0, 0), (0, fill), (0, 0))),
            padded_rows(biases, bias_rows),
        ],
        axis=1,
    ).astype(bf16)
    highway_returned, project_grad, mine, both = run_return(
        first_parts, small, 2 * highway_rows, shared, groups
    )
    highway_weight_grad = (
        highway_returned.reshape(t, x, c, 2 * highway_rows, 2, g, y, -1)
        .transpose(3, 4, 5, 0, 6, 1, 2, 7)
        .reshape(2, highway_rows, 2 * features_all)
        .astype(f32)
    )

    mine_biases = mine[shared:].reshape(-1)
    ends = [2 * lstm_bias.shape[1], 2 * lstm_bias.shape[1] + 2 * highway_bias.shape[1]]
    lstm_bias_grad = mine_biases[: ends[0]].reshape(2, -1)
    highway_bias_grad = mine_biases[ends[0] : ends[1]].reshape(2, -1)
    proj_bias_grad = mine_biases[ends[1] : ends[1] + proj_bias.size]
    grad_kernel, grad_bias = bank_filters(
        both[:, : filter_blocks.shape[1]], bank, bank_cols, groups
    )
    table_end = filter_blocks.shape[1] + table_blocks.shape[1]
    grad_table = both[:, filter_blocks.shape[1] : table_end].reshape(groups, -1)[:, :table_items]
    grad_table = grad_table.reshape(-1)[: char_table.size].reshape(char_table.shape)
    return (
        grad_table,
        grad_kernel,
        grad_bias,
        highway_weight_grad,
        highway_bias_grad,
        project_grad,
        proj_bias_grad,
        lstm_weight_grad,
        lstm_bias_grad,
        lstm_proj_grad,
    )


def solution(mesh):
    dp, bank = mesh.shape["dp"], mesh.shape["bank"]
    fine = Mesh(mesh.devices.reshape(dp // 4, 2, 2, bank // 2, 2), EVERY)
    rows, banks = ("g", "t", "y"), ("x", "c")
    whole = rows + banks
    placed = (
        P(rows, None, None),
        P(whole, None),
        P(whole, None, None),
        P(),
        P(banks, None, None, None),
        P(banks, None),
        P(None, whole, None),
        P(None, whole),
        P(whole, None),
        P(whole),
        P(None, whole, None),
        P(None, whole),
        P(None, None, whole),
    )
    return jax.shard_map(
        shards,
        mesh=fine,
        in_specs=placed,
        out_specs=(
            P(),
            P(banks, None, None, None),
            P(banks, None),
            P(None, whole, None),
            P(None, whole),
            P(whole, None),
            P(whole),
            P(None, whole, None),
            P(None, whole),
            P(None, None, whole),
        ),
        check_vma=False,
    )
```

```python
from functools import partial
import math

import jax
import jax.numpy as jnp
from jax import lax
from jax.experimental import pallas as pl
from jax.experimental.pallas import tpu as pltpu
from jax.sharding import Mesh, PartitionSpec as P

CHAR_COUNT = 50
VOCAB = 262
EMBED = 16
WIDEST = 7
TAPS = WIDEST * EMBED
LANES = 128
PLACES = 64
TIGHT = 48
CHUNK = 256
TOKEN_BLOCK = 16
AHEAD = 6


def bank_plan(bank_cols):
    return [
        [
            (1, 0, bank_cols // 32),
            (2, bank_cols // 32, bank_cols // 32),
            (3, bank_cols // 16, bank_cols // 16),
            (4, bank_cols // 8, bank_cols // 8),
        ],
        [(5, 0, bank_cols // 4)],
        [(6, 0, bank_cols // 2)],
        [(7, 0, bank_cols)],
    ]


def transposed(former, latter):
    return lax.dot_general(
        former, latter, (((1,), (1,)), ((), ())), preferred_element_type=jnp.float32
    )


def outer_sum(former, latter):
    return lax.dot_general(
        former, latter, (((0,), (0,)), ((), ())), preferred_element_type=jnp.float32
    )


def column_sum(values):
    ones_row = jnp.ones((1, values.shape[0]), values.dtype)
    return jnp.dot(ones_row, values, preferred_element_type=jnp.float32)[0]


def filter_columns(bank_cols):
    columns = []
    for bank_index, bank_specs in enumerate(bank_plan(bank_cols)):
        for filter_width, first_col, count in bank_specs:
            columns.append((filter_width, bank_index, first_col, count))
    return columns


def shift_rows(values, amount):
    count = values.shape[0]
    return values if amount % count == 0 else pltpu.roll(values, amount % count, 0)


def block_windows(tiled_ref, windows_wide, windows_tight):
    tokens, places, lanes = tiled_ref.shape
    rows = tokens * places
    tiled = tiled_ref[...].astype(jnp.float32).reshape(rows, lanes)
    lane = lax.broadcasted_iota(jnp.int32, (rows, lanes), 1)
    place = lax.broadcasted_iota(jnp.int32, (rows, lanes), 0) % places
    windows = tiled
    for offset in range(1, WIDEST):
        windows = jnp.where(lane // EMBED == offset, shift_rows(tiled, rows - offset), windows)
    late = place >= CHAR_COUNT - WIDEST + 1 + (lane - TAPS - 1)
    extra = jnp.where((lane == TAPS) | ((lane <= TAPS + WIDEST) & late), 1.0, 0.0)
    windows = jnp.where(lane < TAPS, windows, extra)
    windows_wide[...] = windows.astype(jnp.bfloat16)
    windows_tight[...] = (
        windows.reshape(tokens, places, lanes)[:, :TIGHT]
        .reshape(tokens * TIGHT, lanes)
        .astype(jnp.bfloat16)
    )


def column_chunks(total, tight_from):
    return [
        (start, start < tight_from) for start in range(0, total, CHUNK)
    ]


def pool_kernel(tight_from, tiled_ref, weight_ref, count_ref, features_ref, lse_ref, wide, tight):
    tokens, places, lanes = tiled_ref.shape
    block_windows(tiled_ref, wide, tight)
    for start, is_wide in column_chunks(weight_ref.shape[1], tight_from):
        cols = pl.ds(start, CHUNK)
        windows = wide if is_wide else tight
        conv_out = jnp.dot(
            windows[...], weight_ref[:, cols], preferred_element_type=jnp.float32
        ).reshape(tokens, -1, CHUNK)
        highest = jnp.max(conv_out, axis=1)
        total = jnp.sum(jnp.exp(conv_out - highest[:, None, :]), axis=1)
        pooled_lse = highest + jnp.log(total)
        lse_ref[:, cols] = pooled_lse
        pooled_pre = pooled_lse - count_ref[0:1, cols]
        features_ref[:, cols] = (pooled_pre * jax.nn.sigmoid(pooled_pre)).astype(jnp.bfloat16)


def pool_grad_block(
    tight_from,
    tiled_ref,
    ids_row,
    weight_ref,
    count_ref,
    lse_ref,
    upstream_ref,
    grad_weight_ref,
    table_ref,
    wide,
    tight,
    spread,
):
    tokens, places, lanes = tiled_ref.shape
    block_windows(tiled_ref, wide, tight)
    spread[...] = jnp.zeros_like(spread)
    wide_turned = wide[...].T
    tight_turned = tight[...].T
    for start, is_wide in column_chunks(weight_ref.shape[1], tight_from):
        cols = pl.ds(start, CHUNK)
        windows, turned = (wide, wide_turned) if is_wide else (tight, tight_turned)
        weights = weight_ref[:, cols]
        conv_out = jnp.dot(
            windows[...], weights, preferred_element_type=jnp.float32
        ).reshape(tokens, -1, CHUNK)
        pooled_lse = lse_ref[:, cols]
        pooled_pre = pooled_lse - count_ref[0:1, cols]
        squashed = jax.nn.sigmoid(pooled_pre)
        upstream = (
            upstream_ref[:, cols].astype(jnp.float32)
            * squashed
            * (1.0 + pooled_pre * (1.0 - squashed))
        )
        softened = jnp.exp(conv_out - pooled_lse[:, None, :])
        grad_conv = (softened * upstream[:, None, :]).astype(jnp.bfloat16)
        places_here = grad_conv.shape[1]
        grad_conv = grad_conv.reshape(tokens * places_here, CHUNK)
        grad_weight_ref[:, cols] += jnp.dot(turned, grad_conv, preferred_element_type=jnp.float32)
        part = lax.dot_general(
            grad_conv, weights, (((1,), (1,)), ((), ())), preferred_element_type=jnp.float32
        ).reshape(tokens, places_here, lanes)
        spread[:, :places_here, :] += part
    rows = tokens * places
    flat = spread[...].reshape(rows, lanes)
    lane = lax.broadcasted_iota(jnp.int32, (rows, lanes), 1)
    aligned = jnp.where(lane < EMBED, flat, 0.0)
    for offset in range(1, WIDEST):
        aligned = jnp.where(lane // EMBED == offset, shift_rows(flat, offset), aligned)
    high = aligned.astype(jnp.bfloat16)
    low = (aligned - high.astype(jnp.float32)).astype(jnp.bfloat16)
    vocab = table_ref.shape[0]
    selector = jnp.where(
        lax.broadcasted_iota(jnp.int32, (vocab, rows), 0) == ids_row, 1.0, 0.0
    ).astype(jnp.bfloat16)
    table_ref[...] += jnp.dot(selector, high, preferred_element_type=jnp.float32) + jnp.dot(
        selector, low, preferred_element_type=jnp.float32
    )


def filter_matrix(conv_weight, conv_bias):
    bank_cols = conv_bias.shape[1]
    taps, biases, masks, counts = [], [], [], []
    for filter_width, bank_index, first_col, count in filter_columns(bank_cols):
        piece = conv_weight[bank_index, :filter_width, :, first_col : first_col + count]
        piece = piece.reshape(filter_width * EMBED, count)
        taps.append(jnp.pad(piece, ((0, TAPS - filter_width * EMBED), (0, 0))))
        biases.append(conv_bias[bank_index, first_col : first_col + count])
        rows = lax.broadcasted_iota(jnp.int32, (LANES - TAPS - 1, count), 0)
        masks.append(jnp.where(rows == WIDEST - filter_width, -1e30, 0.0).astype(jnp.bfloat16))
        counts.append(jnp.full((8, count), math.log(CHAR_COUNT - filter_width + 1), jnp.float32))
    weights = jnp.concatenate(
        [
            jnp.concatenate(taps, axis=1),
            jnp.concatenate(biases)[None],
            jnp.concatenate(masks, axis=1),
        ],
        axis=0,
    )
    return (weights, jnp.concatenate(counts, axis=1))


def wide_columns(bank_cols):
    total = sum(count for width, bank, first, count in filter_columns(bank_cols) if CHAR_COUNT - width + 1 > TIGHT - 2)
    return -(-total // CHUNK) * CHUNK


def char_selector(token_ids, vocab_size):
    return token_ids.reshape(-1)[:, None] == lax.broadcasted_iota(jnp.int32, (1, vocab_size), 1)


def embed_tokens(token_ids, char_table):
    tokens = token_ids.shape[0]
    padded = jnp.pad(token_ids, ((0, 0), (0, PLACES - token_ids.shape[1])), constant_values=-1)
    table_tiled = jnp.pad(jnp.tile(char_table, (1, WIDEST)), ((0, 0), (0, LANES - TAPS)))
    selector = char_selector(padded, char_table.shape[0]).astype(jnp.bfloat16)
    tiled = jnp.dot(selector, table_tiled, preferred_element_type=jnp.float32)
    tiled = tiled.astype(jnp.bfloat16).reshape(tokens, PLACES, LANES)
    return (padded, tiled)


TEAM = ("t", "x", "c")
GRID = ("g", "y")
EVERY = ("g", "t", "y", "x", "c")


def team_place():
    x_size, c_size = lax.axis_size("x"), lax.axis_size("c")
    return (lax.axis_index("t") * x_size + lax.axis_index("x")) * c_size + lax.axis_index("c")


def team_size():
    return lax.axis_size("t") * lax.axis_size("x") * lax.axis_size("c")


def team_coords(place):
    x_size, c_size = lax.axis_size("x"), lax.axis_size("c")
    return {
        "t": place // (x_size * c_size),
        "x": lax.rem(place // c_size, x_size),
        "c": lax.rem(place, c_size),
    }


def swap_team(values):
    return lax.all_to_all(values, TEAM, split_axis=0, concat_axis=0, tiled=True)


def share_team(values):
    team = team_size()
    return swap_team(jnp.broadcast_to(values[None], (team,) + values.shape))


def sigmoid(values):
    return 0.5 * jnp.tanh(0.5 * values) + 0.5


def wait_bytes(ref, sem):
    pltpu.make_async_copy(ref, ref, sem).wait()


def lstm_kernel(
    team,
    lin_ref,
    out_grad_ref,
    weight_hbm,
    turned_hbm,
    bias_ref,
    keep_ref,
    grad_lin_all_ref,
    grad_weight_hbm,
    grad_turned_hbm,
    grad_bias_ref,
    weight_ref,
    proj_ref,
    grad_gates_ref,
    lin_all_ref,
    state_ref,
    full_ref,
    grad_proj_ref,
    gates,
    cell_start,
    projected,
    stage,
    received,
    received_back,
    grad_cell,
    grad_lin_sum,
    stage_lin,
    received_lin,
    grad_state_own,
    grad_stage,
    turned_stage,
    load_sems,
    lin_sems,
    send_sems,
    sum_sems,
    share_send_sems,
    share_sems,
    out_sems,
):
    _, steps, own, width = lin_ref.shape
    group = team * own
    cells = proj_ref.shape[2]
    row_block = 32
    place = team_place()
    own_rows = pl.ds(pl.multiple_of(place * own, own), own)
    peers = [lax.rem(place + k, team) for k in range(1, team)]
    last = steps - 1
    others = pl.ds(0, team - 1)
    other_rows = pl.ds(0, (team - 1) * own)
    g_size, y_size = lax.axis_size("g"), lax.axis_size("y")
    t_size = lax.axis_size("t")
    blocks = [
        (g * y_size + y, t, (g * t_size + t) * y_size + y)
        for g in range(g_size)
        for t in range(t_size)
        for y in range(y_size)
    ]
    run = weight_hbm.shape[4]
    turned_run = turned_hbm.shape[3]

    for d in range(2):
        for source, t, at in blocks:
            for q in range(4):
                pltpu.make_async_copy(
                    weight_hbm.at[source, t, d, q],
                    weight_ref.at[d, pl.ds(at * run, run), pl.ds(q * cells, cells)],
                    load_sems.at[0],
                ).start()
            pltpu.make_async_copy(
                turned_hbm.at[source, t, d],
                proj_ref.at[d, pl.ds(at * turned_run, turned_run)],
                load_sems.at[1],
            ).start()

    barrier = pltpu.get_barrier_semaphore()
    for peer in peers:
        pl.semaphore_signal(
            barrier, inc=1, device_id=team_coords(peer), device_id_type=pl.DeviceIdType.MESH
        )
    pl.semaphore_wait(barrier, team - 1)

    def send(source, target, send_sem, recv_sem, peer):
        pltpu.make_async_remote_copy(
            src_ref=source,
            dst_ref=target,
            send_sem=send_sem,
            recv_sem=recv_sem,
            device_id=team_coords(peer),
            device_id_type=pl.DeviceIdType.MESH,
        ).start()

    for t in range(steps):
        lin_all_ref[t] = lin_ref[:, t].reshape(group, width)
    for d in range(2):
        first = 0 if d == 0 else last
        state_ref[d, first] = jnp.zeros((group, width), jnp.bfloat16)
        cell_start[d, first] = jnp.zeros((group, cells), jnp.float32)
        grad_cell[d] = jnp.zeros((group, cells), jnp.float32)
    grad_lin_sum[...] = jnp.zeros_like(grad_lin_sum)
    wait_bytes(weight_ref, load_sems.at[0])
    wait_bytes(proj_ref, load_sems.at[1])

    @pl.loop(0, steps)
    def _(t):
        for d in range(2):
            for q in range(4):
                cols = pl.ds(q * cells, cells)
                gates[d, t, :, cols] = (
                    jnp.dot(
                        lin_all_ref[t],
                        weight_ref[d, :width, cols],
                        preferred_element_type=jnp.float32,
                    )
                    + bias_ref[d, :, cols]
                )

    def time_of(d, s):
        return s if d == 0 else last - s

    @pl.loop(0, steps)
    def _(s):
        for d in range(2):
            t = time_of(d, s)
            later = time_of(d, jnp.minimum(s + 1, last))

            @pl.when(s > 0)
            def _():
                wait_bytes(
                    state_ref.at[d, t, other_rows], share_sems.at[0, d, s]
                )
                for q in range(4):
                    cols = pl.ds(q * cells, cells)
                    gates[d, t, :, cols] += jnp.dot(
                        state_ref[d, t],
                        weight_ref[d, width:, cols],
                        preferred_element_type=jnp.float32,
                    )

            @pl.loop(0, group // row_block)
            def _(block):
                rows = pl.ds(pl.multiple_of(block * row_block, row_block), row_block)
                in_gate = sigmoid(gates[d, t, rows, pl.ds(0, cells)])
                forget_gate = sigmoid(gates[d, t, rows, pl.ds(cells, cells)])
                candidate = jnp.tanh(gates[d, t, rows, pl.ds(2 * cells, cells)])
                out_gate = sigmoid(gates[d, t, rows, pl.ds(3 * cells, cells)])
                gates[d, t, rows, pl.ds(0, cells)] = in_gate
                gates[d, t, rows, pl.ds(cells, cells)] = forget_gate
                gates[d, t, rows, pl.ds(2 * cells, cells)] = candidate
                gates[d, t, rows, pl.ds(3 * cells, cells)] = out_gate
                mixed = forget_gate * cell_start[d, t, rows] + in_gate * candidate
                cell_new = 3.0 * jnp.tanh(mixed * (1.0 / 3.0))
                full_ref[d, t, rows] = (out_gate * jnp.tanh(cell_new)).astype(jnp.bfloat16)

                @pl.when(s < last)
                def _():
                    cell_start[d, later, rows] = cell_new * keep_ref[d, later, rows]

            @pl.when(s > 0)
            def _():
                wait_bytes(stage.at[d, others], send_sems.at[d])

            part = lax.dot_general(
                full_ref[d, t],
                proj_ref[d],
                (((1,), (1,)), ((), ())),
                preferred_element_type=jnp.float32,
            )
            part = part.astype(jnp.bfloat16).reshape(team, own, width)
            stage[d] = part
            received[d, s, place] = stage[d, place]
            for peer in peers:
                send(
                    stage.at[d, peer],
                    received.at[d, s, place],
                    send_sems.at[d],
                    sum_sems.at[0, d, s],
                    peer,
                )
        for d in range(2):
            t = time_of(d, s)
            later = time_of(d, jnp.minimum(s + 1, last))
            wait_bytes(received.at[d, s, others], sum_sems.at[0, d, s])
            total = jnp.sum(received[d, s].astype(jnp.float32), axis=0)
            projected[d, t] = total

            @pl.when(s > 0)
            def _():
                wait_bytes(
                    state_ref.at[d, t, other_rows], share_send_sems.at[0, d]
                )

            @pl.when(s < last)
            def _():
                state_new = (3.0 * jnp.tanh(total * (1.0 / 3.0))).astype(jnp.bfloat16)
                kept = state_new.astype(jnp.float32) * keep_ref[d, later, own_rows]
                state_ref[d, later, own_rows] = kept.astype(jnp.bfloat16)
                for peer in peers:
                    send(
                        state_ref.at[d, later, own_rows],
                        state_ref.at[d, later, own_rows],
                        share_send_sems.at[0, d],
                        share_sems.at[0, d, s + 1],
                        peer,
                    )

    @pl.loop(0, steps)
    def _(s):
        for d in range(2):
            t = time_of(1 - d, s)

            @pl.when(s > 0)
            def _():
                wait_bytes(
                    received_back.at[d, jnp.maximum(s - 1, 0), others],
                    sum_sems.at[1, d, jnp.maximum(s - 1, 0)],
                )
                grad_state_own[...] = jnp.sum(
                    received_back[d, jnp.maximum(s - 1, 0)].astype(jnp.float32), axis=0
                )

            @pl.when(s == 0)
            def _():
                grad_state_own[...] = jnp.zeros((own, width), jnp.float32)

            grad_state = grad_state_own[...] + out_grad_ref[d, t].astype(jnp.float32)
            squashed = jnp.tanh(projected[d, t] * (1.0 / 3.0))
            grad_proj_ref[d, t, own_rows] = (grad_state * (1.0 - squashed * squashed)).astype(
                jnp.bfloat16
            )
            for peer in peers:
                send(
                    grad_proj_ref.at[d, t, own_rows],
                    grad_proj_ref.at[d, t, own_rows],
                    share_send_sems.at[1, d],
                    share_sems.at[1, d, s],
                    peer,
                )
        for d in range(2):
            t = time_of(1 - d, s)
            wait_bytes(grad_proj_ref.at[d, t, other_rows], share_sems.at[1, d, s])
            wait_bytes(
                grad_proj_ref.at[d, t, other_rows], share_send_sems.at[1, d]
            )

            @pl.loop(0, group // row_block)
            def _(block):
                rows = pl.ds(pl.multiple_of(block * row_block, row_block), row_block)
                grad_full = jnp.dot(
                    grad_proj_ref[d, t, rows], proj_ref[d], preferred_element_type=jnp.float32
                )
                in_gate = gates[d, t, rows, pl.ds(0, cells)]
                forget_gate = gates[d, t, rows, pl.ds(cells, cells)]
                candidate = gates[d, t, rows, pl.ds(2 * cells, cells)]
                out_gate = gates[d, t, rows, pl.ds(3 * cells, cells)]
                start = cell_start[d, t, rows]
                clipped = jnp.tanh((forget_gate * start + in_gate * candidate) * (1.0 / 3.0))
                tanh_cell = jnp.tanh(3.0 * clipped)
                total = grad_cell[d, rows] + grad_full * out_gate * (1.0 - tanh_cell * tanh_cell)
                grad_raw = total * (1.0 - clipped * clipped)
                grad_gates_ref[d, t, rows, pl.ds(0, cells)] = (
                    grad_raw * candidate * in_gate * (1.0 - in_gate)
                ).astype(jnp.bfloat16)
                grad_gates_ref[d, t, rows, pl.ds(cells, cells)] = (
                    grad_raw * start * forget_gate * (1.0 - forget_gate)
                ).astype(jnp.bfloat16)
                grad_gates_ref[d, t, rows, pl.ds(2 * cells, cells)] = (
                    grad_raw * in_gate * (1.0 - candidate * candidate)
                ).astype(jnp.bfloat16)
                grad_gates_ref[d, t, rows, pl.ds(3 * cells, cells)] = (
                    grad_full * tanh_cell * out_gate * (1.0 - out_gate)
                ).astype(jnp.bfloat16)
                grad_cell[d, rows] = grad_raw * forget_gate * keep_ref[d, t, rows]

            wait_bytes(stage.at[d, others], send_sems.at[d])

            @pl.when(s < last)
            def _():
                part = (
                    lax.dot_general(
                        grad_gates_ref[d, t],
                        weight_ref[d, width:],
                        (((1,), (1,)), ((), ())),
                        preferred_element_type=jnp.float32,
                    )
                    * keep_ref[d, t]
                )
                stage[d] = part.astype(jnp.bfloat16).reshape(team, own, width)
                received_back[d, s, place] = stage[d, place]
                for peer in peers:
                    send(
                        stage.at[d, peer],
                        received_back.at[d, s, place],
                        send_sems.at[d],
                        sum_sems.at[1, d, s],
                        peer,
                    )

            grad_lin_sum[t] += lax.dot_general(
                grad_gates_ref[d, t],
                weight_ref[d, :width],
                (((1,), (1,)), ((), ())),
                preferred_element_type=jnp.float32,
            )

    for t in range(steps):
        stage_lin[:, t] = grad_lin_sum[t].astype(jnp.bfloat16).reshape(team, own, width)
    received_lin[place] = stage_lin[place]
    for peer in peers:
        send(stage_lin.at[peer], received_lin.at[place], lin_sems.at[4], lin_sems.at[5], peer)

    count = steps * group
    half_blocks = len(blocks) // 2

    def weight_grads(d):
        for half in range(2):

            @pl.loop(0, 4)
            def _(q):
                cols = pl.ds(pl.multiple_of(q * cells, cells), cells)
                slot = lax.rem(q, 2)
                rows_in = (lin_all_ref[...] if half == 0 else state_ref[d]).reshape(count, width)
                gate_part = grad_gates_ref[d, :, :, cols].reshape(count, cells)
                part = lax.dot_general(
                    rows_in,
                    gate_part,
                    (((0,), (0,)), ((), ())),
                    preferred_element_type=jnp.float32,
                )

                @pl.when(q >= 2)
                def _():
                    wait_bytes(grad_stage.at[slot], out_sems.at[slot])

                grad_stage[slot] = part.astype(jnp.bfloat16)
                for source, t, at in blocks[half * half_blocks : (half + 1) * half_blocks]:
                    pltpu.make_async_copy(
                        grad_stage.at[slot, pl.ds((at - half * half_blocks) * run, run)],
                        grad_weight_hbm.at[source, t, d, :, cols],
                        out_sems.at[slot],
                    ).start()

            for slot in range(2):
                wait_bytes(grad_stage.at[slot], out_sems.at[slot])
        turned = lax.dot_general(
            grad_proj_ref[d].reshape(count, width),
            full_ref[d].reshape(count, cells),
            (((0,), (0,)), ((), ())),
            preferred_element_type=jnp.float32,
        )
        turned_stage[d] = turned.astype(jnp.bfloat16)
        for source, t, at in blocks:
            pltpu.make_async_copy(
                turned_stage.at[d, pl.ds(at * turned_run, turned_run)],
                grad_turned_hbm.at[source, t, d],
                out_sems.at[2 + d],
            ).start()
        ones = jnp.ones((8, count), jnp.bfloat16)
        for q in range(4):
            cols = pl.ds(q * cells, cells)
            grad_bias_ref[d, :, cols] = jnp.dot(
                ones,
                grad_gates_ref[d, :, :, cols].reshape(count, cells),
                preferred_element_type=jnp.float32,
            )

    weight_grads(0)
    wait_bytes(received_lin.at[others], lin_sems.at[5])
    grad_lin_all_ref[place] = jnp.sum(received_lin[...].astype(jnp.float32), axis=0).astype(
        jnp.bfloat16
    )
    for peer in peers:
        send(
            grad_lin_all_ref.at[place],
            grad_lin_all_ref.at[place],
            lin_sems.at[6],
            lin_sems.at[7],
            peer,
        )
    weight_grads(1)
    wait_bytes(grad_lin_all_ref.at[others], lin_sems.at[7])
    wait_bytes(stage_lin.at[others], lin_sems.at[4])
    wait_bytes(grad_lin_all_ref.at[others], lin_sems.at[6])
    for d in range(2):
        wait_bytes(turned_stage.at[d], out_sems.at[2 + d])


def run_lstm(lin, out_grad, weights, turned, bias, keep):
    team, steps, own, width = lin.shape
    group = team * own
    cells = turned.shape[4]
    bf16, f32 = jnp.bfloat16, jnp.float32
    vmem = pl.BlockSpec(memory_space=pltpu.VMEM)
    hbm = pl.BlockSpec(memory_space=pl.ANY)
    return pl.pallas_call(
        partial(lstm_kernel, team),
        in_specs=[vmem, vmem, hbm, hbm, vmem, vmem],
        out_specs=[vmem, hbm, hbm, vmem],
        out_shape=[
            jax.ShapeDtypeStruct(lin.shape, bf16),
            jax.ShapeDtypeStruct(weights.shape[:3] + (weights.shape[4], 4 * cells), bf16),
            jax.ShapeDtypeStruct(turned.shape, bf16),
            jax.ShapeDtypeStruct((2, 8, 4 * cells), f32),
        ],
        scratch_shapes=[
            pltpu.VMEM((2, 2 * width, 4 * cells), bf16),
            pltpu.VMEM((2, width, cells), bf16),
            pltpu.VMEM((2, steps, group, 4 * cells), bf16),
            pltpu.VMEM((steps, group, width), bf16),
            pltpu.VMEM((2, steps, group, width), bf16),
            pltpu.VMEM((2, steps, group, cells), bf16),
            pltpu.VMEM((2, steps, group, width), bf16),
            pltpu.VMEM((2, steps, group, 4 * cells), f32),
            pltpu.VMEM((2, steps, group, cells), f32),
            pltpu.VMEM((2, steps, own, width), f32),
            pltpu.VMEM((2, team, own, width), bf16),
            pltpu.VMEM((2, steps, team, own, width), bf16),
            pltpu.VMEM((2, steps, team, own, width), bf16),
            pltpu.VMEM((2, group, cells), f32),
            pltpu.VMEM((steps, group, width), f32),
            pltpu.VMEM((team, steps, own, width), bf16),
            pltpu.VMEM((team, steps, own, width), bf16),
            pltpu.VMEM((own, width), f32),
            pltpu.VMEM((2, width, cells), bf16),
            pltpu.VMEM((2, width, cells), bf16),
            pltpu.SemaphoreType.DMA((2,)),
            pltpu.SemaphoreType.DMA((8,)),
            pltpu.SemaphoreType.DMA((2,)),
            pltpu.SemaphoreType.DMA((2, 2, steps)),
            pltpu.SemaphoreType.DMA((2, 2)),
            pltpu.SemaphoreType.DMA((2, 2, steps)),
            pltpu.SemaphoreType.DMA((4,)),
        ],
        compiler_params=pltpu.CompilerParams(
            collective_id=1, has_side_effects=True, vmem_limit_bytes=63 * 1024 * 1024
        ),
        name="lstm_team",
    )(lin, out_grad, weights, turned, bias, keep)


def member_at(offset):
    t_size, x_size, c_size = lax.axis_size("t"), lax.axis_size("x"), lax.axis_size("c")
    dt, dx, dc = offset // (x_size * c_size), lax.rem(offset // c_size, x_size), lax.rem(offset, c_size)
    t = lax.rem(lax.axis_index("t") + dt, t_size)
    x = lax.rem(lax.axis_index("x") + dx, x_size)
    c = lax.rem(lax.axis_index("c") + dc, c_size)
    return (t * x_size + x) * c_size + c


def opposite(offset):
    t_size, x_size, c_size = lax.axis_size("t"), lax.axis_size("x"), lax.axis_size("c")
    dt, dx, dc = offset // (x_size * c_size), offset // c_size % x_size, offset % c_size
    return (-dt % t_size * x_size + -dx % x_size) * c_size + -dc % c_size


def send_block(source, target, send_sem, recv_sem, peer):
    pltpu.make_async_remote_copy(
        src_ref=source,
        dst_ref=target,
        send_sem=send_sem,
        recv_sem=recv_sem,
        device_id=team_coords(peer),
        device_id_type=pl.DeviceIdType.MESH,
    ).start()


def greet(offsets, with_grid=False):
    barrier = pltpu.get_barrier_semaphore()
    for offset in offsets:
        pl.semaphore_signal(
            barrier,
            inc=1,
            device_id=team_coords(member_at(offset)),
            device_id_type=pl.DeviceIdType.MESH,
        )
    extra = greet_grid(barrier) if with_grid else 0
    pl.semaphore_wait(barrier, len(offsets) + extra)


def load_highway(first_hbm, weights, project, sems):
    grid = first_hbm.shape[0]
    team = team_size()
    run = project.shape[0] // grid

    @pl.loop(0, team)
    def _(member):
        for block in range(grid):
            for level in range(2):
                pltpu.make_async_copy(
                    first_hbm.at[
                        block, pl.ds(pl.multiple_of((member * 2 + level) * run, run), run)
                    ],
                    weights.at[
                        level, pl.ds(pl.multiple_of((member * grid + block) * run, run), run)
                    ],
                    sems.at[0],
                ).start()

    for block in range(grid):
        pltpu.make_async_copy(
            first_hbm.at[block, pl.ds(team * 2 * run, run)],
            project.at[pl.ds(block * run, run)],
            sems.at[1],
        ).start()


def grid_coords(dg, dy):
    g_size, y_size = lax.axis_size("g"), lax.axis_size("y")
    return {
        "g": lax.rem(lax.axis_index("g") + dg, g_size),
        "y": lax.rem(lax.axis_index("y") + dy, y_size),
    }


def grid_block(dg, dy):
    coords = grid_coords(dg, dy)
    return coords["g"] * lax.axis_size("y") + coords["y"]


def send_grid(source, target, send_sem, recv_sem, dg, dy):
    pltpu.make_async_remote_copy(
        src_ref=source,
        dst_ref=target,
        send_sem=send_sem,
        recv_sem=recv_sem,
        device_id=grid_coords(dg, dy),
        device_id_type=pl.DeviceIdType.MESH,
    ).start()


def greet_grid(barrier):
    for dg in range(1, lax.axis_size("g")):
        pl.semaphore_signal(
            barrier, inc=1, device_id=grid_coords(dg, 0), device_id_type=pl.DeviceIdType.MESH
        )
    pl.semaphore_signal(
        barrier, inc=1, device_id=grid_coords(0, 1), device_id_type=pl.DeviceIdType.MESH
    )
    return lax.axis_size("g")


class Gather:
    def __init__(self, blocks, targets, send_sem, recv_sems):
        self.blocks = blocks
        self.targets = targets
        self.send_sem = send_sem
        self.recv_sems = recv_sems

    def start(self, pieces):
        home = grid_block(0, 0)
        g_size = lax.axis_size("g")
        for piece in pieces:
            source = self.blocks[piece]
            target = self.targets[piece](home)
            for dg in range(1, g_size):
                send_grid(
                    source, target, self.send_sem, self.recv_sems.at[piece, g_size - dg, 0], dg, 0
                )
            send_grid(source, target, self.send_sem, self.recv_sems.at[piece, 0, 1], 0, 1)

    def forward(self, pieces):
        for piece in pieces:
            for dg in range(1, lax.axis_size("g")):
                target = self.targets[piece](grid_block(dg, 0))
                wait_bytes(target, self.recv_sems.at[piece, dg, 0])
                send_grid(target, target, self.send_sem, self.recv_sems.at[piece, dg, 1], 0, 1)

    def finish(self, pieces):
        for piece in pieces:
            for dg in range(lax.axis_size("g")):
                wait_bytes(self.targets[piece](grid_block(dg, 1)), self.recv_sems.at[piece, dg, 1])

    def sent(self, pieces):
        for piece in pieces:
            for _ in range(2 * lax.axis_size("g") - 1):
                wait_bytes(self.blocks[piece], self.send_sem)


def row_pieces(total, parts):
    step = -(-total // (parts * 16)) * 16
    return [(start, min(step, total - start)) for start in range(0, total, step)]


def highway_kernel(
    tight_from,
    tiled_ref,
    filter_ref,
    count_ref,
    block_hbm,
    lstm_block_hbm,
    turned_block_hbm,
    bias_ref,
    lin_bias_ref,
    lse_ref,
    first_hbm,
    lstm_hbm,
    turned_hbm,
    first_ref,
    second_ref,
    mixed_ref,
    hidden_ref,
    top_ref,
    lin_ref,
    parts,
    parts_recv,
    features_own,
    wide,
    tight,
    weights,
    project,
    load_sems,
    send_sems,
    first_sems,
    second_sems,
    gather_send_sems,
    block_sems,
    turned_sems,
    lstm_sems,
    lin_sems,
):
    team, tokens, features = first_ref.shape
    part = features // team
    cores = lax.axis_size("c")
    g_size, y_size = lax.axis_size("g"), lax.axis_size("y")
    place = team_place()
    sibling = member_at(1)
    near = list(range(cores, team, cores))
    chunks = lstm_block_hbm.shape[0]
    greet([1] + near, True)
    home = grid_block(0, 0)
    places = [pl.ds(start, size) for start, size in row_pieces(block_hbm.shape[0], 8)]
    block_gather = Gather(
        [block_hbm.at[rows] for rows in places],
        [lambda at, rows=rows: first_hbm.at[at, rows] for rows in places],
        gather_send_sems.at[0],
        block_sems,
    )
    turned_gather = Gather(
        [turned_block_hbm],
        [lambda at: turned_hbm.at[at]],
        gather_send_sems.at[1],
        turned_sems,
    )
    all_places = list(range(len(places)))
    block_gather.start(all_places)
    pltpu.make_async_copy(block_hbm, first_hbm.at[home], load_sems.at[2]).start()
    pltpu.make_async_copy(turned_block_hbm, turned_hbm.at[home], load_sems.at[3]).start()
    pltpu.make_async_copy(lstm_block_hbm, lstm_hbm.at[home], load_sems.at[4]).start()

    def columns(member):
        return pl.ds(pl.multiple_of(member * part, part), part)

    token_block = wide.shape[0] // tiled_ref.shape[1]

    @pl.loop(0, tokens // token_block)
    def _(step):
        rows = pl.ds(pl.multiple_of(step * token_block, token_block), token_block)
        pool_kernel(
            tight_from,
            tiled_ref.at[rows],
            filter_ref,
            count_ref,
            features_own.at[rows],
            lse_ref.at[rows],
            wide,
            tight,
        )

    g, t, y, x, c = axis_sizes()
    run = part // (g * y)
    natural = features_own[...]
    starts = [
        ((((gi * t + ti) * y + yi) * x + xi) * c + ci) * run
        for ti in range(t)
        for xi in range(x)
        for ci in range(c)
        for gi in range(g)
        for yi in range(y)
    ]
    features_own[...] = jnp.concatenate([natural[:, at : at + run] for at in starts], axis=1)

    for offset in near + [1]:
        send_block(
            features_own,
            first_ref.at[place],
            send_sems.at[0],
            first_sems.at[opposite(offset)],
            member_at(offset),
        )
    first_ref[place] = features_own[...]
    block_gather.forward(all_places)

    def lstm_start(chunk):
        for dg in range(1, g_size):
            send_grid(
                lstm_block_hbm.at[chunk],
                lstm_hbm.at[home, chunk],
                gather_send_sems.at[2],
                lstm_sems.at[chunk, g_size - dg, 0],
                dg,
                0,
            )

    def lstm_forward(chunk):
        for dg in range(1, g_size):
            target = lstm_hbm.at[grid_block(dg, 0), chunk]
            wait_bytes(target, lstm_sems.at[chunk, dg, 0])
            send_grid(
                target, target, gather_send_sems.at[3], lstm_sems.at[chunk, dg, 1], 0, 1
            )

    def pump(chunk):
        @pl.when(chunk < chunks)
        def _():
            lstm_forward(jnp.minimum(chunk, chunks - 1))

            @pl.when(chunk + AHEAD < chunks)
            def _():
                lstm_start(jnp.minimum(chunk + AHEAD, chunks - 1))

    turned_gather.start([0])
    for chunk in range(AHEAD):
        lstm_start(chunk)
    for offset in near:
        member = member_at(offset)
        wait_bytes(first_ref.at[member], first_sems.at[offset])
        send_block(
            first_ref.at[member],
            first_ref.at[member],
            send_sems.at[0],
            first_sems.at[offset + 1],
            sibling,
        )
    block_gather.finish(all_places)
    wait_bytes(block_hbm, load_sems.at[2])
    load_highway(first_hbm, weights, project, load_sems)

    @pl.loop(0, chunks)
    def _(chunk):
        send_grid(
            lstm_block_hbm.at[chunk],
            lstm_hbm.at[home, chunk],
            gather_send_sems.at[4],
            lstm_sems.at[chunk, 0, 1],
            0,
            1,
        )

    wait_bytes(weights, load_sems.at[0])
    wait_bytes(project, load_sems.at[1])

    def mix(level, member, operand):
        mixed = (
            jnp.dot(operand, weights[level], preferred_element_type=jnp.float32)
            + bias_ref[level : level + 1]
        )
        mixed_ref[level, member] = mixed
        gate = sigmoid(mixed[:, part:])
        pre_act = mixed[:, :part]
        return (gate, pre_act * sigmoid(pre_act))

    @pl.loop(0, team)
    def _(offset):
        member = member_at(offset)

        @pl.when(lax.rem(offset, cores) == 1)
        def _():
            wait_bytes(first_ref.at[member], first_sems.at[offset])

        gate, act = mix(0, member, first_ref[member])
        carried = first_ref[member, :, columns(place)].astype(jnp.float32)
        hidden = gate * carried + (1.0 - gate) * act
        hidden_ref[member] = hidden
        mine = second_ref.at[member, :, columns(place)]
        mine[...] = hidden.astype(jnp.bfloat16)
        for to in near + [1]:
            send_block(
                mine,
                mine,
                send_sems.at[1],
                second_sems.at[member, opposite(to)],
                member_at(to),
            )

        pump(offset)

    @pl.loop(0, team + 1)
    def _(step):
        @pl.when(step < team)
        def _():
            member = member_at(jnp.minimum(step, team - 1))
            for origin in near:
                piece = second_ref.at[member, :, columns(member_at(origin))]
                wait_bytes(piece, second_sems.at[member, origin])
                send_block(
                    piece,
                    piece,
                    send_sems.at[1],
                    second_sems.at[member, origin + 1],
                    sibling,
                )

        @pl.when(step > 0)
        def _():
            member = member_at(jnp.maximum(step - 1, 0))
            for origin in [0] + near:
                piece = second_ref.at[member, :, columns(member_at(origin + 1))]
                wait_bytes(piece, second_sems.at[member, origin + 1])
            gate, act = mix(1, member, second_ref[member])
            top = (gate * hidden_ref[member] + (1.0 - gate) * act).astype(jnp.bfloat16)
            top_ref[member] = top
            parts[member] = jnp.dot(
                top, project[...], preferred_element_type=jnp.float32
            ).astype(jnp.bfloat16)

            @pl.when(step > 1)
            def _():
                send_block(
                    parts.at[member],
                    parts_recv.at[place],
                    lin_sems.at[0],
                    lin_sems.at[1],
                    member,
                )

        pump(team + step)

    parts_recv[place] = parts[place]
    others = pl.ds(0, team - 1)
    wait_bytes(parts_recv.at[others], lin_sems.at[1])
    lin = jnp.sum(parts_recv[...].astype(jnp.float32), axis=0) + lin_bias_ref[...]
    lin_ref[place] = lin.astype(jnp.bfloat16)
    for offset in range(1, team):
        send_block(
            lin_ref.at[place],
            lin_ref.at[place],
            lin_sems.at[2],
            lin_sems.at[3],
            member_at(offset),
        )

    @pl.loop(2 * team + 1, max(chunks, 2 * team + 1))
    def _(chunk):
        pump(chunk)

    wait_bytes(lin_ref.at[others], lin_sems.at[3])
    wait_bytes(lin_ref.at[others], lin_sems.at[2])
    wait_bytes(parts.at[others], lin_sems.at[0])

    turned_gather.forward([0])
    turned_gather.finish([0])

    @pl.loop(0, chunks)
    def _(chunk):
        for dg in range(g_size):
            wait_bytes(lstm_hbm.at[grid_block(dg, 1), chunk], lstm_sems.at[chunk, dg, 1])

    wait_bytes(first_ref.at[pl.ds(0, team - 1)], send_sems.at[0])
    wait_bytes(second_ref.at[pl.ds(0, team - 1)], send_sems.at[1])
    block_gather.sent(all_places)
    turned_gather.sent([0])
    for _ in range(g_size - 1):
        wait_bytes(lstm_block_hbm, gather_send_sems.at[2])
        wait_bytes(lstm_block_hbm, gather_send_sems.at[3])
    wait_bytes(lstm_block_hbm, gather_send_sems.at[4])
    wait_bytes(turned_block_hbm, load_sems.at[3])
    wait_bytes(lstm_block_hbm, load_sems.at[4])


def run_highway(
    tight_from, tiled, filters, counts, block, lstm_block, turned_block, bias, lin_bias
):
    team = team_size()
    tokens, features = tiled.shape[0], filters.shape[1]
    part = features // team
    g_size, y_size = lax.axis_size("g"), lax.axis_size("y")
    grid = g_size * y_size
    width = block.shape[1]
    bf16, f32 = jnp.bfloat16, jnp.float32
    vmem = pl.BlockSpec(memory_space=pltpu.VMEM)
    hbm = pl.BlockSpec(memory_space=pl.ANY)
    pieces = len(row_pieces(block.shape[0], 8))
    token_block = math.gcd(tokens, TOKEN_BLOCK)
    return pl.pallas_call(
        partial(highway_kernel, tight_from),
        in_specs=[vmem] * 3 + [hbm] * 3 + [vmem] * 2,
        out_specs=[vmem] + [hbm] * 3 + [vmem] * 6,
        out_shape=[
            jax.ShapeDtypeStruct((tokens, features), f32),
            jax.ShapeDtypeStruct((grid,) + block.shape, bf16),
            jax.ShapeDtypeStruct((grid,) + lstm_block.shape, bf16),
            jax.ShapeDtypeStruct((grid,) + turned_block.shape, bf16),
            jax.ShapeDtypeStruct((team, tokens, features), bf16),
            jax.ShapeDtypeStruct((team, tokens, features), bf16),
            jax.ShapeDtypeStruct((2, team, tokens, 2 * part), f32),
            jax.ShapeDtypeStruct((team, tokens, part), f32),
            jax.ShapeDtypeStruct((team, tokens, part), bf16),
            jax.ShapeDtypeStruct((team, tokens, width), bf16),
        ],
        scratch_shapes=[
            pltpu.VMEM((team, tokens, width), bf16),
            pltpu.VMEM((team, tokens, width), bf16),
            pltpu.VMEM((tokens, features), bf16),
            pltpu.VMEM((token_block * PLACES, LANES), bf16),
            pltpu.VMEM((token_block * TIGHT, LANES), bf16),
            pltpu.VMEM((2, features, 2 * part), bf16),
            pltpu.VMEM((part, width), bf16),
            pltpu.SemaphoreType.DMA((5,)),
            pltpu.SemaphoreType.DMA((2,)),
            pltpu.SemaphoreType.DMA((team,)),
            pltpu.SemaphoreType.DMA((team, team)),
            pltpu.SemaphoreType.DMA((5,)),
            pltpu.SemaphoreType.DMA((pieces, g_size, y_size)),
            pltpu.SemaphoreType.DMA((1, g_size, y_size)),
            pltpu.SemaphoreType.DMA((lstm_block.shape[0], g_size, y_size)),
            pltpu.SemaphoreType.DMA((4,)),
        ],
        compiler_params=pltpu.CompilerParams(
            collective_id=2, has_side_effects=True, vmem_limit_bytes=60 * 1024 * 1024
        ),
        name="highway_team",
    )(tiled, filters, counts, block, lstm_block, turned_block, bias, lin_bias)


def highway_back_kernel(
    grad_lin_ref,
    first_hbm,
    first_ref,
    second_ref,
    mixed_ref,
    hidden_ref,
    top_ref,
    features_ref,
    grads_hbm,
    bias_ref,
    weights,
    project,
    grad_mixed,
    direct,
    column_parts,
    column_sibling,
    column_send,
    column_recv,
    column_sum_own,
    row_part,
    row_keep,
    row_give,
    row_sibling,
    row_send,
    row_recv,
    row_sum_own,
    grad_stage,
    load_sems,
    send_sems,
    column_sib_sems,
    column_sems,
    row_sib_sems,
    row_sems,
    out_sems,
):
    team, tokens, features = first_ref.shape
    part = features // team
    grid = first_hbm.shape[0]
    run = part // grid
    cores = lax.axis_size("c")
    chips = team // cores
    place = team_place()
    sibling = member_at(1)
    near = list(range(1, chips))
    load_highway(first_hbm, weights, project, load_sems)
    greet([1] + [chip * cores for chip in near])
    f32, bf16 = jnp.float32, jnp.bfloat16

    def columns(member):
        return pl.ds(pl.multiple_of(member * part, part), part)

    def opposite_chip(chip):
        return opposite(chip * cores) // cores

    wait_bytes(weights, load_sems.at[0])
    wait_bytes(project, load_sems.at[1])

    def mix_grads(level, member, grad, carried):
        pre_act = mixed_ref[level, member, :, pl.ds(0, part)]
        gate = sigmoid(mixed_ref[level, member, :, pl.ds(part, part)])
        act_sig = sigmoid(pre_act)
        grad_mixed[level, member, :, pl.ds(0, part)] = (
            grad * (1.0 - gate) * act_sig * (1.0 + pre_act * (1.0 - act_sig))
        ).astype(bf16)
        grad_mixed[level, member, :, pl.ds(part, part)] = (
            grad * (carried - pre_act * act_sig) * gate * (1.0 - gate)
        ).astype(bf16)
        return grad * gate

    def spread(level, member):
        return lax.dot_general(
            grad_mixed[level, member],
            weights[level],
            (((1,), (1,)), ((), ())),
            preferred_element_type=f32,
        )

    @pl.loop(0, team)
    def _(member):
        grad = lax.dot_general(
            grad_lin_ref[member], project[...], (((1,), (1,)), ((), ())), preferred_element_type=f32
        )
        direct[member] = mix_grads(1, member, grad, hidden_ref[member])
        column_parts[member] = spread(1, member).astype(bf16)
        for chip in range(chips):
            send_block(
                column_parts.at[member, :, columns(member_at(chip * cores + 1))],
                column_sibling.at[member, chip],
                send_sems.at[0],
                column_sib_sems.at[member],
                sibling,
            )

    @pl.loop(0, team)
    def _(member):
        wait_bytes(column_sibling.at[member], column_sib_sems.at[member])
        for chip in near + [0]:
            target = member_at(chip * cores)
            both = column_parts[member, :, columns(target)].astype(f32) + column_sibling[
                member, chip
            ].astype(f32)
            if chip == 0:
                column_sum_own[member] = both
            else:
                column_send[chip - 1, member] = both.astype(bf16)
                send_block(
                    column_send.at[chip - 1, member],
                    column_recv.at[opposite_chip(chip) - 1, member],
                    send_sems.at[1],
                    column_sems.at[member, opposite_chip(chip) - 1],
                    target,
                )

    def weight_grads(level, source_ref):
        @pl.loop(0, team)
        def _(member):
            slot = lax.rem(member, 2)

            @pl.when(member >= 2)
            def _():
                wait_bytes(grad_stage.at[slot], out_sems.at[slot])

            grad_stage[slot] = lax.dot_general(
                source_ref[:, :, columns(member)].reshape(team * tokens, part),
                grad_mixed[level].reshape(team * tokens, 2 * part),
                (((0,), (0,)), ((), ())),
                preferred_element_type=f32,
            ).astype(bf16)
            for block in range(grid):
                pltpu.make_async_copy(
                    grad_stage.at[slot, pl.ds(block * run, run)],
                    grads_hbm.at[
                        block, pl.ds(pl.multiple_of((member * 2 + level) * run, run), run)
                    ],
                    out_sems.at[slot],
                ).start()

        for slot in range(2):
            wait_bytes(grad_stage.at[slot], out_sems.at[slot])
        bias_ref[level] = jnp.dot(
            jnp.ones((8, team * tokens), bf16),
            grad_mixed[level].reshape(team * tokens, 2 * part),
            preferred_element_type=f32,
        )

    weight_grads(1, second_ref)

    @pl.loop(0, team)
    def _(step):
        offset = team - 1 - step
        member = member_at(offset)
        chip = offset // cores
        grad = column_sum_own[member] + direct[member]
        for other in near:
            wait_bytes(column_recv.at[other - 1, member], column_sems.at[member, other - 1])
            grad = grad + column_recv[other - 1, member].astype(f32)
        carried = first_ref[member, :, columns(place)].astype(f32)
        straight = mix_grads(0, member, grad, carried)
        row_part[...] = spread(0, member)
        row_part[:, columns(place)] += straight

        @pl.when(lax.rem(offset, cores) == 1)
        def _():
            row_give[chip] = row_part[...].astype(bf16)
            send_block(
                row_give.at[chip],
                row_sibling.at[chip],
                send_sems.at[2],
                row_sib_sems.at[chip],
                sibling,
            )

        @pl.when(lax.rem(offset, cores) == 0)
        def _():
            row_keep[chip] = row_part[...].astype(bf16)

    for chip in near[::-1] + [0]:
        wait_bytes(row_sibling.at[chip], row_sib_sems.at[chip])
        both = row_keep[chip].astype(f32) + row_sibling[chip].astype(f32)
        if chip == 0:
            row_sum_own[...] = both
        else:
            row_send[chip - 1] = both.astype(bf16)
            send_block(
                row_send.at[chip - 1],
                row_recv.at[opposite_chip(chip) - 1],
                send_sems.at[3],
                row_sems.at[opposite_chip(chip) - 1],
                member_at(chip * cores),
            )

    weight_grads(0, first_ref)
    grad_stage[0] = lax.dot_general(
        top_ref[...].reshape(team * tokens, part),
        grad_lin_ref[...].reshape(team * tokens, 2 * part),
        (((0,), (0,)), ((), ())),
        preferred_element_type=f32,
    ).astype(bf16)
    for block in range(grid):
        pltpu.make_async_copy(
            grad_stage.at[0, pl.ds(block * run, run)],
            grads_hbm.at[block, pl.ds(team * 2 * run, run)],
            out_sems.at[0],
        ).start()
    total = row_sum_own[...]
    for other in near:
        wait_bytes(row_recv.at[other - 1], row_sems.at[other - 1])
        total = total + row_recv[other - 1].astype(f32)
    features_ref[...] = total.astype(bf16)
    wait_bytes(grad_stage.at[0], out_sems.at[0])
    wait_bytes(column_sibling, send_sems.at[0])
    wait_bytes(column_send, send_sems.at[1])
    wait_bytes(row_give, send_sems.at[2])
    wait_bytes(row_send, send_sems.at[3])


def run_highway_back(grad_lin, first_all, first, second, mixed, hidden, top):
    team, tokens, features = first.shape
    part = features // team
    chips = team // lax.axis_size("c")
    width = first_all.shape[2]
    bf16, f32 = jnp.bfloat16, jnp.float32
    vmem = pl.BlockSpec(memory_space=pltpu.VMEM)
    hbm = pl.BlockSpec(memory_space=pl.ANY)
    return pl.pallas_call(
        highway_back_kernel,
        in_specs=[vmem, hbm] + [vmem] * 5,
        out_specs=[vmem, hbm, vmem],
        out_shape=[
            jax.ShapeDtypeStruct((tokens, features), bf16),
            jax.ShapeDtypeStruct(first_all.shape, bf16),
            jax.ShapeDtypeStruct((2, 8, 2 * part), f32),
        ],
        scratch_shapes=[
            pltpu.VMEM((2, features, 2 * part), bf16),
            pltpu.VMEM((part, width), bf16),
            pltpu.VMEM((2, team, tokens, 2 * part), bf16),
            pltpu.VMEM((team, tokens, part), f32),
            pltpu.VMEM((team, tokens, features), bf16),
            pltpu.VMEM((team, chips, tokens, part), bf16),
            pltpu.VMEM((chips - 1, team, tokens, part), bf16),
            pltpu.VMEM((chips - 1, team, tokens, part), bf16),
            pltpu.VMEM((team, tokens, part), f32),
            pltpu.VMEM((tokens, features), f32),
            pltpu.VMEM((chips, tokens, features), bf16),
            pltpu.VMEM((chips, tokens, features), bf16),
            pltpu.VMEM((chips, tokens, features), bf16),
            pltpu.VMEM((chips - 1, tokens, features), bf16),
            pltpu.VMEM((chips - 1, tokens, features), bf16),
            pltpu.VMEM((tokens, features), f32),
            pltpu.VMEM((2, part, width), bf16),
            pltpu.SemaphoreType.DMA((2,)),
            pltpu.SemaphoreType.DMA((4,)),
            pltpu.SemaphoreType.DMA((team,)),
            pltpu.SemaphoreType.DMA((team, chips - 1)),
            pltpu.SemaphoreType.DMA((chips,)),
            pltpu.SemaphoreType.DMA((chips - 1,)),
            pltpu.SemaphoreType.DMA((2,)),
        ],
        compiler_params=pltpu.CompilerParams(
            collective_id=3, has_side_effects=True, vmem_limit_bytes=60 * 1024 * 1024
        ),
        name="highway_team_back",
    )(grad_lin, first_all, first, second, mixed, hidden, top)


def every_coords(shift):
    g, t, y, x, c = axis_sizes()
    sizes = (g, t, y, x, c)
    coords, rest = {}, shift
    for name, size in list(zip(EVERY, sizes))[::-1]:
        coords[name] = lax.rem(lax.axis_index(name) + lax.rem(rest, size), size)
        rest = rest // size
    return coords


def every_place(coords):
    place = 0
    for name in EVERY:
        place = place * lax.axis_size(name) + coords[name]
    return place


def final_kernel(
    tight_from,
    bank_counts,
    grads_ref,
    tiled_ref,
    ids_ref,
    filter_ref,
    count_ref,
    lse_ref,
    upstream_ref,
    bias_ref,
    highway_ref,
    project_ref,
    sums_ref,
    conv_ref,
    table_ref,
    natural,
    grad_filters,
    table_sum,
    wide,
    tight,
    spread,
    y_recv,
    g_send,
    g_recv,
    kept,
    team_send,
    team_recv,
    bias_recv,
    small,
    small_team,
    small_send,
    small_grid,
    y_sems,
    g_sems,
    team_sems,
    small_sems,
    send_sems,
):
    grid, rows, lanes = grads_ref.shape
    team = team_size()
    g, t, y, x, c = axis_sizes()
    devices = bias_ref.shape[0]
    step = team_recv.shape[1]
    cut = step * team
    table_rows = table_ref.shape[0] // team
    f32, bf16 = jnp.float32, jnp.bfloat16
    here = every_place({name: lax.axis_index(name) for name in EVERY})
    place = team_place()
    bank = lax.rem(place, x * c)
    conv_ref[...] = jnp.zeros_like(conv_ref)
    barrier = pltpu.get_barrier_semaphore()

    @pl.loop(1, devices)
    def _(shift):
        pl.semaphore_signal(
            barrier, inc=1, device_id=every_coords(shift), device_id_type=pl.DeviceIdType.MESH
        )

    pl.semaphore_wait(barrier, devices - 1)
    pieces = [pl.ds(k * step, step) for k in range(team)] + [pl.ds(cut, rows - cut)]
    g_index, y_index = lax.axis_index("g"), lax.axis_index("y")
    other_y = lax.rem(y_index + 1, y)
    for k, piece in enumerate(pieces):
        for dg in list(range(1, g)) + [0]:
            send_grid(
                grads_ref.at[lax.rem(g_index + dg, g) * y + other_y, piece],
                y_recv.at[dg, piece],
                send_sems.at[0],
                y_sems.at[k, dg],
                0,
                1,
            )

    @pl.loop(1, devices)
    def _(shift):
        coords = every_coords(shift)
        pltpu.make_async_remote_copy(
            src_ref=bias_ref.at[every_place(coords)],
            dst_ref=bias_recv.at[here],
            send_sem=send_sems.at[3],
            recv_sem=small_sems.at[0],
            device_id=coords,
            device_id_type=pl.DeviceIdType.MESH,
        ).start()

    bias_recv[here] = bias_ref[here]
    run = upstream_ref.shape[1] // devices
    order = [
        (((ti * x + xi) * c + ci) * g + gi) * y + yi
        for gi in range(g)
        for ti in range(t)
        for yi in range(y)
        for xi in range(x)
        for ci in range(c)
    ]
    permuted = upstream_ref[...]
    natural[...] = jnp.concatenate([permuted[:, at * run : (at + 1) * run] for at in order], axis=1)
    grad_filters[...] = jnp.zeros_like(grad_filters)
    table_sum[...] = jnp.zeros_like(table_sum)

    def pass_on(k):
        piece = pieces[k]
        for dg in list(range(1, g)) + [0]:
            wait_bytes(y_recv.at[dg, piece], y_sems.at[k, dg])
            both = grads_ref[lax.rem(g_index + dg, g) * y + y_index, piece].astype(f32)
            both = both + y_recv[dg, piece].astype(f32)
            if dg == 0:
                kept[piece] = both
            else:
                g_send[dg - 1, piece] = both.astype(bf16)
                send_grid(
                    g_send.at[dg - 1, piece],
                    g_recv.at[g - dg - 1, piece],
                    send_sems.at[1],
                    g_sems.at[k, g - dg - 1],
                    dg,
                    0,
                )

    token_block = spread.shape[0]
    blocks = tiled_ref.shape[0] // token_block
    early = min(4, team)

    def pool_block(at):
        picked = pl.ds(pl.multiple_of(at * token_block, token_block), token_block)
        pool_grad_block(
            tight_from,
            tiled_ref.at[picked],
            ids_ref[pl.ds(at, 1)],
            filter_ref,
            count_ref,
            lse_ref.at[picked],
            natural.at[picked],
            grad_filters,
            table_sum,
            wide,
            tight,
            spread,
        )

    for k in range(early):

        @pl.loop(blocks * k // early, blocks * (k + 1) // early)
        def _(at):
            pool_block(at)

        pass_on(k)

    lane = lax.broadcasted_iota(jnp.int32, (LANES, LANES), 0)
    fold = jnp.where(
        (lane < TAPS)
        & (lax.rem(lane, EMBED) == lax.broadcasted_iota(jnp.int32, (LANES, LANES), 1)),
        1.0,
        0.0,
    ).astype(bf16)
    by_tap = table_sum[...]
    high = by_tap.astype(bf16)
    low = (by_tap - high.astype(f32)).astype(bf16)
    table = jnp.dot(high, fold, preferred_element_type=f32)
    table = (table + jnp.dot(low, fold, preferred_element_type=f32)).astype(bf16)
    starts, halves, at, column = [], [], 0, 0
    for half in range(t):
        for b, count in enumerate(bank_counts):
            starts.append(at)
            halves.append(count // t)
            at += count // t + table_rows
    for b, count in enumerate(bank_counts):
        for half in range(t):
            member = half * len(bank_counts) + b
            each = count // t
            turned = grad_filters[:, pl.ds(column, each)].T.astype(bf16)
            small[pl.ds(starts[member], each)] = turned
            column += each
    vocab = table_sum.shape[0]
    for member in range(team):
        top = min(table_rows, vocab - member * table_rows)
        begin = starts[member] + halves[member]
        if top > 0:
            small[pl.ds(begin, top)] = table[member * table_rows : member * table_rows + top]
        if top < table_rows:
            low_row = max(top, 0)
            small[pl.ds(begin + low_row, table_rows - low_row)] = jnp.zeros(
                (table_rows - low_row, LANES), bf16
            )
    for member in range(team):
        size = halves[member] + table_rows
        source = small.at[pl.ds(starts[member], size)]

        @pl.when(place == member)
        def _():
            small_team[member, pl.ds(0, size)] = small[pl.ds(starts[member], size)]

        @pl.when(place != member)
        def _():
            send_block(
                source,
                small_team.at[place, pl.ds(0, size)],
                send_sems.at[4],
                small_sems.at[1],
                member,
            )

    for k in range(early, team - 2):
        pass_on(k)
    home = grid_block(0, 0)
    for b, count in enumerate(bank_counts):
        size = count // t + table_rows

        @pl.when(bank == b)
        def _():
            wait_bytes(small_team.at[pl.ds(0, team - 1), pl.ds(0, size)], small_sems.at[1])
            total = small_team[0, pl.ds(0, size)].astype(f32)
            for origin in range(1, team):
                total = total + small_team[origin, pl.ds(0, size)].astype(f32)
            small_send[pl.ds(0, size)] = total.astype(bf16)
            small_grid[home, pl.ds(0, size)] = total.astype(bf16)
            for dg in range(g):
                for dy in range(y):
                    if dg or dy:
                        send_grid(
                            small_send.at[pl.ds(0, size)],
                            small_grid.at[home, pl.ds(0, size)],
                            send_sems.at[5],
                            small_sems.at[2],
                            dg,
                            dy,
                        )

    for k in range(team - 2, team + 1):
        pass_on(k)
    t_index = lax.axis_index("t")
    for b, count in enumerate(bank_counts):
        each = count // t
        size = each + table_rows

        @pl.when(bank == b)
        def _():
            wait_bytes(small_grid.at[pl.ds(0, grid - 1), pl.ds(0, size)], small_sems.at[2])
            total = small_grid[0, pl.ds(0, size)].astype(f32)
            for origin in range(1, grid):
                total = total + small_grid[origin, pl.ds(0, size)].astype(f32)
            mine = conv_ref.at[pl.ds(pl.multiple_of(t_index * each, each), each)]
            mine[...] = total[:each]
            for dt in range(1, t):
                send_block(
                    mine, mine, send_sems.at[6], small_sems.at[3], member_at(dt * x * c)
                )
            piece = table_ref.at[pl.ds(pl.multiple_of(place * table_rows, 16), table_rows)]
            piece[...] = total[each:]
            for offset in range(1, team):
                send_block(piece, piece, send_sems.at[7], small_sems.at[4], member_at(offset))

    for k, piece in enumerate(pieces):
        total = kept[piece]
        for dg in range(1, g):
            wait_bytes(g_recv.at[dg - 1, piece], g_sems.at[k, dg - 1])
            total = total + g_recv[dg - 1, piece].astype(f32)
        if k == team:
            project_ref[...] = total
        else:
            team_send[piece] = total.astype(bf16)

            @pl.when(place == k)
            def _():
                team_recv[k] = team_send[piece]

            @pl.when(place != k)
            def _():
                send_block(
                    team_send.at[piece], team_recv.at[place], send_sems.at[2], team_sems.at[0], k
                )

    wait_bytes(bias_recv.at[pl.ds(0, devices - 1)], small_sems.at[0])
    sums_ref[...] = jnp.sum(bias_recv[...].astype(f32), axis=0)
    wait_bytes(team_recv.at[pl.ds(0, team - 1)], team_sems.at[0])
    half_lanes = lanes // 2
    for half in range(2):
        parts = [
            team_recv[
                (ti * x + xi) * c + ci,
                :,
                half * half_lanes + (gi * y + yi) * run : half * half_lanes + (gi * y + yi + 1) * run,
            ]
            for gi in range(g)
            for ti in range(t)
            for yi in range(y)
            for xi in range(x)
            for ci in range(c)
        ]
        wide_half = half_lanes * team
        highway_ref[:, pl.ds(half * wide_half, wide_half)] = jnp.concatenate(parts, axis=1).astype(
            f32
        )
    for b, count in enumerate(bank_counts):
        each = count // t
        size = each + table_rows

        @pl.when(bank == b)
        def _():
            for _ in range(t - 1):
                wait_bytes(conv_ref.at[pl.ds(0, each)], small_sems.at[3])
                wait_bytes(conv_ref.at[pl.ds(0, each)], send_sems.at[6])
            wait_bytes(small_grid.at[pl.ds(0, grid - 1), pl.ds(0, size)], send_sems.at[5])

    wait_bytes(table_ref.at[pl.ds(0, (team - 1) * table_rows)], small_sems.at[4])
    wait_bytes(table_ref.at[pl.ds(0, (team - 1) * table_rows)], send_sems.at[7])
    wait_bytes(y_recv, send_sems.at[0])
    wait_bytes(g_recv, send_sems.at[1])
    wait_bytes(team_recv.at[pl.ds(0, team - 1)], send_sems.at[2])
    wait_bytes(bias_recv.at[pl.ds(0, devices - 1)], send_sems.at[3])
    for member in range(team):

        @pl.when(place != member)
        def _():
            size = halves[member] + table_rows
            wait_bytes(small.at[pl.ds(starts[member], size)], send_sems.at[4])


def run_final(tight_from, bank_counts, grads, tiled, ids, filters, counts, lse, upstream, biases, step):
    grid, rows, lanes = grads.shape
    team = team_size()
    g, t, y, x, c = axis_sizes()
    tokens, features = upstream.shape
    devices, bias_rows, _ = biases.shape
    bf16, f32 = jnp.bfloat16, jnp.float32
    vmem = pl.BlockSpec(memory_space=pltpu.VMEM)
    token_block = math.gcd(tokens, TOKEN_BLOCK)
    vocab = -(-VOCAB // 16) * 16
    table_rows = -(-vocab // (16 * team)) * 16
    most = max(bank_counts) // t + table_rows
    return pl.pallas_call(
        partial(final_kernel, tight_from, bank_counts),
        in_specs=[vmem] * 8,
        out_specs=[vmem] * 5,
        out_shape=[
            jax.ShapeDtypeStruct((step, lanes * team), f32),
            jax.ShapeDtypeStruct((rows - team * step, lanes), f32),
            jax.ShapeDtypeStruct((bias_rows, LANES), f32),
            jax.ShapeDtypeStruct((max(bank_counts), LANES), f32),
            jax.ShapeDtypeStruct((team * table_rows, LANES), f32),
        ],
        scratch_shapes=[
            pltpu.VMEM((tokens, features), bf16),
            pltpu.VMEM((LANES, features), f32),
            pltpu.VMEM((vocab, LANES), f32),
            pltpu.VMEM((token_block * PLACES, LANES), bf16),
            pltpu.VMEM((token_block * TIGHT, LANES), bf16),
            pltpu.VMEM((token_block, PLACES, LANES), f32),
            pltpu.VMEM((g, rows, lanes), bf16),
            pltpu.VMEM((g - 1, rows, lanes), bf16),
            pltpu.VMEM((g - 1, rows, lanes), bf16),
            pltpu.VMEM((rows, lanes), f32),
            pltpu.VMEM((rows, lanes), bf16),
            pltpu.VMEM((team, step, lanes), bf16),
            pltpu.VMEM(biases.shape, bf16),
            pltpu.VMEM((sum(bank_counts) + team * table_rows, LANES), bf16),
            pltpu.VMEM((team, most, LANES), bf16),
            pltpu.VMEM((most, LANES), bf16),
            pltpu.VMEM((grid, most, LANES), bf16),
            pltpu.SemaphoreType.DMA((team + 1, g)),
            pltpu.SemaphoreType.DMA((team + 1, g - 1)),
            pltpu.SemaphoreType.DMA((1,)),
            pltpu.SemaphoreType.DMA((5,)),
            pltpu.SemaphoreType.DMA((8,)),
        ],
        compiler_params=pltpu.CompilerParams(
            collective_id=4, has_side_effects=True, vmem_limit_bytes=60 * 1024 * 1024
        ),
        name="final_sums",
    )(grads, tiled, ids, filters, counts, lse, upstream, biases)


def pack_kernel(parts, received_ref, out_ref):
    team, rows, lanes = received_ref.shape
    each = lanes // parts
    for member in range(team):
        for part in range(parts):
            out_ref[:, pl.ds((part * team + member) * each, each)] = received_ref[
                member, :, pl.ds(part * each, each)
            ].astype(jnp.float32)


def pack_columns(received, parts):
    team, rows, lanes = received.shape
    return pl.pallas_call(
        partial(pack_kernel, parts),
        in_specs=[pl.BlockSpec(memory_space=pltpu.VMEM)],
        out_specs=pl.BlockSpec(memory_space=pltpu.VMEM),
        out_shape=jax.ShapeDtypeStruct((rows, team * lanes), jnp.float32),
        compiler_params=pltpu.CompilerParams(vmem_limit_bytes=40 * 1024 * 1024),
        name="pack_columns",
    )(received)


def axis_sizes():
    return tuple(lax.axis_size(name) for name in EVERY)


def run_rows(received):
    g, t, y, x, c = axis_sizes()
    lanes = received.shape[-1]
    split = received.reshape(t, x * c, 2, -1, lanes).transpose(0, 2, 1, 3, 4)
    return split.reshape(t, 2, -1, lanes)


def member_rows(runs):
    g, t, y, x, c = axis_sizes()
    lanes = runs.shape[-1]
    split = runs.reshape(t, 2, x * c, -1, lanes).transpose(0, 2, 1, 3, 4)
    return split.reshape(t * x * c, -1, lanes)


def team_slices(values, parts):
    team = team_size()
    two, rows, columns = values.shape
    lanes = columns // (parts * team)
    split = values.reshape(two, rows, parts, team, lanes).transpose(3, 0, 1, 2, 4)
    return split.reshape(team, two * rows, parts * lanes)


def whole_columns(received, parts):
    team, two_rows, lanes = received.shape
    split = received.reshape(team, 2, two_rows // 2, parts, lanes // parts)
    return split.transpose(1, 2, 3, 0, 4).reshape(2, two_rows // 2, team * lanes)


def team_first(values):
    g, t, y, x, c = axis_sizes()
    rows = values.shape[0]
    split = values.reshape(rows, -1, g, t, y, x, c, values.shape[1] // (2 * g * t * y * x * c))
    return split.transpose(3, 5, 6, 0, 1, 2, 4, 7)


def permuted_columns(values):
    g, t, y, x, c = axis_sizes()
    split = values.reshape(values.shape[0], g, t, y, x, c, -1)
    return split.transpose(0, 2, 4, 5, 1, 3, 6).reshape(values.shape)


def restored_columns(values):
    g, t, y, x, c = axis_sizes()
    split = values.reshape(values.shape[0], t, x, c, g, y, -1)
    return split.transpose(0, 4, 1, 5, 2, 3, 6).reshape(values.shape)


def padded_rows(values, rows):
    blocks = values.shape[0]
    flat = values.reshape(blocks, -1)
    return jnp.pad(flat, ((0, 0), (0, rows * LANES - flat.shape[1]))).reshape(blocks, rows, LANES)


def row_count(items):
    return -(-items // LANES)


def bank_filters(turned, bank, bank_cols):
    taps = [
        [width * EMBED for width, first, count in bank_specs for _ in range(count)]
        for bank_specs in bank_plan(bank_cols)
    ]
    taps = [row + [0] * (bank_cols - len(row)) for row in taps]
    limit = lax.dynamic_index_in_dim(jnp.asarray(taps, jnp.int32), bank, 0, False)
    turned = turned.T
    row = lax.broadcasted_iota(jnp.int32, (TAPS, 1), 0)
    kernel = jnp.where(row < limit[None, :], turned[:TAPS], 0.0)
    bias = jnp.where(limit > 0, turned[TAPS], 0.0)
    return (kernel.reshape(1, WIDEST, EMBED, bank_cols), bias[None])


def shards(
    char_ids,
    resets,
    out_grad,
    char_table,
    conv_weight,
    conv_bias,
    highway_weight,
    highway_bias,
    proj_weight,
    proj_bias,
    lstm_weight,
    lstm_bias,
    lstm_proj,
):
    f32, bf16 = jnp.float32, jnp.bfloat16
    own, steps = resets.shape
    team = team_size()
    place = team_place()
    devices = team * lax.axis_size("g") * lax.axis_size("y")
    bank_cols = conv_weight.shape[3]
    highway_rows = highway_weight.shape[1]
    features_all = highway_rows * devices
    part = features_all // team
    lstm_rows = lstm_weight.shape[1]
    width = proj_weight.shape[1]
    cells_all = lstm_proj.shape[1]
    cells = cells_all // team

    conv_own = jnp.concatenate([conv_weight.reshape(-1, bank_cols), conv_bias], axis=0)
    banks = lax.axis_size("x") * lax.axis_size("c")
    conv_all = lax.all_to_all(
        jnp.broadcast_to(conv_own[None], (banks,) + conv_own.shape),
        ("x", "c"),
        split_axis=0,
        concat_axis=0,
        tiled=True,
    )
    conv_weight_all = conv_all[:, :-1].reshape((banks,) + conv_weight.shape[1:])
    conv_bias_all = conv_all[:, -1]
    sizes = [highway_bias.size, proj_bias.size, lstm_bias.size, resets.size]
    small = jnp.concatenate(
        [
            highway_bias.reshape(-1),
            proj_bias.reshape(-1),
            lstm_bias.reshape(-1),
            resets.astype(bf16).reshape(-1),
        ]
    )
    small_all = lax.all_to_all(
        jnp.broadcast_to(small[None], (devices, small.size)),
        EVERY,
        split_axis=0,
        concat_axis=0,
        tiled=True,
    )
    cut = [sum(sizes[:k]) for k in range(5)]
    highway_bias_all = small_all[:, cut[0] : cut[1]].reshape(devices, 2, -1)
    highway_bias_all = highway_bias_all.transpose(1, 0, 2).reshape(2, 2 * features_all)
    highway_bias_all = team_first(highway_bias_all).reshape(team, 2, 2 * part)
    proj_bias_all = small_all[:, cut[1] : cut[2]].reshape(-1).astype(f32)
    lstm_bias_all = small_all[:, cut[2] : cut[3]].reshape(devices, 2, -1)
    lstm_bias_all = lstm_bias_all.transpose(1, 0, 2).reshape(2, 4, team, cells)
    resets_all = small_all[:, cut[3] : cut[4]].reshape(
        lax.axis_size("g"), lax.axis_size("t"), lax.axis_size("y"), -1, own, steps
    )
    resets_team = lax.dynamic_index_in_dim(resets_all, lax.axis_index("g"), 0, False)
    resets_team = lax.dynamic_index_in_dim(resets_team, lax.axis_index("y"), 1, False)
    resets_team = resets_team.reshape(team * own, steps).astype(f32)
    highway_bias_own = lax.dynamic_index_in_dim(highway_bias_all, place, 0, False).astype(f32)
    lstm_bias_own = lax.dynamic_index_in_dim(lstm_bias_all, place, 2, False)
    lstm_bias_own = lstm_bias_own.reshape(2, 1, 4 * cells).astype(f32)

    highway_slices = team_first(highway_weight.reshape(2 * highway_rows, -1))
    turned_rows = lstm_proj.shape[2]
    gate_slices = lstm_weight.reshape(2, lstm_rows, 4, team, cells).transpose(3, 0, 2, 1, 4)
    swapped = swap_team(
        jnp.concatenate(
            [
                highway_slices.reshape(team, 2 * highway_rows, 2 * part),
                gate_slices.reshape(team, 8 * lstm_rows, cells),
                team_slices(jnp.swapaxes(lstm_proj, 1, 2), 1),
            ],
            axis=1,
        )
    )
    ends = [2 * highway_rows, 2 * highway_rows + 8 * lstm_rows]
    block = jnp.concatenate([swapped[:, : ends[0]].reshape(-1, 2 * part), proj_weight], axis=0)
    t, x, c = lax.axis_size("t"), lax.axis_size("x"), lax.axis_size("c")
    lstm_block = (
        swapped[:, ends[0] : ends[1]]
        .reshape(t, x * c, 8, lstm_rows, cells)
        .transpose(0, 2, 1, 3, 4)
        .reshape(t * 8, x * c * lstm_rows, cells)
    )
    turned_block = run_rows(swapped[:, ends[1] :])
    cut_rows = team * 2 * highway_rows
    grid = lax.axis_size("g") * lax.axis_size("y")
    bank = lax.axis_index("x") * lax.axis_size("c") + lax.axis_index("c")
    own_ids = lax.dynamic_slice_in_dim(char_ids, bank * own, own, axis=0)
    own_ids = jnp.swapaxes(own_ids, 0, 1).reshape(own * steps, char_ids.shape[2])
    filters, counts = filter_matrix(conv_weight_all, conv_bias_all)
    tight_from = wide_columns(bank_cols)
    padded_ids, tiled = embed_tokens(own_ids, char_table)

    tokens = own * steps
    (
        pooled_lse,
        first_all,
        lstm_own,
        turned_own,
        first,
        second,
        mixed,
        hidden,
        top_own,
        lin_all,
    ) = run_highway(
        tight_from,
        tiled,
        filters,
        counts,
        block,
        lstm_block,
        turned_block,
        highway_bias_own,
        proj_bias_all[None],
    )
    lstm_own = lstm_own.reshape(grid, t, 2, 4, x * c * lstm_rows, cells)

    keep_forward = 1.0 - resets_team
    keep_backward = 1.0 - jnp.concatenate(
        [resets_team[:, 1:], jnp.zeros((team * own, 1), f32)], axis=1
    )
    keep = jnp.stack([keep_forward.T, keep_backward.T])[..., None]
    grad_time = out_grad.reshape(own, steps, 2, width).transpose(2, 1, 0, 3)
    grad_lin_all, lstm_grads, turned_grads, bias_sums = run_lstm(
        lin_all.reshape(team, steps, own, width),
        grad_time,
        lstm_own,
        turned_own,
        lstm_bias_own,
        keep,
    )
    lstm_summed = lax.psum_scatter(lstm_grads, GRID, scatter_dimension=0, tiled=False)
    turned_summed = lax.all_to_all(turned_grads, GRID, split_axis=0, concat_axis=0, tiled=True)
    turned_summed = turned_summed.astype(f32).sum(axis=0).astype(bf16)
    grad_input = lax.dynamic_index_in_dim(grad_lin_all, place, 0, False).reshape(tokens, width)
    grad_project_b = column_sum(grad_input)
    grad_features, first_parts, highway_bias_sums = run_highway_back(
        grad_lin_all.reshape(team, tokens, width),
        first_all,
        first,
        second,
        mixed,
        hidden,
        top_own,
    )
    turned_summed, grad_features = lax.optimization_barrier((turned_summed, grad_features))
    turned_grad = whole_columns(swap_team(member_rows(turned_summed)), 1).astype(f32)
    lstm_proj_grad = jnp.swapaxes(turned_grad, 1, 2)
    g, t, y, x, c = axis_sizes()

    def own_place(values, parts):
        lanes = values.shape[-1] // parts
        split = values.reshape(2, parts, 1, lanes)
        full = jnp.zeros((2, parts, team, lanes), f32)
        return lax.dynamic_update_slice(full, split, (0, 0, place, 0)).reshape(2, -1)

    lstm_bias_parts = own_place(bias_sums[:, 0], 4)
    highway_bias_parts = own_place(highway_bias_sums[:, 0], 2)
    highway_bias_parts = (
        highway_bias_parts.reshape(2, 2, t, x, c, g, y, -1)
        .transpose(0, 1, 5, 2, 6, 3, 4, 7)
        .reshape(2, 2 * features_all)
    )
    biases = jnp.concatenate(
        [
            lstm_bias_parts.reshape(2, devices, -1).transpose(1, 0, 2).reshape(devices, -1),
            highway_bias_parts.reshape(2, devices, -1).transpose(1, 0, 2).reshape(devices, -1),
            grad_project_b.reshape(devices, -1),
        ],
        axis=1,
    )
    bank_counts = [sum(item[2] for item in specs) for specs in bank_plan(bank_cols)]
    bias_rows = -(-row_count(biases.shape[1]) // 16) * 16
    highway_weight_grad, project_grad, mine, conv_sums, table_sums = run_final(
        tight_from,
        bank_counts,
        first_parts,
        tiled,
        padded_ids.reshape(-1, math.gcd(tokens, TOKEN_BLOCK) * PLACES),
        filters,
        counts,
        pooled_lse,
        grad_features,
        padded_rows(biases, bias_rows).astype(bf16),
        2 * highway_rows,
    )
    lstm_summed, highway_weight_grad = lax.optimization_barrier((lstm_summed, highway_weight_grad))
    lstm_returned = swap_team(member_rows(lstm_summed))
    lstm_weight_grad = pack_columns(lstm_returned, 4).reshape(2, lstm_rows, -1)
    highway_weight_grad = highway_weight_grad.reshape(2, highway_rows, -1)
    mine_biases = mine.reshape(-1)
    ends = [2 * lstm_bias.shape[1], 2 * lstm_bias.shape[1] + 2 * highway_bias.shape[1]]
    lstm_bias_grad = mine_biases[: ends[0]].reshape(2, -1)
    highway_bias_grad = mine_biases[ends[0] : ends[1]].reshape(2, -1)
    proj_bias_grad = mine_biases[ends[1] : ends[1] + proj_bias.size]
    grad_kernel, grad_bias = bank_filters(conv_sums, bank, bank_cols)
    grad_table = table_sums[: char_table.shape[0], :EMBED]
    return (
        grad_table,
        grad_kernel,
        grad_bias,
        highway_weight_grad,
        highway_bias_grad,
        project_grad,
        proj_bias_grad,
        lstm_weight_grad,
        lstm_bias_grad,
        lstm_proj_grad,
    )


def solution(mesh):
    dp, bank = mesh.shape["dp"], mesh.shape["bank"]
    fine = Mesh(mesh.devices.reshape(dp // 4, 2, 2, bank // 2, 2), EVERY)
    rows, banks = ("g", "t", "y"), ("x", "c")
    whole = rows + banks
    placed = (
        P(rows, None, None),
        P(whole, None),
        P(whole, None, None),
        P(),
        P(banks, None, None, None),
        P(banks, None),
        P(None, whole, None),
        P(None, whole),
        P(whole, None),
        P(whole),
        P(None, whole, None),
        P(None, whole),
        P(None, None, whole),
    )
    return jax.shard_map(
        shards,
        mesh=fine,
        in_specs=placed,
        out_specs=(
            P(),
            P(banks, None, None, None),
            P(banks, None),
            P(None, whole, None),
            P(None, whole),
            P(whole, None),
            P(whole),
            P(None, whole, None),
            P(None, whole),
            P(None, None, whole),
        ),
        check_vma=False,
    )
```

```python
from functools import partial
import math

import jax
import jax.numpy as jnp
from jax import lax
from jax.experimental import pallas as pl
from jax.experimental.pallas import tpu as pltpu
from jax.sharding import Mesh, PartitionSpec as P

CHAR_COUNT = 50
VOCAB = 262
EMBED = 16
WIDEST = 7
TAPS = WIDEST * EMBED
LANES = 128
PLACES = 64
TIGHT = 48
CHUNK = 256
TOKEN_BLOCK = 16
AHEAD = 6


def bank_plan(bank_cols):
    return [
        [
            (1, 0, bank_cols // 32),
            (2, bank_cols // 32, bank_cols // 32),
            (3, bank_cols // 16, bank_cols // 16),
            (4, bank_cols // 8, bank_cols // 8),
        ],
        [(5, 0, bank_cols // 4)],
        [(6, 0, bank_cols // 2)],
        [(7, 0, bank_cols)],
    ]


def transposed(former, latter):
    return lax.dot_general(
        former, latter, (((1,), (1,)), ((), ())), preferred_element_type=jnp.float32
    )


def outer_sum(former, latter):
    return lax.dot_general(
        former, latter, (((0,), (0,)), ((), ())), preferred_element_type=jnp.float32
    )


def column_sum(values):
    ones_row = jnp.ones((1, values.shape[0]), values.dtype)
    return jnp.dot(ones_row, values, preferred_element_type=jnp.float32)[0]


def filter_columns(bank_cols):
    columns = []
    for bank_index, bank_specs in enumerate(bank_plan(bank_cols)):
        for filter_width, first_col, count in bank_specs:
            columns.append((filter_width, bank_index, first_col, count))
    return columns


def shift_rows(values, amount):
    count = values.shape[0]
    return values if amount % count == 0 else pltpu.roll(values, amount % count, 0)


def block_windows(tiled_ref, windows_wide, windows_tight):
    tokens, places, lanes = tiled_ref.shape
    rows = tokens * places
    tiled = tiled_ref[...].astype(jnp.float32).reshape(rows, lanes)
    lane = lax.broadcasted_iota(jnp.int32, (rows, lanes), 1)
    place = lax.broadcasted_iota(jnp.int32, (rows, lanes), 0) % places
    windows = tiled
    for offset in range(1, WIDEST):
        windows = jnp.where(lane // EMBED == offset, shift_rows(tiled, rows - offset), windows)
    late = place >= CHAR_COUNT - WIDEST + 1 + (lane - TAPS - 1)
    extra = jnp.where((lane == TAPS) | ((lane <= TAPS + WIDEST) & late), 1.0, 0.0)
    windows = jnp.where(lane < TAPS, windows, extra)
    windows_wide[...] = windows.astype(jnp.bfloat16)
    windows_tight[...] = (
        windows.reshape(tokens, places, lanes)[:, :TIGHT]
        .reshape(tokens * TIGHT, lanes)
        .astype(jnp.bfloat16)
    )


def column_chunks(total, tight_from):
    return [
        (start, start < tight_from) for start in range(0, total, CHUNK)
    ]


def pool_kernel(tight_from, tiled_ref, weight_ref, count_ref, features_ref, lse_ref, wide, tight):
    tokens, places, lanes = tiled_ref.shape
    block_windows(tiled_ref, wide, tight)
    for start, is_wide in column_chunks(weight_ref.shape[1], tight_from):
        cols = pl.ds(start, CHUNK)
        windows = wide if is_wide else tight
        conv_out = jnp.dot(
            windows[...], weight_ref[:, cols], preferred_element_type=jnp.float32
        ).reshape(tokens, -1, CHUNK)
        highest = jnp.max(conv_out, axis=1)
        total = jnp.sum(jnp.exp(conv_out - highest[:, None, :]), axis=1)
        pooled_lse = highest + jnp.log(total)
        lse_ref[:, cols] = pooled_lse
        pooled_pre = pooled_lse - count_ref[0:1, cols]
        features_ref[:, cols] = (pooled_pre * jax.nn.sigmoid(pooled_pre)).astype(jnp.bfloat16)


def pool_grad_block(
    tight_from,
    tiled_ref,
    ids_row,
    weight_ref,
    count_ref,
    lse_ref,
    upstream_ref,
    grad_weight_ref,
    table_ref,
    wide,
    tight,
    spread,
):
    tokens, places, lanes = tiled_ref.shape
    block_windows(tiled_ref, wide, tight)
    spread[...] = jnp.zeros_like(spread)
    wide_turned = wide[...].T
    tight_turned = tight[...].T
    for start, is_wide in column_chunks(weight_ref.shape[1], tight_from):
        cols = pl.ds(start, CHUNK)
        windows, turned = (wide, wide_turned) if is_wide else (tight, tight_turned)
        weights = weight_ref[:, cols]
        conv_out = jnp.dot(
            windows[...], weights, preferred_element_type=jnp.float32
        ).reshape(tokens, -1, CHUNK)
        pooled_lse = lse_ref[:, cols]
        pooled_pre = pooled_lse - count_ref[0:1, cols]
        squashed = jax.nn.sigmoid(pooled_pre)
        upstream = (
            upstream_ref[:, cols].astype(jnp.float32)
            * squashed
            * (1.0 + pooled_pre * (1.0 - squashed))
        )
        softened = jnp.exp(conv_out - pooled_lse[:, None, :])
        grad_conv = (softened * upstream[:, None, :]).astype(jnp.bfloat16)
        places_here = grad_conv.shape[1]
        grad_conv = grad_conv.reshape(tokens * places_here, CHUNK)
        grad_weight_ref[:, cols] += jnp.dot(turned, grad_conv, preferred_element_type=jnp.float32)
        part = lax.dot_general(
            grad_conv, weights, (((1,), (1,)), ((), ())), preferred_element_type=jnp.float32
        ).reshape(tokens, places_here, lanes)
        spread[:, :places_here, :] += part
    rows = tokens * places
    flat = spread[...].reshape(rows, lanes)
    lane = lax.broadcasted_iota(jnp.int32, (rows, lanes), 1)
    aligned = jnp.where(lane < EMBED, flat, 0.0)
    for offset in range(1, WIDEST):
        aligned = jnp.where(lane // EMBED == offset, shift_rows(flat, offset), aligned)
    high = aligned.astype(jnp.bfloat16)
    low = (aligned - high.astype(jnp.float32)).astype(jnp.bfloat16)
    vocab = table_ref.shape[0]
    selector = jnp.where(
        lax.broadcasted_iota(jnp.int32, (vocab, rows), 0) == ids_row, 1.0, 0.0
    ).astype(jnp.bfloat16)
    table_ref[...] += jnp.dot(selector, high, preferred_element_type=jnp.float32) + jnp.dot(
        selector, low, preferred_element_type=jnp.float32
    )


def filter_matrix(conv_weight, conv_bias):
    bank_cols = conv_bias.shape[1]
    taps, biases, masks, counts = [], [], [], []
    for filter_width, bank_index, first_col, count in filter_columns(bank_cols):
        piece = conv_weight[bank_index, :filter_width, :, first_col : first_col + count]
        piece = piece.reshape(filter_width * EMBED, count)
        taps.append(jnp.pad(piece, ((0, TAPS - filter_width * EMBED), (0, 0))))
        biases.append(conv_bias[bank_index, first_col : first_col + count])
        rows = lax.broadcasted_iota(jnp.int32, (LANES - TAPS - 1, count), 0)
        masks.append(jnp.where(rows == WIDEST - filter_width, -1e30, 0.0).astype(jnp.bfloat16))
        counts.append(jnp.full((8, count), math.log(CHAR_COUNT - filter_width + 1), jnp.float32))
    weights = jnp.concatenate(
        [
            jnp.concatenate(taps, axis=1),
            jnp.concatenate(biases)[None],
            jnp.concatenate(masks, axis=1),
        ],
        axis=0,
    )
    return (weights, jnp.concatenate(counts, axis=1))


def wide_columns(bank_cols):
    total = sum(count for width, bank, first, count in filter_columns(bank_cols) if CHAR_COUNT - width + 1 > TIGHT - 2)
    return -(-total // CHUNK) * CHUNK


def char_selector(token_ids, vocab_size):
    return token_ids.reshape(-1)[:, None] == lax.broadcasted_iota(jnp.int32, (1, vocab_size), 1)


def embed_tokens(token_ids, char_table):
    tokens = token_ids.shape[0]
    padded = jnp.pad(token_ids, ((0, 0), (0, PLACES - token_ids.shape[1])), constant_values=-1)
    table_tiled = jnp.pad(jnp.tile(char_table, (1, WIDEST)), ((0, 0), (0, LANES - TAPS)))
    selector = char_selector(padded, char_table.shape[0]).astype(jnp.bfloat16)
    tiled = jnp.dot(selector, table_tiled, preferred_element_type=jnp.float32)
    tiled = tiled.astype(jnp.bfloat16).reshape(tokens, PLACES, LANES)
    return (padded, tiled)


TEAM = ("t", "x", "c")
GRID = ("g", "y")
EVERY = ("g", "t", "y", "x", "c")


def team_place():
    x_size, c_size = lax.axis_size("x"), lax.axis_size("c")
    return (lax.axis_index("t") * x_size + lax.axis_index("x")) * c_size + lax.axis_index("c")


def team_size():
    return lax.axis_size("t") * lax.axis_size("x") * lax.axis_size("c")


def team_coords(place):
    x_size, c_size = lax.axis_size("x"), lax.axis_size("c")
    return {
        "t": place // (x_size * c_size),
        "x": lax.rem(place // c_size, x_size),
        "c": lax.rem(place, c_size),
    }


def swap_team(values):
    return lax.all_to_all(values, TEAM, split_axis=0, concat_axis=0, tiled=True)


def share_team(values):
    team = team_size()
    return swap_team(jnp.broadcast_to(values[None], (team,) + values.shape))


def sigmoid(values):
    return 0.5 * jnp.tanh(0.5 * values) + 0.5


def wait_bytes(ref, sem):
    pltpu.make_async_copy(ref, ref, sem).wait()


def lstm_kernel(
    team,
    lin_ref,
    out_grad_ref,
    weight_hbm,
    turned_hbm,
    bias_ref,
    keep_ref,
    grad_lin_all_ref,
    grad_weight_hbm,
    grad_turned_hbm,
    grad_bias_ref,
    weight_ref,
    proj_ref,
    grad_gates_ref,
    lin_all_ref,
    state_ref,
    full_ref,
    grad_proj_ref,
    gates,
    cell_start,
    projected,
    stage,
    received,
    received_back,
    grad_cell,
    grad_lin_sum,
    stage_lin,
    received_lin,
    grad_state_own,
    grad_stage,
    turned_stage,
    load_sems,
    lin_sems,
    send_sems,
    sum_sems,
    share_send_sems,
    share_sems,
    out_sems,
):
    _, steps, own, width = lin_ref.shape
    group = team * own
    cells = proj_ref.shape[2]
    row_block = 32
    place = team_place()
    own_rows = pl.ds(pl.multiple_of(place * own, own), own)
    peers = [lax.rem(place + k, team) for k in range(1, team)]
    last = steps - 1
    others = pl.ds(0, team - 1)
    other_rows = pl.ds(0, (team - 1) * own)
    g_size, y_size = lax.axis_size("g"), lax.axis_size("y")
    t_size = lax.axis_size("t")
    blocks = [
        (g * y_size + y, t, (g * t_size + t) * y_size + y)
        for g in range(g_size)
        for t in range(t_size)
        for y in range(y_size)
    ]
    run = weight_hbm.shape[4]
    turned_run = turned_hbm.shape[3]

    for d in range(2):
        for source, t, at in blocks:
            for q in range(4):
                pltpu.make_async_copy(
                    weight_hbm.at[source, t, d, q],
                    weight_ref.at[d, pl.ds(at * run, run), pl.ds(q * cells, cells)],
                    load_sems.at[0],
                ).start()
            pltpu.make_async_copy(
                turned_hbm.at[source, t, d],
                proj_ref.at[d, pl.ds(at * turned_run, turned_run)],
                load_sems.at[1],
            ).start()

    barrier = pltpu.get_barrier_semaphore()
    for peer in peers:
        pl.semaphore_signal(
            barrier, inc=1, device_id=team_coords(peer), device_id_type=pl.DeviceIdType.MESH
        )
    pl.semaphore_wait(barrier, team - 1)

    def send(source, target, send_sem, recv_sem, peer):
        pltpu.make_async_remote_copy(
            src_ref=source,
            dst_ref=target,
            send_sem=send_sem,
            recv_sem=recv_sem,
            device_id=team_coords(peer),
            device_id_type=pl.DeviceIdType.MESH,
        ).start()

    for t in range(steps):
        lin_all_ref[t] = lin_ref[:, t].reshape(group, width)
    for d in range(2):
        first = 0 if d == 0 else last
        state_ref[d, first] = jnp.zeros((group, width), jnp.bfloat16)
        cell_start[d, first] = jnp.zeros((group, cells), jnp.float32)
        grad_cell[d] = jnp.zeros((group, cells), jnp.float32)
    grad_lin_sum[...] = jnp.zeros_like(grad_lin_sum)
    wait_bytes(weight_ref, load_sems.at[0])
    wait_bytes(proj_ref, load_sems.at[1])

    @pl.loop(0, steps)
    def _(t):
        for d in range(2):
            for q in range(4):
                cols = pl.ds(q * cells, cells)
                gates[d, t, :, cols] = (
                    jnp.dot(
                        lin_all_ref[t],
                        weight_ref[d, :width, cols],
                        preferred_element_type=jnp.float32,
                    )
                    + bias_ref[d, :, cols]
                )

    def time_of(d, s):
        return s if d == 0 else last - s

    @pl.loop(0, steps)
    def _(s):
        for d in range(2):
            t = time_of(d, s)
            later = time_of(d, jnp.minimum(s + 1, last))

            @pl.when(s > 0)
            def _():
                wait_bytes(
                    state_ref.at[d, t, other_rows], share_sems.at[0, d, s]
                )
                for q in range(4):
                    cols = pl.ds(q * cells, cells)
                    gates[d, t, :, cols] += jnp.dot(
                        state_ref[d, t],
                        weight_ref[d, width:, cols],
                        preferred_element_type=jnp.float32,
                    )

            @pl.loop(0, group // row_block)
            def _(block):
                rows = pl.ds(pl.multiple_of(block * row_block, row_block), row_block)
                in_gate = sigmoid(gates[d, t, rows, pl.ds(0, cells)])
                forget_gate = sigmoid(gates[d, t, rows, pl.ds(cells, cells)])
                candidate = jnp.tanh(gates[d, t, rows, pl.ds(2 * cells, cells)])
                out_gate = sigmoid(gates[d, t, rows, pl.ds(3 * cells, cells)])
                gates[d, t, rows, pl.ds(0, cells)] = in_gate
                gates[d, t, rows, pl.ds(cells, cells)] = forget_gate
                gates[d, t, rows, pl.ds(2 * cells, cells)] = candidate
                gates[d, t, rows, pl.ds(3 * cells, cells)] = out_gate
                mixed = forget_gate * cell_start[d, t, rows] + in_gate * candidate
                cell_new = 3.0 * jnp.tanh(mixed * (1.0 / 3.0))
                full_ref[d, t, rows] = (out_gate * jnp.tanh(cell_new)).astype(jnp.bfloat16)

                @pl.when(s < last)
                def _():
                    cell_start[d, later, rows] = cell_new * keep_ref[d, later, rows]

            @pl.when(s > 0)
            def _():
                wait_bytes(stage.at[d, others], send_sems.at[d])

            part = lax.dot_general(
                full_ref[d, t],
                proj_ref[d],
                (((1,), (1,)), ((), ())),
                preferred_element_type=jnp.float32,
            )
            part = part.astype(jnp.bfloat16).reshape(team, own, width)
            stage[d] = part
            received[d, s, place] = stage[d, place]
            for peer in peers:
                send(
                    stage.at[d, peer],
                    received.at[d, s, place],
                    send_sems.at[d],
                    sum_sems.at[0, d, s],
                    peer,
                )
        for d in range(2):
            t = time_of(d, s)
            later = time_of(d, jnp.minimum(s + 1, last))
            wait_bytes(received.at[d, s, others], sum_sems.at[0, d, s])
            total = jnp.sum(received[d, s].astype(jnp.float32), axis=0)
            projected[d, t] = total

            @pl.when(s > 0)
            def _():
                wait_bytes(
                    state_ref.at[d, t, other_rows], share_send_sems.at[0, d]
                )

            @pl.when(s < last)
            def _():
                state_new = (3.0 * jnp.tanh(total * (1.0 / 3.0))).astype(jnp.bfloat16)
                kept = state_new.astype(jnp.float32) * keep_ref[d, later, own_rows]
                state_ref[d, later, own_rows] = kept.astype(jnp.bfloat16)
                for peer in peers:
                    send(
                        state_ref.at[d, later, own_rows],
                        state_ref.at[d, later, own_rows],
                        share_send_sems.at[0, d],
                        share_sems.at[0, d, s + 1],
                        peer,
                    )

    @pl.loop(0, steps)
    def _(s):
        for d in range(2):
            t = time_of(1 - d, s)

            @pl.when(s > 0)
            def _():
                wait_bytes(
                    received_back.at[d, jnp.maximum(s - 1, 0), others],
                    sum_sems.at[1, d, jnp.maximum(s - 1, 0)],
                )
                grad_state_own[...] = jnp.sum(
                    received_back[d, jnp.maximum(s - 1, 0)].astype(jnp.float32), axis=0
                )

            @pl.when(s == 0)
            def _():
                grad_state_own[...] = jnp.zeros((own, width), jnp.float32)

            grad_state = grad_state_own[...] + out_grad_ref[d, t].astype(jnp.float32)
            squashed = jnp.tanh(projected[d, t] * (1.0 / 3.0))
            grad_proj_ref[d, t, own_rows] = (grad_state * (1.0 - squashed * squashed)).astype(
                jnp.bfloat16
            )
            for peer in peers:
                send(
                    grad_proj_ref.at[d, t, own_rows],
                    grad_proj_ref.at[d, t, own_rows],
                    share_send_sems.at[1, d],
                    share_sems.at[1, d, s],
                    peer,
                )
        for d in range(2):
            t = time_of(1 - d, s)
            wait_bytes(grad_proj_ref.at[d, t, other_rows], share_sems.at[1, d, s])
            wait_bytes(
                grad_proj_ref.at[d, t, other_rows], share_send_sems.at[1, d]
            )

            @pl.loop(0, group // row_block)
            def _(block):
                rows = pl.ds(pl.multiple_of(block * row_block, row_block), row_block)
                grad_full = jnp.dot(
                    grad_proj_ref[d, t, rows], proj_ref[d], preferred_element_type=jnp.float32
                )
                in_gate = gates[d, t, rows, pl.ds(0, cells)]
                forget_gate = gates[d, t, rows, pl.ds(cells, cells)]
                candidate = gates[d, t, rows, pl.ds(2 * cells, cells)]
                out_gate = gates[d, t, rows, pl.ds(3 * cells, cells)]
                start = cell_start[d, t, rows]
                clipped = jnp.tanh((forget_gate * start + in_gate * candidate) * (1.0 / 3.0))
                tanh_cell = jnp.tanh(3.0 * clipped)
                total = grad_cell[d, rows] + grad_full * out_gate * (1.0 - tanh_cell * tanh_cell)
                grad_raw = total * (1.0 - clipped * clipped)
                grad_gates_ref[d, t, rows, pl.ds(0, cells)] = (
                    grad_raw * candidate * in_gate * (1.0 - in_gate)
                ).astype(jnp.bfloat16)
                grad_gates_ref[d, t, rows, pl.ds(cells, cells)] = (
                    grad_raw * start * forget_gate * (1.0 - forget_gate)
                ).astype(jnp.bfloat16)
                grad_gates_ref[d, t, rows, pl.ds(2 * cells, cells)] = (
                    grad_raw * in_gate * (1.0 - candidate * candidate)
                ).astype(jnp.bfloat16)
                grad_gates_ref[d, t, rows, pl.ds(3 * cells, cells)] = (
                    grad_full * tanh_cell * out_gate * (1.0 - out_gate)
                ).astype(jnp.bfloat16)
                grad_cell[d, rows] = grad_raw * forget_gate * keep_ref[d, t, rows]

            wait_bytes(stage.at[d, others], send_sems.at[d])

            @pl.when(s < last)
            def _():
                part = (
                    lax.dot_general(
                        grad_gates_ref[d, t],
                        weight_ref[d, width:],
                        (((1,), (1,)), ((), ())),
                        preferred_element_type=jnp.float32,
                    )
                    * keep_ref[d, t]
                )
                stage[d] = part.astype(jnp.bfloat16).reshape(team, own, width)
                received_back[d, s, place] = stage[d, place]
                for peer in peers:
                    send(
                        stage.at[d, peer],
                        received_back.at[d, s, place],
                        send_sems.at[d],
                        sum_sems.at[1, d, s],
                        peer,
                    )

            grad_lin_sum[t] += lax.dot_general(
                grad_gates_ref[d, t],
                weight_ref[d, :width],
                (((1,), (1,)), ((), ())),
                preferred_element_type=jnp.float32,
            )

    for t in range(steps):
        stage_lin[:, t] = grad_lin_sum[t].astype(jnp.bfloat16).reshape(team, own, width)
    received_lin[place] = stage_lin[place]
    for peer in peers:
        send(stage_lin.at[peer], received_lin.at[place], lin_sems.at[4], lin_sems.at[5], peer)

    count = steps * group
    half_blocks = len(blocks) // 2

    def weight_grads(d):
        for half in range(2):

            @pl.loop(0, 4)
            def _(q):
                cols = pl.ds(pl.multiple_of(q * cells, cells), cells)
                slot = lax.rem(q, 2)
                rows_in = (lin_all_ref[...] if half == 0 else state_ref[d]).reshape(count, width)
                gate_part = grad_gates_ref[d, :, :, cols].reshape(count, cells)
                part = lax.dot_general(
                    rows_in,
                    gate_part,
                    (((0,), (0,)), ((), ())),
                    preferred_element_type=jnp.float32,
                )

                @pl.when(q >= 2)
                def _():
                    wait_bytes(grad_stage.at[slot], out_sems.at[slot])

                grad_stage[slot] = part.astype(jnp.bfloat16)
                for source, t, at in blocks[half * half_blocks : (half + 1) * half_blocks]:
                    pltpu.make_async_copy(
                        grad_stage.at[slot, pl.ds((at - half * half_blocks) * run, run)],
                        grad_weight_hbm.at[source, t, d, :, cols],
                        out_sems.at[slot],
                    ).start()

            for slot in range(2):
                wait_bytes(grad_stage.at[slot], out_sems.at[slot])
        turned = lax.dot_general(
            grad_proj_ref[d].reshape(count, width),
            full_ref[d].reshape(count, cells),
            (((0,), (0,)), ((), ())),
            preferred_element_type=jnp.float32,
        )
        turned_stage[d] = turned.astype(jnp.bfloat16)
        for source, t, at in blocks:
            pltpu.make_async_copy(
                turned_stage.at[d, pl.ds(at * turned_run, turned_run)],
                grad_turned_hbm.at[source, t, d],
                out_sems.at[2 + d],
            ).start()
        ones = jnp.ones((8, count), jnp.bfloat16)
        for q in range(4):
            cols = pl.ds(q * cells, cells)
            grad_bias_ref[d, :, cols] = jnp.dot(
                ones,
                grad_gates_ref[d, :, :, cols].reshape(count, cells),
                preferred_element_type=jnp.float32,
            )

    weight_grads(0)
    wait_bytes(received_lin.at[others], lin_sems.at[5])
    grad_lin_all_ref[place] = jnp.sum(received_lin[...].astype(jnp.float32), axis=0).astype(
        jnp.bfloat16
    )
    for peer in peers:
        send(
            grad_lin_all_ref.at[place],
            grad_lin_all_ref.at[place],
            lin_sems.at[6],
            lin_sems.at[7],
            peer,
        )
    weight_grads(1)
    wait_bytes(grad_lin_all_ref.at[others], lin_sems.at[7])
    wait_bytes(stage_lin.at[others], lin_sems.at[4])
    wait_bytes(grad_lin_all_ref.at[others], lin_sems.at[6])
    for d in range(2):
        wait_bytes(turned_stage.at[d], out_sems.at[2 + d])


def run_lstm(lin, out_grad, weights, turned, bias, keep):
    team, steps, own, width = lin.shape
    group = team * own
    cells = turned.shape[4]
    bf16, f32 = jnp.bfloat16, jnp.float32
    vmem = pl.BlockSpec(memory_space=pltpu.VMEM)
    hbm = pl.BlockSpec(memory_space=pl.ANY)
    return pl.pallas_call(
        partial(lstm_kernel, team),
        in_specs=[vmem, vmem, hbm, hbm, vmem, vmem],
        out_specs=[vmem, hbm, hbm, vmem],
        out_shape=[
            jax.ShapeDtypeStruct(lin.shape, bf16),
            jax.ShapeDtypeStruct(weights.shape[:3] + (weights.shape[4], 4 * cells), bf16),
            jax.ShapeDtypeStruct(turned.shape, bf16),
            jax.ShapeDtypeStruct((2, 8, 4 * cells), f32),
        ],
        scratch_shapes=[
            pltpu.VMEM((2, 2 * width, 4 * cells), bf16),
            pltpu.VMEM((2, width, cells), bf16),
            pltpu.VMEM((2, steps, group, 4 * cells), bf16),
            pltpu.VMEM((steps, group, width), bf16),
            pltpu.VMEM((2, steps, group, width), bf16),
            pltpu.VMEM((2, steps, group, cells), bf16),
            pltpu.VMEM((2, steps, group, width), bf16),
            pltpu.VMEM((2, steps, group, 4 * cells), f32),
            pltpu.VMEM((2, steps, group, cells), f32),
            pltpu.VMEM((2, steps, own, width), f32),
            pltpu.VMEM((2, team, own, width), bf16),
            pltpu.VMEM((2, steps, team, own, width), bf16),
            pltpu.VMEM((2, steps, team, own, width), bf16),
            pltpu.VMEM((2, group, cells), f32),
            pltpu.VMEM((steps, group, width), f32),
            pltpu.VMEM((team, steps, own, width), bf16),
            pltpu.VMEM((team, steps, own, width), bf16),
            pltpu.VMEM((own, width), f32),
            pltpu.VMEM((2, width, cells), bf16),
            pltpu.VMEM((2, width, cells), bf16),
            pltpu.SemaphoreType.DMA((2,)),
            pltpu.SemaphoreType.DMA((8,)),
            pltpu.SemaphoreType.DMA((2,)),
            pltpu.SemaphoreType.DMA((2, 2, steps)),
            pltpu.SemaphoreType.DMA((2, 2)),
            pltpu.SemaphoreType.DMA((2, 2, steps)),
            pltpu.SemaphoreType.DMA((4,)),
        ],
        compiler_params=pltpu.CompilerParams(
            collective_id=1, has_side_effects=True, vmem_limit_bytes=63 * 1024 * 1024
        ),
        name="lstm_team",
    )(lin, out_grad, weights, turned, bias, keep)


def member_at(offset):
    t_size, x_size, c_size = lax.axis_size("t"), lax.axis_size("x"), lax.axis_size("c")
    dt, dx, dc = offset // (x_size * c_size), lax.rem(offset // c_size, x_size), lax.rem(offset, c_size)
    t = lax.rem(lax.axis_index("t") + dt, t_size)
    x = lax.rem(lax.axis_index("x") + dx, x_size)
    c = lax.rem(lax.axis_index("c") + dc, c_size)
    return (t * x_size + x) * c_size + c


def opposite(offset):
    t_size, x_size, c_size = lax.axis_size("t"), lax.axis_size("x"), lax.axis_size("c")
    dt, dx, dc = offset // (x_size * c_size), offset // c_size % x_size, offset % c_size
    return (-dt % t_size * x_size + -dx % x_size) * c_size + -dc % c_size


def send_block(source, target, send_sem, recv_sem, peer):
    pltpu.make_async_remote_copy(
        src_ref=source,
        dst_ref=target,
        send_sem=send_sem,
        recv_sem=recv_sem,
        device_id=team_coords(peer),
        device_id_type=pl.DeviceIdType.MESH,
    ).start()


def greet(offsets, with_grid=False):
    barrier = pltpu.get_barrier_semaphore()
    for offset in offsets:
        pl.semaphore_signal(
            barrier,
            inc=1,
            device_id=team_coords(member_at(offset)),
            device_id_type=pl.DeviceIdType.MESH,
        )
    extra = greet_grid(barrier) if with_grid else 0
    pl.semaphore_wait(barrier, len(offsets) + extra)


def load_highway(first_hbm, weights, project, sems):
    grid = first_hbm.shape[0]
    team = team_size()
    run = project.shape[0] // grid

    @pl.loop(0, team)
    def _(member):
        for block in range(grid):
            for level in range(2):
                pltpu.make_async_copy(
                    first_hbm.at[
                        block, pl.ds(pl.multiple_of((member * 2 + level) * run, run), run)
                    ],
                    weights.at[
                        level, pl.ds(pl.multiple_of((member * grid + block) * run, run), run)
                    ],
                    sems.at[0],
                ).start()

    for block in range(grid):
        pltpu.make_async_copy(
            first_hbm.at[block, pl.ds(team * 2 * run, run)],
            project.at[pl.ds(block * run, run)],
            sems.at[1],
        ).start()


def grid_coords(dg, dy):
    g_size, y_size = lax.axis_size("g"), lax.axis_size("y")
    return {
        "g": lax.rem(lax.axis_index("g") + dg, g_size),
        "y": lax.rem(lax.axis_index("y") + dy, y_size),
    }


def grid_block(dg, dy):
    coords = grid_coords(dg, dy)
    return coords["g"] * lax.axis_size("y") + coords["y"]


def send_grid(source, target, send_sem, recv_sem, dg, dy):
    pltpu.make_async_remote_copy(
        src_ref=source,
        dst_ref=target,
        send_sem=send_sem,
        recv_sem=recv_sem,
        device_id=grid_coords(dg, dy),
        device_id_type=pl.DeviceIdType.MESH,
    ).start()


def greet_grid(barrier):
    for dg in range(1, lax.axis_size("g")):
        pl.semaphore_signal(
            barrier, inc=1, device_id=grid_coords(dg, 0), device_id_type=pl.DeviceIdType.MESH
        )
    pl.semaphore_signal(
        barrier, inc=1, device_id=grid_coords(0, 1), device_id_type=pl.DeviceIdType.MESH
    )
    return lax.axis_size("g")


class Gather:
    def __init__(self, blocks, targets, send_sem, recv_sems):
        self.blocks = blocks
        self.targets = targets
        self.send_sem = send_sem
        self.recv_sems = recv_sems

    def start(self, pieces):
        home = grid_block(0, 0)
        g_size = lax.axis_size("g")
        for piece in pieces:
            source = self.blocks[piece]
            target = self.targets[piece](home)
            for dg in range(1, g_size):
                send_grid(
                    source, target, self.send_sem, self.recv_sems.at[piece, g_size - dg, 0], dg, 0
                )
            send_grid(source, target, self.send_sem, self.recv_sems.at[piece, 0, 1], 0, 1)

    def forward(self, pieces):
        for piece in pieces:
            for dg in range(1, lax.axis_size("g")):
                target = self.targets[piece](grid_block(dg, 0))
                wait_bytes(target, self.recv_sems.at[piece, dg, 0])
                send_grid(target, target, self.send_sem, self.recv_sems.at[piece, dg, 1], 0, 1)

    def finish(self, pieces):
        for piece in pieces:
            for dg in range(lax.axis_size("g")):
                wait_bytes(self.targets[piece](grid_block(dg, 1)), self.recv_sems.at[piece, dg, 1])

    def sent(self, pieces):
        for piece in pieces:
            for _ in range(2 * lax.axis_size("g") - 1):
                wait_bytes(self.blocks[piece], self.send_sem)


def row_pieces(total, parts):
    step = -(-total // (parts * 16)) * 16
    return [(start, min(step, total - start)) for start in range(0, total, step)]


def highway_kernel(
    tight_from,
    tiled_ref,
    filter_ref,
    count_ref,
    block_hbm,
    lstm_block_hbm,
    turned_block_hbm,
    bias_ref,
    lin_bias_ref,
    lse_ref,
    first_hbm,
    lstm_hbm,
    turned_hbm,
    first_ref,
    second_ref,
    mixed_ref,
    hidden_ref,
    top_ref,
    lin_ref,
    parts,
    parts_recv,
    features_own,
    wide,
    tight,
    weights,
    project,
    load_sems,
    send_sems,
    first_sems,
    second_sems,
    gather_send_sems,
    block_sems,
    turned_sems,
    lstm_sems,
    lin_sems,
):
    team, tokens, features = first_ref.shape
    part = features // team
    cores = lax.axis_size("c")
    g_size, y_size = lax.axis_size("g"), lax.axis_size("y")
    place = team_place()
    sibling = member_at(1)
    near = list(range(cores, team, cores))
    chunks = lstm_block_hbm.shape[0]
    greet([1] + near, True)
    home = grid_block(0, 0)
    places = [pl.ds(start, size) for start, size in row_pieces(block_hbm.shape[0], 8)]
    block_gather = Gather(
        [block_hbm.at[rows] for rows in places],
        [lambda at, rows=rows: first_hbm.at[at, rows] for rows in places],
        gather_send_sems.at[0],
        block_sems,
    )
    turned_gather = Gather(
        [turned_block_hbm],
        [lambda at: turned_hbm.at[at]],
        gather_send_sems.at[1],
        turned_sems,
    )
    all_places = list(range(len(places)))
    block_gather.start(all_places)
    pltpu.make_async_copy(block_hbm, first_hbm.at[home], load_sems.at[2]).start()
    pltpu.make_async_copy(turned_block_hbm, turned_hbm.at[home], load_sems.at[3]).start()
    pltpu.make_async_copy(lstm_block_hbm, lstm_hbm.at[home], load_sems.at[4]).start()

    def columns(member):
        return pl.ds(pl.multiple_of(member * part, part), part)

    token_block = wide.shape[0] // tiled_ref.shape[1]

    @pl.loop(0, tokens // token_block)
    def _(step):
        rows = pl.ds(pl.multiple_of(step * token_block, token_block), token_block)
        pool_kernel(
            tight_from,
            tiled_ref.at[rows],
            filter_ref,
            count_ref,
            features_own.at[rows],
            lse_ref.at[rows],
            wide,
            tight,
        )

    g, t, y, x, c = axis_sizes()
    run = part // (g * y)
    natural = features_own[...]
    starts = [
        ((((gi * t + ti) * y + yi) * x + xi) * c + ci) * run
        for ti in range(t)
        for xi in range(x)
        for ci in range(c)
        for gi in range(g)
        for yi in range(y)
    ]
    features_own[...] = jnp.concatenate([natural[:, at : at + run] for at in starts], axis=1)

    for offset in near + [1]:
        send_block(
            features_own,
            first_ref.at[place],
            send_sems.at[0],
            first_sems.at[opposite(offset)],
            member_at(offset),
        )
    first_ref[place] = features_own[...]
    block_gather.forward(all_places)

    def lstm_start(chunk):
        for dg in range(1, g_size):
            send_grid(
                lstm_block_hbm.at[chunk],
                lstm_hbm.at[home, chunk],
                gather_send_sems.at[2],
                lstm_sems.at[chunk, g_size - dg, 0],
                dg,
                0,
            )

    def lstm_forward(chunk):
        for dg in range(1, g_size):
            target = lstm_hbm.at[grid_block(dg, 0), chunk]
            wait_bytes(target, lstm_sems.at[chunk, dg, 0])
            send_grid(
                target, target, gather_send_sems.at[3], lstm_sems.at[chunk, dg, 1], 0, 1
            )

    def pump(chunk):
        @pl.when(chunk < chunks)
        def _():
            lstm_forward(jnp.minimum(chunk, chunks - 1))

            @pl.when(chunk + AHEAD < chunks)
            def _():
                lstm_start(jnp.minimum(chunk + AHEAD, chunks - 1))

    turned_gather.start([0])
    for chunk in range(AHEAD):
        lstm_start(chunk)
    for offset in near:
        member = member_at(offset)
        wait_bytes(first_ref.at[member], first_sems.at[offset])
        send_block(
            first_ref.at[member],
            first_ref.at[member],
            send_sems.at[0],
            first_sems.at[offset + 1],
            sibling,
        )
    block_gather.finish(all_places)
    wait_bytes(block_hbm, load_sems.at[2])
    load_highway(first_hbm, weights, project, load_sems)

    @pl.loop(0, chunks)
    def _(chunk):
        send_grid(
            lstm_block_hbm.at[chunk],
            lstm_hbm.at[home, chunk],
            gather_send_sems.at[4],
            lstm_sems.at[chunk, 0, 1],
            0,
            1,
        )

    wait_bytes(weights, load_sems.at[0])
    wait_bytes(project, load_sems.at[1])

    def mix(level, member, operand):
        mixed = (
            jnp.dot(operand, weights[level], preferred_element_type=jnp.float32)
            + bias_ref[level : level + 1]
        )
        mixed_ref[level, member] = mixed
        gate = sigmoid(mixed[:, part:])
        pre_act = mixed[:, :part]
        return (gate, pre_act * sigmoid(pre_act))

    @pl.loop(0, team)
    def _(offset):
        member = member_at(offset)

        @pl.when(lax.rem(offset, cores) == 1)
        def _():
            wait_bytes(first_ref.at[member], first_sems.at[offset])

        gate, act = mix(0, member, first_ref[member])
        carried = first_ref[member, :, columns(place)].astype(jnp.float32)
        hidden = gate * carried + (1.0 - gate) * act
        hidden_ref[member] = hidden
        mine = second_ref.at[member, :, columns(place)]
        mine[...] = hidden.astype(jnp.bfloat16)
        for to in near + [1]:
            send_block(
                mine,
                mine,
                send_sems.at[1],
                second_sems.at[member, opposite(to)],
                member_at(to),
            )

        pump(offset)

    @pl.loop(0, team + 1)
    def _(step):
        @pl.when(step < team)
        def _():
            member = member_at(jnp.minimum(step, team - 1))
            for origin in near:
                piece = second_ref.at[member, :, columns(member_at(origin))]
                wait_bytes(piece, second_sems.at[member, origin])
                send_block(
                    piece,
                    piece,
                    send_sems.at[1],
                    second_sems.at[member, origin + 1],
                    sibling,
                )

        @pl.when(step > 0)
        def _():
            member = member_at(jnp.maximum(step - 1, 0))
            for origin in [0] + near:
                piece = second_ref.at[member, :, columns(member_at(origin + 1))]
                wait_bytes(piece, second_sems.at[member, origin + 1])
            gate, act = mix(1, member, second_ref[member])
            top = (gate * hidden_ref[member] + (1.0 - gate) * act).astype(jnp.bfloat16)
            top_ref[member] = top
            parts[member] = jnp.dot(
                top, project[...], preferred_element_type=jnp.float32
            ).astype(jnp.bfloat16)

            @pl.when(step > 1)
            def _():
                send_block(
                    parts.at[member],
                    parts_recv.at[place],
                    lin_sems.at[0],
                    lin_sems.at[1],
                    member,
                )

        pump(team + step)

    parts_recv[place] = parts[place]
    others = pl.ds(0, team - 1)
    wait_bytes(parts_recv.at[others], lin_sems.at[1])
    lin = jnp.sum(parts_recv[...].astype(jnp.float32), axis=0) + lin_bias_ref[...]
    lin_ref[place] = lin.astype(jnp.bfloat16)
    for offset in range(1, team):
        send_block(
            lin_ref.at[place],
            lin_ref.at[place],
            lin_sems.at[2],
            lin_sems.at[3],
            member_at(offset),
        )

    @pl.loop(2 * team + 1, max(chunks, 2 * team + 1))
    def _(chunk):
        pump(chunk)

    wait_bytes(lin_ref.at[others], lin_sems.at[3])
    wait_bytes(lin_ref.at[others], lin_sems.at[2])
    wait_bytes(parts.at[others], lin_sems.at[0])

    turned_gather.forward([0])
    turned_gather.finish([0])

    @pl.loop(0, chunks)
    def _(chunk):
        for dg in range(g_size):
            wait_bytes(lstm_hbm.at[grid_block(dg, 1), chunk], lstm_sems.at[chunk, dg, 1])

    wait_bytes(first_ref.at[pl.ds(0, team - 1)], send_sems.at[0])
    wait_bytes(second_ref.at[pl.ds(0, team - 1)], send_sems.at[1])
    block_gather.sent(all_places)
    turned_gather.sent([0])
    for _ in range(g_size - 1):
        wait_bytes(lstm_block_hbm, gather_send_sems.at[2])
        wait_bytes(lstm_block_hbm, gather_send_sems.at[3])
    wait_bytes(lstm_block_hbm, gather_send_sems.at[4])
    wait_bytes(turned_block_hbm, load_sems.at[3])
    wait_bytes(lstm_block_hbm, load_sems.at[4])


def run_highway(
    tight_from, tiled, filters, counts, block, lstm_block, turned_block, bias, lin_bias
):
    team = team_size()
    tokens, features = tiled.shape[0], filters.shape[1]
    part = features // team
    g_size, y_size = lax.axis_size("g"), lax.axis_size("y")
    grid = g_size * y_size
    width = block.shape[1]
    bf16, f32 = jnp.bfloat16, jnp.float32
    vmem = pl.BlockSpec(memory_space=pltpu.VMEM)
    hbm = pl.BlockSpec(memory_space=pl.ANY)
    pieces = len(row_pieces(block.shape[0], 8))
    token_block = math.gcd(tokens, TOKEN_BLOCK)
    return pl.pallas_call(
        partial(highway_kernel, tight_from),
        in_specs=[vmem] * 3 + [hbm] * 3 + [vmem] * 2,
        out_specs=[vmem] + [hbm] * 3 + [vmem] * 6,
        out_shape=[
            jax.ShapeDtypeStruct((tokens, features), f32),
            jax.ShapeDtypeStruct((grid,) + block.shape, bf16),
            jax.ShapeDtypeStruct((grid,) + lstm_block.shape, bf16),
            jax.ShapeDtypeStruct((grid,) + turned_block.shape, bf16),
            jax.ShapeDtypeStruct((team, tokens, features), bf16),
            jax.ShapeDtypeStruct((team, tokens, features), bf16),
            jax.ShapeDtypeStruct((2, team, tokens, 2 * part), f32),
            jax.ShapeDtypeStruct((team, tokens, part), f32),
            jax.ShapeDtypeStruct((team, tokens, part), bf16),
            jax.ShapeDtypeStruct((team, tokens, width), bf16),
        ],
        scratch_shapes=[
            pltpu.VMEM((team, tokens, width), bf16),
            pltpu.VMEM((team, tokens, width), bf16),
            pltpu.VMEM((tokens, features), bf16),
            pltpu.VMEM((token_block * PLACES, LANES), bf16),
            pltpu.VMEM((token_block * TIGHT, LANES), bf16),
            pltpu.VMEM((2, features, 2 * part), bf16),
            pltpu.VMEM((part, width), bf16),
            pltpu.SemaphoreType.DMA((5,)),
            pltpu.SemaphoreType.DMA((2,)),
            pltpu.SemaphoreType.DMA((team,)),
            pltpu.SemaphoreType.DMA((team, team)),
            pltpu.SemaphoreType.DMA((5,)),
            pltpu.SemaphoreType.DMA((pieces, g_size, y_size)),
            pltpu.SemaphoreType.DMA((1, g_size, y_size)),
            pltpu.SemaphoreType.DMA((lstm_block.shape[0], g_size, y_size)),
            pltpu.SemaphoreType.DMA((4,)),
        ],
        compiler_params=pltpu.CompilerParams(
            collective_id=2, has_side_effects=True, vmem_limit_bytes=60 * 1024 * 1024
        ),
        name="highway_team",
    )(tiled, filters, counts, block, lstm_block, turned_block, bias, lin_bias)


def highway_back_kernel(
    grad_lin_ref,
    first_hbm,
    first_ref,
    second_ref,
    mixed_ref,
    hidden_ref,
    top_ref,
    lstm_hbm,
    features_ref,
    grads_hbm,
    bias_ref,
    lstm_ref,
    lstm_own,
    lstm_y,
    lstm_send,
    lstm_g,
    weights,
    project,
    grad_mixed,
    direct,
    column_parts,
    column_sibling,
    column_send,
    column_recv,
    column_sum_own,
    row_part,
    row_keep,
    row_give,
    row_sibling,
    row_send,
    row_recv,
    row_sum_own,
    grad_stage,
    load_sems,
    send_sems,
    column_sib_sems,
    column_sems,
    row_sib_sems,
    row_sems,
    out_sems,
    lstm_load_sems,
    lstm_send_sems,
    lstm_y_sems,
    lstm_g_sems,
):
    team, tokens, features = first_ref.shape
    part = features // team
    grid = first_hbm.shape[0]
    run = part // grid
    cores = lax.axis_size("c")
    chips = team // cores
    place = team_place()
    sibling = member_at(1)
    near = list(range(1, chips))
    load_highway(first_hbm, weights, project, load_sems)
    greet([1] + [chip * cores for chip in near], True)
    f32, bf16 = jnp.float32, jnp.bfloat16
    g_size, y_size = lax.axis_size("g"), lax.axis_size("y")
    y_index = lax.axis_index("y")
    other_y = lax.rem(y_index + 1, y_size)
    chunks = lstm_ref.shape[0]

    def lstm_block(dg, y):
        return lax.rem(lax.axis_index("g") + dg, g_size) * y_size + y

    @pl.loop(0, chunks)
    def _(chunk):
        for dg in list(range(1, g_size)) + [0]:
            send_grid(
                lstm_hbm.at[lstm_block(dg, other_y), chunk],
                lstm_y.at[dg, chunk],
                lstm_send_sems.at[0],
                lstm_y_sems.at[chunk, dg],
                0,
                1,
            )

    pltpu.make_async_copy(
        lstm_hbm.at[lstm_block(0, y_index)], lstm_ref, lstm_load_sems.at[0]
    ).start()
    for dg in range(1, g_size):
        pltpu.make_async_copy(
            lstm_hbm.at[lstm_block(dg, y_index)], lstm_own.at[dg - 1], lstm_load_sems.at[1]
        ).start()

    def pump(chunk):
        for dg in range(1, g_size):
            wait_bytes(lstm_y.at[dg, chunk], lstm_y_sems.at[chunk, dg])
            both = lstm_own[dg - 1, chunk].astype(f32) + lstm_y[dg, chunk].astype(f32)
            lstm_send[dg - 1, chunk] = both.astype(bf16)
            send_grid(
                lstm_send.at[dg - 1, chunk],
                lstm_g.at[g_size - dg - 1, chunk],
                lstm_send_sems.at[1],
                lstm_g_sems.at[chunk, g_size - dg - 1],
                dg,
                0,
            )

    def columns(member):
        return pl.ds(pl.multiple_of(member * part, part), part)

    def opposite_chip(chip):
        return opposite(chip * cores) // cores

    wait_bytes(weights, load_sems.at[0])
    wait_bytes(project, load_sems.at[1])

    def mix_grads(level, member, grad, carried):
        pre_act = mixed_ref[level, member, :, pl.ds(0, part)]
        gate = sigmoid(mixed_ref[level, member, :, pl.ds(part, part)])
        act_sig = sigmoid(pre_act)
        grad_mixed[level, member, :, pl.ds(0, part)] = (
            grad * (1.0 - gate) * act_sig * (1.0 + pre_act * (1.0 - act_sig))
        ).astype(bf16)
        grad_mixed[level, member, :, pl.ds(part, part)] = (
            grad * (carried - pre_act * act_sig) * gate * (1.0 - gate)
        ).astype(bf16)
        return grad * gate

    def spread(level, member):
        return lax.dot_general(
            grad_mixed[level, member],
            weights[level],
            (((1,), (1,)), ((), ())),
            preferred_element_type=f32,
        )

    @pl.loop(0, team)
    def _(member):
        grad = lax.dot_general(
            grad_lin_ref[member], project[...], (((1,), (1,)), ((), ())), preferred_element_type=f32
        )
        direct[member] = mix_grads(1, member, grad, hidden_ref[member])
        column_parts[member] = spread(1, member).astype(bf16)
        for chip in range(chips):
            send_block(
                column_parts.at[member, :, columns(member_at(chip * cores + 1))],
                column_sibling.at[member, chip],
                send_sems.at[0],
                column_sib_sems.at[member],
                sibling,
            )

    wait_bytes(lstm_own, lstm_load_sems.at[1])
    pump(0)

    @pl.loop(0, team)
    def _(member):
        wait_bytes(column_sibling.at[member], column_sib_sems.at[member])
        for chip in near + [0]:
            target = member_at(chip * cores)
            both = column_parts[member, :, columns(target)].astype(f32) + column_sibling[
                member, chip
            ].astype(f32)
            if chip == 0:
                column_sum_own[member] = both
            else:
                column_send[chip - 1, member] = both.astype(bf16)
                send_block(
                    column_send.at[chip - 1, member],
                    column_recv.at[opposite_chip(chip) - 1, member],
                    send_sems.at[1],
                    column_sems.at[member, opposite_chip(chip) - 1],
                    target,
                )

    def weight_grads(level, source_ref):
        @pl.loop(0, team)
        def _(member):
            slot = lax.rem(member, 2)

            @pl.when(member >= 2)
            def _():
                wait_bytes(grad_stage.at[slot], out_sems.at[slot])

            grad_stage[slot] = lax.dot_general(
                source_ref[:, :, columns(member)].reshape(team * tokens, part),
                grad_mixed[level].reshape(team * tokens, 2 * part),
                (((0,), (0,)), ((), ())),
                preferred_element_type=f32,
            ).astype(bf16)
            for block in range(grid):
                pltpu.make_async_copy(
                    grad_stage.at[slot, pl.ds(block * run, run)],
                    grads_hbm.at[
                        block, pl.ds(pl.multiple_of((member * 2 + level) * run, run), run)
                    ],
                    out_sems.at[slot],
                ).start()

        for slot in range(2):
            wait_bytes(grad_stage.at[slot], out_sems.at[slot])
        bias_ref[level] = jnp.dot(
            jnp.ones((8, team * tokens), bf16),
            grad_mixed[level].reshape(team * tokens, 2 * part),
            preferred_element_type=f32,
        )

    pump(1)
    weight_grads(1, second_ref)
    pump(2)

    @pl.loop(0, team)
    def _(step):
        offset = team - 1 - step
        member = member_at(offset)
        chip = offset // cores
        grad = column_sum_own[member] + direct[member]
        for other in near:
            wait_bytes(column_recv.at[other - 1, member], column_sems.at[member, other - 1])
            grad = grad + column_recv[other - 1, member].astype(f32)
        carried = first_ref[member, :, columns(place)].astype(f32)
        straight = mix_grads(0, member, grad, carried)
        row_part[...] = spread(0, member)
        row_part[:, columns(place)] += straight

        @pl.when(lax.rem(offset, cores) == 1)
        def _():
            row_give[chip] = row_part[...].astype(bf16)
            send_block(
                row_give.at[chip],
                row_sibling.at[chip],
                send_sems.at[2],
                row_sib_sems.at[chip],
                sibling,
            )

        @pl.when(lax.rem(offset, cores) == 0)
        def _():
            row_keep[chip] = row_part[...].astype(bf16)

        @pl.when((step == team // 2 - 1) | (step == team - 1))
        def _():
            pump(3 + (step + 1) // team)

    for chip in near[::-1] + [0]:
        wait_bytes(row_sibling.at[chip], row_sib_sems.at[chip])
        both = row_keep[chip].astype(f32) + row_sibling[chip].astype(f32)
        if chip == 0:
            row_sum_own[...] = both
        else:
            row_send[chip - 1] = both.astype(bf16)
            send_block(
                row_send.at[chip - 1],
                row_recv.at[opposite_chip(chip) - 1],
                send_sems.at[3],
                row_sems.at[opposite_chip(chip) - 1],
                member_at(chip * cores),
            )

    pump(5)
    weight_grads(0, first_ref)

    @pl.loop(6, chunks)
    def _(chunk):
        pump(chunk)

    grad_stage[0] = lax.dot_general(
        top_ref[...].reshape(team * tokens, part),
        grad_lin_ref[...].reshape(team * tokens, 2 * part),
        (((0,), (0,)), ((), ())),
        preferred_element_type=f32,
    ).astype(bf16)
    for block in range(grid):
        pltpu.make_async_copy(
            grad_stage.at[0, pl.ds(block * run, run)],
            grads_hbm.at[block, pl.ds(team * 2 * run, run)],
            out_sems.at[0],
        ).start()
    total = row_sum_own[...]
    for other in near:
        wait_bytes(row_recv.at[other - 1], row_sems.at[other - 1])
        total = total + row_recv[other - 1].astype(f32)
    features_ref[...] = total.astype(bf16)
    wait_bytes(lstm_ref, lstm_load_sems.at[0])

    @pl.loop(0, chunks)
    def _(chunk):
        wait_bytes(lstm_y.at[0, chunk], lstm_y_sems.at[chunk, 0])
        whole = lstm_ref[chunk].astype(f32) + lstm_y[0, chunk].astype(f32)
        for dg in range(1, g_size):
            wait_bytes(lstm_g.at[dg - 1, chunk], lstm_g_sems.at[chunk, dg - 1])
            whole = whole + lstm_g[dg - 1, chunk].astype(f32)
        lstm_ref[chunk] = whole.astype(bf16)

    wait_bytes(lstm_y, lstm_send_sems.at[0])
    wait_bytes(lstm_g, lstm_send_sems.at[1])
    wait_bytes(grad_stage.at[0], out_sems.at[0])
    wait_bytes(column_sibling, send_sems.at[0])
    wait_bytes(column_send, send_sems.at[1])
    wait_bytes(row_give, send_sems.at[2])
    wait_bytes(row_send, send_sems.at[3])


def run_highway_back(grad_lin, first_all, first, second, mixed, hidden, top, lstm_grads):
    team, tokens, features = first.shape
    part = features // team
    chips = team // lax.axis_size("c")
    width = first_all.shape[2]
    bf16, f32 = jnp.bfloat16, jnp.float32
    g_size = lax.axis_size("g")
    chunk_shape = lstm_grads.shape[1:]
    vmem = pl.BlockSpec(memory_space=pltpu.VMEM)
    hbm = pl.BlockSpec(memory_space=pl.ANY)
    return pl.pallas_call(
        highway_back_kernel,
        in_specs=[vmem, hbm] + [vmem] * 5 + [hbm],
        out_specs=[vmem, hbm, vmem, vmem],
        out_shape=[
            jax.ShapeDtypeStruct((tokens, features), bf16),
            jax.ShapeDtypeStruct(first_all.shape, bf16),
            jax.ShapeDtypeStruct((2, 8, 2 * part), f32),
            jax.ShapeDtypeStruct(chunk_shape, bf16),
        ],
        scratch_shapes=[
            pltpu.VMEM((g_size - 1,) + chunk_shape, bf16),
            pltpu.VMEM((g_size,) + chunk_shape, bf16),
            pltpu.VMEM((g_size - 1,) + chunk_shape, bf16),
            pltpu.VMEM((g_size - 1,) + chunk_shape, bf16),
            pltpu.VMEM((2, features, 2 * part), bf16),
            pltpu.VMEM((part, width), bf16),
            pltpu.VMEM((2, team, tokens, 2 * part), bf16),
            pltpu.VMEM((team, tokens, part), f32),
            pltpu.VMEM((team, tokens, features), bf16),
            pltpu.VMEM((team, chips, tokens, part), bf16),
            pltpu.VMEM((chips - 1, team, tokens, part), bf16),
            pltpu.VMEM((chips - 1, team, tokens, part), bf16),
            pltpu.VMEM((team, tokens, part), f32),
            pltpu.VMEM((tokens, features), f32),
            pltpu.VMEM((chips, tokens, features), bf16),
            pltpu.VMEM((chips, tokens, features), bf16),
            pltpu.VMEM((chips, tokens, features), bf16),
            pltpu.VMEM((chips - 1, tokens, features), bf16),
            pltpu.VMEM((chips - 1, tokens, features), bf16),
            pltpu.VMEM((tokens, features), f32),
            pltpu.VMEM((2, part, width), bf16),
            pltpu.SemaphoreType.DMA((2,)),
            pltpu.SemaphoreType.DMA((4,)),
            pltpu.SemaphoreType.DMA((team,)),
            pltpu.SemaphoreType.DMA((team, chips - 1)),
            pltpu.SemaphoreType.DMA((chips,)),
            pltpu.SemaphoreType.DMA((chips - 1,)),
            pltpu.SemaphoreType.DMA((2,)),
            pltpu.SemaphoreType.DMA((2,)),
            pltpu.SemaphoreType.DMA((2,)),
            pltpu.SemaphoreType.DMA((chunk_shape[0], g_size)),
            pltpu.SemaphoreType.DMA((chunk_shape[0], g_size - 1)),
        ],
        compiler_params=pltpu.CompilerParams(
            collective_id=3, has_side_effects=True, vmem_limit_bytes=63 * 1024 * 1024
        ),
        name="highway_team_back",
    )(grad_lin, first_all, first, second, mixed, hidden, top, lstm_grads)


def every_coords(shift):
    g, t, y, x, c = axis_sizes()
    sizes = (g, t, y, x, c)
    coords, rest = {}, shift
    for name, size in list(zip(EVERY, sizes))[::-1]:
        coords[name] = lax.rem(lax.axis_index(name) + lax.rem(rest, size), size)
        rest = rest // size
    return coords


def every_place(coords):
    place = 0
    for name in EVERY:
        place = place * lax.axis_size(name) + coords[name]
    return place


def final_kernel(
    tight_from,
    bank_counts,
    grads_ref,
    tiled_ref,
    ids_ref,
    filter_ref,
    count_ref,
    lse_ref,
    upstream_ref,
    bias_ref,
    highway_ref,
    project_ref,
    sums_ref,
    conv_ref,
    table_ref,
    natural,
    grad_filters,
    table_sum,
    wide,
    tight,
    spread,
    y_recv,
    g_send,
    g_recv,
    kept,
    team_send,
    team_recv,
    bias_recv,
    small,
    small_team,
    small_send,
    small_grid,
    y_sems,
    g_sems,
    team_sems,
    small_sems,
    send_sems,
):
    grid, rows, lanes = grads_ref.shape
    team = team_size()
    g, t, y, x, c = axis_sizes()
    devices = bias_ref.shape[0]
    step = team_recv.shape[1]
    cut = step * team
    table_rows = table_ref.shape[0] // team
    f32, bf16 = jnp.float32, jnp.bfloat16
    here = every_place({name: lax.axis_index(name) for name in EVERY})
    place = team_place()
    bank = lax.rem(place, x * c)
    conv_ref[...] = jnp.zeros_like(conv_ref)
    barrier = pltpu.get_barrier_semaphore()

    @pl.loop(1, devices)
    def _(shift):
        pl.semaphore_signal(
            barrier, inc=1, device_id=every_coords(shift), device_id_type=pl.DeviceIdType.MESH
        )

    pl.semaphore_wait(barrier, devices - 1)
    pieces = [pl.ds(k * step, step) for k in range(team)] + [pl.ds(cut, rows - cut)]
    g_index, y_index = lax.axis_index("g"), lax.axis_index("y")
    other_y = lax.rem(y_index + 1, y)
    for k, piece in enumerate(pieces):
        for dg in list(range(1, g)) + [0]:
            send_grid(
                grads_ref.at[lax.rem(g_index + dg, g) * y + other_y, piece],
                y_recv.at[dg, piece],
                send_sems.at[0],
                y_sems.at[k, dg],
                0,
                1,
            )

    @pl.loop(1, devices)
    def _(shift):
        coords = every_coords(shift)
        pltpu.make_async_remote_copy(
            src_ref=bias_ref.at[every_place(coords)],
            dst_ref=bias_recv.at[here],
            send_sem=send_sems.at[3],
            recv_sem=small_sems.at[0],
            device_id=coords,
            device_id_type=pl.DeviceIdType.MESH,
        ).start()

    bias_recv[here] = bias_ref[here]
    run = upstream_ref.shape[1] // devices
    order = [
        (((ti * x + xi) * c + ci) * g + gi) * y + yi
        for gi in range(g)
        for ti in range(t)
        for yi in range(y)
        for xi in range(x)
        for ci in range(c)
    ]
    permuted = upstream_ref[...]
    natural[...] = jnp.concatenate([permuted[:, at * run : (at + 1) * run] for at in order], axis=1)
    grad_filters[...] = jnp.zeros_like(grad_filters)
    table_sum[...] = jnp.zeros_like(table_sum)

    def pass_on(k):
        piece = pieces[k]
        for dg in list(range(1, g)) + [0]:
            wait_bytes(y_recv.at[dg, piece], y_sems.at[k, dg])
            both = grads_ref[lax.rem(g_index + dg, g) * y + y_index, piece].astype(f32)
            both = both + y_recv[dg, piece].astype(f32)
            if dg == 0:
                kept[piece] = both
            else:
                g_send[dg - 1, piece] = both.astype(bf16)
                send_grid(
                    g_send.at[dg - 1, piece],
                    g_recv.at[g - dg - 1, piece],
                    send_sems.at[1],
                    g_sems.at[k, g - dg - 1],
                    dg,
                    0,
                )

    token_block = spread.shape[0]
    blocks = tiled_ref.shape[0] // token_block
    early = min(4, team)

    def pool_block(at):
        picked = pl.ds(pl.multiple_of(at * token_block, token_block), token_block)
        pool_grad_block(
            tight_from,
            tiled_ref.at[picked],
            ids_ref[pl.ds(at, 1)],
            filter_ref,
            count_ref,
            lse_ref.at[picked],
            natural.at[picked],
            grad_filters,
            table_sum,
            wide,
            tight,
            spread,
        )

    for k in range(early):

        @pl.loop(blocks * k // early, blocks * (k + 1) // early)
        def _(at):
            pool_block(at)

        pass_on(k)

    lane = lax.broadcasted_iota(jnp.int32, (LANES, LANES), 0)
    fold = jnp.where(
        (lane < TAPS)
        & (lax.rem(lane, EMBED) == lax.broadcasted_iota(jnp.int32, (LANES, LANES), 1)),
        1.0,
        0.0,
    ).astype(bf16)
    by_tap = table_sum[...]
    high = by_tap.astype(bf16)
    low = (by_tap - high.astype(f32)).astype(bf16)
    table = jnp.dot(high, fold, preferred_element_type=f32)
    table = (table + jnp.dot(low, fold, preferred_element_type=f32)).astype(bf16)
    starts, halves, at, column = [], [], 0, 0
    for half in range(t):
        for b, count in enumerate(bank_counts):
            starts.append(at)
            halves.append(count // t)
            at += count // t + table_rows
    for b, count in enumerate(bank_counts):
        for half in range(t):
            member = half * len(bank_counts) + b
            each = count // t
            turned = grad_filters[:, pl.ds(column, each)].T.astype(bf16)
            small[pl.ds(starts[member], each)] = turned
            column += each
    vocab = table_sum.shape[0]
    for member in range(team):
        top = min(table_rows, vocab - member * table_rows)
        begin = starts[member] + halves[member]
        if top > 0:
            small[pl.ds(begin, top)] = table[member * table_rows : member * table_rows + top]
        if top < table_rows:
            low_row = max(top, 0)
            small[pl.ds(begin + low_row, table_rows - low_row)] = jnp.zeros(
                (table_rows - low_row, LANES), bf16
            )
    for member in range(team):
        size = halves[member] + table_rows
        source = small.at[pl.ds(starts[member], size)]

        @pl.when(place == member)
        def _():
            small_team[member, pl.ds(0, size)] = small[pl.ds(starts[member], size)]

        @pl.when(place != member)
        def _():
            send_block(
                source,
                small_team.at[place, pl.ds(0, size)],
                send_sems.at[4],
                small_sems.at[1],
                member,
            )

    for k in range(early, team - 2):
        pass_on(k)
    home = grid_block(0, 0)
    for b, count in enumerate(bank_counts):
        size = count // t + table_rows

        @pl.when(bank == b)
        def _():
            wait_bytes(small_team.at[pl.ds(0, team - 1), pl.ds(0, size)], small_sems.at[1])
            total = small_team[0, pl.ds(0, size)].astype(f32)
            for origin in range(1, team):
                total = total + small_team[origin, pl.ds(0, size)].astype(f32)
            small_send[pl.ds(0, size)] = total.astype(bf16)
            small_grid[home, pl.ds(0, size)] = total.astype(bf16)
            for dg in range(g):
                for dy in range(y):
                    if dg or dy:
                        send_grid(
                            small_send.at[pl.ds(0, size)],
                            small_grid.at[home, pl.ds(0, size)],
                            send_sems.at[5],
                            small_sems.at[2],
                            dg,
                            dy,
                        )

    for k in range(team - 2, team + 1):
        pass_on(k)
    t_index = lax.axis_index("t")
    for b, count in enumerate(bank_counts):
        each = count // t
        size = each + table_rows

        @pl.when(bank == b)
        def _():
            wait_bytes(small_grid.at[pl.ds(0, grid - 1), pl.ds(0, size)], small_sems.at[2])
            total = small_grid[0, pl.ds(0, size)].astype(f32)
            for origin in range(1, grid):
                total = total + small_grid[origin, pl.ds(0, size)].astype(f32)
            mine = conv_ref.at[pl.ds(pl.multiple_of(t_index * each, each), each)]
            mine[...] = total[:each]
            for dt in range(1, t):
                send_block(
                    mine, mine, send_sems.at[6], small_sems.at[3], member_at(dt * x * c)
                )
            piece = table_ref.at[pl.ds(pl.multiple_of(place * table_rows, 16), table_rows)]
            piece[...] = total[each:]
            for offset in range(1, team):
                send_block(piece, piece, send_sems.at[7], small_sems.at[4], member_at(offset))

    for k, piece in enumerate(pieces):
        total = kept[piece]
        for dg in range(1, g):
            wait_bytes(g_recv.at[dg - 1, piece], g_sems.at[k, dg - 1])
            total = total + g_recv[dg - 1, piece].astype(f32)
        if k == team:
            project_ref[...] = total
        else:
            team_send[piece] = total.astype(bf16)

            @pl.when(place == k)
            def _():
                team_recv[k] = team_send[piece]

            @pl.when(place != k)
            def _():
                send_block(
                    team_send.at[piece], team_recv.at[place], send_sems.at[2], team_sems.at[0], k
                )

    wait_bytes(bias_recv.at[pl.ds(0, devices - 1)], small_sems.at[0])
    sums_ref[...] = jnp.sum(bias_recv[...].astype(f32), axis=0)
    wait_bytes(team_recv.at[pl.ds(0, team - 1)], team_sems.at[0])
    half_lanes = lanes // 2
    for half in range(2):
        parts = [
            team_recv[
                (ti * x + xi) * c + ci,
                :,
                half * half_lanes + (gi * y + yi) * run : half * half_lanes + (gi * y + yi + 1) * run,
            ]
            for gi in range(g)
            for ti in range(t)
            for yi in range(y)
            for xi in range(x)
            for ci in range(c)
        ]
        wide_half = half_lanes * team
        highway_ref[:, pl.ds(half * wide_half, wide_half)] = jnp.concatenate(parts, axis=1).astype(
            f32
        )
    for b, count in enumerate(bank_counts):
        each = count // t
        size = each + table_rows

        @pl.when(bank == b)
        def _():
            for _ in range(t - 1):
                wait_bytes(conv_ref.at[pl.ds(0, each)], small_sems.at[3])
                wait_bytes(conv_ref.at[pl.ds(0, each)], send_sems.at[6])
            wait_bytes(small_grid.at[pl.ds(0, grid - 1), pl.ds(0, size)], send_sems.at[5])

    wait_bytes(table_ref.at[pl.ds(0, (team - 1) * table_rows)], small_sems.at[4])
    wait_bytes(table_ref.at[pl.ds(0, (team - 1) * table_rows)], send_sems.at[7])
    wait_bytes(y_recv, send_sems.at[0])
    wait_bytes(g_recv, send_sems.at[1])
    wait_bytes(team_recv.at[pl.ds(0, team - 1)], send_sems.at[2])
    wait_bytes(bias_recv.at[pl.ds(0, devices - 1)], send_sems.at[3])
    for member in range(team):

        @pl.when(place != member)
        def _():
            size = halves[member] + table_rows
            wait_bytes(small.at[pl.ds(starts[member], size)], send_sems.at[4])


def run_final(tight_from, bank_counts, grads, tiled, ids, filters, counts, lse, upstream, biases, step):
    grid, rows, lanes = grads.shape
    team = team_size()
    g, t, y, x, c = axis_sizes()
    tokens, features = upstream.shape
    devices, bias_rows, _ = biases.shape
    bf16, f32 = jnp.bfloat16, jnp.float32
    vmem = pl.BlockSpec(memory_space=pltpu.VMEM)
    token_block = math.gcd(tokens, TOKEN_BLOCK)
    vocab = -(-VOCAB // 16) * 16
    table_rows = -(-vocab // (16 * team)) * 16
    most = max(bank_counts) // t + table_rows
    return pl.pallas_call(
        partial(final_kernel, tight_from, bank_counts),
        in_specs=[vmem] * 8,
        out_specs=[vmem] * 5,
        out_shape=[
            jax.ShapeDtypeStruct((step, lanes * team), f32),
            jax.ShapeDtypeStruct((rows - team * step, lanes), f32),
            jax.ShapeDtypeStruct((bias_rows, LANES), f32),
            jax.ShapeDtypeStruct((max(bank_counts), LANES), f32),
            jax.ShapeDtypeStruct((team * table_rows, LANES), f32),
        ],
        scratch_shapes=[
            pltpu.VMEM((tokens, features), bf16),
            pltpu.VMEM((LANES, features), f32),
            pltpu.VMEM((vocab, LANES), f32),
            pltpu.VMEM((token_block * PLACES, LANES), bf16),
            pltpu.VMEM((token_block * TIGHT, LANES), bf16),
            pltpu.VMEM((token_block, PLACES, LANES), f32),
            pltpu.VMEM((g, rows, lanes), bf16),
            pltpu.VMEM((g - 1, rows, lanes), bf16),
            pltpu.VMEM((g - 1, rows, lanes), bf16),
            pltpu.VMEM((rows, lanes), f32),
            pltpu.VMEM((rows, lanes), bf16),
            pltpu.VMEM((team, step, lanes), bf16),
            pltpu.VMEM(biases.shape, bf16),
            pltpu.VMEM((sum(bank_counts) + team * table_rows, LANES), bf16),
            pltpu.VMEM((team, most, LANES), bf16),
            pltpu.VMEM((most, LANES), bf16),
            pltpu.VMEM((grid, most, LANES), bf16),
            pltpu.SemaphoreType.DMA((team + 1, g)),
            pltpu.SemaphoreType.DMA((team + 1, g - 1)),
            pltpu.SemaphoreType.DMA((1,)),
            pltpu.SemaphoreType.DMA((5,)),
            pltpu.SemaphoreType.DMA((8,)),
        ],
        compiler_params=pltpu.CompilerParams(
            collective_id=4, has_side_effects=True, vmem_limit_bytes=60 * 1024 * 1024
        ),
        name="final_sums",
    )(grads, tiled, ids, filters, counts, lse, upstream, biases)


def pack_kernel(parts, received_ref, out_ref):
    team, rows, lanes = received_ref.shape
    each = lanes // parts
    for member in range(team):
        for part in range(parts):
            out_ref[:, pl.ds((part * team + member) * each, each)] = received_ref[
                member, :, pl.ds(part * each, each)
            ].astype(jnp.float32)


def pack_columns(received, parts):
    team, rows, lanes = received.shape
    return pl.pallas_call(
        partial(pack_kernel, parts),
        in_specs=[pl.BlockSpec(memory_space=pltpu.VMEM)],
        out_specs=pl.BlockSpec(memory_space=pltpu.VMEM),
        out_shape=jax.ShapeDtypeStruct((rows, team * lanes), jnp.float32),
        compiler_params=pltpu.CompilerParams(vmem_limit_bytes=40 * 1024 * 1024),
        name="pack_columns",
    )(received)


def axis_sizes():
    return tuple(lax.axis_size(name) for name in EVERY)


def run_rows(received):
    g, t, y, x, c = axis_sizes()
    lanes = received.shape[-1]
    split = received.reshape(t, x * c, 2, -1, lanes).transpose(0, 2, 1, 3, 4)
    return split.reshape(t, 2, -1, lanes)


def member_rows(runs):
    g, t, y, x, c = axis_sizes()
    lanes = runs.shape[-1]
    split = runs.reshape(t, 2, x * c, -1, lanes).transpose(0, 2, 1, 3, 4)
    return split.reshape(t * x * c, -1, lanes)


def team_slices(values, parts):
    team = team_size()
    two, rows, columns = values.shape
    lanes = columns // (parts * team)
    split = values.reshape(two, rows, parts, team, lanes).transpose(3, 0, 1, 2, 4)
    return split.reshape(team, two * rows, parts * lanes)


def whole_columns(received, parts):
    team, two_rows, lanes = received.shape
    split = received.reshape(team, 2, two_rows // 2, parts, lanes // parts)
    return split.transpose(1, 2, 3, 0, 4).reshape(2, two_rows // 2, team * lanes)


def team_first(values):
    g, t, y, x, c = axis_sizes()
    rows = values.shape[0]
    split = values.reshape(rows, -1, g, t, y, x, c, values.shape[1] // (2 * g * t * y * x * c))
    return split.transpose(3, 5, 6, 0, 1, 2, 4, 7)


def permuted_columns(values):
    g, t, y, x, c = axis_sizes()
    split = values.reshape(values.shape[0], g, t, y, x, c, -1)
    return split.transpose(0, 2, 4, 5, 1, 3, 6).reshape(values.shape)


def restored_columns(values):
    g, t, y, x, c = axis_sizes()
    split = values.reshape(values.shape[0], t, x, c, g, y, -1)
    return split.transpose(0, 4, 1, 5, 2, 3, 6).reshape(values.shape)


def padded_rows(values, rows):
    blocks = values.shape[0]
    flat = values.reshape(blocks, -1)
    return jnp.pad(flat, ((0, 0), (0, rows * LANES - flat.shape[1]))).reshape(blocks, rows, LANES)


def row_count(items):
    return -(-items // LANES)


def bank_filters(turned, bank, bank_cols):
    taps = [
        [width * EMBED for width, first, count in bank_specs for _ in range(count)]
        for bank_specs in bank_plan(bank_cols)
    ]
    taps = [row + [0] * (bank_cols - len(row)) for row in taps]
    limit = lax.dynamic_index_in_dim(jnp.asarray(taps, jnp.int32), bank, 0, False)
    turned = turned.T
    row = lax.broadcasted_iota(jnp.int32, (TAPS, 1), 0)
    kernel = jnp.where(row < limit[None, :], turned[:TAPS], 0.0)
    bias = jnp.where(limit > 0, turned[TAPS], 0.0)
    return (kernel.reshape(1, WIDEST, EMBED, bank_cols), bias[None])


def shards(
    char_ids,
    resets,
    out_grad,
    char_table,
    conv_weight,
    conv_bias,
    highway_weight,
    highway_bias,
    proj_weight,
    proj_bias,
    lstm_weight,
    lstm_bias,
    lstm_proj,
):
    f32, bf16 = jnp.float32, jnp.bfloat16
    own, steps = resets.shape
    team = team_size()
    place = team_place()
    devices = team * lax.axis_size("g") * lax.axis_size("y")
    bank_cols = conv_weight.shape[3]
    highway_rows = highway_weight.shape[1]
    features_all = highway_rows * devices
    part = features_all // team
    lstm_rows = lstm_weight.shape[1]
    width = proj_weight.shape[1]
    cells_all = lstm_proj.shape[1]
    cells = cells_all // team

    conv_own = jnp.concatenate([conv_weight.reshape(-1, bank_cols), conv_bias], axis=0)
    banks = lax.axis_size("x") * lax.axis_size("c")
    conv_all = lax.all_to_all(
        jnp.broadcast_to(conv_own[None], (banks,) + conv_own.shape),
        ("x", "c"),
        split_axis=0,
        concat_axis=0,
        tiled=True,
    )
    conv_weight_all = conv_all[:, :-1].reshape((banks,) + conv_weight.shape[1:])
    conv_bias_all = conv_all[:, -1]
    sizes = [highway_bias.size, proj_bias.size, lstm_bias.size, resets.size]
    small = jnp.concatenate(
        [
            highway_bias.reshape(-1),
            proj_bias.reshape(-1),
            lstm_bias.reshape(-1),
            resets.astype(bf16).reshape(-1),
        ]
    )
    small_all = lax.all_to_all(
        jnp.broadcast_to(small[None], (devices, small.size)),
        EVERY,
        split_axis=0,
        concat_axis=0,
        tiled=True,
    )
    cut = [sum(sizes[:k]) for k in range(5)]
    highway_bias_all = small_all[:, cut[0] : cut[1]].reshape(devices, 2, -1)
    highway_bias_all = highway_bias_all.transpose(1, 0, 2).reshape(2, 2 * features_all)
    highway_bias_all = team_first(highway_bias_all).reshape(team, 2, 2 * part)
    proj_bias_all = small_all[:, cut[1] : cut[2]].reshape(-1).astype(f32)
    lstm_bias_all = small_all[:, cut[2] : cut[3]].reshape(devices, 2, -1)
    lstm_bias_all = lstm_bias_all.transpose(1, 0, 2).reshape(2, 4, team, cells)
    resets_all = small_all[:, cut[3] : cut[4]].reshape(
        lax.axis_size("g"), lax.axis_size("t"), lax.axis_size("y"), -1, own, steps
    )
    resets_team = lax.dynamic_index_in_dim(resets_all, lax.axis_index("g"), 0, False)
    resets_team = lax.dynamic_index_in_dim(resets_team, lax.axis_index("y"), 1, False)
    resets_team = resets_team.reshape(team * own, steps).astype(f32)
    highway_bias_own = lax.dynamic_index_in_dim(highway_bias_all, place, 0, False).astype(f32)
    lstm_bias_own = lax.dynamic_index_in_dim(lstm_bias_all, place, 2, False)
    lstm_bias_own = lstm_bias_own.reshape(2, 1, 4 * cells).astype(f32)

    highway_slices = team_first(highway_weight.reshape(2 * highway_rows, -1))
    turned_rows = lstm_proj.shape[2]
    gate_slices = lstm_weight.reshape(2, lstm_rows, 4, team, cells).transpose(3, 0, 2, 1, 4)
    swapped = swap_team(
        jnp.concatenate(
            [
                highway_slices.reshape(team, 2 * highway_rows, 2 * part),
                gate_slices.reshape(team, 8 * lstm_rows, cells),
                team_slices(jnp.swapaxes(lstm_proj, 1, 2), 1),
            ],
            axis=1,
        )
    )
    ends = [2 * highway_rows, 2 * highway_rows + 8 * lstm_rows]
    block = jnp.concatenate([swapped[:, : ends[0]].reshape(-1, 2 * part), proj_weight], axis=0)
    t, x, c = lax.axis_size("t"), lax.axis_size("x"), lax.axis_size("c")
    lstm_block = (
        swapped[:, ends[0] : ends[1]]
        .reshape(t, x * c, 8, lstm_rows, cells)
        .transpose(0, 2, 1, 3, 4)
        .reshape(t * 8, x * c * lstm_rows, cells)
    )
    turned_block = run_rows(swapped[:, ends[1] :])
    cut_rows = team * 2 * highway_rows
    grid = lax.axis_size("g") * lax.axis_size("y")
    bank = lax.axis_index("x") * lax.axis_size("c") + lax.axis_index("c")
    own_ids = lax.dynamic_slice_in_dim(char_ids, bank * own, own, axis=0)
    own_ids = jnp.swapaxes(own_ids, 0, 1).reshape(own * steps, char_ids.shape[2])
    filters, counts = filter_matrix(conv_weight_all, conv_bias_all)
    tight_from = wide_columns(bank_cols)
    padded_ids, tiled = embed_tokens(own_ids, char_table)

    tokens = own * steps
    (
        pooled_lse,
        first_all,
        lstm_own,
        turned_own,
        first,
        second,
        mixed,
        hidden,
        top_own,
        lin_all,
    ) = run_highway(
        tight_from,
        tiled,
        filters,
        counts,
        block,
        lstm_block,
        turned_block,
        highway_bias_own,
        proj_bias_all[None],
    )
    lstm_own = lstm_own.reshape(grid, t, 2, 4, x * c * lstm_rows, cells)

    keep_forward = 1.0 - resets_team
    keep_backward = 1.0 - jnp.concatenate(
        [resets_team[:, 1:], jnp.zeros((team * own, 1), f32)], axis=1
    )
    keep = jnp.stack([keep_forward.T, keep_backward.T])[..., None]
    grad_time = out_grad.reshape(own, steps, 2, width).transpose(2, 1, 0, 3)
    grad_lin_all, lstm_grads, turned_grads, bias_sums = run_lstm(
        lin_all.reshape(team, steps, own, width),
        grad_time,
        lstm_own,
        turned_own,
        lstm_bias_own,
        keep,
    )
    turned_summed = lax.all_to_all(turned_grads, GRID, split_axis=0, concat_axis=0, tiled=True)
    turned_summed = turned_summed.astype(f32).sum(axis=0).astype(bf16)
    grad_input = lax.dynamic_index_in_dim(grad_lin_all, place, 0, False).reshape(tokens, width)
    grad_project_b = column_sum(grad_input)
    grad_features, first_parts, highway_bias_sums, lstm_summed = run_highway_back(
        grad_lin_all.reshape(team, tokens, width),
        first_all,
        first,
        second,
        mixed,
        hidden,
        top_own,
        lstm_grads.reshape(grid, 8, -1, 4 * cells),
    )
    lstm_summed = lstm_summed.reshape(t, 2, -1, 4 * cells)
    turned_summed, grad_features = lax.optimization_barrier((turned_summed, grad_features))
    turned_grad = whole_columns(swap_team(member_rows(turned_summed)), 1).astype(f32)
    lstm_proj_grad = jnp.swapaxes(turned_grad, 1, 2)
    g, t, y, x, c = axis_sizes()

    def own_place(values, parts):
        lanes = values.shape[-1] // parts
        split = values.reshape(2, parts, 1, lanes)
        full = jnp.zeros((2, parts, team, lanes), f32)
        return lax.dynamic_update_slice(full, split, (0, 0, place, 0)).reshape(2, -1)

    lstm_bias_parts = own_place(bias_sums[:, 0], 4)
    highway_bias_parts = own_place(highway_bias_sums[:, 0], 2)
    highway_bias_parts = (
        highway_bias_parts.reshape(2, 2, t, x, c, g, y, -1)
        .transpose(0, 1, 5, 2, 6, 3, 4, 7)
        .reshape(2, 2 * features_all)
    )
    biases = jnp.concatenate(
        [
            lstm_bias_parts.reshape(2, devices, -1).transpose(1, 0, 2).reshape(devices, -1),
            highway_bias_parts.reshape(2, devices, -1).transpose(1, 0, 2).reshape(devices, -1),
            grad_project_b.reshape(devices, -1),
        ],
        axis=1,
    )
    bank_counts = [sum(item[2] for item in specs) for specs in bank_plan(bank_cols)]
    bias_rows = -(-row_count(biases.shape[1]) // 16) * 16
    highway_weight_grad, project_grad, mine, conv_sums, table_sums = run_final(
        tight_from,
        bank_counts,
        first_parts,
        tiled,
        padded_ids.reshape(-1, math.gcd(tokens, TOKEN_BLOCK) * PLACES),
        filters,
        counts,
        pooled_lse,
        grad_features,
        padded_rows(biases, bias_rows).astype(bf16),
        2 * highway_rows,
    )
    lstm_returned = swap_team(member_rows(lstm_summed))
    lstm_weight_grad = pack_columns(lstm_returned, 4).reshape(2, lstm_rows, -1)
    highway_weight_grad = highway_weight_grad.reshape(2, highway_rows, -1)
    mine_biases = mine.reshape(-1)
    ends = [2 * lstm_bias.shape[1], 2 * lstm_bias.shape[1] + 2 * highway_bias.shape[1]]
    lstm_bias_grad = mine_biases[: ends[0]].reshape(2, -1)
    highway_bias_grad = mine_biases[ends[0] : ends[1]].reshape(2, -1)
    proj_bias_grad = mine_biases[ends[1] : ends[1] + proj_bias.size]
    grad_kernel, grad_bias = bank_filters(conv_sums, bank, bank_cols)
    grad_table = table_sums[: char_table.shape[0], :EMBED]
    return (
        grad_table,
        grad_kernel,
        grad_bias,
        highway_weight_grad,
        highway_bias_grad,
        project_grad,
        proj_bias_grad,
        lstm_weight_grad,
        lstm_bias_grad,
        lstm_proj_grad,
    )


def solution(mesh):
    dp, bank = mesh.shape["dp"], mesh.shape["bank"]
    fine = Mesh(mesh.devices.reshape(dp // 4, 2, 2, bank // 2, 2), EVERY)
    rows, banks = ("g", "t", "y"), ("x", "c")
    whole = rows + banks
    placed = (
        P(rows, None, None),
        P(whole, None),
        P(whole, None, None),
        P(),
        P(banks, None, None, None),
        P(banks, None),
        P(None, whole, None),
        P(None, whole),
        P(whole, None),
        P(whole),
        P(None, whole, None),
        P(None, whole),
        P(None, None, whole),
    )
    return jax.shard_map(
        shards,
        mesh=fine,
        in_specs=placed,
        out_specs=(
            P(),
            P(banks, None, None, None),
            P(banks, None),
            P(None, whole, None),
            P(None, whole),
            P(whole, None),
            P(whole),
            P(None, whole, None),
            P(None, whole),
            P(None, None, whole),
        ),
        check_vma=False,
    )
```

```python
from functools import partial
import math

import jax
import jax.numpy as jnp
from jax import lax
from jax.experimental import pallas as pl
from jax.experimental.pallas import tpu as pltpu
from jax.sharding import Mesh, PartitionSpec as P

CHAR_COUNT = 50
VOCAB = 262
EMBED = 16
WIDEST = 7
TAPS = WIDEST * EMBED
LANES = 128
PLACES = 64
TIGHT = 48
CHUNK = 256
TOKEN_BLOCK = 16
AHEAD = 6


def bank_plan(bank_cols):
    return [
        [
            (1, 0, bank_cols // 32),
            (2, bank_cols // 32, bank_cols // 32),
            (3, bank_cols // 16, bank_cols // 16),
            (4, bank_cols // 8, bank_cols // 8),
        ],
        [(5, 0, bank_cols // 4)],
        [(6, 0, bank_cols // 2)],
        [(7, 0, bank_cols)],
    ]


def transposed(former, latter):
    return lax.dot_general(
        former, latter, (((1,), (1,)), ((), ())), preferred_element_type=jnp.float32
    )


def outer_sum(former, latter):
    return lax.dot_general(
        former, latter, (((0,), (0,)), ((), ())), preferred_element_type=jnp.float32
    )


def column_sum(values):
    ones_row = jnp.ones((1, values.shape[0]), values.dtype)
    return jnp.dot(ones_row, values, preferred_element_type=jnp.float32)[0]


def filter_columns(bank_cols):
    columns = []
    for bank_index, bank_specs in enumerate(bank_plan(bank_cols)):
        for filter_width, first_col, count in bank_specs:
            columns.append((filter_width, bank_index, first_col, count))
    return columns


def shift_rows(values, amount):
    count = values.shape[0]
    return values if amount % count == 0 else pltpu.roll(values, amount % count, 0)


def block_windows(tiled_ref, windows_wide, windows_tight):
    tokens, places, lanes = tiled_ref.shape
    rows = tokens * places
    tiled = tiled_ref[...].astype(jnp.float32).reshape(rows, lanes)
    lane = lax.broadcasted_iota(jnp.int32, (rows, lanes), 1)
    place = lax.broadcasted_iota(jnp.int32, (rows, lanes), 0) % places
    windows = tiled
    for offset in range(1, WIDEST):
        windows = jnp.where(lane // EMBED == offset, shift_rows(tiled, rows - offset), windows)
    late = place >= CHAR_COUNT - WIDEST + 1 + (lane - TAPS - 1)
    extra = jnp.where((lane == TAPS) | ((lane <= TAPS + WIDEST) & late), 1.0, 0.0)
    windows = jnp.where(lane < TAPS, windows, extra)
    windows_wide[...] = windows.astype(jnp.bfloat16)
    windows_tight[...] = (
        windows.reshape(tokens, places, lanes)[:, :TIGHT]
        .reshape(tokens * TIGHT, lanes)
        .astype(jnp.bfloat16)
    )


def column_chunks(total, tight_from):
    return [
        (start, start < tight_from) for start in range(0, total, CHUNK)
    ]


def pool_kernel(tight_from, tiled_ref, weight_ref, count_ref, features_ref, lse_ref, wide, tight):
    tokens, places, lanes = tiled_ref.shape
    block_windows(tiled_ref, wide, tight)
    for start, is_wide in column_chunks(weight_ref.shape[1], tight_from):
        cols = pl.ds(start, CHUNK)
        windows = wide if is_wide else tight
        conv_out = jnp.dot(
            windows[...], weight_ref[:, cols], preferred_element_type=jnp.float32
        ).reshape(tokens, -1, CHUNK)
        highest = jnp.max(conv_out, axis=1)
        total = jnp.sum(jnp.exp(conv_out - highest[:, None, :]), axis=1)
        pooled_lse = highest + jnp.log(total)
        lse_ref[:, cols] = pooled_lse
        pooled_pre = pooled_lse - count_ref[0:1, cols]
        features_ref[:, cols] = (pooled_pre * jax.nn.sigmoid(pooled_pre)).astype(jnp.bfloat16)


def pool_grad_block(
    tight_from,
    tiled_ref,
    ids_row,
    weight_ref,
    count_ref,
    lse_ref,
    upstream_ref,
    grad_weight_ref,
    table_ref,
    wide,
    tight,
    spread,
):
    tokens, places, lanes = tiled_ref.shape
    block_windows(tiled_ref, wide, tight)
    spread[...] = jnp.zeros_like(spread)
    wide_turned = wide[...].T
    tight_turned = tight[...].T
    for start, is_wide in column_chunks(weight_ref.shape[1], tight_from):
        cols = pl.ds(start, CHUNK)
        windows, turned = (wide, wide_turned) if is_wide else (tight, tight_turned)
        weights = weight_ref[:, cols]
        conv_out = jnp.dot(
            windows[...], weights, preferred_element_type=jnp.float32
        ).reshape(tokens, -1, CHUNK)
        pooled_lse = lse_ref[:, cols]
        pooled_pre = pooled_lse - count_ref[0:1, cols]
        squashed = jax.nn.sigmoid(pooled_pre)
        upstream = (
            upstream_ref[:, cols].astype(jnp.float32)
            * squashed
            * (1.0 + pooled_pre * (1.0 - squashed))
        )
        softened = jnp.exp(conv_out - pooled_lse[:, None, :])
        grad_conv = (softened * upstream[:, None, :]).astype(jnp.bfloat16)
        places_here = grad_conv.shape[1]
        grad_conv = grad_conv.reshape(tokens * places_here, CHUNK)
        grad_weight_ref[:, cols] += jnp.dot(turned, grad_conv, preferred_element_type=jnp.float32)
        part = lax.dot_general(
            grad_conv, weights, (((1,), (1,)), ((), ())), preferred_element_type=jnp.float32
        ).reshape(tokens, places_here, lanes)
        spread[:, :places_here, :] += part
    rows = tokens * places
    flat = spread[...].reshape(rows, lanes)
    lane = lax.broadcasted_iota(jnp.int32, (rows, lanes), 1)
    aligned = jnp.where(lane < EMBED, flat, 0.0)
    for offset in range(1, WIDEST):
        aligned = jnp.where(lane // EMBED == offset, shift_rows(flat, offset), aligned)
    high = aligned.astype(jnp.bfloat16)
    low = (aligned - high.astype(jnp.float32)).astype(jnp.bfloat16)
    vocab = table_ref.shape[0]
    selector = jnp.where(
        lax.broadcasted_iota(jnp.int32, (vocab, rows), 0) == ids_row, 1.0, 0.0
    ).astype(jnp.bfloat16)
    table_ref[...] += jnp.dot(selector, high, preferred_element_type=jnp.float32) + jnp.dot(
        selector, low, preferred_element_type=jnp.float32
    )


def filter_matrix(conv_weight, conv_bias):
    bank_cols = conv_bias.shape[1]
    taps, biases, masks, counts = [], [], [], []
    for filter_width, bank_index, first_col, count in filter_columns(bank_cols):
        piece = conv_weight[bank_index, :filter_width, :, first_col : first_col + count]
        piece = piece.reshape(filter_width * EMBED, count)
        taps.append(jnp.pad(piece, ((0, TAPS - filter_width * EMBED), (0, 0))))
        biases.append(conv_bias[bank_index, first_col : first_col + count])
        rows = lax.broadcasted_iota(jnp.int32, (LANES - TAPS - 1, count), 0)
        masks.append(jnp.where(rows == WIDEST - filter_width, -1e30, 0.0).astype(jnp.bfloat16))
        counts.append(jnp.full((8, count), math.log(CHAR_COUNT - filter_width + 1), jnp.float32))
    weights = jnp.concatenate(
        [
            jnp.concatenate(taps, axis=1),
            jnp.concatenate(biases)[None],
            jnp.concatenate(masks, axis=1),
        ],
        axis=0,
    )
    return (weights, jnp.concatenate(counts, axis=1))


def wide_columns(bank_cols):
    total = sum(count for width, bank, first, count in filter_columns(bank_cols) if CHAR_COUNT - width + 1 > TIGHT - 2)
    return -(-total // CHUNK) * CHUNK


def char_selector(token_ids, vocab_size):
    return token_ids.reshape(-1)[:, None] == lax.broadcasted_iota(jnp.int32, (1, vocab_size), 1)


def embed_tokens(token_ids, char_table):
    tokens = token_ids.shape[0]
    padded = jnp.pad(token_ids, ((0, 0), (0, PLACES - token_ids.shape[1])), constant_values=-1)
    table_tiled = jnp.pad(jnp.tile(char_table, (1, WIDEST)), ((0, 0), (0, LANES - TAPS)))
    selector = char_selector(padded, char_table.shape[0]).astype(jnp.bfloat16)
    tiled = jnp.dot(selector, table_tiled, preferred_element_type=jnp.float32)
    tiled = tiled.astype(jnp.bfloat16).reshape(tokens, PLACES, LANES)
    return (padded, tiled)


TEAM = ("t", "x", "c")
GRID = ("g", "y")
EVERY = ("g", "t", "y", "x", "c")


def team_place():
    x_size, c_size = lax.axis_size("x"), lax.axis_size("c")
    return (lax.axis_index("t") * x_size + lax.axis_index("x")) * c_size + lax.axis_index("c")


def team_size():
    return lax.axis_size("t") * lax.axis_size("x") * lax.axis_size("c")


def team_coords(place):
    x_size, c_size = lax.axis_size("x"), lax.axis_size("c")
    return {
        "t": place // (x_size * c_size),
        "x": lax.rem(place // c_size, x_size),
        "c": lax.rem(place, c_size),
    }


def swap_team(values):
    return lax.all_to_all(values, TEAM, split_axis=0, concat_axis=0, tiled=True)


def share_team(values):
    team = team_size()
    return swap_team(jnp.broadcast_to(values[None], (team,) + values.shape))


def sigmoid(values):
    return 0.5 * jnp.tanh(0.5 * values) + 0.5


def wait_bytes(ref, sem):
    pltpu.make_async_copy(ref, ref, sem).wait()


def lstm_kernel(
    team,
    lin_ref,
    out_grad_ref,
    weight_hbm,
    turned_hbm,
    bias_ref,
    keep_ref,
    grad_lin_all_ref,
    grad_weight_hbm,
    grad_turned_hbm,
    grad_bias_ref,
    weight_ref,
    proj_ref,
    grad_gates_ref,
    lin_all_ref,
    state_ref,
    full_ref,
    grad_proj_ref,
    gates,
    cell_start,
    projected,
    stage,
    received,
    received_back,
    grad_cell,
    grad_lin_sum,
    stage_lin,
    received_lin,
    grad_state_own,
    grad_stage,
    turned_stage,
    load_sems,
    lin_sems,
    send_sems,
    sum_sems,
    share_send_sems,
    share_sems,
    out_sems,
):
    _, steps, own, width = lin_ref.shape
    group = team * own
    cells = proj_ref.shape[2]
    row_block = 32
    place = team_place()
    own_rows = pl.ds(pl.multiple_of(place * own, own), own)
    peers = [lax.rem(place + k, team) for k in range(1, team)]
    last = steps - 1
    others = pl.ds(0, team - 1)
    other_rows = pl.ds(0, (team - 1) * own)
    g_size, y_size = lax.axis_size("g"), lax.axis_size("y")
    t_size = lax.axis_size("t")
    blocks = [
        (g * y_size + y, t, (g * t_size + t) * y_size + y)
        for g in range(g_size)
        for t in range(t_size)
        for y in range(y_size)
    ]
    run = weight_hbm.shape[4]
    turned_run = turned_hbm.shape[3]

    for d in range(2):
        for source, t, at in blocks:
            for q in range(4):
                pltpu.make_async_copy(
                    weight_hbm.at[source, t, d, q],
                    weight_ref.at[d, pl.ds(at * run, run), pl.ds(q * cells, cells)],
                    load_sems.at[0],
                ).start()
            pltpu.make_async_copy(
                turned_hbm.at[source, t, d],
                proj_ref.at[d, pl.ds(at * turned_run, turned_run)],
                load_sems.at[1],
            ).start()

    barrier = pltpu.get_barrier_semaphore()
    for peer in peers:
        pl.semaphore_signal(
            barrier, inc=1, device_id=team_coords(peer), device_id_type=pl.DeviceIdType.MESH
        )
    pl.semaphore_wait(barrier, team - 1)

    def send(source, target, send_sem, recv_sem, peer):
        pltpu.make_async_remote_copy(
            src_ref=source,
            dst_ref=target,
            send_sem=send_sem,
            recv_sem=recv_sem,
            device_id=team_coords(peer),
            device_id_type=pl.DeviceIdType.MESH,
        ).start()

    for t in range(steps):
        lin_all_ref[t] = lin_ref[:, t].reshape(group, width)
    for d in range(2):
        first = 0 if d == 0 else last
        state_ref[d, first] = jnp.zeros((group, width), jnp.bfloat16)
        cell_start[d, first] = jnp.zeros((group, cells), jnp.float32)
        grad_cell[d] = jnp.zeros((group, cells), jnp.float32)
    grad_lin_sum[...] = jnp.zeros_like(grad_lin_sum)
    wait_bytes(weight_ref, load_sems.at[0])
    wait_bytes(proj_ref, load_sems.at[1])

    @pl.loop(0, steps)
    def _(t):
        for d in range(2):
            for q in range(4):
                cols = pl.ds(q * cells, cells)
                gates[d, t, :, cols] = (
                    jnp.dot(
                        lin_all_ref[t],
                        weight_ref[d, :width, cols],
                        preferred_element_type=jnp.float32,
                    )
                    + bias_ref[d, :, cols]
                )

    def time_of(d, s):
        return s if d == 0 else last - s

    @pl.loop(0, steps)
    def _(s):
        for d in range(2):
            t = time_of(d, s)
            later = time_of(d, jnp.minimum(s + 1, last))

            @pl.when(s > 0)
            def _():
                wait_bytes(
                    state_ref.at[d, t, other_rows], share_sems.at[0, d, s]
                )
                for q in range(4):
                    cols = pl.ds(q * cells, cells)
                    gates[d, t, :, cols] += jnp.dot(
                        state_ref[d, t],
                        weight_ref[d, width:, cols],
                        preferred_element_type=jnp.float32,
                    )

            @pl.loop(0, group // row_block)
            def _(block):
                rows = pl.ds(pl.multiple_of(block * row_block, row_block), row_block)
                in_gate = sigmoid(gates[d, t, rows, pl.ds(0, cells)])
                forget_gate = sigmoid(gates[d, t, rows, pl.ds(cells, cells)])
                candidate = jnp.tanh(gates[d, t, rows, pl.ds(2 * cells, cells)])
                out_gate = sigmoid(gates[d, t, rows, pl.ds(3 * cells, cells)])
                gates[d, t, rows, pl.ds(0, cells)] = in_gate
                gates[d, t, rows, pl.ds(cells, cells)] = forget_gate
                gates[d, t, rows, pl.ds(2 * cells, cells)] = candidate
                gates[d, t, rows, pl.ds(3 * cells, cells)] = out_gate
                mixed = forget_gate * cell_start[d, t, rows] + in_gate * candidate
                cell_new = 3.0 * jnp.tanh(mixed * (1.0 / 3.0))
                full_ref[d, t, rows] = (out_gate * jnp.tanh(cell_new)).astype(jnp.bfloat16)

                @pl.when(s < last)
                def _():
                    cell_start[d, later, rows] = cell_new * keep_ref[d, later, rows]

            @pl.when(s > 0)
            def _():
                wait_bytes(stage.at[d, others], send_sems.at[d])

            part = lax.dot_general(
                full_ref[d, t],
                proj_ref[d],
                (((1,), (1,)), ((), ())),
                preferred_element_type=jnp.float32,
            )
            part = part.astype(jnp.bfloat16).reshape(team, own, width)
            stage[d] = part
            received[d, s, place] = stage[d, place]
            for peer in peers:
                send(
                    stage.at[d, peer],
                    received.at[d, s, place],
                    send_sems.at[d],
                    sum_sems.at[0, d, s],
                    peer,
                )
        for d in range(2):
            t = time_of(d, s)
            later = time_of(d, jnp.minimum(s + 1, last))
            wait_bytes(received.at[d, s, others], sum_sems.at[0, d, s])
            total = jnp.sum(received[d, s].astype(jnp.float32), axis=0)
            projected[d, t] = total

            @pl.when(s > 0)
            def _():
                wait_bytes(
                    state_ref.at[d, t, other_rows], share_send_sems.at[0, d]
                )

            @pl.when(s < last)
            def _():
                state_new = (3.0 * jnp.tanh(total * (1.0 / 3.0))).astype(jnp.bfloat16)
                kept = state_new.astype(jnp.float32) * keep_ref[d, later, own_rows]
                state_ref[d, later, own_rows] = kept.astype(jnp.bfloat16)
                for peer in peers:
                    send(
                        state_ref.at[d, later, own_rows],
                        state_ref.at[d, later, own_rows],
                        share_send_sems.at[0, d],
                        share_sems.at[0, d, s + 1],
                        peer,
                    )

    @pl.loop(0, steps)
    def _(s):
        for d in range(2):
            t = time_of(1 - d, s)

            @pl.when(s > 0)
            def _():
                wait_bytes(
                    received_back.at[d, jnp.maximum(s - 1, 0), others],
                    sum_sems.at[1, d, jnp.maximum(s - 1, 0)],
                )
                grad_state_own[...] = jnp.sum(
                    received_back[d, jnp.maximum(s - 1, 0)].astype(jnp.float32), axis=0
                )

            @pl.when(s == 0)
            def _():
                grad_state_own[...] = jnp.zeros((own, width), jnp.float32)

            grad_state = grad_state_own[...] + out_grad_ref[d, t].astype(jnp.float32)
            squashed = jnp.tanh(projected[d, t] * (1.0 / 3.0))
            grad_proj_ref[d, t, own_rows] = (grad_state * (1.0 - squashed * squashed)).astype(
                jnp.bfloat16
            )
            for peer in peers:
                send(
                    grad_proj_ref.at[d, t, own_rows],
                    grad_proj_ref.at[d, t, own_rows],
                    share_send_sems.at[1, d],
                    share_sems.at[1, d, s],
                    peer,
                )
        for d in range(2):
            t = time_of(1 - d, s)
            wait_bytes(grad_proj_ref.at[d, t, other_rows], share_sems.at[1, d, s])
            wait_bytes(
                grad_proj_ref.at[d, t, other_rows], share_send_sems.at[1, d]
            )

            @pl.loop(0, group // row_block)
            def _(block):
                rows = pl.ds(pl.multiple_of(block * row_block, row_block), row_block)
                grad_full = jnp.dot(
                    grad_proj_ref[d, t, rows], proj_ref[d], preferred_element_type=jnp.float32
                )
                in_gate = gates[d, t, rows, pl.ds(0, cells)]
                forget_gate = gates[d, t, rows, pl.ds(cells, cells)]
                candidate = gates[d, t, rows, pl.ds(2 * cells, cells)]
                out_gate = gates[d, t, rows, pl.ds(3 * cells, cells)]
                start = cell_start[d, t, rows]
                clipped = jnp.tanh((forget_gate * start + in_gate * candidate) * (1.0 / 3.0))
                tanh_cell = jnp.tanh(3.0 * clipped)
                total = grad_cell[d, rows] + grad_full * out_gate * (1.0 - tanh_cell * tanh_cell)
                grad_raw = total * (1.0 - clipped * clipped)
                grad_gates_ref[d, t, rows, pl.ds(0, cells)] = (
                    grad_raw * candidate * in_gate * (1.0 - in_gate)
                ).astype(jnp.bfloat16)
                grad_gates_ref[d, t, rows, pl.ds(cells, cells)] = (
                    grad_raw * start * forget_gate * (1.0 - forget_gate)
                ).astype(jnp.bfloat16)
                grad_gates_ref[d, t, rows, pl.ds(2 * cells, cells)] = (
                    grad_raw * in_gate * (1.0 - candidate * candidate)
                ).astype(jnp.bfloat16)
                grad_gates_ref[d, t, rows, pl.ds(3 * cells, cells)] = (
                    grad_full * tanh_cell * out_gate * (1.0 - out_gate)
                ).astype(jnp.bfloat16)
                grad_cell[d, rows] = grad_raw * forget_gate * keep_ref[d, t, rows]

            wait_bytes(stage.at[d, others], send_sems.at[d])

            @pl.when(s < last)
            def _():
                part = (
                    lax.dot_general(
                        grad_gates_ref[d, t],
                        weight_ref[d, width:],
                        (((1,), (1,)), ((), ())),
                        preferred_element_type=jnp.float32,
                    )
                    * keep_ref[d, t]
                )
                stage[d] = part.astype(jnp.bfloat16).reshape(team, own, width)
                received_back[d, s, place] = stage[d, place]
                for peer in peers:
                    send(
                        stage.at[d, peer],
                        received_back.at[d, s, place],
                        send_sems.at[d],
                        sum_sems.at[1, d, s],
                        peer,
                    )

            grad_lin_sum[t] += lax.dot_general(
                grad_gates_ref[d, t],
                weight_ref[d, :width],
                (((1,), (1,)), ((), ())),
                preferred_element_type=jnp.float32,
            )

    for t in range(steps):
        stage_lin[:, t] = grad_lin_sum[t].astype(jnp.bfloat16).reshape(team, own, width)
    received_lin[place] = stage_lin[place]
    for peer in peers:
        send(stage_lin.at[peer], received_lin.at[place], lin_sems.at[4], lin_sems.at[5], peer)

    count = steps * group
    half_blocks = len(blocks) // 2

    def weight_grads(d):
        for half in range(2):

            @pl.loop(0, 4)
            def _(q):
                cols = pl.ds(pl.multiple_of(q * cells, cells), cells)
                slot = lax.rem(q, 2)
                rows_in = (lin_all_ref[...] if half == 0 else state_ref[d]).reshape(count, width)
                gate_part = grad_gates_ref[d, :, :, cols].reshape(count, cells)
                part = lax.dot_general(
                    rows_in,
                    gate_part,
                    (((0,), (0,)), ((), ())),
                    preferred_element_type=jnp.float32,
                )

                @pl.when(q >= 2)
                def _():
                    wait_bytes(grad_stage.at[slot], out_sems.at[slot])

                grad_stage[slot] = part.astype(jnp.bfloat16)
                for source, t, at in blocks[half * half_blocks : (half + 1) * half_blocks]:
                    pltpu.make_async_copy(
                        grad_stage.at[slot, pl.ds((at - half * half_blocks) * run, run)],
                        grad_weight_hbm.at[source, t, d, :, cols],
                        out_sems.at[slot],
                    ).start()

            for slot in range(2):
                wait_bytes(grad_stage.at[slot], out_sems.at[slot])
        turned = lax.dot_general(
            grad_proj_ref[d].reshape(count, width),
            full_ref[d].reshape(count, cells),
            (((0,), (0,)), ((), ())),
            preferred_element_type=jnp.float32,
        )
        turned_stage[d] = turned.astype(jnp.bfloat16)
        for source, t, at in blocks:
            pltpu.make_async_copy(
                turned_stage.at[d, pl.ds(at * turned_run, turned_run)],
                grad_turned_hbm.at[source, t, d],
                out_sems.at[2 + d],
            ).start()
        ones = jnp.ones((8, count), jnp.bfloat16)
        for q in range(4):
            cols = pl.ds(q * cells, cells)
            grad_bias_ref[d, :, cols] = jnp.dot(
                ones,
                grad_gates_ref[d, :, :, cols].reshape(count, cells),
                preferred_element_type=jnp.float32,
            )

    weight_grads(0)
    wait_bytes(received_lin.at[others], lin_sems.at[5])
    grad_lin_all_ref[place] = jnp.sum(received_lin[...].astype(jnp.float32), axis=0).astype(
        jnp.bfloat16
    )
    for peer in peers:
        send(
            grad_lin_all_ref.at[place],
            grad_lin_all_ref.at[place],
            lin_sems.at[6],
            lin_sems.at[7],
            peer,
        )
    weight_grads(1)
    wait_bytes(grad_lin_all_ref.at[others], lin_sems.at[7])
    wait_bytes(stage_lin.at[others], lin_sems.at[4])
    wait_bytes(grad_lin_all_ref.at[others], lin_sems.at[6])
    for d in range(2):
        wait_bytes(turned_stage.at[d], out_sems.at[2 + d])


def run_lstm(lin, out_grad, weights, turned, bias, keep):
    team, steps, own, width = lin.shape
    group = team * own
    cells = turned.shape[4]
    bf16, f32 = jnp.bfloat16, jnp.float32
    vmem = pl.BlockSpec(memory_space=pltpu.VMEM)
    hbm = pl.BlockSpec(memory_space=pl.ANY)
    return pl.pallas_call(
        partial(lstm_kernel, team),
        in_specs=[vmem, vmem, hbm, hbm, vmem, vmem],
        out_specs=[vmem, hbm, hbm, vmem],
        out_shape=[
            jax.ShapeDtypeStruct(lin.shape, bf16),
            jax.ShapeDtypeStruct(weights.shape[:3] + (weights.shape[4], 4 * cells), bf16),
            jax.ShapeDtypeStruct(turned.shape, bf16),
            jax.ShapeDtypeStruct((2, 8, 4 * cells), f32),
        ],
        scratch_shapes=[
            pltpu.VMEM((2, 2 * width, 4 * cells), bf16),
            pltpu.VMEM((2, width, cells), bf16),
            pltpu.VMEM((2, steps, group, 4 * cells), bf16),
            pltpu.VMEM((steps, group, width), bf16),
            pltpu.VMEM((2, steps, group, width), bf16),
            pltpu.VMEM((2, steps, group, cells), bf16),
            pltpu.VMEM((2, steps, group, width), bf16),
            pltpu.VMEM((2, steps, group, 4 * cells), f32),
            pltpu.VMEM((2, steps, group, cells), f32),
            pltpu.VMEM((2, steps, own, width), f32),
            pltpu.VMEM((2, team, own, width), bf16),
            pltpu.VMEM((2, steps, team, own, width), bf16),
            pltpu.VMEM((2, steps, team, own, width), bf16),
            pltpu.VMEM((2, group, cells), f32),
            pltpu.VMEM((steps, group, width), f32),
            pltpu.VMEM((team, steps, own, width), bf16),
            pltpu.VMEM((team, steps, own, width), bf16),
            pltpu.VMEM((own, width), f32),
            pltpu.VMEM((2, width, cells), bf16),
            pltpu.VMEM((2, width, cells), bf16),
            pltpu.SemaphoreType.DMA((2,)),
            pltpu.SemaphoreType.DMA((8,)),
            pltpu.SemaphoreType.DMA((2,)),
            pltpu.SemaphoreType.DMA((2, 2, steps)),
            pltpu.SemaphoreType.DMA((2, 2)),
            pltpu.SemaphoreType.DMA((2, 2, steps)),
            pltpu.SemaphoreType.DMA((4,)),
        ],
        compiler_params=pltpu.CompilerParams(
            collective_id=1, has_side_effects=True, vmem_limit_bytes=63 * 1024 * 1024
        ),
        name="lstm_team",
    )(lin, out_grad, weights, turned, bias, keep)


def member_at(offset):
    t_size, x_size, c_size = lax.axis_size("t"), lax.axis_size("x"), lax.axis_size("c")
    dt, dx, dc = offset // (x_size * c_size), lax.rem(offset // c_size, x_size), lax.rem(offset, c_size)
    t = lax.rem(lax.axis_index("t") + dt, t_size)
    x = lax.rem(lax.axis_index("x") + dx, x_size)
    c = lax.rem(lax.axis_index("c") + dc, c_size)
    return (t * x_size + x) * c_size + c


def opposite(offset):
    t_size, x_size, c_size = lax.axis_size("t"), lax.axis_size("x"), lax.axis_size("c")
    dt, dx, dc = offset // (x_size * c_size), offset // c_size % x_size, offset % c_size
    return (-dt % t_size * x_size + -dx % x_size) * c_size + -dc % c_size


def send_block(source, target, send_sem, recv_sem, peer):
    pltpu.make_async_remote_copy(
        src_ref=source,
        dst_ref=target,
        send_sem=send_sem,
        recv_sem=recv_sem,
        device_id=team_coords(peer),
        device_id_type=pl.DeviceIdType.MESH,
    ).start()


def greet(offsets, with_grid=False):
    barrier = pltpu.get_barrier_semaphore()
    for offset in offsets:
        pl.semaphore_signal(
            barrier,
            inc=1,
            device_id=team_coords(member_at(offset)),
            device_id_type=pl.DeviceIdType.MESH,
        )
    extra = greet_grid(barrier) if with_grid else 0
    pl.semaphore_wait(barrier, len(offsets) + extra)


def load_level(first_hbm, weights, level, run, sem):
    grid = first_hbm.shape[0]
    team = team_size()

    @pl.loop(0, team)
    def _(member):
        for block in range(grid):
            pltpu.make_async_copy(
                first_hbm.at[
                    block, pl.ds(pl.multiple_of((level * team + member) * run, run), run)
                ],
                weights.at[level, pl.ds(pl.multiple_of((member * grid + block) * run, run), run)],
                sem,
            ).start()


def load_project(first_hbm, project, sem):
    grid = first_hbm.shape[0]
    run = project.shape[0] // grid
    for block in range(grid):
        pltpu.make_async_copy(
            first_hbm.at[block, pl.ds(team_size() * 2 * run, run)],
            project.at[pl.ds(block * run, run)],
            sem,
        ).start()


def grid_coords(dg, dy):
    g_size, y_size = lax.axis_size("g"), lax.axis_size("y")
    return {
        "g": lax.rem(lax.axis_index("g") + dg, g_size),
        "y": lax.rem(lax.axis_index("y") + dy, y_size),
    }


def grid_block(dg, dy):
    coords = grid_coords(dg, dy)
    return coords["g"] * lax.axis_size("y") + coords["y"]


def send_grid(source, target, send_sem, recv_sem, dg, dy):
    pltpu.make_async_remote_copy(
        src_ref=source,
        dst_ref=target,
        send_sem=send_sem,
        recv_sem=recv_sem,
        device_id=grid_coords(dg, dy),
        device_id_type=pl.DeviceIdType.MESH,
    ).start()


def greet_grid(barrier):
    for dg in range(1, lax.axis_size("g")):
        pl.semaphore_signal(
            barrier, inc=1, device_id=grid_coords(dg, 0), device_id_type=pl.DeviceIdType.MESH
        )
    pl.semaphore_signal(
        barrier, inc=1, device_id=grid_coords(0, 1), device_id_type=pl.DeviceIdType.MESH
    )
    return lax.axis_size("g")


class Gather:
    def __init__(self, blocks, targets, send_sem, recv_sems):
        self.blocks = blocks
        self.targets = targets
        self.send_sem = send_sem
        self.recv_sems = recv_sems

    def start(self, pieces):
        home = grid_block(0, 0)
        g_size = lax.axis_size("g")
        for piece in pieces:
            source = self.blocks[piece]
            target = self.targets[piece](home)
            for dg in range(1, g_size):
                send_grid(
                    source, target, self.send_sem, self.recv_sems.at[piece, g_size - dg, 0], dg, 0
                )
            send_grid(source, target, self.send_sem, self.recv_sems.at[piece, 0, 1], 0, 1)

    def forward(self, pieces):
        for piece in pieces:
            for dg in range(1, lax.axis_size("g")):
                target = self.targets[piece](grid_block(dg, 0))
                wait_bytes(target, self.recv_sems.at[piece, dg, 0])
                send_grid(target, target, self.send_sem, self.recv_sems.at[piece, dg, 1], 0, 1)

    def finish(self, pieces):
        for piece in pieces:
            for dg in range(lax.axis_size("g")):
                wait_bytes(self.targets[piece](grid_block(dg, 1)), self.recv_sems.at[piece, dg, 1])

    def sent(self, pieces):
        for piece in pieces:
            for _ in range(2 * lax.axis_size("g") - 1):
                wait_bytes(self.blocks[piece], self.send_sem)


def highway_kernel(
    tight_from,
    direct,
    tiled_ref,
    filter_ref,
    count_ref,
    block_hbm,
    lstm_block_hbm,
    turned_block_hbm,
    bias_ref,
    lin_bias_ref,
    lse_ref,
    first_hbm,
    lstm_hbm,
    turned_hbm,
    first_ref,
    second_ref,
    mixed_ref,
    hidden_ref,
    top_ref,
    lin_ref,
    parts,
    parts_recv,
    features_own,
    wide,
    tight,
    weights,
    project,
    load_sems,
    send_sems,
    first_sems,
    second_sems,
    gather_send_sems,
    block_sems,
    turned_sems,
    lstm_sems,
    lin_sems,
    swap_sems,
):
    team, tokens, features = first_ref.shape
    part = features // team
    cores = lax.axis_size("c")
    g_size, y_size = lax.axis_size("g"), lax.axis_size("y")
    place = team_place()
    sibling = member_at(1)
    near = list(range(cores, team, cores))
    chips = team // cores
    chunks = lstm_hbm.shape[1]
    greet(list(range(1, team)) if direct else [1] + near, True)
    home = grid_block(0, 0)
    run = project.shape[0] // first_hbm.shape[0]
    quarter = team * run // 4
    places = [pl.ds(k * quarter, quarter) for k in range(8)] + [pl.ds(8 * quarter, run)]
    block_gather = Gather(
        [block_hbm.at[rows] for rows in places],
        [lambda at, rows=rows: first_hbm.at[at, rows] for rows in places],
        gather_send_sems.at[0],
        block_sems,
    )
    turned_gather = Gather(
        [turned_hbm.at[home]],
        [lambda at: turned_hbm.at[at]],
        gather_send_sems.at[1],
        turned_sems,
    )
    all_places = list(range(len(places)))
    block_gather.start(all_places[:4])
    pltpu.make_async_copy(block_hbm, first_hbm.at[home], load_sems.at[3]).start()
    over_x = cores
    over_t = lax.axis_size("x") * cores
    across = over_t + over_x
    x_peer = member_at(over_x)
    if direct:
        banks = lax.axis_size("x") * cores
        t_index, bank = place // banks, lax.rem(place, banks)
        each = lstm_block_hbm.shape[1] // 8
        short = turned_block_hbm.shape[1] // 2

        def routes(member):
            for k in range(8):
                rows = pl.ds(pl.multiple_of(bank * each, each), each)
                yield (
                    lstm_block_hbm.at[member, pl.ds(k * each, each)],
                    lstm_hbm.at[home, t_index * 8 + k, rows],
                    0,
                )
            for d in range(2):
                rows = pl.ds(pl.multiple_of(bank * short, short), short)
                yield (
                    turned_block_hbm.at[member, pl.ds(d * short, short)],
                    turned_hbm.at[home, t_index, d, rows],
                    1,
                )

        def swap(offsets):
            for offset in offsets:
                member = member_at(offset)
                for source, target, which in routes(member):
                    send_block(
                        source, target, swap_sems.at[which], swap_sems.at[2 + which], member
                    )

        swap(range(1, over_t))
        for source, target, which in routes(place):
            pltpu.make_async_copy(source, target, swap_sems.at[4 + which]).start()
    else:
        pltpu.make_async_copy(turned_block_hbm, turned_hbm.at[home], swap_sems.at[5]).start()
        pltpu.make_async_copy(lstm_block_hbm, lstm_hbm.at[home], swap_sems.at[4]).start()

    def columns(member):
        return pl.ds(pl.multiple_of(member * part, part), part)

    token_block = wide.shape[0] // tiled_ref.shape[1]

    @pl.loop(0, tokens // token_block)
    def _(step):
        rows = pl.ds(pl.multiple_of(step * token_block, token_block), token_block)
        pool_kernel(
            tight_from,
            tiled_ref.at[rows],
            filter_ref,
            count_ref,
            features_own.at[rows],
            lse_ref.at[rows],
            wide,
            tight,
        )

    g, t, y, x, c = axis_sizes()
    natural = features_own[...]
    starts = [
        ((((gi * t + ti) * y + yi) * x + xi) * c + ci) * run
        for ti in range(t)
        for xi in range(x)
        for ci in range(c)
        for gi in range(g)
        for yi in range(y)
    ]
    features_own[...] = jnp.concatenate([natural[:, at : at + run] for at in starts], axis=1)

    for offset in (over_t, over_x, 1):
        send_block(
            features_own,
            first_ref.at[place],
            send_sems.at[0],
            first_sems.at[opposite(offset)],
            member_at(offset),
        )
    first_ref[place] = features_own[...]
    block_gather.start(all_places[4:])
    if direct:
        swap(range(over_t, team))
    block_gather.forward(all_places[:4])

    def lstm_start(chunk):
        for dg in range(1, g_size):
            send_grid(
                lstm_hbm.at[home, chunk],
                lstm_hbm.at[home, chunk],
                gather_send_sems.at[2],
                lstm_sems.at[chunk, g_size - dg, 0],
                dg,
                0,
            )

    def lstm_forward(chunk):
        for dg in range(1, g_size):
            target = lstm_hbm.at[grid_block(dg, 0), chunk]
            wait_bytes(target, lstm_sems.at[chunk, dg, 0])
            send_grid(
                target, target, gather_send_sems.at[3], lstm_sems.at[chunk, dg, 1], 0, 1
            )

    def pump(chunk):
        @pl.when(chunk < chunks)
        def _():
            lstm_forward(jnp.minimum(chunk, chunks - 1))

            @pl.when(chunk + AHEAD < chunks)
            def _():
                lstm_start(jnp.minimum(chunk + AHEAD, chunks - 1))

    for offset in (over_t, over_x, across):
        member = member_at(offset)
        block = first_ref.at[member]
        wait_bytes(block, first_sems.at[offset])
        if offset == over_t:
            send_block(block, block, send_sems.at[0], first_sems.at[across], x_peer)
        send_block(block, block, send_sems.at[0], first_sems.at[offset + 1], sibling)
    block_gather.finish(all_places[:4])
    wait_bytes(block_hbm, load_sems.at[3])
    load_level(first_hbm, weights, 0, run, load_sems.at[0])
    wait_bytes(weights.at[0], load_sems.at[0])

    rows = cores * tokens

    def mix(level, pair, operand):
        mixed = (
            jnp.dot(
                operand.reshape(rows, features), weights[level], preferred_element_type=jnp.float32
            )
            + bias_ref[level : level + 1]
        )
        mixed_ref[level, pair] = mixed.reshape(cores, tokens, 2 * part)
        gate = sigmoid(mixed[:, part:])
        pre_act = mixed[:, :part]
        return (gate, pre_act * sigmoid(pre_act))

    for step in range(chips):
        chip = member_at(step * cores) // cores
        pair = pl.ds(chip * cores, cores)
        wait_bytes(first_ref.at[member_at(step * cores + 1)], first_sems.at[step * cores + 1])
        gate, act = mix(0, pair, first_ref[pair])
        carried = first_ref[pair, :, columns(place)].astype(jnp.float32).reshape(rows, part)
        hidden = gate * carried + (1.0 - gate) * act
        hidden_ref[pair] = hidden.reshape(cores, tokens, part)
        mine = second_ref.at[pair, :, columns(place)]
        mine[...] = hidden.astype(jnp.bfloat16).reshape(cores, tokens, part)
        for to in (over_t, over_x, 1):
            send_block(
                mine, mine, send_sems.at[1], second_sems.at[chip, opposite(to)], member_at(to)
            )
        block_gather.forward([4 + k for k in range(4 * step // chips, 4 * (step + 1) // chips)])

    if direct:
        wait_bytes(lstm_block_hbm.at[pl.ds(0, team - 1)], swap_sems.at[2])
        wait_bytes(turned_block_hbm.at[pl.ds(0, team - 1)], swap_sems.at[3])
        wait_bytes(lstm_block_hbm.at[0], swap_sems.at[4])
        wait_bytes(turned_block_hbm.at[0], swap_sems.at[5])
    else:
        wait_bytes(lstm_block_hbm, swap_sems.at[4])
        wait_bytes(turned_block_hbm, swap_sems.at[5])
    for chunk in range(min(AHEAD, chunks)):
        lstm_start(chunk)
    block_gather.forward(all_places[8:])
    block_gather.finish(all_places[4:])
    load_level(first_hbm, weights, 1, run, load_sems.at[1])
    load_project(first_hbm, project, load_sems.at[2])

    @pl.loop(0, chunks)
    def _(chunk):
        send_grid(
            lstm_hbm.at[home, chunk],
            lstm_hbm.at[home, chunk],
            gather_send_sems.at[4],
            lstm_sems.at[chunk, 0, 1],
            0,
            1,
        )

    wait_bytes(weights.at[1], load_sems.at[1])
    wait_bytes(project, load_sems.at[2])
    x_size, t_size = lax.axis_size("x"), lax.axis_size("t")

    def ordered_chip(step):
        t_at = lax.rem(lax.axis_index("t") + step // x_size, t_size)
        return t_at * x_size + step % x_size

    for step in range(chips + 1):
        if step < chips:
            chip = ordered_chip(step)
            pair = pl.ds(chip * cores, cores)
            for origin in (over_t, over_x, across):
                piece = second_ref.at[pair, :, columns(member_at(origin))]
                wait_bytes(piece, second_sems.at[chip, origin])
                if origin == over_t:
                    send_block(
                        piece, piece, send_sems.at[1], second_sems.at[chip, across], x_peer
                    )
                send_block(
                    piece, piece, send_sems.at[1], second_sems.at[chip, origin + 1], sibling
                )
        if step > 0:
            chip = ordered_chip(step - 1)
            pair = pl.ds(chip * cores, cores)
            for origin in [0] + near:
                piece = second_ref.at[pair, :, columns(member_at(origin + 1))]
                wait_bytes(piece, second_sems.at[chip, origin + 1])
            gate, act = mix(1, pair, second_ref[pair])
            carried = hidden_ref[pair].reshape(rows, part)
            top = (gate * carried + (1.0 - gate) * act).astype(jnp.bfloat16)
            top_ref[pair] = top.reshape(cores, tokens, part)
            parts[pair] = (
                jnp.dot(top, project[...], preferred_element_type=jnp.float32)
                .astype(jnp.bfloat16)
                .reshape(cores, tokens, -1)
            )
            for core in range(cores):
                member = chip * cores + core

                @pl.when(member != place)
                def _():
                    send_block(
                        parts.at[member],
                        parts_recv.at[place],
                        lin_sems.at[0],
                        lin_sems.at[1],
                        member,
                    )

            pump(step - 1)

    turned_gather.start([0])
    parts_recv[place] = parts[place]
    others = pl.ds(0, team - 1)
    pump(chips)
    pump(chips + 1)
    wait_bytes(parts_recv.at[others], lin_sems.at[1])
    lin = jnp.sum(parts_recv[...].astype(jnp.float32), axis=0) + lin_bias_ref[...]
    lin_ref[place] = lin.astype(jnp.bfloat16)
    for offset in range(1, team):
        send_block(
            lin_ref.at[place],
            lin_ref.at[place],
            lin_sems.at[2],
            lin_sems.at[3],
            member_at(offset),
        )

    @pl.loop(chips + 2, chunks)
    def _(chunk):
        pump(chunk)

    wait_bytes(lin_ref.at[others], lin_sems.at[3])
    wait_bytes(lin_ref.at[others], lin_sems.at[2])
    wait_bytes(parts.at[others], lin_sems.at[0])

    turned_gather.forward([0])
    turned_gather.finish([0])

    @pl.loop(0, chunks)
    def _(chunk):
        for dg in range(g_size):
            wait_bytes(lstm_hbm.at[grid_block(dg, 1), chunk], lstm_sems.at[chunk, dg, 1])

    wait_bytes(first_ref.at[pl.ds(0, team - 1)], send_sems.at[0])
    wait_bytes(second_ref.at[pl.ds(0, team - 1)], send_sems.at[1])
    block_gather.sent(all_places)
    turned_gather.sent([0])
    for _ in range(g_size - 1):
        wait_bytes(lstm_hbm.at[0], gather_send_sems.at[2])
        wait_bytes(lstm_hbm.at[0], gather_send_sems.at[3])
    wait_bytes(lstm_hbm.at[0], gather_send_sems.at[4])
    if direct:
        wait_bytes(lstm_block_hbm.at[pl.ds(0, team - 1)], swap_sems.at[0])
        wait_bytes(turned_block_hbm.at[pl.ds(0, team - 1)], swap_sems.at[1])


def run_highway(
    tight_from, direct, tiled, filters, counts, block, lstm_block, turned_block, bias, lin_bias
):
    team = team_size()
    tokens, features = tiled.shape[0], filters.shape[1]
    part = features // team
    g_size, y_size = lax.axis_size("g"), lax.axis_size("y")
    grid = g_size * y_size
    width = block.shape[1]
    bf16, f32 = jnp.bfloat16, jnp.float32
    vmem = pl.BlockSpec(memory_space=pltpu.VMEM)
    hbm = pl.BlockSpec(memory_space=pl.ANY)
    pieces = 9
    if direct:
        banks = lax.axis_size("x") * lax.axis_size("c")
        halves = lax.axis_size("t")
        lstm_shape = (8 * halves, banks * lstm_block.shape[1] // 8, lstm_block.shape[2])
        turned_shape = (halves, 2, banks * turned_block.shape[1] // 2, turned_block.shape[2])
    else:
        lstm_shape, turned_shape = lstm_block.shape, turned_block.shape
    token_block = math.gcd(tokens, TOKEN_BLOCK)
    return pl.pallas_call(
        partial(highway_kernel, tight_from, direct),
        in_specs=[vmem] * 3 + [hbm] * 3 + [vmem] * 2,
        out_specs=[vmem] + [hbm] * 3 + [vmem] * 6,
        out_shape=[
            jax.ShapeDtypeStruct((tokens, features), f32),
            jax.ShapeDtypeStruct((grid,) + block.shape, bf16),
            jax.ShapeDtypeStruct((grid,) + lstm_shape, bf16),
            jax.ShapeDtypeStruct((grid,) + turned_shape, bf16),
            jax.ShapeDtypeStruct((team, tokens, features), bf16),
            jax.ShapeDtypeStruct((team, tokens, features), bf16),
            jax.ShapeDtypeStruct((2, team, tokens, 2 * part), f32),
            jax.ShapeDtypeStruct((team, tokens, part), f32),
            jax.ShapeDtypeStruct((team, tokens, part), bf16),
            jax.ShapeDtypeStruct((team, tokens, width), bf16),
        ],
        scratch_shapes=[
            pltpu.VMEM((team, tokens, width), bf16),
            pltpu.VMEM((team, tokens, width), bf16),
            pltpu.VMEM((tokens, features), bf16),
            pltpu.VMEM((token_block * PLACES, LANES), bf16),
            pltpu.VMEM((token_block * TIGHT, LANES), bf16),
            pltpu.VMEM((2, features, 2 * part), bf16),
            pltpu.VMEM((part, width), bf16),
            pltpu.SemaphoreType.DMA((5,)),
            pltpu.SemaphoreType.DMA((2,)),
            pltpu.SemaphoreType.DMA((team,)),
            pltpu.SemaphoreType.DMA((team // lax.axis_size("c"), team)),
            pltpu.SemaphoreType.DMA((5,)),
            pltpu.SemaphoreType.DMA((pieces, g_size, y_size)),
            pltpu.SemaphoreType.DMA((1, g_size, y_size)),
            pltpu.SemaphoreType.DMA((lstm_shape[0], g_size, y_size)),
            pltpu.SemaphoreType.DMA((4,)),
            pltpu.SemaphoreType.DMA((6,)),
        ],
        compiler_params=pltpu.CompilerParams(
            collective_id=2, has_side_effects=True, vmem_limit_bytes=60 * 1024 * 1024
        ),
        name="highway_team",
    )(tiled, filters, counts, block, lstm_block, turned_block, bias, lin_bias)


def highway_back_kernel(
    grad_lin_ref,
    first_hbm,
    first_ref,
    second_ref,
    mixed_ref,
    hidden_ref,
    top_ref,
    lstm_hbm,
    features_ref,
    grads_hbm,
    bias_ref,
    lstm_ref,
    lstm_own,
    lstm_y,
    lstm_send,
    lstm_g,
    weights,
    project,
    grad_mixed,
    direct,
    column_parts,
    column_sibling,
    column_send,
    column_recv,
    column_sum_own,
    row_part,
    row_keep,
    row_give,
    row_sibling,
    row_send,
    row_recv,
    row_sum_own,
    grad_stage,
    load_sems,
    send_sems,
    column_sib_sems,
    column_sems,
    row_sib_sems,
    row_sems,
    out_sems,
    lstm_load_sems,
    lstm_send_sems,
    lstm_y_sems,
    lstm_g_sems,
):
    team, tokens, features = first_ref.shape
    part = features // team
    grid = first_hbm.shape[0]
    run = part // grid
    cores = lax.axis_size("c")
    chips = team // cores
    place = team_place()
    sibling = member_at(1)
    near = list(range(1, chips))
    for level in range(2):
        load_level(first_hbm, weights, level, run, load_sems.at[level])
    load_project(first_hbm, project, load_sems.at[2])
    greet([1] + [chip * cores for chip in near], True)
    f32, bf16 = jnp.float32, jnp.bfloat16
    g_size, y_size = lax.axis_size("g"), lax.axis_size("y")
    y_index = lax.axis_index("y")
    other_y = lax.rem(y_index + 1, y_size)
    chunks = lstm_ref.shape[0]

    def lstm_block(dg, y):
        return lax.rem(lax.axis_index("g") + dg, g_size) * y_size + y

    @pl.loop(0, chunks)
    def _(chunk):
        for dg in list(range(1, g_size)) + [0]:
            send_grid(
                lstm_hbm.at[lstm_block(dg, other_y), chunk],
                lstm_y.at[dg, chunk],
                lstm_send_sems.at[0],
                lstm_y_sems.at[chunk, dg],
                0,
                1,
            )

    pltpu.make_async_copy(
        lstm_hbm.at[lstm_block(0, y_index)], lstm_ref, lstm_load_sems.at[0]
    ).start()
    for dg in range(1, g_size):
        pltpu.make_async_copy(
            lstm_hbm.at[lstm_block(dg, y_index)], lstm_own.at[dg - 1], lstm_load_sems.at[1]
        ).start()

    def pump(chunk):
        for dg in range(1, g_size):
            wait_bytes(lstm_y.at[dg, chunk], lstm_y_sems.at[chunk, dg])
            both = lstm_own[dg - 1, chunk].astype(f32) + lstm_y[dg, chunk].astype(f32)
            lstm_send[dg - 1, chunk] = both.astype(bf16)
            send_grid(
                lstm_send.at[dg - 1, chunk],
                lstm_g.at[g_size - dg - 1, chunk],
                lstm_send_sems.at[1],
                lstm_g_sems.at[chunk, g_size - dg - 1],
                dg,
                0,
            )

    def columns(member):
        return pl.ds(pl.multiple_of(member * part, part), part)

    def opposite_chip(chip):
        return opposite(chip * cores) // cores

    for level in range(2):
        wait_bytes(weights.at[level], load_sems.at[level])
    wait_bytes(project, load_sems.at[2])

    def mix_grads(level, member, grad, carried):
        pre_act = mixed_ref[level, member, :, pl.ds(0, part)]
        gate = sigmoid(mixed_ref[level, member, :, pl.ds(part, part)])
        act_sig = sigmoid(pre_act)
        grad_mixed[level, member, :, pl.ds(0, part)] = (
            grad * (1.0 - gate) * act_sig * (1.0 + pre_act * (1.0 - act_sig))
        ).astype(bf16)
        grad_mixed[level, member, :, pl.ds(part, part)] = (
            grad * (carried - pre_act * act_sig) * gate * (1.0 - gate)
        ).astype(bf16)
        return grad * gate

    def spread(level, member):
        return lax.dot_general(
            grad_mixed[level, member],
            weights[level],
            (((1,), (1,)), ((), ())),
            preferred_element_type=f32,
        )

    @pl.loop(0, team)
    def _(member):
        grad = lax.dot_general(
            grad_lin_ref[member], project[...], (((1,), (1,)), ((), ())), preferred_element_type=f32
        )
        direct[member] = mix_grads(1, member, grad, hidden_ref[member])
        column_parts[member] = spread(1, member).astype(bf16)
        for chip in range(chips):
            send_block(
                column_parts.at[member, :, columns(member_at(chip * cores + 1))],
                column_sibling.at[member, chip],
                send_sems.at[0],
                column_sib_sems.at[member],
                sibling,
            )

    wait_bytes(lstm_own, lstm_load_sems.at[1])
    pump(0)

    @pl.loop(0, team)
    def _(member):
        wait_bytes(column_sibling.at[member], column_sib_sems.at[member])
        for chip in near + [0]:
            target = member_at(chip * cores)
            both = column_parts[member, :, columns(target)].astype(f32) + column_sibling[
                member, chip
            ].astype(f32)
            if chip == 0:
                column_sum_own[member] = both
            else:
                column_send[chip - 1, member] = both.astype(bf16)
                send_block(
                    column_send.at[chip - 1, member],
                    column_recv.at[opposite_chip(chip) - 1, member],
                    send_sems.at[1],
                    column_sems.at[member, opposite_chip(chip) - 1],
                    target,
                )

    def weight_grads(level, source_ref):
        @pl.loop(0, team)
        def _(member):
            slot = lax.rem(member, 2)

            @pl.when(member >= 2)
            def _():
                wait_bytes(grad_stage.at[slot], out_sems.at[slot])

            grad_stage[slot] = lax.dot_general(
                source_ref[:, :, columns(member)].reshape(team * tokens, part),
                grad_mixed[level].reshape(team * tokens, 2 * part),
                (((0,), (0,)), ((), ())),
                preferred_element_type=f32,
            ).astype(bf16)
            for block in range(grid):
                pltpu.make_async_copy(
                    grad_stage.at[slot, pl.ds(block * run, run)],
                    grads_hbm.at[
                        block, pl.ds(pl.multiple_of((member * 2 + level) * run, run), run)
                    ],
                    out_sems.at[slot],
                ).start()

        for slot in range(2):
            wait_bytes(grad_stage.at[slot], out_sems.at[slot])
        bias_ref[level] = jnp.dot(
            jnp.ones((8, team * tokens), bf16),
            grad_mixed[level].reshape(team * tokens, 2 * part),
            preferred_element_type=f32,
        )

    pump(1)
    weight_grads(1, second_ref)
    pump(2)

    @pl.loop(0, team)
    def _(step):
        offset = team - 1 - step
        member = member_at(offset)
        chip = offset // cores
        grad = column_sum_own[member] + direct[member]
        for other in near:
            wait_bytes(column_recv.at[other - 1, member], column_sems.at[member, other - 1])
            grad = grad + column_recv[other - 1, member].astype(f32)
        carried = first_ref[member, :, columns(place)].astype(f32)
        straight = mix_grads(0, member, grad, carried)
        row_part[...] = spread(0, member)
        row_part[:, columns(place)] += straight

        @pl.when(lax.rem(offset, cores) == 1)
        def _():
            row_give[chip] = row_part[...].astype(bf16)
            send_block(
                row_give.at[chip],
                row_sibling.at[chip],
                send_sems.at[2],
                row_sib_sems.at[chip],
                sibling,
            )

        @pl.when(lax.rem(offset, cores) == 0)
        def _():
            row_keep[chip] = row_part[...].astype(bf16)

        @pl.when((step == team // 2 - 1) | (step == team - 1))
        def _():
            pump(3 + (step + 1) // team)

    for chip in near[::-1] + [0]:
        wait_bytes(row_sibling.at[chip], row_sib_sems.at[chip])
        both = row_keep[chip].astype(f32) + row_sibling[chip].astype(f32)
        if chip == 0:
            row_sum_own[...] = both
        else:
            row_send[chip - 1] = both.astype(bf16)
            send_block(
                row_send.at[chip - 1],
                row_recv.at[opposite_chip(chip) - 1],
                send_sems.at[3],
                row_sems.at[opposite_chip(chip) - 1],
                member_at(chip * cores),
            )

    pump(5)
    weight_grads(0, first_ref)

    @pl.loop(6, chunks)
    def _(chunk):
        pump(chunk)

    grad_stage[0] = lax.dot_general(
        top_ref[...].reshape(team * tokens, part),
        grad_lin_ref[...].reshape(team * tokens, 2 * part),
        (((0,), (0,)), ((), ())),
        preferred_element_type=f32,
    ).astype(bf16)
    for block in range(grid):
        pltpu.make_async_copy(
            grad_stage.at[0, pl.ds(block * run, run)],
            grads_hbm.at[block, pl.ds(team * 2 * run, run)],
            out_sems.at[0],
        ).start()
    total = row_sum_own[...]
    for other in near:
        wait_bytes(row_recv.at[other - 1], row_sems.at[other - 1])
        total = total + row_recv[other - 1].astype(f32)
    features_ref[...] = total.astype(bf16)
    wait_bytes(lstm_ref, lstm_load_sems.at[0])

    @pl.loop(0, chunks)
    def _(chunk):
        wait_bytes(lstm_y.at[0, chunk], lstm_y_sems.at[chunk, 0])
        whole = lstm_ref[chunk].astype(f32) + lstm_y[0, chunk].astype(f32)
        for dg in range(1, g_size):
            wait_bytes(lstm_g.at[dg - 1, chunk], lstm_g_sems.at[chunk, dg - 1])
            whole = whole + lstm_g[dg - 1, chunk].astype(f32)
        lstm_ref[chunk] = whole.astype(bf16)

    wait_bytes(lstm_y, lstm_send_sems.at[0])
    wait_bytes(lstm_g, lstm_send_sems.at[1])
    wait_bytes(grad_stage.at[0], out_sems.at[0])
    wait_bytes(column_sibling, send_sems.at[0])
    wait_bytes(column_send, send_sems.at[1])
    wait_bytes(row_give, send_sems.at[2])
    wait_bytes(row_send, send_sems.at[3])


def run_highway_back(grad_lin, first_all, first, second, mixed, hidden, top, lstm_grads):
    team, tokens, features = first.shape
    part = features // team
    chips = team // lax.axis_size("c")
    width = first_all.shape[2]
    bf16, f32 = jnp.bfloat16, jnp.float32
    g_size = lax.axis_size("g")
    chunk_shape = lstm_grads.shape[1:]
    vmem = pl.BlockSpec(memory_space=pltpu.VMEM)
    hbm = pl.BlockSpec(memory_space=pl.ANY)
    return pl.pallas_call(
        highway_back_kernel,
        in_specs=[vmem, hbm] + [vmem] * 5 + [hbm],
        out_specs=[vmem, hbm, vmem, vmem],
        out_shape=[
            jax.ShapeDtypeStruct((tokens, features), bf16),
            jax.ShapeDtypeStruct(first_all.shape, bf16),
            jax.ShapeDtypeStruct((2, 8, 2 * part), f32),
            jax.ShapeDtypeStruct(chunk_shape, bf16),
        ],
        scratch_shapes=[
            pltpu.VMEM((g_size - 1,) + chunk_shape, bf16),
            pltpu.VMEM((g_size,) + chunk_shape, bf16),
            pltpu.VMEM((g_size - 1,) + chunk_shape, bf16),
            pltpu.VMEM((g_size - 1,) + chunk_shape, bf16),
            pltpu.VMEM((2, features, 2 * part), bf16),
            pltpu.VMEM((part, width), bf16),
            pltpu.VMEM((2, team, tokens, 2 * part), bf16),
            pltpu.VMEM((team, tokens, part), f32),
            pltpu.VMEM((team, tokens, features), bf16),
            pltpu.VMEM((team, chips, tokens, part), bf16),
            pltpu.VMEM((chips - 1, team, tokens, part), bf16),
            pltpu.VMEM((chips - 1, team, tokens, part), bf16),
            pltpu.VMEM((team, tokens, part), f32),
            pltpu.VMEM((tokens, features), f32),
            pltpu.VMEM((chips, tokens, features), bf16),
            pltpu.VMEM((chips, tokens, features), bf16),
            pltpu.VMEM((chips, tokens, features), bf16),
            pltpu.VMEM((chips - 1, tokens, features), bf16),
            pltpu.VMEM((chips - 1, tokens, features), bf16),
            pltpu.VMEM((tokens, features), f32),
            pltpu.VMEM((2, part, width), bf16),
            pltpu.SemaphoreType.DMA((3,)),
            pltpu.SemaphoreType.DMA((4,)),
            pltpu.SemaphoreType.DMA((team,)),
            pltpu.SemaphoreType.DMA((team, chips - 1)),
            pltpu.SemaphoreType.DMA((chips,)),
            pltpu.SemaphoreType.DMA((chips - 1,)),
            pltpu.SemaphoreType.DMA((2,)),
            pltpu.SemaphoreType.DMA((2,)),
            pltpu.SemaphoreType.DMA((2,)),
            pltpu.SemaphoreType.DMA((chunk_shape[0], g_size)),
            pltpu.SemaphoreType.DMA((chunk_shape[0], g_size - 1)),
        ],
        compiler_params=pltpu.CompilerParams(
            collective_id=3, has_side_effects=True, vmem_limit_bytes=63 * 1024 * 1024
        ),
        name="highway_team_back",
    )(grad_lin, first_all, first, second, mixed, hidden, top, lstm_grads)


def every_coords(shift):
    g, t, y, x, c = axis_sizes()
    sizes = (g, t, y, x, c)
    coords, rest = {}, shift
    for name, size in list(zip(EVERY, sizes))[::-1]:
        coords[name] = lax.rem(lax.axis_index(name) + lax.rem(rest, size), size)
        rest = rest // size
    return coords


def every_place(coords):
    place = 0
    for name in EVERY:
        place = place * lax.axis_size(name) + coords[name]
    return place


def final_kernel(
    tight_from,
    bank_counts,
    grads_ref,
    tiled_ref,
    ids_ref,
    filter_ref,
    count_ref,
    lse_ref,
    upstream_ref,
    bias_ref,
    highway_ref,
    project_ref,
    sums_ref,
    conv_ref,
    table_ref,
    natural,
    grad_filters,
    table_sum,
    wide,
    tight,
    spread,
    y_recv,
    g_send,
    g_recv,
    kept,
    team_send,
    team_recv,
    bias_recv,
    small,
    small_team,
    small_send,
    small_grid,
    y_sems,
    g_sems,
    team_sems,
    small_sems,
    send_sems,
):
    grid, rows, lanes = grads_ref.shape
    team = team_size()
    g, t, y, x, c = axis_sizes()
    devices = bias_ref.shape[0]
    step = team_recv.shape[1]
    cut = step * team
    table_rows = table_ref.shape[0] // team
    f32, bf16 = jnp.float32, jnp.bfloat16
    here = every_place({name: lax.axis_index(name) for name in EVERY})
    place = team_place()
    bank = lax.rem(place, x * c)
    conv_ref[...] = jnp.zeros_like(conv_ref)
    barrier = pltpu.get_barrier_semaphore()

    @pl.loop(1, devices)
    def _(shift):
        pl.semaphore_signal(
            barrier, inc=1, device_id=every_coords(shift), device_id_type=pl.DeviceIdType.MESH
        )

    pl.semaphore_wait(barrier, devices - 1)
    pieces = [pl.ds(k * step, step) for k in range(team)] + [pl.ds(cut, rows - cut)]
    g_index, y_index = lax.axis_index("g"), lax.axis_index("y")
    other_y = lax.rem(y_index + 1, y)
    for k, piece in enumerate(pieces):
        for dg in list(range(1, g)) + [0]:
            send_grid(
                grads_ref.at[lax.rem(g_index + dg, g) * y + other_y, piece],
                y_recv.at[dg, piece],
                send_sems.at[0],
                y_sems.at[k, dg],
                0,
                1,
            )

    @pl.loop(1, devices)
    def _(shift):
        coords = every_coords(shift)
        pltpu.make_async_remote_copy(
            src_ref=bias_ref.at[every_place(coords)],
            dst_ref=bias_recv.at[here],
            send_sem=send_sems.at[3],
            recv_sem=small_sems.at[0],
            device_id=coords,
            device_id_type=pl.DeviceIdType.MESH,
        ).start()

    bias_recv[here] = bias_ref[here]
    run = upstream_ref.shape[1] // devices
    order = [
        (((ti * x + xi) * c + ci) * g + gi) * y + yi
        for gi in range(g)
        for ti in range(t)
        for yi in range(y)
        for xi in range(x)
        for ci in range(c)
    ]
    permuted = upstream_ref[...]
    natural[...] = jnp.concatenate([permuted[:, at * run : (at + 1) * run] for at in order], axis=1)
    grad_filters[...] = jnp.zeros_like(grad_filters)
    table_sum[...] = jnp.zeros_like(table_sum)

    def pass_on(k):
        piece = pieces[k]
        for dg in list(range(1, g)) + [0]:
            wait_bytes(y_recv.at[dg, piece], y_sems.at[k, dg])
            both = grads_ref[lax.rem(g_index + dg, g) * y + y_index, piece].astype(f32)
            both = both + y_recv[dg, piece].astype(f32)
            if dg == 0:
                kept[piece] = both
            else:
                g_send[dg - 1, piece] = both.astype(bf16)
                send_grid(
                    g_send.at[dg - 1, piece],
                    g_recv.at[g - dg - 1, piece],
                    send_sems.at[1],
                    g_sems.at[k, g - dg - 1],
                    dg,
                    0,
                )

    token_block = spread.shape[0]
    blocks = tiled_ref.shape[0] // token_block
    early = min(4, team)

    def pool_block(at):
        picked = pl.ds(pl.multiple_of(at * token_block, token_block), token_block)
        pool_grad_block(
            tight_from,
            tiled_ref.at[picked],
            ids_ref[pl.ds(at, 1)],
            filter_ref,
            count_ref,
            lse_ref.at[picked],
            natural.at[picked],
            grad_filters,
            table_sum,
            wide,
            tight,
            spread,
        )

    for k in range(early):

        @pl.loop(blocks * k // early, blocks * (k + 1) // early)
        def _(at):
            pool_block(at)

        pass_on(k)

    lane = lax.broadcasted_iota(jnp.int32, (LANES, LANES), 0)
    fold = jnp.where(
        (lane < TAPS)
        & (lax.rem(lane, EMBED) == lax.broadcasted_iota(jnp.int32, (LANES, LANES), 1)),
        1.0,
        0.0,
    ).astype(bf16)
    by_tap = table_sum[...]
    high = by_tap.astype(bf16)
    low = (by_tap - high.astype(f32)).astype(bf16)
    table = jnp.dot(high, fold, preferred_element_type=f32)
    table = (table + jnp.dot(low, fold, preferred_element_type=f32)).astype(bf16)
    starts, halves, at, column = [], [], 0, 0
    for half in range(t):
        for b, count in enumerate(bank_counts):
            starts.append(at)
            halves.append(count // t)
            at += count // t + table_rows
    for b, count in enumerate(bank_counts):
        for half in range(t):
            member = half * len(bank_counts) + b
            each = count // t
            turned = grad_filters[:, pl.ds(column, each)].T.astype(bf16)
            small[pl.ds(starts[member], each)] = turned
            column += each
    vocab = table_sum.shape[0]
    for member in range(team):
        top = min(table_rows, vocab - member * table_rows)
        begin = starts[member] + halves[member]
        if top > 0:
            small[pl.ds(begin, top)] = table[member * table_rows : member * table_rows + top]
        if top < table_rows:
            low_row = max(top, 0)
            small[pl.ds(begin + low_row, table_rows - low_row)] = jnp.zeros(
                (table_rows - low_row, LANES), bf16
            )
    for member in range(team):
        size = halves[member] + table_rows
        source = small.at[pl.ds(starts[member], size)]

        @pl.when(place == member)
        def _():
            small_team[member, pl.ds(0, size)] = small[pl.ds(starts[member], size)]

        @pl.when(place != member)
        def _():
            send_block(
                source,
                small_team.at[place, pl.ds(0, size)],
                send_sems.at[4],
                small_sems.at[1],
                member,
            )

    for k in range(early, team - 2):
        pass_on(k)
    home = grid_block(0, 0)
    for b, count in enumerate(bank_counts):
        size = count // t + table_rows

        @pl.when(bank == b)
        def _():
            wait_bytes(small_team.at[pl.ds(0, team - 1), pl.ds(0, size)], small_sems.at[1])
            total = small_team[0, pl.ds(0, size)].astype(f32)
            for origin in range(1, team):
                total = total + small_team[origin, pl.ds(0, size)].astype(f32)
            small_send[pl.ds(0, size)] = total.astype(bf16)
            small_grid[home, pl.ds(0, size)] = total.astype(bf16)
            for dg in range(g):
                for dy in range(y):
                    if dg or dy:
                        send_grid(
                            small_send.at[pl.ds(0, size)],
                            small_grid.at[home, pl.ds(0, size)],
                            send_sems.at[5],
                            small_sems.at[2],
                            dg,
                            dy,
                        )

    for k in range(team - 2, team + 1):
        pass_on(k)
    t_index = lax.axis_index("t")
    for b, count in enumerate(bank_counts):
        each = count // t
        size = each + table_rows

        @pl.when(bank == b)
        def _():
            wait_bytes(small_grid.at[pl.ds(0, grid - 1), pl.ds(0, size)], small_sems.at[2])
            total = small_grid[0, pl.ds(0, size)].astype(f32)
            for origin in range(1, grid):
                total = total + small_grid[origin, pl.ds(0, size)].astype(f32)
            mine = conv_ref.at[pl.ds(pl.multiple_of(t_index * each, each), each)]
            mine[...] = total[:each]
            for dt in range(1, t):
                send_block(
                    mine, mine, send_sems.at[6], small_sems.at[3], member_at(dt * x * c)
                )
            piece = table_ref.at[pl.ds(pl.multiple_of(place * table_rows, 16), table_rows)]
            piece[...] = total[each:]
            for offset in range(1, team):
                send_block(piece, piece, send_sems.at[7], small_sems.at[4], member_at(offset))

    for k, piece in enumerate(pieces):
        total = kept[piece]
        for dg in range(1, g):
            wait_bytes(g_recv.at[dg - 1, piece], g_sems.at[k, dg - 1])
            total = total + g_recv[dg - 1, piece].astype(f32)
        if k == team:
            project_ref[...] = total
        else:
            team_send[piece] = total.astype(bf16)

            @pl.when(place == k)
            def _():
                team_recv[k] = team_send[piece]

            @pl.when(place != k)
            def _():
                send_block(
                    team_send.at[piece], team_recv.at[place], send_sems.at[2], team_sems.at[0], k
                )

    wait_bytes(bias_recv.at[pl.ds(0, devices - 1)], small_sems.at[0])
    sums_ref[...] = jnp.sum(bias_recv[...].astype(f32), axis=0)
    wait_bytes(team_recv.at[pl.ds(0, team - 1)], team_sems.at[0])
    half_lanes = lanes // 2
    for half in range(2):
        parts = [
            team_recv[
                (ti * x + xi) * c + ci,
                :,
                half * half_lanes + (gi * y + yi) * run : half * half_lanes + (gi * y + yi + 1) * run,
            ]
            for gi in range(g)
            for ti in range(t)
            for yi in range(y)
            for xi in range(x)
            for ci in range(c)
        ]
        wide_half = half_lanes * team
        highway_ref[:, pl.ds(half * wide_half, wide_half)] = jnp.concatenate(parts, axis=1).astype(
            f32
        )
    for b, count in enumerate(bank_counts):
        each = count // t
        size = each + table_rows

        @pl.when(bank == b)
        def _():
            for _ in range(t - 1):
                wait_bytes(conv_ref.at[pl.ds(0, each)], small_sems.at[3])
                wait_bytes(conv_ref.at[pl.ds(0, each)], send_sems.at[6])
            wait_bytes(small_grid.at[pl.ds(0, grid - 1), pl.ds(0, size)], send_sems.at[5])

    wait_bytes(table_ref.at[pl.ds(0, (team - 1) * table_rows)], small_sems.at[4])
    wait_bytes(table_ref.at[pl.ds(0, (team - 1) * table_rows)], send_sems.at[7])
    wait_bytes(y_recv, send_sems.at[0])
    wait_bytes(g_recv, send_sems.at[1])
    wait_bytes(team_recv.at[pl.ds(0, team - 1)], send_sems.at[2])
    wait_bytes(bias_recv.at[pl.ds(0, devices - 1)], send_sems.at[3])
    for member in range(team):

        @pl.when(place != member)
        def _():
            size = halves[member] + table_rows
            wait_bytes(small.at[pl.ds(starts[member], size)], send_sems.at[4])


def run_final(tight_from, bank_counts, grads, tiled, ids, filters, counts, lse, upstream, biases, step):
    grid, rows, lanes = grads.shape
    team = team_size()
    g, t, y, x, c = axis_sizes()
    tokens, features = upstream.shape
    devices, bias_rows, _ = biases.shape
    bf16, f32 = jnp.bfloat16, jnp.float32
    vmem = pl.BlockSpec(memory_space=pltpu.VMEM)
    token_block = math.gcd(tokens, TOKEN_BLOCK)
    vocab = -(-VOCAB // 16) * 16
    table_rows = -(-vocab // (16 * team)) * 16
    most = max(bank_counts) // t + table_rows
    return pl.pallas_call(
        partial(final_kernel, tight_from, bank_counts),
        in_specs=[vmem] * 8,
        out_specs=[vmem] * 5,
        out_shape=[
            jax.ShapeDtypeStruct((step, lanes * team), f32),
            jax.ShapeDtypeStruct((rows - team * step, lanes), f32),
            jax.ShapeDtypeStruct((bias_rows, LANES), f32),
            jax.ShapeDtypeStruct((max(bank_counts), LANES), f32),
            jax.ShapeDtypeStruct((team * table_rows, LANES), f32),
        ],
        scratch_shapes=[
            pltpu.VMEM((tokens, features), bf16),
            pltpu.VMEM((LANES, features), f32),
            pltpu.VMEM((vocab, LANES), f32),
            pltpu.VMEM((token_block * PLACES, LANES), bf16),
            pltpu.VMEM((token_block * TIGHT, LANES), bf16),
            pltpu.VMEM((token_block, PLACES, LANES), f32),
            pltpu.VMEM((g, rows, lanes), bf16),
            pltpu.VMEM((g - 1, rows, lanes), bf16),
            pltpu.VMEM((g - 1, rows, lanes), bf16),
            pltpu.VMEM((rows, lanes), f32),
            pltpu.VMEM((rows, lanes), bf16),
            pltpu.VMEM((team, step, lanes), bf16),
            pltpu.VMEM(biases.shape, bf16),
            pltpu.VMEM((sum(bank_counts) + team * table_rows, LANES), bf16),
            pltpu.VMEM((team, most, LANES), bf16),
            pltpu.VMEM((most, LANES), bf16),
            pltpu.VMEM((grid, most, LANES), bf16),
            pltpu.SemaphoreType.DMA((team + 1, g)),
            pltpu.SemaphoreType.DMA((team + 1, g - 1)),
            pltpu.SemaphoreType.DMA((1,)),
            pltpu.SemaphoreType.DMA((5,)),
            pltpu.SemaphoreType.DMA((8,)),
        ],
        compiler_params=pltpu.CompilerParams(
            collective_id=4, has_side_effects=True, vmem_limit_bytes=60 * 1024 * 1024
        ),
        name="final_sums",
    )(grads, tiled, ids, filters, counts, lse, upstream, biases)


def pack_kernel(parts, received_ref, out_ref):
    team, rows, lanes = received_ref.shape
    each = lanes // parts
    for member in range(team):
        for part in range(parts):
            out_ref[:, pl.ds((part * team + member) * each, each)] = received_ref[
                member, :, pl.ds(part * each, each)
            ].astype(jnp.float32)


def pack_columns(received, parts):
    team, rows, lanes = received.shape
    return pl.pallas_call(
        partial(pack_kernel, parts),
        in_specs=[pl.BlockSpec(memory_space=pltpu.VMEM)],
        out_specs=pl.BlockSpec(memory_space=pltpu.VMEM),
        out_shape=jax.ShapeDtypeStruct((rows, team * lanes), jnp.float32),
        compiler_params=pltpu.CompilerParams(vmem_limit_bytes=40 * 1024 * 1024),
        name="pack_columns",
    )(received)


def axis_sizes():
    return tuple(lax.axis_size(name) for name in EVERY)


def run_rows(received):
    g, t, y, x, c = axis_sizes()
    lanes = received.shape[-1]
    split = received.reshape(t, x * c, 2, -1, lanes).transpose(0, 2, 1, 3, 4)
    return split.reshape(t, 2, -1, lanes)


def member_rows(runs):
    g, t, y, x, c = axis_sizes()
    lanes = runs.shape[-1]
    split = runs.reshape(t, 2, x * c, -1, lanes).transpose(0, 2, 1, 3, 4)
    return split.reshape(t * x * c, -1, lanes)


def team_slices(values, parts):
    team = team_size()
    two, rows, columns = values.shape
    lanes = columns // (parts * team)
    split = values.reshape(two, rows, parts, team, lanes).transpose(3, 0, 1, 2, 4)
    return split.reshape(team, two * rows, parts * lanes)


def whole_columns(received, parts):
    team, two_rows, lanes = received.shape
    split = received.reshape(team, 2, two_rows // 2, parts, lanes // parts)
    return split.transpose(1, 2, 3, 0, 4).reshape(2, two_rows // 2, team * lanes)


def team_first(values):
    g, t, y, x, c = axis_sizes()
    rows = values.shape[0]
    split = values.reshape(rows, -1, g, t, y, x, c, values.shape[1] // (2 * g * t * y * x * c))
    return split.transpose(3, 5, 6, 0, 1, 2, 4, 7)


def permuted_columns(values):
    g, t, y, x, c = axis_sizes()
    split = values.reshape(values.shape[0], g, t, y, x, c, -1)
    return split.transpose(0, 2, 4, 5, 1, 3, 6).reshape(values.shape)


def restored_columns(values):
    g, t, y, x, c = axis_sizes()
    split = values.reshape(values.shape[0], t, x, c, g, y, -1)
    return split.transpose(0, 4, 1, 5, 2, 3, 6).reshape(values.shape)


def padded_rows(values, rows):
    blocks = values.shape[0]
    flat = values.reshape(blocks, -1)
    return jnp.pad(flat, ((0, 0), (0, rows * LANES - flat.shape[1]))).reshape(blocks, rows, LANES)


def row_count(items):
    return -(-items // LANES)


def bank_filters(turned, bank, bank_cols):
    taps = [
        [width * EMBED for width, first, count in bank_specs for _ in range(count)]
        for bank_specs in bank_plan(bank_cols)
    ]
    taps = [row + [0] * (bank_cols - len(row)) for row in taps]
    limit = lax.dynamic_index_in_dim(jnp.asarray(taps, jnp.int32), bank, 0, False)
    turned = turned.T
    row = lax.broadcasted_iota(jnp.int32, (TAPS, 1), 0)
    kernel = jnp.where(row < limit[None, :], turned[:TAPS], 0.0)
    bias = jnp.where(limit > 0, turned[TAPS], 0.0)
    return (kernel.reshape(1, WIDEST, EMBED, bank_cols), bias[None])


def shards(
    char_ids,
    resets,
    out_grad,
    char_table,
    conv_weight,
    conv_bias,
    highway_weight,
    highway_bias,
    proj_weight,
    proj_bias,
    lstm_weight,
    lstm_bias,
    lstm_proj,
):
    f32, bf16 = jnp.float32, jnp.bfloat16
    own, steps = resets.shape
    team = team_size()
    place = team_place()
    devices = team * lax.axis_size("g") * lax.axis_size("y")
    bank_cols = conv_weight.shape[3]
    highway_rows = highway_weight.shape[1]
    features_all = highway_rows * devices
    part = features_all // team
    lstm_rows = lstm_weight.shape[1]
    width = proj_weight.shape[1]
    cells_all = lstm_proj.shape[1]
    cells = cells_all // team

    conv_own = jnp.concatenate([conv_weight.reshape(-1, bank_cols), conv_bias], axis=0)
    banks = lax.axis_size("x") * lax.axis_size("c")
    conv_all = lax.all_to_all(
        jnp.broadcast_to(conv_own[None], (banks,) + conv_own.shape),
        ("x", "c"),
        split_axis=0,
        concat_axis=0,
        tiled=True,
    )
    conv_weight_all = conv_all[:, :-1].reshape((banks,) + conv_weight.shape[1:])
    conv_bias_all = conv_all[:, -1]
    sizes = [highway_bias.size, proj_bias.size, lstm_bias.size, resets.size]
    small = jnp.concatenate(
        [
            highway_bias.reshape(-1),
            proj_bias.reshape(-1),
            lstm_bias.reshape(-1),
            resets.astype(bf16).reshape(-1),
        ]
    )
    small_all = lax.all_to_all(
        jnp.broadcast_to(small[None], (devices, small.size)),
        EVERY,
        split_axis=0,
        concat_axis=0,
        tiled=True,
    )
    cut = [sum(sizes[:k]) for k in range(5)]
    highway_bias_all = small_all[:, cut[0] : cut[1]].reshape(devices, 2, -1)
    highway_bias_all = highway_bias_all.transpose(1, 0, 2).reshape(2, 2 * features_all)
    highway_bias_all = team_first(highway_bias_all).reshape(team, 2, 2 * part)
    proj_bias_all = small_all[:, cut[1] : cut[2]].reshape(-1).astype(f32)
    lstm_bias_all = small_all[:, cut[2] : cut[3]].reshape(devices, 2, -1)
    lstm_bias_all = lstm_bias_all.transpose(1, 0, 2).reshape(2, 4, team, cells)
    resets_all = small_all[:, cut[3] : cut[4]].reshape(
        lax.axis_size("g"), lax.axis_size("t"), lax.axis_size("y"), -1, own, steps
    )
    resets_team = lax.dynamic_index_in_dim(resets_all, lax.axis_index("g"), 0, False)
    resets_team = lax.dynamic_index_in_dim(resets_team, lax.axis_index("y"), 1, False)
    resets_team = resets_team.reshape(team * own, steps).astype(f32)
    highway_bias_own = lax.dynamic_index_in_dim(highway_bias_all, place, 0, False).astype(f32)
    lstm_bias_own = lax.dynamic_index_in_dim(lstm_bias_all, place, 2, False)
    lstm_bias_own = lstm_bias_own.reshape(2, 1, 4 * cells).astype(f32)

    highway_slices = team_first(highway_weight.reshape(2 * highway_rows, -1))
    turned_rows = lstm_proj.shape[2]
    gate_slices = lstm_weight.reshape(2, lstm_rows, 4, team, cells).transpose(3, 0, 2, 1, 4)
    swapped = swap_team(highway_slices.reshape(team, 2 * highway_rows, 2 * part))
    block = swapped.reshape(team, 2, highway_rows, 2 * part).transpose(1, 0, 2, 3)
    block = jnp.concatenate([block.reshape(-1, 2 * part), proj_weight], axis=0)
    t, x, c = lax.axis_size("t"), lax.axis_size("x"), lax.axis_size("c")
    lstm_block = gate_slices.reshape(team, 8 * lstm_rows, cells)
    turned_block = team_slices(jnp.swapaxes(lstm_proj, 1, 2), 1)
    direct = lstm_rows % 16 == 0 and turned_rows % 16 == 0
    if not direct:
        lstm_block = (
            swap_team(lstm_block)
            .reshape(t, x * c, 8, lstm_rows, cells)
            .transpose(0, 2, 1, 3, 4)
            .reshape(t * 8, x * c * lstm_rows, cells)
        )
        turned_block = run_rows(swap_team(turned_block))
    cut_rows = team * 2 * highway_rows
    grid = lax.axis_size("g") * lax.axis_size("y")
    bank = lax.axis_index("x") * lax.axis_size("c") + lax.axis_index("c")
    own_ids = lax.dynamic_slice_in_dim(char_ids, bank * own, own, axis=0)
    own_ids = jnp.swapaxes(own_ids, 0, 1).reshape(own * steps, char_ids.shape[2])
    filters, counts = filter_matrix(conv_weight_all, conv_bias_all)
    tight_from = wide_columns(bank_cols)
    padded_ids, tiled = embed_tokens(own_ids, char_table)

    tokens = own * steps
    (
        pooled_lse,
        first_all,
        lstm_own,
        turned_own,
        first,
        second,
        mixed,
        hidden,
        top_own,
        lin_all,
    ) = run_highway(
        tight_from,
        direct,
        tiled,
        filters,
        counts,
        block,
        lstm_block,
        turned_block,
        highway_bias_own,
        proj_bias_all[None],
    )
    lstm_own = lstm_own.reshape(grid, t, 2, 4, x * c * lstm_rows, cells)

    keep_forward = 1.0 - resets_team
    keep_backward = 1.0 - jnp.concatenate(
        [resets_team[:, 1:], jnp.zeros((team * own, 1), f32)], axis=1
    )
    keep = jnp.stack([keep_forward.T, keep_backward.T])[..., None]
    grad_time = out_grad.reshape(own, steps, 2, width).transpose(2, 1, 0, 3)
    grad_lin_all, lstm_grads, turned_grads, bias_sums = run_lstm(
        lin_all.reshape(team, steps, own, width),
        grad_time,
        lstm_own,
        turned_own,
        lstm_bias_own,
        keep,
    )
    turned_summed = lax.all_to_all(turned_grads, GRID, split_axis=0, concat_axis=0, tiled=True)
    turned_summed = turned_summed.astype(f32).sum(axis=0).astype(bf16)
    grad_input = lax.dynamic_index_in_dim(grad_lin_all, place, 0, False).reshape(tokens, width)
    grad_project_b = column_sum(grad_input)
    grad_features, first_parts, highway_bias_sums, lstm_summed = run_highway_back(
        grad_lin_all.reshape(team, tokens, width),
        first_all,
        first,
        second,
        mixed,
        hidden,
        top_own,
        lstm_grads.reshape(grid, 8, -1, 4 * cells),
    )
    lstm_summed = lstm_summed.reshape(t, 2, -1, 4 * cells)
    turned_summed, grad_features = lax.optimization_barrier((turned_summed, grad_features))
    turned_grad = whole_columns(swap_team(member_rows(turned_summed)), 1).astype(f32)
    lstm_proj_grad = jnp.swapaxes(turned_grad, 1, 2)
    g, t, y, x, c = axis_sizes()

    def own_place(values, parts):
        lanes = values.shape[-1] // parts
        split = values.reshape(2, parts, 1, lanes)
        full = jnp.zeros((2, parts, team, lanes), f32)
        return lax.dynamic_update_slice(full, split, (0, 0, place, 0)).reshape(2, -1)

    lstm_bias_parts = own_place(bias_sums[:, 0], 4)
    highway_bias_parts = own_place(highway_bias_sums[:, 0], 2)
    highway_bias_parts = (
        highway_bias_parts.reshape(2, 2, t, x, c, g, y, -1)
        .transpose(0, 1, 5, 2, 6, 3, 4, 7)
        .reshape(2, 2 * features_all)
    )
    biases = jnp.concatenate(
        [
            lstm_bias_parts.reshape(2, devices, -1).transpose(1, 0, 2).reshape(devices, -1),
            highway_bias_parts.reshape(2, devices, -1).transpose(1, 0, 2).reshape(devices, -1),
            grad_project_b.reshape(devices, -1),
        ],
        axis=1,
    )
    bank_counts = [sum(item[2] for item in specs) for specs in bank_plan(bank_cols)]
    bias_rows = -(-row_count(biases.shape[1]) // 16) * 16
    highway_weight_grad, project_grad, mine, conv_sums, table_sums = run_final(
        tight_from,
        bank_counts,
        first_parts,
        tiled,
        padded_ids.reshape(-1, math.gcd(tokens, TOKEN_BLOCK) * PLACES),
        filters,
        counts,
        pooled_lse,
        grad_features,
        padded_rows(biases, bias_rows).astype(bf16),
        2 * highway_rows,
    )
    lstm_returned = swap_team(member_rows(lstm_summed))
    lstm_weight_grad = pack_columns(lstm_returned, 4).reshape(2, lstm_rows, -1)
    highway_weight_grad = highway_weight_grad.reshape(2, highway_rows, -1)
    mine_biases = mine.reshape(-1)
    ends = [2 * lstm_bias.shape[1], 2 * lstm_bias.shape[1] + 2 * highway_bias.shape[1]]
    lstm_bias_grad = mine_biases[: ends[0]].reshape(2, -1)
    highway_bias_grad = mine_biases[ends[0] : ends[1]].reshape(2, -1)
    proj_bias_grad = mine_biases[ends[1] : ends[1] + proj_bias.size]
    grad_kernel, grad_bias = bank_filters(conv_sums, bank, bank_cols)
    grad_table = table_sums[: char_table.shape[0], :EMBED]
    return (
        grad_table,
        grad_kernel,
        grad_bias,
        highway_weight_grad,
        highway_bias_grad,
        project_grad,
        proj_bias_grad,
        lstm_weight_grad,
        lstm_bias_grad,
        lstm_proj_grad,
    )


def solution(mesh):
    dp, bank = mesh.shape["dp"], mesh.shape["bank"]
    fine = Mesh(mesh.devices.reshape(dp // 4, 2, 2, bank // 2, 2), EVERY)
    rows, banks = ("g", "t", "y"), ("x", "c")
    whole = rows + banks
    placed = (
        P(rows, None, None),
        P(whole, None),
        P(whole, None, None),
        P(),
        P(banks, None, None, None),
        P(banks, None),
        P(None, whole, None),
        P(None, whole),
        P(whole, None),
        P(whole),
        P(None, whole, None),
        P(None, whole),
        P(None, None, whole),
    )
    return jax.shard_map(
        shards,
        mesh=fine,
        in_specs=placed,
        out_specs=(
            P(),
            P(banks, None, None, None),
            P(banks, None),
            P(None, whole, None),
            P(None, whole),
            P(whole, None),
            P(whole),
            P(None, whole, None),
            P(None, whole),
            P(None, None, whole),
        ),
        check_vma=False,
    )
```

```python
from functools import partial
import math

import jax
import jax.numpy as jnp
from jax import lax
from jax.experimental import pallas as pl
from jax.experimental.pallas import tpu as pltpu
from jax.sharding import Mesh, PartitionSpec as P

CHAR_COUNT = 50
VOCAB = 262
EMBED = 16
WIDEST = 7
TAPS = WIDEST * EMBED
LANES = 128
PLACES = 64
TIGHT = 48
CHUNK = 256
TOKEN_BLOCK = 16
AHEAD = 6


def bank_plan(bank_cols):
    return [
        [
            (1, 0, bank_cols // 32),
            (2, bank_cols // 32, bank_cols // 32),
            (3, bank_cols // 16, bank_cols // 16),
            (4, bank_cols // 8, bank_cols // 8),
        ],
        [(5, 0, bank_cols // 4)],
        [(6, 0, bank_cols // 2)],
        [(7, 0, bank_cols)],
    ]


def transposed(former, latter):
    return lax.dot_general(
        former, latter, (((1,), (1,)), ((), ())), preferred_element_type=jnp.float32
    )


def outer_sum(former, latter):
    return lax.dot_general(
        former, latter, (((0,), (0,)), ((), ())), preferred_element_type=jnp.float32
    )


def column_sum(values):
    ones_row = jnp.ones((1, values.shape[0]), values.dtype)
    return jnp.dot(ones_row, values, preferred_element_type=jnp.float32)[0]


def filter_columns(bank_cols):
    columns = []
    for bank_index, bank_specs in enumerate(bank_plan(bank_cols)):
        for filter_width, first_col, count in bank_specs:
            columns.append((filter_width, bank_index, first_col, count))
    return columns


def shift_rows(values, amount):
    count = values.shape[0]
    return values if amount % count == 0 else pltpu.roll(values, amount % count, 0)


def block_windows(tiled_ref, windows_wide, windows_tight):
    tokens, places, lanes = tiled_ref.shape
    rows = tokens * places
    tiled = tiled_ref[...].astype(jnp.float32).reshape(rows, lanes)
    lane = lax.broadcasted_iota(jnp.int32, (rows, lanes), 1)
    place = lax.broadcasted_iota(jnp.int32, (rows, lanes), 0) % places
    windows = tiled
    for offset in range(1, WIDEST):
        windows = jnp.where(lane // EMBED == offset, shift_rows(tiled, rows - offset), windows)
    late = place >= CHAR_COUNT - WIDEST + 1 + (lane - TAPS - 1)
    extra = jnp.where((lane == TAPS) | ((lane <= TAPS + WIDEST) & late), 1.0, 0.0)
    windows = jnp.where(lane < TAPS, windows, extra)
    windows_wide[...] = windows.astype(jnp.bfloat16)
    windows_tight[...] = (
        windows.reshape(tokens, places, lanes)[:, :TIGHT]
        .reshape(tokens * TIGHT, lanes)
        .astype(jnp.bfloat16)
    )


def column_chunks(total, tight_from):
    return [
        (start, start < tight_from) for start in range(0, total, CHUNK)
    ]


def pool_kernel(tight_from, tiled_ref, weight_ref, count_ref, features_ref, lse_ref, wide, tight):
    tokens, places, lanes = tiled_ref.shape
    block_windows(tiled_ref, wide, tight)
    for start, is_wide in column_chunks(weight_ref.shape[1], tight_from):
        cols = pl.ds(start, CHUNK)
        windows = wide if is_wide else tight
        conv_out = jnp.dot(
            windows[...], weight_ref[:, cols], preferred_element_type=jnp.float32
        ).reshape(tokens, -1, CHUNK)
        highest = jnp.max(conv_out, axis=1)
        total = jnp.sum(jnp.exp(conv_out - highest[:, None, :]), axis=1)
        pooled_lse = highest + jnp.log(total)
        lse_ref[:, cols] = pooled_lse
        pooled_pre = pooled_lse - count_ref[0:1, cols]
        features_ref[:, cols] = (pooled_pre * jax.nn.sigmoid(pooled_pre)).astype(jnp.bfloat16)


def pool_grad_block(
    tight_from,
    tiled_ref,
    ids_row,
    weight_ref,
    count_ref,
    lse_ref,
    upstream_ref,
    grad_weight_ref,
    table_ref,
    wide,
    tight,
    spread,
):
    tokens, places, lanes = tiled_ref.shape
    block_windows(tiled_ref, wide, tight)
    spread[...] = jnp.zeros_like(spread)
    wide_turned = wide[...].T
    tight_turned = tight[...].T
    for start, is_wide in column_chunks(weight_ref.shape[1], tight_from):
        cols = pl.ds(start, CHUNK)
        windows, turned = (wide, wide_turned) if is_wide else (tight, tight_turned)
        weights = weight_ref[:, cols]
        conv_out = jnp.dot(
            windows[...], weights, preferred_element_type=jnp.float32
        ).reshape(tokens, -1, CHUNK)
        pooled_lse = lse_ref[:, cols]
        pooled_pre = pooled_lse - count_ref[0:1, cols]
        squashed = jax.nn.sigmoid(pooled_pre)
        upstream = (
            upstream_ref[:, cols].astype(jnp.float32)
            * squashed
            * (1.0 + pooled_pre * (1.0 - squashed))
        )
        softened = jnp.exp(conv_out - pooled_lse[:, None, :])
        grad_conv = (softened * upstream[:, None, :]).astype(jnp.bfloat16)
        places_here = grad_conv.shape[1]
        grad_conv = grad_conv.reshape(tokens * places_here, CHUNK)
        grad_weight_ref[:, cols] += jnp.dot(turned, grad_conv, preferred_element_type=jnp.float32)
        part = lax.dot_general(
            grad_conv, weights, (((1,), (1,)), ((), ())), preferred_element_type=jnp.float32
        ).reshape(tokens, places_here, lanes)
        spread[:, :places_here, :] += part
    rows = tokens * places
    flat = spread[...].reshape(rows, lanes)
    lane = lax.broadcasted_iota(jnp.int32, (rows, lanes), 1)
    aligned = jnp.where(lane < EMBED, flat, 0.0)
    for offset in range(1, WIDEST):
        aligned = jnp.where(lane // EMBED == offset, shift_rows(flat, offset), aligned)
    high = aligned.astype(jnp.bfloat16)
    low = (aligned - high.astype(jnp.float32)).astype(jnp.bfloat16)
    vocab = table_ref.shape[0]
    selector = jnp.where(
        lax.broadcasted_iota(jnp.int32, (vocab, rows), 0) == ids_row, 1.0, 0.0
    ).astype(jnp.bfloat16)
    table_ref[...] += jnp.dot(selector, high, preferred_element_type=jnp.float32) + jnp.dot(
        selector, low, preferred_element_type=jnp.float32
    )


def filter_matrix(conv_weight, conv_bias):
    bank_cols = conv_bias.shape[1]
    taps, biases, masks, counts = [], [], [], []
    for filter_width, bank_index, first_col, count in filter_columns(bank_cols):
        piece = conv_weight[bank_index, :filter_width, :, first_col : first_col + count]
        piece = piece.reshape(filter_width * EMBED, count)
        taps.append(jnp.pad(piece, ((0, TAPS - filter_width * EMBED), (0, 0))))
        biases.append(conv_bias[bank_index, first_col : first_col + count])
        rows = lax.broadcasted_iota(jnp.int32, (LANES - TAPS - 1, count), 0)
        masks.append(jnp.where(rows == WIDEST - filter_width, -1e30, 0.0).astype(jnp.bfloat16))
        counts.append(jnp.full((8, count), math.log(CHAR_COUNT - filter_width + 1), jnp.float32))
    weights = jnp.concatenate(
        [
            jnp.concatenate(taps, axis=1),
            jnp.concatenate(biases)[None],
            jnp.concatenate(masks, axis=1),
        ],
        axis=0,
    )
    return (weights, jnp.concatenate(counts, axis=1))


def wide_columns(bank_cols):
    total = sum(count for width, bank, first, count in filter_columns(bank_cols) if CHAR_COUNT - width + 1 > TIGHT - 2)
    return -(-total // CHUNK) * CHUNK


def char_selector(token_ids, vocab_size):
    return token_ids.reshape(-1)[:, None] == lax.broadcasted_iota(jnp.int32, (1, vocab_size), 1)


def embed_tokens(token_ids, char_table):
    tokens = token_ids.shape[0]
    padded = jnp.pad(token_ids, ((0, 0), (0, PLACES - token_ids.shape[1])), constant_values=-1)
    table_tiled = jnp.pad(jnp.tile(char_table, (1, WIDEST)), ((0, 0), (0, LANES - TAPS)))
    selector = char_selector(padded, char_table.shape[0]).astype(jnp.bfloat16)
    tiled = jnp.dot(selector, table_tiled, preferred_element_type=jnp.float32)
    tiled = tiled.astype(jnp.bfloat16).reshape(tokens, PLACES, LANES)
    return (padded, tiled)


TEAM = ("t", "x", "c")
GRID = ("g", "y")
EVERY = ("g", "t", "y", "x", "c")


def team_place():
    x_size, c_size = lax.axis_size("x"), lax.axis_size("c")
    return (lax.axis_index("t") * x_size + lax.axis_index("x")) * c_size + lax.axis_index("c")


def team_size():
    return lax.axis_size("t") * lax.axis_size("x") * lax.axis_size("c")


def team_coords(place):
    x_size, c_size = lax.axis_size("x"), lax.axis_size("c")
    return {
        "t": place // (x_size * c_size),
        "x": lax.rem(place // c_size, x_size),
        "c": lax.rem(place, c_size),
    }


def swap_team(values):
    return lax.all_to_all(values, TEAM, split_axis=0, concat_axis=0, tiled=True)


def share_team(values):
    team = team_size()
    return swap_team(jnp.broadcast_to(values[None], (team,) + values.shape))


def sigmoid(values):
    return 0.5 * jnp.tanh(0.5 * values) + 0.5


def wait_bytes(ref, sem):
    pltpu.make_async_copy(ref, ref, sem).wait()


def lstm_kernel(
    team,
    lin_ref,
    out_grad_ref,
    weight_hbm,
    turned_hbm,
    bias_ref,
    keep_ref,
    grad_lin_all_ref,
    grad_weight_hbm,
    grad_turned_hbm,
    grad_bias_ref,
    weight_ref,
    proj_ref,
    grad_gates_ref,
    lin_all_ref,
    state_ref,
    full_ref,
    grad_proj_ref,
    gates,
    cell_start,
    projected,
    stage,
    received,
    received_back,
    grad_cell,
    grad_lin_sum,
    stage_lin,
    received_lin,
    grad_state_own,
    grad_stage,
    turned_stage,
    load_sems,
    lin_sems,
    send_sems,
    sum_sems,
    share_send_sems,
    share_sems,
    out_sems,
):
    _, steps, own, width = lin_ref.shape
    group = team * own
    cells = proj_ref.shape[2]
    row_block = 32
    place = team_place()
    own_rows = pl.ds(pl.multiple_of(place * own, own), own)
    peers = [lax.rem(place + k, team) for k in range(1, team)]
    last = steps - 1
    others = pl.ds(0, team - 1)
    other_rows = pl.ds(0, (team - 1) * own)
    g_size, y_size = lax.axis_size("g"), lax.axis_size("y")
    t_size = lax.axis_size("t")
    blocks = [
        (g * y_size + y, t, (g * t_size + t) * y_size + y)
        for g in range(g_size)
        for t in range(t_size)
        for y in range(y_size)
    ]
    run = weight_hbm.shape[4]
    turned_run = turned_hbm.shape[3]

    for d in range(2):
        for source, t, at in blocks:
            for q in range(4):
                pltpu.make_async_copy(
                    weight_hbm.at[source, t, d, q],
                    weight_ref.at[d, pl.ds(at * run, run), pl.ds(q * cells, cells)],
                    load_sems.at[0],
                ).start()
            pltpu.make_async_copy(
                turned_hbm.at[source, t, d],
                proj_ref.at[d, pl.ds(at * turned_run, turned_run)],
                load_sems.at[1],
            ).start()

    barrier = pltpu.get_barrier_semaphore()
    for peer in peers:
        pl.semaphore_signal(
            barrier, inc=1, device_id=team_coords(peer), device_id_type=pl.DeviceIdType.MESH
        )
    pl.semaphore_wait(barrier, team - 1)

    def send(source, target, send_sem, recv_sem, peer):
        pltpu.make_async_remote_copy(
            src_ref=source,
            dst_ref=target,
            send_sem=send_sem,
            recv_sem=recv_sem,
            device_id=team_coords(peer),
            device_id_type=pl.DeviceIdType.MESH,
        ).start()

    for t in range(steps):
        lin_all_ref[t] = lin_ref[:, t].reshape(group, width)
    for d in range(2):
        first = 0 if d == 0 else last
        state_ref[d, first] = jnp.zeros((group, width), jnp.bfloat16)
        cell_start[d, first] = jnp.zeros((group, cells), jnp.float32)
        grad_cell[d] = jnp.zeros((group, cells), jnp.float32)
    grad_lin_sum[...] = jnp.zeros_like(grad_lin_sum)
    wait_bytes(weight_ref, load_sems.at[0])
    wait_bytes(proj_ref, load_sems.at[1])

    @pl.loop(0, steps)
    def _(t):
        for d in range(2):
            for q in range(4):
                cols = pl.ds(q * cells, cells)
                gates[d, t, :, cols] = (
                    jnp.dot(
                        lin_all_ref[t],
                        weight_ref[d, :width, cols],
                        preferred_element_type=jnp.float32,
                    )
                    + bias_ref[d, :, cols]
                )

    def time_of(d, s):
        return s if d == 0 else last - s

    @pl.loop(0, steps)
    def _(s):
        for d in range(2):
            t = time_of(d, s)
            later = time_of(d, jnp.minimum(s + 1, last))

            @pl.when(s > 0)
            def _():
                wait_bytes(
                    state_ref.at[d, t, other_rows], share_sems.at[0, d, s]
                )
                for q in range(4):
                    cols = pl.ds(q * cells, cells)
                    gates[d, t, :, cols] += jnp.dot(
                        state_ref[d, t],
                        weight_ref[d, width:, cols],
                        preferred_element_type=jnp.float32,
                    )

            @pl.loop(0, group // row_block)
            def _(block):
                rows = pl.ds(pl.multiple_of(block * row_block, row_block), row_block)
                in_gate = sigmoid(gates[d, t, rows, pl.ds(0, cells)])
                forget_gate = sigmoid(gates[d, t, rows, pl.ds(cells, cells)])
                candidate = jnp.tanh(gates[d, t, rows, pl.ds(2 * cells, cells)])
                out_gate = sigmoid(gates[d, t, rows, pl.ds(3 * cells, cells)])
                gates[d, t, rows, pl.ds(0, cells)] = in_gate
                gates[d, t, rows, pl.ds(cells, cells)] = forget_gate
                gates[d, t, rows, pl.ds(2 * cells, cells)] = candidate
                gates[d, t, rows, pl.ds(3 * cells, cells)] = out_gate
                mixed = forget_gate * cell_start[d, t, rows] + in_gate * candidate
                cell_new = 3.0 * jnp.tanh(mixed * (1.0 / 3.0))
                full_ref[d, t, rows] = (out_gate * jnp.tanh(cell_new)).astype(jnp.bfloat16)

                @pl.when(s < last)
                def _():
                    cell_start[d, later, rows] = cell_new * keep_ref[d, later, rows]

            @pl.when(s > 0)
            def _():
                wait_bytes(stage.at[d, others], send_sems.at[d])

            part = lax.dot_general(
                full_ref[d, t],
                proj_ref[d],
                (((1,), (1,)), ((), ())),
                preferred_element_type=jnp.float32,
            )
            part = part.astype(jnp.bfloat16).reshape(team, own, width)
            stage[d] = part
            received[d, s, place] = stage[d, place]
            for peer in peers:
                send(
                    stage.at[d, peer],
                    received.at[d, s, place],
                    send_sems.at[d],
                    sum_sems.at[0, d, s],
                    peer,
                )
        for d in range(2):
            t = time_of(d, s)
            later = time_of(d, jnp.minimum(s + 1, last))
            wait_bytes(received.at[d, s, others], sum_sems.at[0, d, s])
            total = jnp.sum(received[d, s].astype(jnp.float32), axis=0)
            projected[d, t] = total

            @pl.when(s > 0)
            def _():
                wait_bytes(
                    state_ref.at[d, t, other_rows], share_send_sems.at[0, d]
                )

            @pl.when(s < last)
            def _():
                state_new = (3.0 * jnp.tanh(total * (1.0 / 3.0))).astype(jnp.bfloat16)
                kept = state_new.astype(jnp.float32) * keep_ref[d, later, own_rows]
                state_ref[d, later, own_rows] = kept.astype(jnp.bfloat16)
                for peer in peers:
                    send(
                        state_ref.at[d, later, own_rows],
                        state_ref.at[d, later, own_rows],
                        share_send_sems.at[0, d],
                        share_sems.at[0, d, s + 1],
                        peer,
                    )

    @pl.loop(0, steps)
    def _(s):
        for d in range(2):
            t = time_of(1 - d, s)

            @pl.when(s > 0)
            def _():
                wait_bytes(
                    received_back.at[d, jnp.maximum(s - 1, 0), others],
                    sum_sems.at[1, d, jnp.maximum(s - 1, 0)],
                )
                grad_state_own[...] = jnp.sum(
                    received_back[d, jnp.maximum(s - 1, 0)].astype(jnp.float32), axis=0
                )

            @pl.when(s == 0)
            def _():
                grad_state_own[...] = jnp.zeros((own, width), jnp.float32)

            grad_state = grad_state_own[...] + out_grad_ref[d, t].astype(jnp.float32)
            squashed = jnp.tanh(projected[d, t] * (1.0 / 3.0))
            grad_proj_ref[d, t, own_rows] = (grad_state * (1.0 - squashed * squashed)).astype(
                jnp.bfloat16
            )
            for peer in peers:
                send(
                    grad_proj_ref.at[d, t, own_rows],
                    grad_proj_ref.at[d, t, own_rows],
                    share_send_sems.at[1, d],
                    share_sems.at[1, d, s],
                    peer,
                )
        for d in range(2):
            t = time_of(1 - d, s)
            wait_bytes(grad_proj_ref.at[d, t, other_rows], share_sems.at[1, d, s])
            wait_bytes(
                grad_proj_ref.at[d, t, other_rows], share_send_sems.at[1, d]
            )

            @pl.loop(0, group // row_block)
            def _(block):
                rows = pl.ds(pl.multiple_of(block * row_block, row_block), row_block)
                grad_full = jnp.dot(
                    grad_proj_ref[d, t, rows], proj_ref[d], preferred_element_type=jnp.float32
                )
                in_gate = gates[d, t, rows, pl.ds(0, cells)]
                forget_gate = gates[d, t, rows, pl.ds(cells, cells)]
                candidate = gates[d, t, rows, pl.ds(2 * cells, cells)]
                out_gate = gates[d, t, rows, pl.ds(3 * cells, cells)]
                start = cell_start[d, t, rows]
                clipped = jnp.tanh((forget_gate * start + in_gate * candidate) * (1.0 / 3.0))
                tanh_cell = jnp.tanh(3.0 * clipped)
                total = grad_cell[d, rows] + grad_full * out_gate * (1.0 - tanh_cell * tanh_cell)
                grad_raw = total * (1.0 - clipped * clipped)
                grad_gates_ref[d, t, rows, pl.ds(0, cells)] = (
                    grad_raw * candidate * in_gate * (1.0 - in_gate)
                ).astype(jnp.bfloat16)
                grad_gates_ref[d, t, rows, pl.ds(cells, cells)] = (
                    grad_raw * start * forget_gate * (1.0 - forget_gate)
                ).astype(jnp.bfloat16)
                grad_gates_ref[d, t, rows, pl.ds(2 * cells, cells)] = (
                    grad_raw * in_gate * (1.0 - candidate * candidate)
                ).astype(jnp.bfloat16)
                grad_gates_ref[d, t, rows, pl.ds(3 * cells, cells)] = (
                    grad_full * tanh_cell * out_gate * (1.0 - out_gate)
                ).astype(jnp.bfloat16)
                grad_cell[d, rows] = grad_raw * forget_gate * keep_ref[d, t, rows]

            wait_bytes(stage.at[d, others], send_sems.at[d])

            @pl.when(s < last)
            def _():
                part = (
                    lax.dot_general(
                        grad_gates_ref[d, t],
                        weight_ref[d, width:],
                        (((1,), (1,)), ((), ())),
                        preferred_element_type=jnp.float32,
                    )
                    * keep_ref[d, t]
                )
                stage[d] = part.astype(jnp.bfloat16).reshape(team, own, width)
                received_back[d, s, place] = stage[d, place]
                for peer in peers:
                    send(
                        stage.at[d, peer],
                        received_back.at[d, s, place],
                        send_sems.at[d],
                        sum_sems.at[1, d, s],
                        peer,
                    )

            grad_lin_sum[t] += lax.dot_general(
                grad_gates_ref[d, t],
                weight_ref[d, :width],
                (((1,), (1,)), ((), ())),
                preferred_element_type=jnp.float32,
            )

    for t in range(steps):
        stage_lin[:, t] = grad_lin_sum[t].astype(jnp.bfloat16).reshape(team, own, width)
    received_lin[place] = stage_lin[place]
    for peer in peers:
        send(stage_lin.at[peer], received_lin.at[place], lin_sems.at[4], lin_sems.at[5], peer)

    count = steps * group
    half_blocks = len(blocks) // 2

    def weight_grads(d):
        for half in range(2):

            @pl.loop(0, 4)
            def _(q):
                cols = pl.ds(pl.multiple_of(q * cells, cells), cells)
                slot = lax.rem(q, 2)
                rows_in = (lin_all_ref[...] if half == 0 else state_ref[d]).reshape(count, width)
                gate_part = grad_gates_ref[d, :, :, cols].reshape(count, cells)
                part = lax.dot_general(
                    rows_in,
                    gate_part,
                    (((0,), (0,)), ((), ())),
                    preferred_element_type=jnp.float32,
                )

                @pl.when(q >= 2)
                def _():
                    wait_bytes(grad_stage.at[slot], out_sems.at[slot])

                grad_stage[slot] = part.astype(jnp.bfloat16)
                for source, t, at in blocks[half * half_blocks : (half + 1) * half_blocks]:
                    pltpu.make_async_copy(
                        grad_stage.at[slot, pl.ds((at - half * half_blocks) * run, run)],
                        grad_weight_hbm.at[source, t, d, :, cols],
                        out_sems.at[slot],
                    ).start()

            for slot in range(2):
                wait_bytes(grad_stage.at[slot], out_sems.at[slot])
        turned = lax.dot_general(
            grad_proj_ref[d].reshape(count, width),
            full_ref[d].reshape(count, cells),
            (((0,), (0,)), ((), ())),
            preferred_element_type=jnp.float32,
        )
        turned_stage[d] = turned.astype(jnp.bfloat16)
        for source, t, at in blocks:
            pltpu.make_async_copy(
                turned_stage.at[d, pl.ds(at * turned_run, turned_run)],
                grad_turned_hbm.at[source, t, d],
                out_sems.at[2 + d],
            ).start()
        ones = jnp.ones((8, count), jnp.bfloat16)
        for q in range(4):
            cols = pl.ds(q * cells, cells)
            grad_bias_ref[d, :, cols] = jnp.dot(
                ones,
                grad_gates_ref[d, :, :, cols].reshape(count, cells),
                preferred_element_type=jnp.float32,
            )

    weight_grads(0)
    wait_bytes(received_lin.at[others], lin_sems.at[5])
    grad_lin_all_ref[place] = jnp.sum(received_lin[...].astype(jnp.float32), axis=0).astype(
        jnp.bfloat16
    )
    for peer in peers:
        send(
            grad_lin_all_ref.at[place],
            grad_lin_all_ref.at[place],
            lin_sems.at[6],
            lin_sems.at[7],
            peer,
        )
    weight_grads(1)
    wait_bytes(grad_lin_all_ref.at[others], lin_sems.at[7])
    wait_bytes(stage_lin.at[others], lin_sems.at[4])
    wait_bytes(grad_lin_all_ref.at[others], lin_sems.at[6])
    for d in range(2):
        wait_bytes(turned_stage.at[d], out_sems.at[2 + d])


def run_lstm(lin, out_grad, weights, turned, bias, keep):
    team, steps, own, width = lin.shape
    group = team * own
    cells = turned.shape[4]
    bf16, f32 = jnp.bfloat16, jnp.float32
    vmem = pl.BlockSpec(memory_space=pltpu.VMEM)
    hbm = pl.BlockSpec(memory_space=pl.ANY)
    return pl.pallas_call(
        partial(lstm_kernel, team),
        in_specs=[vmem, vmem, hbm, hbm, vmem, vmem],
        out_specs=[vmem, hbm, hbm, vmem],
        out_shape=[
            jax.ShapeDtypeStruct(lin.shape, bf16),
            jax.ShapeDtypeStruct(weights.shape[:3] + (weights.shape[4], 4 * cells), bf16),
            jax.ShapeDtypeStruct(turned.shape, bf16),
            jax.ShapeDtypeStruct((2, 8, 4 * cells), f32),
        ],
        scratch_shapes=[
            pltpu.VMEM((2, 2 * width, 4 * cells), bf16),
            pltpu.VMEM((2, width, cells), bf16),
            pltpu.VMEM((2, steps, group, 4 * cells), bf16),
            pltpu.VMEM((steps, group, width), bf16),
            pltpu.VMEM((2, steps, group, width), bf16),
            pltpu.VMEM((2, steps, group, cells), bf16),
            pltpu.VMEM((2, steps, group, width), bf16),
            pltpu.VMEM((2, steps, group, 4 * cells), f32),
            pltpu.VMEM((2, steps, group, cells), f32),
            pltpu.VMEM((2, steps, own, width), f32),
            pltpu.VMEM((2, team, own, width), bf16),
            pltpu.VMEM((2, steps, team, own, width), bf16),
            pltpu.VMEM((2, steps, team, own, width), bf16),
            pltpu.VMEM((2, group, cells), f32),
            pltpu.VMEM((steps, group, width), f32),
            pltpu.VMEM((team, steps, own, width), bf16),
            pltpu.VMEM((team, steps, own, width), bf16),
            pltpu.VMEM((own, width), f32),
            pltpu.VMEM((2, width, cells), bf16),
            pltpu.VMEM((2, width, cells), bf16),
            pltpu.SemaphoreType.DMA((2,)),
            pltpu.SemaphoreType.DMA((8,)),
            pltpu.SemaphoreType.DMA((2,)),
            pltpu.SemaphoreType.DMA((2, 2, steps)),
            pltpu.SemaphoreType.DMA((2, 2)),
            pltpu.SemaphoreType.DMA((2, 2, steps)),
            pltpu.SemaphoreType.DMA((4,)),
        ],
        compiler_params=pltpu.CompilerParams(
            collective_id=1, has_side_effects=True, vmem_limit_bytes=63 * 1024 * 1024
        ),
        name="lstm_team",
    )(lin, out_grad, weights, turned, bias, keep)


def member_at(offset):
    t_size, x_size, c_size = lax.axis_size("t"), lax.axis_size("x"), lax.axis_size("c")
    dt, dx, dc = offset // (x_size * c_size), lax.rem(offset // c_size, x_size), lax.rem(offset, c_size)
    t = lax.rem(lax.axis_index("t") + dt, t_size)
    x = lax.rem(lax.axis_index("x") + dx, x_size)
    c = lax.rem(lax.axis_index("c") + dc, c_size)
    return (t * x_size + x) * c_size + c


def opposite(offset):
    t_size, x_size, c_size = lax.axis_size("t"), lax.axis_size("x"), lax.axis_size("c")
    dt, dx, dc = offset // (x_size * c_size), offset // c_size % x_size, offset % c_size
    return (-dt % t_size * x_size + -dx % x_size) * c_size + -dc % c_size


def send_block(source, target, send_sem, recv_sem, peer):
    pltpu.make_async_remote_copy(
        src_ref=source,
        dst_ref=target,
        send_sem=send_sem,
        recv_sem=recv_sem,
        device_id=team_coords(peer),
        device_id_type=pl.DeviceIdType.MESH,
    ).start()


def greet(offsets, with_grid=False):
    barrier = pltpu.get_barrier_semaphore()
    for offset in offsets:
        pl.semaphore_signal(
            barrier,
            inc=1,
            device_id=team_coords(member_at(offset)),
            device_id_type=pl.DeviceIdType.MESH,
        )
    extra = greet_grid(barrier) if with_grid else 0
    pl.semaphore_wait(barrier, len(offsets) + extra)


def load_level(first_hbm, weights, level, run, sem):
    grid = first_hbm.shape[0]
    team = team_size()

    @pl.loop(0, team)
    def _(member):
        for block in range(grid):
            pltpu.make_async_copy(
                first_hbm.at[
                    block, pl.ds(pl.multiple_of((level * team + member) * run, run), run)
                ],
                weights.at[level, pl.ds(pl.multiple_of((member * grid + block) * run, run), run)],
                sem,
            ).start()


def load_project(first_hbm, project, sem):
    grid = first_hbm.shape[0]
    run = project.shape[0] // grid
    for block in range(grid):
        pltpu.make_async_copy(
            first_hbm.at[block, pl.ds(team_size() * 2 * run, run)],
            project.at[pl.ds(block * run, run)],
            sem,
        ).start()


def grid_coords(dg, dy):
    g_size, y_size = lax.axis_size("g"), lax.axis_size("y")
    return {
        "g": lax.rem(lax.axis_index("g") + dg, g_size),
        "y": lax.rem(lax.axis_index("y") + dy, y_size),
    }


def grid_block(dg, dy):
    coords = grid_coords(dg, dy)
    return coords["g"] * lax.axis_size("y") + coords["y"]


def send_grid(source, target, send_sem, recv_sem, dg, dy):
    pltpu.make_async_remote_copy(
        src_ref=source,
        dst_ref=target,
        send_sem=send_sem,
        recv_sem=recv_sem,
        device_id=grid_coords(dg, dy),
        device_id_type=pl.DeviceIdType.MESH,
    ).start()


def greet_grid(barrier):
    for dg in range(1, lax.axis_size("g")):
        pl.semaphore_signal(
            barrier, inc=1, device_id=grid_coords(dg, 0), device_id_type=pl.DeviceIdType.MESH
        )
    pl.semaphore_signal(
        barrier, inc=1, device_id=grid_coords(0, 1), device_id_type=pl.DeviceIdType.MESH
    )
    return lax.axis_size("g")


class Gather:
    def __init__(self, blocks, targets, send_sem, recv_sems):
        self.blocks = blocks
        self.targets = targets
        self.send_sem = send_sem
        self.recv_sems = recv_sems

    def start(self, pieces):
        home = grid_block(0, 0)
        g_size = lax.axis_size("g")
        for piece in pieces:
            source = self.blocks[piece]
            target = self.targets[piece](home)
            for dg in range(1, g_size):
                send_grid(
                    source, target, self.send_sem, self.recv_sems.at[piece, g_size - dg, 0], dg, 0
                )
            send_grid(source, target, self.send_sem, self.recv_sems.at[piece, 0, 1], 0, 1)

    def forward(self, pieces):
        for piece in pieces:
            for dg in range(1, lax.axis_size("g")):
                target = self.targets[piece](grid_block(dg, 0))
                wait_bytes(target, self.recv_sems.at[piece, dg, 0])
                send_grid(target, target, self.send_sem, self.recv_sems.at[piece, dg, 1], 0, 1)

    def finish(self, pieces):
        for piece in pieces:
            for dg in range(lax.axis_size("g")):
                wait_bytes(self.targets[piece](grid_block(dg, 1)), self.recv_sems.at[piece, dg, 1])

    def sent(self, pieces):
        for piece in pieces:
            for _ in range(2 * lax.axis_size("g") - 1):
                wait_bytes(self.blocks[piece], self.send_sem)


def highway_kernel(
    tight_from,
    direct,
    tiled_ref,
    filter_ref,
    count_ref,
    block_hbm,
    lstm_block_hbm,
    turned_block_hbm,
    bias_ref,
    lin_bias_ref,
    lse_ref,
    first_hbm,
    lstm_hbm,
    turned_hbm,
    first_ref,
    second_ref,
    mixed_ref,
    hidden_ref,
    top_ref,
    lin_ref,
    parts,
    parts_recv,
    features_own,
    wide,
    tight,
    weights,
    project,
    load_sems,
    send_sems,
    first_sems,
    second_sems,
    gather_send_sems,
    block_sems,
    turned_sems,
    lstm_sems,
    lin_sems,
    swap_sems,
):
    team, tokens, features = first_ref.shape
    part = features // team
    cores = lax.axis_size("c")
    g_size, y_size = lax.axis_size("g"), lax.axis_size("y")
    place = team_place()
    sibling = member_at(1)
    near = list(range(cores, team, cores))
    chips = team // cores
    chunks = lstm_hbm.shape[1]
    greet(list(range(1, team)) if direct else [1] + near, True)
    home = grid_block(0, 0)
    run = project.shape[0] // first_hbm.shape[0]
    quarter = team * run // 4
    places = [pl.ds(k * quarter, quarter) for k in range(8)] + [pl.ds(8 * quarter, run)]
    block_gather = Gather(
        [block_hbm.at[rows] for rows in places],
        [lambda at, rows=rows: first_hbm.at[at, rows] for rows in places],
        gather_send_sems.at[0],
        block_sems,
    )
    turned_gather = Gather(
        [turned_hbm.at[home]],
        [lambda at: turned_hbm.at[at]],
        gather_send_sems.at[1],
        turned_sems,
    )
    all_places = list(range(len(places)))
    block_gather.start(all_places[:4])
    pltpu.make_async_copy(block_hbm, first_hbm.at[home], load_sems.at[3]).start()
    over_x = cores
    over_t = lax.axis_size("x") * cores
    across = over_t + over_x
    x_peer = member_at(over_x)
    if direct:
        banks = lax.axis_size("x") * cores
        t_index, bank = place // banks, lax.rem(place, banks)
        each = lstm_block_hbm.shape[1] // 8
        short = turned_block_hbm.shape[1] // 2

        def routes(member):
            for k in range(8):
                rows = pl.ds(pl.multiple_of(bank * each, each), each)
                yield (
                    lstm_block_hbm.at[member, pl.ds(k * each, each)],
                    lstm_hbm.at[home, t_index * 8 + k, rows],
                    0,
                )
            for d in range(2):
                rows = pl.ds(pl.multiple_of(bank * short, short), short)
                yield (
                    turned_block_hbm.at[member, pl.ds(d * short, short)],
                    turned_hbm.at[home, t_index, d, rows],
                    1,
                )

        def swap(offsets):
            for offset in offsets:
                member = member_at(offset)
                for source, target, which in routes(member):
                    send_block(
                        source, target, swap_sems.at[which], swap_sems.at[2 + which], member
                    )

        swap(range(1, over_t))
        for source, target, which in routes(place):
            pltpu.make_async_copy(source, target, swap_sems.at[4 + which]).start()
    else:
        pltpu.make_async_copy(turned_block_hbm, turned_hbm.at[home], swap_sems.at[5]).start()
        pltpu.make_async_copy(lstm_block_hbm, lstm_hbm.at[home], swap_sems.at[4]).start()

    def columns(member):
        return pl.ds(pl.multiple_of(member * part, part), part)

    token_block = wide.shape[0] // tiled_ref.shape[1]

    @pl.loop(0, tokens // token_block)
    def _(step):
        rows = pl.ds(pl.multiple_of(step * token_block, token_block), token_block)
        pool_kernel(
            tight_from,
            tiled_ref.at[rows],
            filter_ref,
            count_ref,
            features_own.at[rows],
            lse_ref.at[rows],
            wide,
            tight,
        )

    g, t, y, x, c = axis_sizes()
    natural = features_own[...]
    starts = [
        ((((gi * t + ti) * y + yi) * x + xi) * c + ci) * run
        for ti in range(t)
        for xi in range(x)
        for ci in range(c)
        for gi in range(g)
        for yi in range(y)
    ]
    features_own[...] = jnp.concatenate([natural[:, at : at + run] for at in starts], axis=1)

    for offset in (over_t, over_x, 1):
        send_block(
            features_own,
            first_ref.at[place],
            send_sems.at[0],
            first_sems.at[opposite(offset)],
            member_at(offset),
        )
    first_ref[place] = features_own[...]
    block_gather.start(all_places[4:])
    if direct:
        swap(range(over_t, team))
    block_gather.forward(all_places[:4])

    def lstm_start(chunk):
        for dg in range(1, g_size):
            send_grid(
                lstm_hbm.at[home, chunk],
                lstm_hbm.at[home, chunk],
                gather_send_sems.at[2],
                lstm_sems.at[chunk, g_size - dg, 0],
                dg,
                0,
            )

    def lstm_forward(chunk):
        for dg in range(1, g_size):
            target = lstm_hbm.at[grid_block(dg, 0), chunk]
            wait_bytes(target, lstm_sems.at[chunk, dg, 0])
            send_grid(
                target, target, gather_send_sems.at[3], lstm_sems.at[chunk, dg, 1], 0, 1
            )

    def pump(chunk):
        @pl.when(chunk < chunks)
        def _():
            lstm_forward(jnp.minimum(chunk, chunks - 1))

            @pl.when(chunk + AHEAD < chunks)
            def _():
                lstm_start(jnp.minimum(chunk + AHEAD, chunks - 1))

    for offset in (over_t, over_x, across):
        member = member_at(offset)
        block = first_ref.at[member]
        wait_bytes(block, first_sems.at[offset])
        if offset == over_t:
            send_block(block, block, send_sems.at[0], first_sems.at[across], x_peer)
        send_block(block, block, send_sems.at[0], first_sems.at[offset + 1], sibling)
    block_gather.finish(all_places[:4])
    wait_bytes(block_hbm, load_sems.at[3])
    load_level(first_hbm, weights, 0, run, load_sems.at[0])
    wait_bytes(weights.at[0], load_sems.at[0])

    rows = cores * tokens

    def mix(level, pair, operand):
        mixed = (
            jnp.dot(
                operand.reshape(rows, features), weights[level], preferred_element_type=jnp.float32
            )
            + bias_ref[level : level + 1]
        )
        mixed_ref[level, pair] = mixed.reshape(cores, tokens, 2 * part)
        gate = sigmoid(mixed[:, part:])
        pre_act = mixed[:, :part]
        return (gate, pre_act * sigmoid(pre_act))

    for step in range(chips):
        chip = member_at(step * cores) // cores
        pair = pl.ds(chip * cores, cores)
        wait_bytes(first_ref.at[member_at(step * cores + 1)], first_sems.at[step * cores + 1])
        gate, act = mix(0, pair, first_ref[pair])
        carried = first_ref[pair, :, columns(place)].astype(jnp.float32).reshape(rows, part)
        hidden = gate * carried + (1.0 - gate) * act
        hidden_ref[pair] = hidden.reshape(cores, tokens, part)
        mine = second_ref.at[pair, :, columns(place)]
        mine[...] = hidden.astype(jnp.bfloat16).reshape(cores, tokens, part)
        for to in (over_t, over_x, 1):
            send_block(
                mine, mine, send_sems.at[1], second_sems.at[chip, opposite(to)], member_at(to)
            )
        block_gather.forward([4 + k for k in range(4 * step // chips, 4 * (step + 1) // chips)])

    if direct:
        wait_bytes(lstm_block_hbm.at[pl.ds(0, team - 1)], swap_sems.at[2])
        wait_bytes(turned_block_hbm.at[pl.ds(0, team - 1)], swap_sems.at[3])
        wait_bytes(lstm_block_hbm.at[0], swap_sems.at[4])
        wait_bytes(turned_block_hbm.at[0], swap_sems.at[5])
    else:
        wait_bytes(lstm_block_hbm, swap_sems.at[4])
        wait_bytes(turned_block_hbm, swap_sems.at[5])
    for chunk in range(min(AHEAD, chunks)):
        lstm_start(chunk)
    block_gather.forward(all_places[8:])
    block_gather.finish(all_places[4:])
    load_level(first_hbm, weights, 1, run, load_sems.at[1])
    load_project(first_hbm, project, load_sems.at[2])

    @pl.loop(0, chunks)
    def _(chunk):
        send_grid(
            lstm_hbm.at[home, chunk],
            lstm_hbm.at[home, chunk],
            gather_send_sems.at[4],
            lstm_sems.at[chunk, 0, 1],
            0,
            1,
        )

    wait_bytes(weights.at[1], load_sems.at[1])
    wait_bytes(project, load_sems.at[2])
    x_size, t_size = lax.axis_size("x"), lax.axis_size("t")

    def ordered_chip(step):
        t_at = lax.rem(lax.axis_index("t") + step // x_size, t_size)
        return t_at * x_size + step % x_size

    for step in range(chips + 1):
        if step < chips:
            chip = ordered_chip(step)
            pair = pl.ds(chip * cores, cores)
            for origin in (over_t, over_x, across):
                piece = second_ref.at[pair, :, columns(member_at(origin))]
                wait_bytes(piece, second_sems.at[chip, origin])
                if origin == over_t:
                    send_block(
                        piece, piece, send_sems.at[1], second_sems.at[chip, across], x_peer
                    )
                send_block(
                    piece, piece, send_sems.at[1], second_sems.at[chip, origin + 1], sibling
                )
        if step > 0:
            chip = ordered_chip(step - 1)
            pair = pl.ds(chip * cores, cores)
            for origin in [0] + near:
                piece = second_ref.at[pair, :, columns(member_at(origin + 1))]
                wait_bytes(piece, second_sems.at[chip, origin + 1])
            gate, act = mix(1, pair, second_ref[pair])
            carried = hidden_ref[pair].reshape(rows, part)
            top = (gate * carried + (1.0 - gate) * act).astype(jnp.bfloat16)
            top_ref[pair] = top.reshape(cores, tokens, part)
            parts[pair] = (
                jnp.dot(top, project[...], preferred_element_type=jnp.float32)
                .astype(jnp.bfloat16)
                .reshape(cores, tokens, -1)
            )
            for core in range(cores):
                member = chip * cores + core

                @pl.when(member != place)
                def _():
                    send_block(
                        parts.at[member],
                        parts_recv.at[place],
                        lin_sems.at[0],
                        lin_sems.at[1],
                        member,
                    )

            pump(step - 1)

    turned_gather.start([0])
    parts_recv[place] = parts[place]
    others = pl.ds(0, team - 1)
    pump(chips)
    pump(chips + 1)
    wait_bytes(parts_recv.at[others], lin_sems.at[1])
    lin = jnp.sum(parts_recv[...].astype(jnp.float32), axis=0) + lin_bias_ref[...]
    lin_ref[place] = lin.astype(jnp.bfloat16)
    for offset in range(1, team):
        send_block(
            lin_ref.at[place],
            lin_ref.at[place],
            lin_sems.at[2],
            lin_sems.at[3],
            member_at(offset),
        )

    @pl.loop(chips + 2, chunks)
    def _(chunk):
        pump(chunk)

    wait_bytes(lin_ref.at[others], lin_sems.at[3])
    wait_bytes(lin_ref.at[others], lin_sems.at[2])
    wait_bytes(parts.at[others], lin_sems.at[0])

    turned_gather.forward([0])
    turned_gather.finish([0])

    @pl.loop(0, chunks)
    def _(chunk):
        for dg in range(g_size):
            wait_bytes(lstm_hbm.at[grid_block(dg, 1), chunk], lstm_sems.at[chunk, dg, 1])

    wait_bytes(first_ref.at[pl.ds(0, team - 1)], send_sems.at[0])
    wait_bytes(second_ref.at[pl.ds(0, team - 1)], send_sems.at[1])
    block_gather.sent(all_places)
    turned_gather.sent([0])
    for _ in range(g_size - 1):
        wait_bytes(lstm_hbm.at[0], gather_send_sems.at[2])
        wait_bytes(lstm_hbm.at[0], gather_send_sems.at[3])
    wait_bytes(lstm_hbm.at[0], gather_send_sems.at[4])
    if direct:
        wait_bytes(lstm_block_hbm.at[pl.ds(0, team - 1)], swap_sems.at[0])
        wait_bytes(turned_block_hbm.at[pl.ds(0, team - 1)], swap_sems.at[1])


def run_highway(
    tight_from, direct, tiled, filters, counts, block, lstm_block, turned_block, bias, lin_bias
):
    team = team_size()
    tokens, features = tiled.shape[0], filters.shape[1]
    part = features // team
    g_size, y_size = lax.axis_size("g"), lax.axis_size("y")
    grid = g_size * y_size
    width = block.shape[1]
    bf16, f32 = jnp.bfloat16, jnp.float32
    vmem = pl.BlockSpec(memory_space=pltpu.VMEM)
    hbm = pl.BlockSpec(memory_space=pl.ANY)
    pieces = 9
    if direct:
        banks = lax.axis_size("x") * lax.axis_size("c")
        halves = lax.axis_size("t")
        lstm_shape = (8 * halves, banks * lstm_block.shape[1] // 8, lstm_block.shape[2])
        turned_shape = (halves, 2, banks * turned_block.shape[1] // 2, turned_block.shape[2])
    else:
        lstm_shape, turned_shape = lstm_block.shape, turned_block.shape
    token_block = math.gcd(tokens, TOKEN_BLOCK)
    return pl.pallas_call(
        partial(highway_kernel, tight_from, direct),
        in_specs=[vmem] * 3 + [hbm] * 3 + [vmem] * 2,
        out_specs=[vmem] + [hbm] * 3 + [vmem] * 6,
        out_shape=[
            jax.ShapeDtypeStruct((tokens, features), f32),
            jax.ShapeDtypeStruct((grid,) + block.shape, bf16),
            jax.ShapeDtypeStruct((grid,) + lstm_shape, bf16),
            jax.ShapeDtypeStruct((grid,) + turned_shape, bf16),
            jax.ShapeDtypeStruct((team, tokens, features), bf16),
            jax.ShapeDtypeStruct((team, tokens, features), bf16),
            jax.ShapeDtypeStruct((2, team, tokens, 2 * part), f32),
            jax.ShapeDtypeStruct((team, tokens, part), f32),
            jax.ShapeDtypeStruct((team, tokens, part), bf16),
            jax.ShapeDtypeStruct((team, tokens, width), bf16),
        ],
        scratch_shapes=[
            pltpu.VMEM((team, tokens, width), bf16),
            pltpu.VMEM((team, tokens, width), bf16),
            pltpu.VMEM((tokens, features), bf16),
            pltpu.VMEM((token_block * PLACES, LANES), bf16),
            pltpu.VMEM((token_block * TIGHT, LANES), bf16),
            pltpu.VMEM((2, features, 2 * part), bf16),
            pltpu.VMEM((part, width), bf16),
            pltpu.SemaphoreType.DMA((5,)),
            pltpu.SemaphoreType.DMA((2,)),
            pltpu.SemaphoreType.DMA((team,)),
            pltpu.SemaphoreType.DMA((team // lax.axis_size("c"), team)),
            pltpu.SemaphoreType.DMA((5,)),
            pltpu.SemaphoreType.DMA((pieces, g_size, y_size)),
            pltpu.SemaphoreType.DMA((1, g_size, y_size)),
            pltpu.SemaphoreType.DMA((lstm_shape[0], g_size, y_size)),
            pltpu.SemaphoreType.DMA((4,)),
            pltpu.SemaphoreType.DMA((6,)),
        ],
        compiler_params=pltpu.CompilerParams(
            collective_id=2, has_side_effects=True, vmem_limit_bytes=60 * 1024 * 1024
        ),
        name="highway_team",
    )(tiled, filters, counts, block, lstm_block, turned_block, bias, lin_bias)


def highway_back_kernel(
    grad_lin_ref,
    first_hbm,
    first_ref,
    second_ref,
    mixed_ref,
    hidden_ref,
    top_ref,
    lstm_hbm,
    features_ref,
    grads_hbm,
    bias_ref,
    lstm_ref,
    lstm_own,
    lstm_y,
    lstm_send,
    lstm_g,
    weights,
    project,
    grad_mixed,
    direct,
    column_parts,
    column_sibling,
    column_send,
    column_recv,
    column_sum_own,
    row_part,
    row_keep,
    row_give,
    row_sibling,
    row_send,
    row_recv,
    row_sum_own,
    grad_stage,
    load_sems,
    send_sems,
    column_sib_sems,
    column_sems,
    row_sib_sems,
    row_sems,
    out_sems,
    lstm_load_sems,
    lstm_send_sems,
    lstm_y_sems,
    lstm_g_sems,
):
    team, tokens, features = first_ref.shape
    part = features // team
    grid = first_hbm.shape[0]
    run = part // grid
    cores = lax.axis_size("c")
    chips = team // cores
    place = team_place()
    sibling = member_at(1)
    near = list(range(1, chips))
    for level in range(2):
        load_level(first_hbm, weights, level, run, load_sems.at[level])
    load_project(first_hbm, project, load_sems.at[2])
    greet([1] + [chip * cores for chip in near], True)
    f32, bf16 = jnp.float32, jnp.bfloat16
    g_size, y_size = lax.axis_size("g"), lax.axis_size("y")
    y_index = lax.axis_index("y")
    other_y = lax.rem(y_index + 1, y_size)
    chunks = lstm_ref.shape[0]

    def lstm_block(dg, y):
        return lax.rem(lax.axis_index("g") + dg, g_size) * y_size + y

    @pl.loop(0, chunks)
    def _(chunk):
        for dg in list(range(1, g_size)) + [0]:
            send_grid(
                lstm_hbm.at[lstm_block(dg, other_y), chunk],
                lstm_y.at[dg, chunk],
                lstm_send_sems.at[0],
                lstm_y_sems.at[chunk, dg],
                0,
                1,
            )

    pltpu.make_async_copy(
        lstm_hbm.at[lstm_block(0, y_index)], lstm_ref, lstm_load_sems.at[0]
    ).start()
    for dg in range(1, g_size):
        pltpu.make_async_copy(
            lstm_hbm.at[lstm_block(dg, y_index)], lstm_own.at[dg - 1], lstm_load_sems.at[1]
        ).start()

    def pump(chunk):
        for dg in range(1, g_size):
            wait_bytes(lstm_y.at[dg, chunk], lstm_y_sems.at[chunk, dg])
            both = lstm_own[dg - 1, chunk].astype(f32) + lstm_y[dg, chunk].astype(f32)
            lstm_send[dg - 1, chunk] = both.astype(bf16)
            send_grid(
                lstm_send.at[dg - 1, chunk],
                lstm_g.at[g_size - dg - 1, chunk],
                lstm_send_sems.at[1],
                lstm_g_sems.at[chunk, g_size - dg - 1],
                dg,
                0,
            )

    def columns(member):
        return pl.ds(pl.multiple_of(member * part, part), part)

    def opposite_chip(chip):
        return opposite(chip * cores) // cores

    for level in range(2):
        wait_bytes(weights.at[level], load_sems.at[level])
    wait_bytes(project, load_sems.at[2])

    def mix_grads(level, member, grad, carried):
        pre_act = mixed_ref[level, member, :, pl.ds(0, part)]
        gate = sigmoid(mixed_ref[level, member, :, pl.ds(part, part)])
        act_sig = sigmoid(pre_act)
        grad_mixed[level, member, :, pl.ds(0, part)] = (
            grad * (1.0 - gate) * act_sig * (1.0 + pre_act * (1.0 - act_sig))
        ).astype(bf16)
        grad_mixed[level, member, :, pl.ds(part, part)] = (
            grad * (carried - pre_act * act_sig) * gate * (1.0 - gate)
        ).astype(bf16)
        return grad * gate

    def spread(level, member):
        return lax.dot_general(
            grad_mixed[level, member],
            weights[level],
            (((1,), (1,)), ((), ())),
            preferred_element_type=f32,
        )

    @pl.loop(0, team)
    def _(member):
        grad = lax.dot_general(
            grad_lin_ref[member], project[...], (((1,), (1,)), ((), ())), preferred_element_type=f32
        )
        direct[member] = mix_grads(1, member, grad, hidden_ref[member])
        column_parts[member] = spread(1, member).astype(bf16)
        for chip in range(chips):
            send_block(
                column_parts.at[member, :, columns(member_at(chip * cores + 1))],
                column_sibling.at[member, chip],
                send_sems.at[0],
                column_sib_sems.at[member],
                sibling,
            )

    wait_bytes(lstm_own, lstm_load_sems.at[1])
    pump(0)

    @pl.loop(0, team)
    def _(member):
        wait_bytes(column_sibling.at[member], column_sib_sems.at[member])
        for chip in near + [0]:
            target = member_at(chip * cores)
            both = column_parts[member, :, columns(target)].astype(f32) + column_sibling[
                member, chip
            ].astype(f32)
            if chip == 0:
                column_sum_own[member] = both
            else:
                column_send[chip - 1, member] = both.astype(bf16)
                send_block(
                    column_send.at[chip - 1, member],
                    column_recv.at[opposite_chip(chip) - 1, member],
                    send_sems.at[1],
                    column_sems.at[member, opposite_chip(chip) - 1],
                    target,
                )

    def weight_grads(level, source_ref):
        @pl.loop(0, team)
        def _(member):
            slot = lax.rem(member, 2)

            @pl.when(member >= 2)
            def _():
                wait_bytes(grad_stage.at[slot], out_sems.at[slot])

            grad_stage[slot] = lax.dot_general(
                source_ref[:, :, columns(member)].reshape(team * tokens, part),
                grad_mixed[level].reshape(team * tokens, 2 * part),
                (((0,), (0,)), ((), ())),
                preferred_element_type=f32,
            ).astype(bf16)
            for block in range(grid):
                pltpu.make_async_copy(
                    grad_stage.at[slot, pl.ds(block * run, run)],
                    grads_hbm.at[
                        block, pl.ds(pl.multiple_of((member * 2 + level) * run, run), run)
                    ],
                    out_sems.at[slot],
                ).start()

        for slot in range(2):
            wait_bytes(grad_stage.at[slot], out_sems.at[slot])
        bias_ref[level] = jnp.dot(
            jnp.ones((8, team * tokens), bf16),
            grad_mixed[level].reshape(team * tokens, 2 * part),
            preferred_element_type=f32,
        )

    pump(1)
    weight_grads(1, second_ref)
    pump(2)

    @pl.loop(0, team)
    def _(step):
        offset = team - 1 - step
        member = member_at(offset)
        chip = offset // cores
        grad = column_sum_own[member] + direct[member]
        for other in near:
            wait_bytes(column_recv.at[other - 1, member], column_sems.at[member, other - 1])
            grad = grad + column_recv[other - 1, member].astype(f32)
        carried = first_ref[member, :, columns(place)].astype(f32)
        straight = mix_grads(0, member, grad, carried)
        row_part[...] = spread(0, member)
        row_part[:, columns(place)] += straight

        @pl.when(lax.rem(offset, cores) == 1)
        def _():
            row_give[chip] = row_part[...].astype(bf16)
            send_block(
                row_give.at[chip],
                row_sibling.at[chip],
                send_sems.at[2],
                row_sib_sems.at[chip],
                sibling,
            )

        @pl.when(lax.rem(offset, cores) == 0)
        def _():
            row_keep[chip] = row_part[...].astype(bf16)

        @pl.when((step == team // 2 - 1) | (step == team - 1))
        def _():
            pump(3 + (step + 1) // team)

    for chip in near[::-1] + [0]:
        wait_bytes(row_sibling.at[chip], row_sib_sems.at[chip])
        both = row_keep[chip].astype(f32) + row_sibling[chip].astype(f32)
        if chip == 0:
            row_sum_own[...] = both
        else:
            row_send[chip - 1] = both.astype(bf16)
            send_block(
                row_send.at[chip - 1],
                row_recv.at[opposite_chip(chip) - 1],
                send_sems.at[3],
                row_sems.at[opposite_chip(chip) - 1],
                member_at(chip * cores),
            )

    pump(5)
    weight_grads(0, first_ref)

    @pl.loop(6, chunks)
    def _(chunk):
        pump(chunk)

    grad_stage[0] = lax.dot_general(
        top_ref[...].reshape(team * tokens, part),
        grad_lin_ref[...].reshape(team * tokens, 2 * part),
        (((0,), (0,)), ((), ())),
        preferred_element_type=f32,
    ).astype(bf16)
    for block in range(grid):
        pltpu.make_async_copy(
            grad_stage.at[0, pl.ds(block * run, run)],
            grads_hbm.at[block, pl.ds(team * 2 * run, run)],
            out_sems.at[0],
        ).start()
    total = row_sum_own[...]
    for other in near:
        wait_bytes(row_recv.at[other - 1], row_sems.at[other - 1])
        total = total + row_recv[other - 1].astype(f32)
    features_ref[...] = total.astype(bf16)
    wait_bytes(lstm_ref, lstm_load_sems.at[0])

    @pl.loop(0, chunks)
    def _(chunk):
        wait_bytes(lstm_y.at[0, chunk], lstm_y_sems.at[chunk, 0])
        whole = lstm_ref[chunk].astype(f32) + lstm_y[0, chunk].astype(f32)
        for dg in range(1, g_size):
            wait_bytes(lstm_g.at[dg - 1, chunk], lstm_g_sems.at[chunk, dg - 1])
            whole = whole + lstm_g[dg - 1, chunk].astype(f32)
        lstm_ref[chunk] = whole.astype(bf16)

    wait_bytes(lstm_y, lstm_send_sems.at[0])
    wait_bytes(lstm_g, lstm_send_sems.at[1])
    wait_bytes(grad_stage.at[0], out_sems.at[0])
    wait_bytes(column_sibling, send_sems.at[0])
    wait_bytes(column_send, send_sems.at[1])
    wait_bytes(row_give, send_sems.at[2])
    wait_bytes(row_send, send_sems.at[3])


def run_highway_back(grad_lin, first_all, first, second, mixed, hidden, top, lstm_grads):
    team, tokens, features = first.shape
    part = features // team
    chips = team // lax.axis_size("c")
    width = first_all.shape[2]
    bf16, f32 = jnp.bfloat16, jnp.float32
    g_size = lax.axis_size("g")
    chunk_shape = lstm_grads.shape[1:]
    vmem = pl.BlockSpec(memory_space=pltpu.VMEM)
    hbm = pl.BlockSpec(memory_space=pl.ANY)
    return pl.pallas_call(
        highway_back_kernel,
        in_specs=[vmem, hbm] + [vmem] * 5 + [hbm],
        out_specs=[vmem, hbm, vmem, vmem],
        out_shape=[
            jax.ShapeDtypeStruct((tokens, features), bf16),
            jax.ShapeDtypeStruct(first_all.shape, bf16),
            jax.ShapeDtypeStruct((2, 8, 2 * part), f32),
            jax.ShapeDtypeStruct(chunk_shape, bf16),
        ],
        scratch_shapes=[
            pltpu.VMEM((g_size - 1,) + chunk_shape, bf16),
            pltpu.VMEM((g_size,) + chunk_shape, bf16),
            pltpu.VMEM((g_size - 1,) + chunk_shape, bf16),
            pltpu.VMEM((g_size - 1,) + chunk_shape, bf16),
            pltpu.VMEM((2, features, 2 * part), bf16),
            pltpu.VMEM((part, width), bf16),
            pltpu.VMEM((2, team, tokens, 2 * part), bf16),
            pltpu.VMEM((team, tokens, part), f32),
            pltpu.VMEM((team, tokens, features), bf16),
            pltpu.VMEM((team, chips, tokens, part), bf16),
            pltpu.VMEM((chips - 1, team, tokens, part), bf16),
            pltpu.VMEM((chips - 1, team, tokens, part), bf16),
            pltpu.VMEM((team, tokens, part), f32),
            pltpu.VMEM((tokens, features), f32),
            pltpu.VMEM((chips, tokens, features), bf16),
            pltpu.VMEM((chips, tokens, features), bf16),
            pltpu.VMEM((chips, tokens, features), bf16),
            pltpu.VMEM((chips - 1, tokens, features), bf16),
            pltpu.VMEM((chips - 1, tokens, features), bf16),
            pltpu.VMEM((tokens, features), f32),
            pltpu.VMEM((2, part, width), bf16),
            pltpu.SemaphoreType.DMA((3,)),
            pltpu.SemaphoreType.DMA((4,)),
            pltpu.SemaphoreType.DMA((team,)),
            pltpu.SemaphoreType.DMA((team, chips - 1)),
            pltpu.SemaphoreType.DMA((chips,)),
            pltpu.SemaphoreType.DMA((chips - 1,)),
            pltpu.SemaphoreType.DMA((2,)),
            pltpu.SemaphoreType.DMA((2,)),
            pltpu.SemaphoreType.DMA((2,)),
            pltpu.SemaphoreType.DMA((chunk_shape[0], g_size)),
            pltpu.SemaphoreType.DMA((chunk_shape[0], g_size - 1)),
        ],
        compiler_params=pltpu.CompilerParams(
            collective_id=3, has_side_effects=True, vmem_limit_bytes=63 * 1024 * 1024
        ),
        name="highway_team_back",
    )(grad_lin, first_all, first, second, mixed, hidden, top, lstm_grads)


def every_coords(shift):
    g, t, y, x, c = axis_sizes()
    sizes = (g, t, y, x, c)
    coords, rest = {}, shift
    for name, size in list(zip(EVERY, sizes))[::-1]:
        coords[name] = lax.rem(lax.axis_index(name) + lax.rem(rest, size), size)
        rest = rest // size
    return coords


def every_place(coords):
    place = 0
    for name in EVERY:
        place = place * lax.axis_size(name) + coords[name]
    return place


def final_kernel(
    tight_from,
    bank_counts,
    grads_ref,
    tiled_ref,
    ids_ref,
    filter_ref,
    count_ref,
    lse_ref,
    upstream_ref,
    bias_ref,
    highway_ref,
    project_ref,
    sums_ref,
    conv_ref,
    table_ref,
    natural,
    grad_filters,
    table_sum,
    wide,
    tight,
    spread,
    y_recv,
    g_send,
    g_recv,
    kept,
    team_send,
    team_recv,
    bias_recv,
    small,
    small_team,
    small_send,
    small_grid,
    y_sems,
    g_sems,
    team_sems,
    small_sems,
    send_sems,
):
    grid, rows, lanes = grads_ref.shape
    team = team_size()
    g, t, y, x, c = axis_sizes()
    devices = bias_ref.shape[0]
    step = team_recv.shape[1]
    cut = step * team
    table_rows = table_ref.shape[0] // team
    f32, bf16 = jnp.float32, jnp.bfloat16
    here = every_place({name: lax.axis_index(name) for name in EVERY})
    place = team_place()
    bank = lax.rem(place, x * c)
    conv_ref[...] = jnp.zeros_like(conv_ref)
    barrier = pltpu.get_barrier_semaphore()

    @pl.loop(1, devices)
    def _(shift):
        pl.semaphore_signal(
            barrier, inc=1, device_id=every_coords(shift), device_id_type=pl.DeviceIdType.MESH
        )

    pl.semaphore_wait(barrier, devices - 1)
    pieces = [pl.ds(k * step, step) for k in range(team)] + [pl.ds(cut, rows - cut)]
    g_index, y_index = lax.axis_index("g"), lax.axis_index("y")
    other_y = lax.rem(y_index + 1, y)
    for k, piece in enumerate(pieces):
        for dg in list(range(1, g)) + [0]:
            send_grid(
                grads_ref.at[lax.rem(g_index + dg, g) * y + other_y, piece],
                y_recv.at[dg, piece],
                send_sems.at[0],
                y_sems.at[k, dg],
                0,
                1,
            )

    @pl.loop(1, devices)
    def _(shift):
        coords = every_coords(shift)
        pltpu.make_async_remote_copy(
            src_ref=bias_ref.at[every_place(coords)],
            dst_ref=bias_recv.at[here],
            send_sem=send_sems.at[3],
            recv_sem=small_sems.at[0],
            device_id=coords,
            device_id_type=pl.DeviceIdType.MESH,
        ).start()

    bias_recv[here] = bias_ref[here]
    run = upstream_ref.shape[1] // devices
    order = [
        (((ti * x + xi) * c + ci) * g + gi) * y + yi
        for gi in range(g)
        for ti in range(t)
        for yi in range(y)
        for xi in range(x)
        for ci in range(c)
    ]
    permuted = upstream_ref[...]
    natural[...] = jnp.concatenate([permuted[:, at * run : (at + 1) * run] for at in order], axis=1)
    grad_filters[...] = jnp.zeros_like(grad_filters)
    table_sum[...] = jnp.zeros_like(table_sum)

    def pass_on(k):
        piece = pieces[k]
        for dg in list(range(1, g)) + [0]:
            wait_bytes(y_recv.at[dg, piece], y_sems.at[k, dg])
            both = grads_ref[lax.rem(g_index + dg, g) * y + y_index, piece].astype(f32)
            both = both + y_recv[dg, piece].astype(f32)
            if dg == 0:
                kept[piece] = both
            else:
                g_send[dg - 1, piece] = both.astype(bf16)
                send_grid(
                    g_send.at[dg - 1, piece],
                    g_recv.at[g - dg - 1, piece],
                    send_sems.at[1],
                    g_sems.at[k, g - dg - 1],
                    dg,
                    0,
                )

    token_block = spread.shape[0]
    blocks = tiled_ref.shape[0] // token_block
    early = min(4, team)

    def pool_block(at):
        picked = pl.ds(pl.multiple_of(at * token_block, token_block), token_block)
        pool_grad_block(
            tight_from,
            tiled_ref.at[picked],
            ids_ref[pl.ds(at, 1)],
            filter_ref,
            count_ref,
            lse_ref.at[picked],
            natural.at[picked],
            grad_filters,
            table_sum,
            wide,
            tight,
            spread,
        )

    for k in range(early):

        @pl.loop(blocks * k // early, blocks * (k + 1) // early)
        def _(at):
            pool_block(at)

        pass_on(k)

    lane = lax.broadcasted_iota(jnp.int32, (LANES, LANES), 0)
    fold = jnp.where(
        (lane < TAPS)
        & (lax.rem(lane, EMBED) == lax.broadcasted_iota(jnp.int32, (LANES, LANES), 1)),
        1.0,
        0.0,
    ).astype(bf16)
    by_tap = table_sum[...]
    high = by_tap.astype(bf16)
    low = (by_tap - high.astype(f32)).astype(bf16)
    table = jnp.dot(high, fold, preferred_element_type=f32)
    table = (table + jnp.dot(low, fold, preferred_element_type=f32)).astype(bf16)
    starts, halves, at, column = [], [], 0, 0
    for half in range(t):
        for b, count in enumerate(bank_counts):
            starts.append(at)
            halves.append(count // t)
            at += count // t + table_rows
    for b, count in enumerate(bank_counts):
        for half in range(t):
            member = half * len(bank_counts) + b
            each = count // t
            turned = grad_filters[:, pl.ds(column, each)].T.astype(bf16)
            small[pl.ds(starts[member], each)] = turned
            column += each
    vocab = table_sum.shape[0]
    for member in range(team):
        top = min(table_rows, vocab - member * table_rows)
        begin = starts[member] + halves[member]
        if top > 0:
            small[pl.ds(begin, top)] = table[member * table_rows : member * table_rows + top]
        if top < table_rows:
            low_row = max(top, 0)
            small[pl.ds(begin + low_row, table_rows - low_row)] = jnp.zeros(
                (table_rows - low_row, LANES), bf16
            )
    for member in range(team):
        size = halves[member] + table_rows
        source = small.at[pl.ds(starts[member], size)]

        @pl.when(place == member)
        def _():
            small_team[member, pl.ds(0, size)] = small[pl.ds(starts[member], size)]

        @pl.when(place != member)
        def _():
            send_block(
                source,
                small_team.at[place, pl.ds(0, size)],
                send_sems.at[4],
                small_sems.at[1],
                member,
            )

    for k in range(early, team - 2):
        pass_on(k)
    home = grid_block(0, 0)
    for b, count in enumerate(bank_counts):
        size = count // t + table_rows

        @pl.when(bank == b)
        def _():
            wait_bytes(small_team.at[pl.ds(0, team - 1), pl.ds(0, size)], small_sems.at[1])
            total = small_team[0, pl.ds(0, size)].astype(f32)
            for origin in range(1, team):
                total = total + small_team[origin, pl.ds(0, size)].astype(f32)
            small_send[pl.ds(0, size)] = total.astype(bf16)
            small_grid[home, pl.ds(0, size)] = total.astype(bf16)
            for dg in range(g):
                for dy in range(y):
                    if dg or dy:
                        send_grid(
                            small_send.at[pl.ds(0, size)],
                            small_grid.at[home, pl.ds(0, size)],
                            send_sems.at[5],
                            small_sems.at[2],
                            dg,
                            dy,
                        )

    for k in range(team - 2, team + 1):
        pass_on(k)
    t_index = lax.axis_index("t")
    for b, count in enumerate(bank_counts):
        each = count // t
        size = each + table_rows

        @pl.when(bank == b)
        def _():
            wait_bytes(small_grid.at[pl.ds(0, grid - 1), pl.ds(0, size)], small_sems.at[2])
            total = small_grid[0, pl.ds(0, size)].astype(f32)
            for origin in range(1, grid):
                total = total + small_grid[origin, pl.ds(0, size)].astype(f32)
            mine = conv_ref.at[pl.ds(pl.multiple_of(t_index * each, each), each)]
            mine[...] = total[:each]
            for dt in range(1, t):
                send_block(
                    mine, mine, send_sems.at[6], small_sems.at[3], member_at(dt * x * c)
                )
            piece = table_ref.at[pl.ds(pl.multiple_of(place * table_rows, 16), table_rows)]
            piece[...] = total[each:]
            for offset in range(1, team):
                send_block(piece, piece, send_sems.at[7], small_sems.at[4], member_at(offset))

    for k, piece in enumerate(pieces):
        total = kept[piece]
        for dg in range(1, g):
            wait_bytes(g_recv.at[dg - 1, piece], g_sems.at[k, dg - 1])
            total = total + g_recv[dg - 1, piece].astype(f32)
        if k == team:
            project_ref[...] = total
        else:
            team_send[piece] = total.astype(bf16)

            @pl.when(place == k)
            def _():
                team_recv[k] = team_send[piece]

            @pl.when(place != k)
            def _():
                send_block(
                    team_send.at[piece], team_recv.at[place], send_sems.at[2], team_sems.at[0], k
                )

    wait_bytes(bias_recv.at[pl.ds(0, devices - 1)], small_sems.at[0])
    sums_ref[...] = jnp.sum(bias_recv[...].astype(f32), axis=0)
    wait_bytes(team_recv.at[pl.ds(0, team - 1)], team_sems.at[0])
    half_lanes = lanes // 2
    for half in range(2):
        parts = [
            team_recv[
                (ti * x + xi) * c + ci,
                :,
                half * half_lanes + (gi * y + yi) * run : half * half_lanes + (gi * y + yi + 1) * run,
            ]
            for gi in range(g)
            for ti in range(t)
            for yi in range(y)
            for xi in range(x)
            for ci in range(c)
        ]
        wide_half = half_lanes * team
        highway_ref[:, pl.ds(half * wide_half, wide_half)] = jnp.concatenate(parts, axis=1).astype(
            f32
        )
    for b, count in enumerate(bank_counts):
        each = count // t
        size = each + table_rows

        @pl.when(bank == b)
        def _():
            for _ in range(t - 1):
                wait_bytes(conv_ref.at[pl.ds(0, each)], small_sems.at[3])
                wait_bytes(conv_ref.at[pl.ds(0, each)], send_sems.at[6])
            wait_bytes(small_grid.at[pl.ds(0, grid - 1), pl.ds(0, size)], send_sems.at[5])

    wait_bytes(table_ref.at[pl.ds(0, (team - 1) * table_rows)], small_sems.at[4])
    wait_bytes(table_ref.at[pl.ds(0, (team - 1) * table_rows)], send_sems.at[7])
    wait_bytes(y_recv, send_sems.at[0])
    wait_bytes(g_recv, send_sems.at[1])
    wait_bytes(team_recv.at[pl.ds(0, team - 1)], send_sems.at[2])
    wait_bytes(bias_recv.at[pl.ds(0, devices - 1)], send_sems.at[3])
    for member in range(team):

        @pl.when(place != member)
        def _():
            size = halves[member] + table_rows
            wait_bytes(small.at[pl.ds(starts[member], size)], send_sems.at[4])


def run_final(tight_from, bank_counts, grads, tiled, ids, filters, counts, lse, upstream, biases, step):
    grid, rows, lanes = grads.shape
    team = team_size()
    g, t, y, x, c = axis_sizes()
    tokens, features = upstream.shape
    devices, bias_rows, _ = biases.shape
    bf16, f32 = jnp.bfloat16, jnp.float32
    vmem = pl.BlockSpec(memory_space=pltpu.VMEM)
    token_block = math.gcd(tokens, TOKEN_BLOCK)
    vocab = -(-VOCAB // 16) * 16
    table_rows = -(-vocab // (16 * team)) * 16
    most = max(bank_counts) // t + table_rows
    return pl.pallas_call(
        partial(final_kernel, tight_from, bank_counts),
        in_specs=[vmem] * 8,
        out_specs=[vmem] * 5,
        out_shape=[
            jax.ShapeDtypeStruct((step, lanes * team), f32),
            jax.ShapeDtypeStruct((rows - team * step, lanes), f32),
            jax.ShapeDtypeStruct((bias_rows, LANES), f32),
            jax.ShapeDtypeStruct((max(bank_counts), LANES), f32),
            jax.ShapeDtypeStruct((team * table_rows, LANES), f32),
        ],
        scratch_shapes=[
            pltpu.VMEM((tokens, features), bf16),
            pltpu.VMEM((LANES, features), f32),
            pltpu.VMEM((vocab, LANES), f32),
            pltpu.VMEM((token_block * PLACES, LANES), bf16),
            pltpu.VMEM((token_block * TIGHT, LANES), bf16),
            pltpu.VMEM((token_block, PLACES, LANES), f32),
            pltpu.VMEM((g, rows, lanes), bf16),
            pltpu.VMEM((g - 1, rows, lanes), bf16),
            pltpu.VMEM((g - 1, rows, lanes), bf16),
            pltpu.VMEM((rows, lanes), f32),
            pltpu.VMEM((rows, lanes), bf16),
            pltpu.VMEM((team, step, lanes), bf16),
            pltpu.VMEM(biases.shape, bf16),
            pltpu.VMEM((sum(bank_counts) + team * table_rows, LANES), bf16),
            pltpu.VMEM((team, most, LANES), bf16),
            pltpu.VMEM((most, LANES), bf16),
            pltpu.VMEM((grid, most, LANES), bf16),
            pltpu.SemaphoreType.DMA((team + 1, g)),
            pltpu.SemaphoreType.DMA((team + 1, g - 1)),
            pltpu.SemaphoreType.DMA((1,)),
            pltpu.SemaphoreType.DMA((5,)),
            pltpu.SemaphoreType.DMA((8,)),
        ],
        compiler_params=pltpu.CompilerParams(
            collective_id=4, has_side_effects=True, vmem_limit_bytes=60 * 1024 * 1024
        ),
        name="final_sums",
    )(grads, tiled, ids, filters, counts, lse, upstream, biases)


def pack_kernel(parts, received_ref, out_ref):
    team, rows, lanes = received_ref.shape
    each = lanes // parts
    for member in range(team):
        for part in range(parts):
            out_ref[:, pl.ds((part * team + member) * each, each)] = received_ref[
                member, pl.ds(0, out_ref.shape[0]), pl.ds(part * each, each)
            ].astype(jnp.float32)


def pack_columns(received, parts, rows):
    team, _, lanes = received.shape
    return pl.pallas_call(
        partial(pack_kernel, parts),
        in_specs=[pl.BlockSpec(memory_space=pltpu.VMEM)],
        out_specs=pl.BlockSpec(memory_space=pltpu.VMEM),
        out_shape=jax.ShapeDtypeStruct((rows, team * lanes), jnp.float32),
        compiler_params=pltpu.CompilerParams(vmem_limit_bytes=40 * 1024 * 1024),
        name="pack_columns",
    )(received)


def axis_sizes():
    return tuple(lax.axis_size(name) for name in EVERY)


def run_rows(received):
    g, t, y, x, c = axis_sizes()
    lanes = received.shape[-1]
    split = received.reshape(t, x * c, 2, -1, lanes).transpose(0, 2, 1, 3, 4)
    return split.reshape(t, 2, -1, lanes)


def member_rows(runs):
    g, t, y, x, c = axis_sizes()
    lanes = runs.shape[-1]
    split = runs.reshape(t, 2, x * c, -1, lanes).transpose(0, 2, 1, 3, 4)
    return split.reshape(t * x * c, -1, lanes)


def team_slices(values, parts):
    team = team_size()
    two, rows, columns = values.shape
    lanes = columns // (parts * team)
    split = values.reshape(two, rows, parts, team, lanes).transpose(3, 0, 1, 2, 4)
    return split.reshape(team, two * rows, parts * lanes)


def whole_columns(received, parts):
    team, two_rows, lanes = received.shape
    split = received.reshape(team, 2, two_rows // 2, parts, lanes // parts)
    return split.transpose(1, 2, 3, 0, 4).reshape(2, two_rows // 2, team * lanes)


def team_first(values):
    g, t, y, x, c = axis_sizes()
    rows = values.shape[0]
    split = values.reshape(rows, -1, g, t, y, x, c, values.shape[1] // (2 * g * t * y * x * c))
    return split.transpose(3, 5, 6, 0, 1, 2, 4, 7)


def permuted_columns(values):
    g, t, y, x, c = axis_sizes()
    split = values.reshape(values.shape[0], g, t, y, x, c, -1)
    return split.transpose(0, 2, 4, 5, 1, 3, 6).reshape(values.shape)


def restored_columns(values):
    g, t, y, x, c = axis_sizes()
    split = values.reshape(values.shape[0], t, x, c, g, y, -1)
    return split.transpose(0, 4, 1, 5, 2, 3, 6).reshape(values.shape)


def padded_rows(values, rows):
    blocks = values.shape[0]
    flat = values.reshape(blocks, -1)
    return jnp.pad(flat, ((0, 0), (0, rows * LANES - flat.shape[1]))).reshape(blocks, rows, LANES)


def row_count(items):
    return -(-items // LANES)


def bank_filters(turned, bank, bank_cols):
    taps = [
        [width * EMBED for width, first, count in bank_specs for _ in range(count)]
        for bank_specs in bank_plan(bank_cols)
    ]
    taps = [row + [0] * (bank_cols - len(row)) for row in taps]
    limit = lax.dynamic_index_in_dim(jnp.asarray(taps, jnp.int32), bank, 0, False)
    turned = turned.T
    row = lax.broadcasted_iota(jnp.int32, (TAPS, 1), 0)
    kernel = jnp.where(row < limit[None, :], turned[:TAPS], 0.0)
    bias = jnp.where(limit > 0, turned[TAPS], 0.0)
    return (kernel.reshape(1, WIDEST, EMBED, bank_cols), bias[None])


def shards(
    char_ids,
    resets,
    out_grad,
    char_table,
    conv_weight,
    conv_bias,
    highway_weight,
    highway_bias,
    proj_weight,
    proj_bias,
    lstm_weight,
    lstm_bias,
    lstm_proj,
):
    f32, bf16 = jnp.float32, jnp.bfloat16
    own, steps = resets.shape
    team = team_size()
    place = team_place()
    devices = team * lax.axis_size("g") * lax.axis_size("y")
    bank_cols = conv_weight.shape[3]
    highway_rows = highway_weight.shape[1]
    features_all = highway_rows * devices
    part = features_all // team
    lstm_rows = lstm_weight.shape[1]
    width = proj_weight.shape[1]
    cells_all = lstm_proj.shape[1]
    cells = cells_all // team

    conv_own = jnp.concatenate([conv_weight.reshape(-1, bank_cols), conv_bias], axis=0)
    banks = lax.axis_size("x") * lax.axis_size("c")
    conv_all = lax.all_to_all(
        jnp.broadcast_to(conv_own[None], (banks,) + conv_own.shape),
        ("x", "c"),
        split_axis=0,
        concat_axis=0,
        tiled=True,
    )
    conv_weight_all = conv_all[:, :-1].reshape((banks,) + conv_weight.shape[1:])
    conv_bias_all = conv_all[:, -1]
    sizes = [highway_bias.size, proj_bias.size, lstm_bias.size, resets.size]
    small = jnp.concatenate(
        [
            highway_bias.reshape(-1),
            proj_bias.reshape(-1),
            lstm_bias.reshape(-1),
            resets.astype(bf16).reshape(-1),
        ]
    )
    small_all = lax.all_to_all(
        jnp.broadcast_to(small[None], (devices, small.size)),
        EVERY,
        split_axis=0,
        concat_axis=0,
        tiled=True,
    )
    cut = [sum(sizes[:k]) for k in range(5)]
    highway_bias_all = small_all[:, cut[0] : cut[1]].reshape(devices, 2, -1)
    highway_bias_all = highway_bias_all.transpose(1, 0, 2).reshape(2, 2 * features_all)
    highway_bias_all = team_first(highway_bias_all).reshape(team, 2, 2 * part)
    proj_bias_all = small_all[:, cut[1] : cut[2]].reshape(-1).astype(f32)
    lstm_bias_all = small_all[:, cut[2] : cut[3]].reshape(devices, 2, -1)
    lstm_bias_all = lstm_bias_all.transpose(1, 0, 2).reshape(2, 4, team, cells)
    resets_all = small_all[:, cut[3] : cut[4]].reshape(
        lax.axis_size("g"), lax.axis_size("t"), lax.axis_size("y"), -1, own, steps
    )
    resets_team = lax.dynamic_index_in_dim(resets_all, lax.axis_index("g"), 0, False)
    resets_team = lax.dynamic_index_in_dim(resets_team, lax.axis_index("y"), 1, False)
    resets_team = resets_team.reshape(team * own, steps).astype(f32)
    highway_bias_own = lax.dynamic_index_in_dim(highway_bias_all, place, 0, False).astype(f32)
    lstm_bias_own = lax.dynamic_index_in_dim(lstm_bias_all, place, 2, False)
    lstm_bias_own = lstm_bias_own.reshape(2, 1, 4 * cells).astype(f32)

    highway_slices = team_first(highway_weight.reshape(2 * highway_rows, -1))
    turned_rows = lstm_proj.shape[2]
    gate_slices = lstm_weight.reshape(2, lstm_rows, 4, team, cells).transpose(3, 0, 2, 1, 4)
    swapped = swap_team(highway_slices.reshape(team, 2 * highway_rows, 2 * part))
    block = swapped.reshape(team, 2, highway_rows, 2 * part).transpose(1, 0, 2, 3)
    block = jnp.concatenate([block.reshape(-1, 2 * part), proj_weight], axis=0)
    t, x, c = lax.axis_size("t"), lax.axis_size("x"), lax.axis_size("c")
    lstm_block = gate_slices.reshape(team, 8 * lstm_rows, cells)
    turned_block = team_slices(jnp.swapaxes(lstm_proj, 1, 2), 1)
    direct = lstm_rows % 16 == 0 and turned_rows % 16 == 0
    if not direct:
        lstm_block = (
            swap_team(lstm_block)
            .reshape(t, x * c, 8, lstm_rows, cells)
            .transpose(0, 2, 1, 3, 4)
            .reshape(t * 8, x * c * lstm_rows, cells)
        )
        turned_block = run_rows(swap_team(turned_block))
    cut_rows = team * 2 * highway_rows
    grid = lax.axis_size("g") * lax.axis_size("y")
    bank = lax.axis_index("x") * lax.axis_size("c") + lax.axis_index("c")
    own_ids = lax.dynamic_slice_in_dim(char_ids, bank * own, own, axis=0)
    own_ids = jnp.swapaxes(own_ids, 0, 1).reshape(own * steps, char_ids.shape[2])
    filters, counts = filter_matrix(conv_weight_all, conv_bias_all)
    tight_from = wide_columns(bank_cols)
    padded_ids, tiled = embed_tokens(own_ids, char_table)

    tokens = own * steps
    (
        pooled_lse,
        first_all,
        lstm_own,
        turned_own,
        first,
        second,
        mixed,
        hidden,
        top_own,
        lin_all,
    ) = run_highway(
        tight_from,
        direct,
        tiled,
        filters,
        counts,
        block,
        lstm_block,
        turned_block,
        highway_bias_own,
        proj_bias_all[None],
    )
    lstm_own = lstm_own.reshape(grid, t, 2, 4, x * c * lstm_rows, cells)

    keep_forward = 1.0 - resets_team
    keep_backward = 1.0 - jnp.concatenate(
        [resets_team[:, 1:], jnp.zeros((team * own, 1), f32)], axis=1
    )
    keep = jnp.stack([keep_forward.T, keep_backward.T])[..., None]
    grad_time = out_grad.reshape(own, steps, 2, width).transpose(2, 1, 0, 3)
    grad_lin_all, lstm_grads, turned_grads, bias_sums = run_lstm(
        lin_all.reshape(team, steps, own, width),
        grad_time,
        lstm_own,
        turned_own,
        lstm_bias_own,
        keep,
    )
    turned_summed = lax.all_to_all(turned_grads, GRID, split_axis=0, concat_axis=0, tiled=True)
    turned_summed = turned_summed.astype(f32).sum(axis=0).astype(bf16)
    grad_input = lax.dynamic_index_in_dim(grad_lin_all, place, 0, False).reshape(tokens, width)
    grad_project_b = column_sum(grad_input)
    grad_features, first_parts, highway_bias_sums, lstm_summed = run_highway_back(
        grad_lin_all.reshape(team, tokens, width),
        first_all,
        first,
        second,
        mixed,
        hidden,
        top_own,
        lstm_grads.reshape(grid, 8, -1, 4 * cells),
    )
    lstm_summed = lstm_summed.reshape(t, 2, -1, 4 * cells)
    lstm_returned = swap_team(
        jnp.concatenate(
            [
                member_rows(lstm_summed),
                member_rows(turned_summed).reshape(team, -1, 4 * cells),
            ],
            axis=1,
        )
    )
    g, t, y, x, c = axis_sizes()

    def own_place(values, parts):
        lanes = values.shape[-1] // parts
        split = values.reshape(2, parts, 1, lanes)
        full = jnp.zeros((2, parts, team, lanes), f32)
        return lax.dynamic_update_slice(full, split, (0, 0, place, 0)).reshape(2, -1)

    lstm_bias_parts = own_place(bias_sums[:, 0], 4)
    highway_bias_parts = own_place(highway_bias_sums[:, 0], 2)
    highway_bias_parts = (
        highway_bias_parts.reshape(2, 2, t, x, c, g, y, -1)
        .transpose(0, 1, 5, 2, 6, 3, 4, 7)
        .reshape(2, 2 * features_all)
    )
    biases = jnp.concatenate(
        [
            lstm_bias_parts.reshape(2, devices, -1).transpose(1, 0, 2).reshape(devices, -1),
            highway_bias_parts.reshape(2, devices, -1).transpose(1, 0, 2).reshape(devices, -1),
            grad_project_b.reshape(devices, -1),
        ],
        axis=1,
    )
    bank_counts = [sum(item[2] for item in specs) for specs in bank_plan(bank_cols)]
    bias_rows = -(-row_count(biases.shape[1]) // 16) * 16
    highway_weight_grad, project_grad, mine, conv_sums, table_sums = run_final(
        tight_from,
        bank_counts,
        first_parts,
        tiled,
        padded_ids.reshape(-1, math.gcd(tokens, TOKEN_BLOCK) * PLACES),
        filters,
        counts,
        pooled_lse,
        grad_features,
        padded_rows(biases, bias_rows).astype(bf16),
        2 * highway_rows,
    )
    lstm_weight_grad = pack_columns(lstm_returned, 4, 2 * lstm_rows).reshape(2, lstm_rows, -1)
    turned_back = lstm_returned[:, 2 * lstm_rows :].reshape(team, 2 * turned_rows, cells)
    lstm_proj_grad = jnp.swapaxes(whole_columns(turned_back, 1).astype(f32), 1, 2)
    highway_weight_grad = highway_weight_grad.reshape(2, highway_rows, -1)
    mine_biases = mine.reshape(-1)
    ends = [2 * lstm_bias.shape[1], 2 * lstm_bias.shape[1] + 2 * highway_bias.shape[1]]
    lstm_bias_grad = mine_biases[: ends[0]].reshape(2, -1)
    highway_bias_grad = mine_biases[ends[0] : ends[1]].reshape(2, -1)
    proj_bias_grad = mine_biases[ends[1] : ends[1] + proj_bias.size]
    grad_kernel, grad_bias = bank_filters(conv_sums, bank, bank_cols)
    grad_table = table_sums[: char_table.shape[0], :EMBED]
    return (
        grad_table,
        grad_kernel,
        grad_bias,
        highway_weight_grad,
        highway_bias_grad,
        project_grad,
        proj_bias_grad,
        lstm_weight_grad,
        lstm_bias_grad,
        lstm_proj_grad,
    )


def solution(mesh):
    dp, bank = mesh.shape["dp"], mesh.shape["bank"]
    fine = Mesh(mesh.devices.reshape(dp // 4, 2, 2, bank // 2, 2), EVERY)
    rows, banks = ("g", "t", "y"), ("x", "c")
    whole = rows + banks
    placed = (
        P(rows, None, None),
        P(whole, None),
        P(whole, None, None),
        P(),
        P(banks, None, None, None),
        P(banks, None),
        P(None, whole, None),
        P(None, whole),
        P(whole, None),
        P(whole),
        P(None, whole, None),
        P(None, whole),
        P(None, None, whole),
    )
    return jax.shard_map(
        shards,
        mesh=fine,
        in_specs=placed,
        out_specs=(
            P(),
            P(banks, None, None, None),
            P(banks, None),
            P(None, whole, None),
            P(None, whole),
            P(whole, None),
            P(whole),
            P(None, whole, None),
            P(None, whole),
            P(None, None, whole),
        ),
        check_vma=False,
    )
```
